32 devices in a mesh: seq: 4 (over x, core), batch: 8 (over z, y).
Axes of the slice: x: 2, y: 2, z: 4, core: 2. Of those that a mesh axis runs over, the one named last changes fastest.
Arguments:
- residual: float32 [8, 2048, 767], P('batch', 'seq'), may hold values from -6 to 6
- documents: int32 [8, 2048], P('batch', 'seq'), may hold values from 1 to 16383, as said below
- gain_one: float32 [768], replicated, may hold values from 0.25 to 1.75
- gain_two: float32 [768], replicated, may hold values from 0.25 to 1.75
- w_qkv: bfloat16 [768, 2304], replicated, may hold values from -0.3125 to 0.3125
- w_out: bfloat16 [768, 768], replicated, may hold values from -0.4375 to 0.4375
- w_up: bfloat16 [768, 3072], replicated, may hold values from -0.21875 to 0.21875
- w_down: bfloat16 [3072, 768], replicated, may hold values from -0.109375 to 0.109375
- cotangent: float32 [8, 2048, 767], P('batch', 'seq'), may hold values from -6 to 6
Outputs:
- new_residual: float32 [8, 2048, 767], P('batch', 'seq')
- residual_grad: float32 [8, 2048, 767], P('batch', 'seq')
- gain_one_grad: float32 [768], P('seq')
- gain_two_grad: float32 [768], P('seq')
- w_qkv_grad: float32 [768, 2304], P('seq')
- w_out_grad: float32 [768, 768], P('seq')
- w_up_grad: float32 [768, 3072], P('seq')
- w_down_grad: float32 [3072, 768], P('seq')
The draws below stay inside these ranges and needn't reach their ends.
Inputs may be any that keep to these rules, and one draw needn't show every extreme that they name: `documents`: every document is one unbroken run within a row, or the end of one row's last document followed by the start of the next row's first; the last row's last document, with id 8 * 2048 - 1, continues at the start of the first row. Within a row, ids after its first document rise. A continued document lies within the last 512 positions of the earlier row and the first 512 positions of the later one. No other document has tokens in two rows. In every row some document begins within its first 512 positions and ends within its last 512.
All inputs are finite; a program needn't handle non-finite values.
Results may differ from the reference program's by a relative error of at most 0.04.
Values may be sent and summed in bfloat16 or wider, within the bound.
A program may use at most 192 MiB of HBM per device.

```python
import math
import jax
import jax.numpy as jnp
from jax import lax

D = 768
H = 12
HD = 64
FF = 3072
TOK_DEV = 512
DC = 767
ROW = 2048
ROWS = 8


def draw_documents(key, part):
    key = jax.random.fold_in(key, 7)
    subkeys = jax.random.split(key, 5)
    half_block = TOK_DEV // 2
    head_end = jax.random.randint(subkeys[0], (ROWS, 1), 1, half_block + 1)
    middle_start = head_end + jax.random.randint(subkeys[1], (ROWS, 1), 0, half_block)
    middle_end = ROW - TOK_DEV + jax.random.randint(subkeys[2], (ROWS, 1), 1, half_block + 1)
    tail_start = middle_end + jax.random.randint(subkeys[3], (ROWS, 1), 1, half_block)
    position = jnp.arange(ROW, dtype=jnp.int32)[None, :]
    extra_cut = jax.random.randint(subkeys[4], (ROWS, ROW), 0, 32) == 0
    inner_zone = (position > head_end) & (position < middle_start) | (position > middle_end) & (position < tail_start)
    starts = (position == head_end) | (position == middle_start) | (position == middle_end) | (position == tail_start) | extra_cut & inner_zone
    local_ids = jnp.cumsum(starts.astype(jnp.int32), axis=1)
    last_local = local_ids[:, -1]
    row_base = jnp.arange(ROWS, dtype=jnp.int32) * ROW
    global_ids = row_base[:, None] + local_ids
    carried = jnp.concatenate([jnp.full((1,), ROWS * ROW - 1, jnp.int32), (row_base + last_local)[:-1]])
    ids = jnp.where(local_ids == 0, carried[:, None], global_ids)
    row_number = jnp.arange(ROWS, dtype=jnp.int32)[:, None]
    final_doc = (row_number == ROWS - 1) & (local_ids == last_local[:, None]) & (local_ids > 0)
    return jnp.where(final_doc, ROWS * ROW - 1, ids).astype(jnp.int32)


def levels(key, dims, shards, least, high):
    loudness = 1.0
    for dim, parts in shards:
        heights = jax.random.uniform(jax.random.fold_in(jax.random.fold_in(key, 6), dim), (parts,), jnp.float32, least / len(shards), high / len(shards))
        loudness = loudness * jnp.repeat(jnp.exp(heights), dims[dim] // parts).reshape((-1,) + (1,) * (len(dims) - 1 - dim))
    return loudness


def noise(key, shape, spread, reach, cuts=(), kind=jnp.bfloat16):
    entries = jax.random.normal(key, shape, jnp.float32) * spread
    if len(cuts) > 0:
        entries = levels(key, shape, cuts, -0.22, 0.18) * entries
    return jnp.clip(entries, min=-reach, max=reach).astype(kind)


def setup_inputs(seed: int = 0) -> dict:
    streams_of = jax.random.split(jax.random.key(seed), 10)
    return {
        "residual": noise(streams_of[0], (ROWS, ROW, DC), 1.0, 6.0, ((0, 8), (1, 4)), jnp.float32),
        "documents": draw_documents(jax.random.fold_in(streams_of[9], 71), 0),
        "gain_one": jnp.clip(1.0 + 0.15 * jax.random.normal(streams_of[2], (D,), jnp.float32), 0.25, 1.75),
        "gain_two": jnp.clip(1.0 + 0.15 * jax.random.normal(streams_of[3], (D,), jnp.float32), 0.25, 1.75),
        "w_qkv": noise(streams_of[4], (D, 3 * D), (D // 2) ** -0.5, 0.3125),
        "w_out": noise(streams_of[5], (D, D), (D // 4) ** -0.5, 0.4375),
        "w_up": noise(streams_of[6], (D, FF), D ** -0.5, 0.21875),
        "w_down": noise(streams_of[7], (FF, D), FF ** -0.5, 0.109375),
        "cotangent": noise(streams_of[8], (ROWS, ROW, DC), 1.0, 6.0, ((0, 8), (1, 4)), jnp.float32),
    }


EPSILON = 1e-06
MASKED = -1e+30
PRECISE = lax.Precision.HIGHEST

@jax.custom_vjp
def low(v):
    return lax.optimization_barrier(v.astype(jnp.bfloat16)).astype(jnp.float32)

@jax.custom_vjp
def low_back(v):
    return v

def low_keep(v):
    return (low(v), None)

def low_pass(kept, grad):
    return (grad,)

def back_keep(v):
    return (v, None)

def back_low(kept, grad):
    return (low(grad),)
low.defvjp(low_keep, low_pass)
low_back.defvjp(back_keep, back_low)

def expand(narrow):
    return jnp.concatenate([narrow, -lax.optimization_barrier(jnp.sum(narrow, axis=-1, keepdims=True))], axis=-1)

def shrink(full_vec):
    return full_vec[..., :-1] - lax.optimization_barrier(jnp.mean(full_vec, axis=-1, keepdims=True))

def crms_norm(narrow, gain_vec):
    full_vec = expand(narrow)
    return gain_vec * full_vec * lax.rsqrt(lax.optimization_barrier(jnp.mean(full_vec * full_vec, axis=-1, keepdims=True)) + EPSILON)

def row_attention(operands):
    queries, key_rows, value_rows, query_docs, key_docs = operands
    query_pos = jnp.arange(ROW, dtype=jnp.int32)
    key_pos = jnp.concatenate([jnp.full((TOK_DEV,), -1, jnp.int32), query_pos])
    scores = jnp.einsum('qhd,khd->hqk', queries, key_rows, precision=PRECISE) * (1.0 / math.sqrt(HD))
    scores = low_back(scores)
    pairs = (query_docs[:, None] == key_docs[None, :]) & (key_pos[None, :] <= query_pos[:, None])
    scores = jnp.where(pairs[None], scores, MASKED)
    peak_value = lax.optimization_barrier(jnp.max(scores, axis=-1, keepdims=True))
    log_total = jnp.log(lax.optimization_barrier(jnp.sum(jnp.exp(scores - peak_value), axis=-1, keepdims=True))) + peak_value
    attn_probs = low(jnp.exp(scores - log_total))
    return jnp.einsum('hqk,khd->qhd', attn_probs, value_rows, precision=PRECISE)

def earlier(block):
    tail_part = block[:, ROW - TOK_DEV:]
    return jnp.concatenate([tail_part[-1:], tail_part[:-1]], axis=0)

def layer(residual, gain_one, gain_two, w_qkv, w_out, w_up, w_down, documents):
    h_one = low(crms_norm(residual, gain_one))
    packed = low_back(low(jnp.matmul(h_one, w_qkv, precision=PRECISE)))
    heads_split = packed.reshape(ROWS, ROW, 3, H, HD)
    queries = heads_split[:, :, 0]
    key_rows = heads_split[:, :, 1]
    value_rows = heads_split[:, :, 2]
    all_keys = jnp.concatenate([earlier(key_rows), key_rows], axis=1)
    all_values = jnp.concatenate([earlier(value_rows), value_rows], axis=1)
    all_docs = jnp.concatenate([earlier(documents), documents], axis=1)
    attended = lax.map(jax.checkpoint(row_attention), (queries, all_keys, all_values, documents, all_docs))
    attended = low_back(low(attended.reshape(ROWS, ROW, D)))
    branch_one = low_back(jnp.matmul(attended, w_out, precision=PRECISE))
    middle = residual + shrink(branch_one)
    h_two = low(crms_norm(middle, gain_two))
    up_proj = low_back(jnp.matmul(h_two, w_up, precision=PRECISE))
    gelu_out = low(jax.nn.gelu(up_proj))
    branch_two = low_back(jnp.matmul(gelu_out, w_down, precision=PRECISE))
    return middle + shrink(branch_two)

def reference(residual, documents, gain_one, gain_two, w_qkv, w_out, w_up, w_down, cotangent):

    def forward(residual, gain_one, gain_two, w_qkv, w_out, w_up, w_down):
        return layer(residual, gain_one, gain_two, w_qkv, w_out, w_up, w_down, documents)
    new_residual, pullback = jax.vjp(forward, residual, gain_one, gain_two, w_qkv.astype(jnp.float32), w_out.astype(jnp.float32), w_up.astype(jnp.float32), w_down.astype(jnp.float32))
    grads = pullback(cotangent)
    return (new_residual, grads[0], grads[1], grads[2], grads[3], grads[4], grads[5], grads[6])
```

```python
import functools
import math

import jax
import jax.numpy as jnp
from jax import lax
from jax.experimental import pallas as pl
from jax.experimental.pallas import tpu as pltpu
from jax.sharding import PartitionSpec as P

H = 12
HD = 64
EPSILON = 1e-06
NEG = -1e30
F32, BF16 = jnp.float32, jnp.bfloat16
VMEM_LIMIT = 56 * 2**20


def passed_along(block, axis, distance):
    devices = range(lax.axis_size(axis))
    route = [((i - distance) % len(devices), i) for i in devices]
    return lax.ppermute(block, axis, route)


def expand(narrow):
    return jnp.concatenate([narrow, -jnp.sum(narrow, axis=-1, keepdims=True)], axis=-1)


def shrink(full_vec):
    return full_vec[..., :-1] - jnp.mean(full_vec, axis=-1, keepdims=True)


def shrink_back(grad_narrow):
    padded = jnp.concatenate([grad_narrow, jnp.zeros_like(grad_narrow[..., :1])], axis=-1)
    return padded - jnp.sum(grad_narrow, axis=-1, keepdims=True) / padded.shape[-1]


def crms_norm(narrow, gain_vec):
    full_vec = expand(narrow)
    return (
        gain_vec
        * full_vec
        * lax.rsqrt(jnp.mean(full_vec * full_vec, axis=-1, keepdims=True) + EPSILON)
    )


def dot(a, b):
    return lax.dot_general(a, b, (((1,), (0,)), ((), ())), preferred_element_type=F32)


def masked(s, key_docs, query_docs, key_at, query_at, causal, docs, fill):
    keep = None
    if docs:
        keep = key_docs == query_docs
    if causal:
        key_pos = lax.broadcasted_iota(jnp.int32, s.shape, 0) + key_at
        query_pos = lax.broadcasted_iota(jnp.int32, s.shape, 1) + query_at
        earlier = key_pos <= query_pos
        keep = earlier if keep is None else keep & earlier
    return s if keep is None else jnp.where(keep, s, fill)


def fwd_kernel(tok, blocks, heads, k_ref, qT_ref, vT_ref, dk_ref, dq_ref, oT_ref, lse_ref):
    def head(h, carry):
        for i in range(blocks):
            q0 = i * tok
            qT = qT_ref[h, :, q0 : q0 + tok]
            docs_q = dq_ref[:, q0 : q0 + tok]
            m = jnp.full((1, tok), NEG, F32)
            total = jnp.zeros((1, tok), F32)
            acc = jnp.zeros(qT.shape, F32)
            edge = i == 0 or i == blocks - 1
            chunks = [(0, False, True)] if i == 0 else []
            for j in range(i):
                chunks.append(((j + 1) * tok, False, j == 0 or edge))
            chunks.append(((i + 1) * tok, True, edge))
            for k0, causal, docs in chunks:
                keys = slice(k0, k0 + tok)
                s = dot(k_ref[h, keys, :], qT)
                docs_k = dk_ref[keys, :] if docs else None
                s = masked(s, docs_k, docs_q, k0 - tok, q0, causal, docs, NEG)
                new_m = jnp.maximum(m, jnp.max(s, axis=0, keepdims=True))
                p = jnp.exp(s - new_m)
                shift = jnp.exp(m - new_m)
                total = total * shift + jnp.sum(p, axis=0, keepdims=True)
                acc = acc * shift + dot(vT_ref[h, :, keys], p.astype(BF16))
                m = new_m
            oT_ref[h, :, q0 : q0 + tok] = acc / total
            lse_ref[h, :, q0 : q0 + tok] = m + jnp.log(total)
        return carry

    lax.fori_loop(0, heads, head, 0)


def pairs_of(i, tok, blocks, sub):
    out = []
    if i == 0:
        out.append((0, tok, 0, tok, False, True))
    edge = i == 0 or i == blocks - 1
    for j in range(i):
        out.append(((j + 1) * tok, tok, 0, tok, False, j == 0 or edge))
    for a in range(tok // sub):
        out.append(((i + 1) * tok + a * sub, sub, a * sub, tok - a * sub, True, edge))
    return out


def bwd_kernel(
    tok, blocks, heads, sub,
    k_ref, kT_ref, v_ref, q_ref, qT_ref, do_ref, doT_ref, oT_ref, lse_ref, dk_ref, dq_ref,
    dqT_out, dk_out, dv_out, delta,
):
    def head(h, carry):
        for i in range(blocks):
            sl = slice(i * tok, (i + 1) * tok)
            delta[:, sl] = jnp.sum(
                doT_ref[h, :, sl].astype(F32) * oT_ref[h, :, sl], axis=0, keepdims=True
            )
        dk_out[h] = jnp.zeros_like(dk_out[h])
        dv_out[h] = jnp.zeros_like(dv_out[h])
        dqT_out[h] = jnp.zeros_like(dqT_out[h])
        for i in range(blocks):
            q0 = i * tok
            for k0, kw, qo, qw, causal, docs in pairs_of(i, tok, blocks, sub):
                ks, qs = slice(k0, k0 + kw), slice(q0 + qo, q0 + qo + qw)
                s = dot(k_ref[h, ks, :], qT_ref[h, :, qs])
                p = jnp.exp(s - lse_ref[h, :, qs])
                docs_k = dk_ref[ks, :] if docs else None
                p = masked(p, docs_k, dq_ref[:, qs], k0 - tok, q0 + qo, causal, docs, 0.0)
                dp = dot(v_ref[h, ks, :], doT_ref[h, :, qs])
                ds = (p * (dp - delta[:, qs])).astype(BF16)
                dv_out[h, ks, :] += dot(p.astype(BF16), do_ref[h, qs, :])
                dk_out[h, ks, :] += dot(ds, q_ref[h, qs, :])
                dqT_out[h, :, qs] += dot(kT_ref[h, :, ks], ds)
        return carry

    lax.fori_loop(0, heads, head, 0)


def attend(k, qT, vT, docs_k, docs_q, tok):
    heads, hd, row = qT.shape
    return pl.pallas_call(
        functools.partial(fwd_kernel, tok, row // tok, heads),
        out_shape=[
            jax.ShapeDtypeStruct((heads, hd, row), F32),
            jax.ShapeDtypeStruct((heads, 1, row), F32),
        ],
        compiler_params=pltpu.CompilerParams(vmem_limit_bytes=VMEM_LIMIT),
    )(k, qT, vT, docs_k, docs_q)


def attend_back(k, kT, v, q, qT, do, doT, oT, lse, docs_k, docs_q, tok):
    heads, hd, row = qT.shape
    return pl.pallas_call(
        functools.partial(bwd_kernel, tok, row // tok, heads, tok // 2),
        out_shape=[
            jax.ShapeDtypeStruct((heads, hd, row), F32),
            jax.ShapeDtypeStruct(k.shape, F32),
            jax.ShapeDtypeStruct(k.shape, F32),
        ],
        scratch_shapes=[pltpu.VMEM((1, row), F32)],
        compiler_params=pltpu.CompilerParams(vmem_limit_bytes=VMEM_LIMIT),
    )(k, kT, v, q, qT, do, doT, oT, lse, docs_k, docs_q)


def per_device(residual, documents, gain_one, gain_two, w_qkv, w_out, w_up, w_down, cotangent):
    seq_count = lax.axis_size("seq")
    place = lax.axis_index("seq")
    narrow = residual[0]
    tok = narrow.shape[0]
    width = w_out.shape[0]
    row = seq_count * tok
    heads = H // seq_count
    mine = heads * HD
    scale = 1.0 / math.sqrt(HD)

    h_one = crms_norm(narrow, gain_one).astype(BF16)
    h_all = lax.all_gather(h_one, "seq", axis=0, tiled=True)
    row_docs = lax.all_gather(documents[0], "seq", axis=0, tiled=True)
    w_mine = lax.dynamic_slice_in_dim(w_qkv.reshape(width, 3, width), place * mine, mine, axis=2)
    packed = jnp.dot(h_all, w_mine.reshape(width, 3 * mine), preferred_element_type=F32)
    packed = packed.astype(BF16)
    tail = slice(row - tok, row)
    prior, prior_docs = passed_along((packed[tail, mine:], row_docs[tail]), "batch", 1)
    kv = jnp.concatenate([prior, packed[:, mine:]], axis=0)
    docs_k = jnp.concatenate([prior_docs, row_docs])[:, None]
    docs_q = row_docs[None]

    def by_head(flat):
        return flat.reshape(flat.shape[0], heads, HD).transpose(1, 0, 2)

    q = by_head(packed[:, :mine] * jnp.bfloat16(scale))
    k = by_head(kv[:, :mine])
    v = by_head(kv[:, mine:])
    qT, kT, vT = q.swapaxes(1, 2), k.swapaxes(1, 2), v.swapaxes(1, 2)
    oT, lse = attend(k, qT, vT, docs_k, docs_q, tok)
    o_rows = oT.astype(BF16).transpose(2, 0, 1).reshape(row, mine)
    attended = lax.all_to_all(o_rows, "seq", split_axis=0, concat_axis=1, tiled=True)

    branch_one = jnp.dot(attended, w_out, preferred_element_type=F32)
    middle = narrow + shrink(branch_one)
    h_two = crms_norm(middle, gain_two).astype(BF16)
    up_proj = jnp.dot(h_two, w_up, preferred_element_type=F32)
    gelu_out = jax.nn.gelu(up_proj).astype(BF16)
    branch_two = jnp.dot(gelu_out, w_down, preferred_element_type=F32)
    new_residual = middle + shrink(branch_two)
    grad_new = cotangent[0]
    grad_two = shrink_back(grad_new).astype(BF16)
    grad_w_down = jnp.einsum("tf,td->fd", gelu_out, grad_two, preferred_element_type=F32)
    grad_gelu = jnp.einsum("td,fd->tf", grad_two, w_down, preferred_element_type=F32)
    _, gelu_pull = jax.vjp(jax.nn.gelu, up_proj)
    grad_up = gelu_pull(grad_gelu)[0].astype(BF16)
    grad_w_up = jnp.einsum("td,tf->df", h_two, grad_up, preferred_element_type=F32)
    grad_h_two = jnp.einsum("tf,df->td", grad_up, w_up, preferred_element_type=F32)
    _, norm_pull_two = jax.vjp(crms_norm, middle, gain_two)
    grad_middle_norm, grad_gain_two = norm_pull_two(grad_h_two)
    grad_middle = grad_new + grad_middle_norm
    grad_one = shrink_back(grad_middle).astype(BF16)
    grad_w_out = jnp.einsum("td,te->de", attended, grad_one, preferred_element_type=F32)
    grad_attended = jnp.einsum("te,de->td", grad_one, w_out, preferred_element_type=F32)
    do_rows = lax.all_to_all(
        grad_attended.astype(BF16), "seq", split_axis=1, concat_axis=0, tiled=True
    )

    mlp_shares = [
        lax.psum_scatter(g.astype(BF16), "seq", scatter_dimension=0, tiled=True)
        for g in (grad_w_down, grad_w_up, grad_w_out)
    ]
    mlp_totals = lax.psum(tuple(mlp_shares), "batch")

    do = by_head(do_rows)
    doT = do.swapaxes(1, 2)
    dqT, dk, dv = attend_back(k, kT, v, q, qT, do, doT, oT, lse, docs_k, docs_q, tok)
    back_k, back_v = passed_along((dk[:, :tok].astype(BF16), dv[:, :tok].astype(BF16)), "batch", -1)

    def with_tail(own, back):
        return jnp.concatenate([own[:, tok:-tok], own[:, -tok:] + back.astype(F32)], axis=1)

    def rows_of(heads_first):
        return heads_first.transpose(1, 0, 2).reshape(row, mine).astype(BF16)

    grad_packed = jnp.concatenate(
        [
            rows_of(dqT.swapaxes(1, 2) * scale),
            rows_of(with_tail(dk, back_k)),
            rows_of(with_tail(dv, back_v)),
        ],
        axis=1,
    )
    grad_w_mine = jnp.einsum("td,tf->df", h_all, grad_packed, preferred_element_type=F32)
    grad_h_part = jnp.einsum(
        "tf,df->td", grad_packed, w_mine.reshape(width, 3 * mine), preferred_element_type=F32
    )
    grad_h_one = lax.psum_scatter(
        grad_h_part.astype(BF16), "seq", scatter_dimension=0, tiled=True
    ).astype(F32)
    _, norm_pull_one = jax.vjp(crms_norm, narrow, gain_one)
    grad_narrow_norm, grad_gain_one = norm_pull_one(grad_h_one)
    residual_grad = grad_middle + grad_narrow_norm
    grad_w_rows = lax.all_to_all(
        grad_w_mine.astype(BF16), "seq", split_axis=0, concat_axis=1, tiled=True
    )
    grad_w_rows = lax.psum(grad_w_rows, "batch").astype(F32)
    share = width // seq_count
    grad_w_qkv = (
        grad_w_rows.reshape(share, seq_count, 3, mine)
        .transpose(0, 2, 1, 3)
        .reshape(share, 3 * width)
    )
    gains = jnp.stack([grad_gain_one, grad_gain_two])
    gains = lax.psum(
        lax.psum_scatter(gains, "seq", scatter_dimension=1, tiled=True), "batch"
    )
    return (
        new_residual[None],
        residual_grad[None],
        gains[0],
        gains[1],
        grad_w_qkv,
        mlp_totals[2].astype(F32),
        mlp_totals[1].astype(F32),
        mlp_totals[0].astype(F32),
    )


def solution(mesh):
    placed = (
        P("batch", "seq", None),
        P("batch", "seq"),
        P(),
        P(),
        P(),
        P(),
        P(),
        P(),
        P("batch", "seq", None),
    )
    return jax.shard_map(
        per_device,
        mesh=mesh,
        in_specs=placed,
        out_specs=(
            P("batch", "seq", None),
            P("batch", "seq", None),
            P("seq"),
            P("seq"),
            P("seq", None),
            P("seq", None),
            P("seq", None),
            P("seq", None),
        ),
        check_vma=False,
    )
```

```python
import functools
import math

import jax
import jax.numpy as jnp
from jax import lax
from jax.experimental import pallas as pl
from jax.experimental.pallas import tpu as pltpu
from jax.sharding import PartitionSpec as P

H = 12
HD = 64
EPSILON = 1e-06
NEG = -1e30
F32, BF16 = jnp.float32, jnp.bfloat16
VMEM_LIMIT = 56 * 2**20


def passed_along(block, axis, distance):
    devices = range(lax.axis_size(axis))
    route = [((i - distance) % len(devices), i) for i in devices]
    return lax.ppermute(block, axis, route)


def expand(narrow):
    return jnp.concatenate([narrow, -jnp.sum(narrow, axis=-1, keepdims=True)], axis=-1)


def shrink(full_vec):
    return full_vec[..., :-1] - jnp.mean(full_vec, axis=-1, keepdims=True)


def shrink_back(grad_narrow):
    padded = jnp.concatenate([grad_narrow, jnp.zeros_like(grad_narrow[..., :1])], axis=-1)
    return padded - jnp.sum(grad_narrow, axis=-1, keepdims=True) / padded.shape[-1]


def crms_norm(narrow, gain_vec):
    full_vec = expand(narrow)
    return (
        gain_vec
        * full_vec
        * lax.rsqrt(jnp.mean(full_vec * full_vec, axis=-1, keepdims=True) + EPSILON)
    )


def dot(a, b):
    return lax.dot_general(a, b, (((1,), (0,)), ((), ())), preferred_element_type=F32)


def masked(s, key_docs, query_docs, key_at, query_at, causal, docs, fill):
    keep = None
    if docs:
        keep = key_docs == query_docs
    if causal:
        key_pos = lax.broadcasted_iota(jnp.int32, s.shape, 0) + key_at
        query_pos = lax.broadcasted_iota(jnp.int32, s.shape, 1) + query_at
        earlier = key_pos <= query_pos
        keep = earlier if keep is None else keep & earlier
    return s if keep is None else jnp.where(keep, s, fill)


def fwd_kernel(tok, blocks, heads, k_ref, qT_ref, vT_ref, dk_ref, dq_ref, oT_ref, lse_ref):
    def head(h, carry):
        for i in range(blocks):
            q0 = i * tok
            qT = qT_ref[h, :, q0 : q0 + tok]
            docs_q = dq_ref[:, q0 : q0 + tok]
            m = jnp.full((1, tok), NEG, F32)
            total = jnp.zeros((1, tok), F32)
            acc = jnp.zeros(qT.shape, F32)
            edge = i == 0 or i == blocks - 1
            chunks = [(0, False, True)] if i == 0 else []
            for j in range(i):
                chunks.append(((j + 1) * tok, False, j == 0 or edge))
            chunks.append(((i + 1) * tok, True, edge))
            for k0, causal, docs in chunks:
                keys = slice(k0, k0 + tok)
                s = dot(k_ref[h, keys, :], qT)
                docs_k = dk_ref[keys, :] if docs else None
                s = masked(s, docs_k, docs_q, k0 - tok, q0, causal, docs, NEG)
                new_m = jnp.maximum(m, jnp.max(s, axis=0, keepdims=True))
                p = jnp.exp(s - new_m)
                shift = jnp.exp(m - new_m)
                total = total * shift + jnp.sum(p, axis=0, keepdims=True)
                acc = acc * shift + dot(vT_ref[h, :, keys], p.astype(BF16))
                m = new_m
            oT_ref[h, :, q0 : q0 + tok] = acc / total
            lse_ref[h, :, q0 : q0 + tok] = m + jnp.log(total)
        return carry

    lax.fori_loop(0, heads, head, 0)


def pairs_of(i, tok, blocks, sub):
    out = []
    if i == 0:
        out.append((0, tok, 0, tok, False, True))
    edge = i == 0 or i == blocks - 1
    for j in range(i):
        out.append(((j + 1) * tok, tok, 0, tok, False, j == 0 or edge))
    for a in range(tok // sub):
        out.append(((i + 1) * tok + a * sub, sub, a * sub, tok - a * sub, True, edge))
    return out


def bwd_kernel(
    tok, blocks, heads, sub,
    k_ref, kT_ref, v_ref, q_ref, qT_ref, do_ref, doT_ref, oT_ref, lse_ref, dk_ref, dq_ref,
    dqT_out, dk_out, dv_out, delta,
):
    def head(h, carry):
        for i in range(blocks):
            sl = slice(i * tok, (i + 1) * tok)
            delta[:, sl] = jnp.sum(
                doT_ref[h, :, sl].astype(F32) * oT_ref[h, :, sl], axis=0, keepdims=True
            )
        dk_out[h] = jnp.zeros_like(dk_out[h])
        dv_out[h] = jnp.zeros_like(dv_out[h])
        dqT_out[h] = jnp.zeros_like(dqT_out[h])
        for i in range(blocks):
            q0 = i * tok
            for k0, kw, qo, qw, causal, docs in pairs_of(i, tok, blocks, sub):
                ks, qs = slice(k0, k0 + kw), slice(q0 + qo, q0 + qo + qw)
                s = dot(k_ref[h, ks, :], qT_ref[h, :, qs])
                p = jnp.exp(s - lse_ref[h, :, qs])
                docs_k = dk_ref[ks, :] if docs else None
                p = masked(p, docs_k, dq_ref[:, qs], k0 - tok, q0 + qo, causal, docs, 0.0)
                dp = dot(v_ref[h, ks, :], doT_ref[h, :, qs])
                ds = (p * (dp - delta[:, qs])).astype(BF16)
                dv_out[h, ks, :] += dot(p.astype(BF16), do_ref[h, qs, :])
                dk_out[h, ks, :] += dot(ds, q_ref[h, qs, :])
                dqT_out[h, :, qs] += dot(kT_ref[h, :, ks], ds)
        return carry

    lax.fori_loop(0, heads, head, 0)


def attend(k, qT, vT, docs_k, docs_q, tok):
    heads, hd, row = qT.shape
    return pl.pallas_call(
        functools.partial(fwd_kernel, tok, row // tok, heads),
        out_shape=[
            jax.ShapeDtypeStruct((heads, hd, row), F32),
            jax.ShapeDtypeStruct((heads, 1, row), F32),
        ],
        compiler_params=pltpu.CompilerParams(vmem_limit_bytes=VMEM_LIMIT),
    )(k, qT, vT, docs_k, docs_q)


def attend_back(k, kT, v, q, qT, do, doT, oT, lse, docs_k, docs_q, tok):
    heads, hd, row = qT.shape
    return pl.pallas_call(
        functools.partial(bwd_kernel, tok, row // tok, heads, tok // 2),
        out_shape=[
            jax.ShapeDtypeStruct((heads, hd, row), F32),
            jax.ShapeDtypeStruct(k.shape, F32),
            jax.ShapeDtypeStruct(k.shape, F32),
        ],
        scratch_shapes=[pltpu.VMEM((1, row), F32)],
        compiler_params=pltpu.CompilerParams(vmem_limit_bytes=VMEM_LIMIT),
    )(k, kT, v, q, qT, do, doT, oT, lse, docs_k, docs_q)


MESH = pl.DeviceIdType.MESH


class Place:
    def __init__(self, n):
        self.s = lax.axis_index("seq")
        self.b = lax.axis_index("batch")
        self.core = lax.rem(self.s, 2)
        self.chip = self.s // 2
        self.y = lax.rem(self.b, 2)
        self.z = lax.rem(self.b // 2, 4)
        self.far = self.b // 8
        self.n = n

    def core_mate(self):
        return (self.s + 1 - 2 * self.core, self.b)

    def chip_mate(self):
        return (self.s + 2 - 4 * self.chip, self.b)

    def y_mate(self):
        return (self.s, self.b + 1 - 2 * self.y)

    def z_of(self, d):
        return lax.rem(self.z + d, 4)

    def z_mate(self, d):
        return (self.s, self.b + 2 * (self.z_of(d) - self.z))

    def far_mate(self, d):
        f = lax.rem(self.far + d, self.n // 8)
        return (self.s, self.b + 8 * (f - self.far))

    def all_mates(self):
        mates = [self.core_mate(), self.chip_mate(), self.y_mate()]
        mates += [self.z_mate(d) for d in (1, 2, 3)]
        return mates + [self.far_mate(d) for d in range(1, self.n // 8)]


def greet(mates):
    barrier = pltpu.get_barrier_semaphore()
    for mate in mates:
        pl.semaphore_signal(barrier, inc=1, device_id=mate, device_id_type=MESH)
    pl.semaphore_wait(barrier, len(mates))


def send(src, dst, sems, mate):
    copy = pltpu.make_async_remote_copy(
        src_ref=src, dst_ref=dst, send_sem=sems[0], recv_sem=sems[1], device_id=mate, device_id_type=MESH
    )
    copy.start()
    return copy


def rows_of(at, count):
    return pl.ds(pl.multiple_of(at, 16), count)


def blockwise(rows, step, body):
    def one(i, carry):
        body(pl.ds(pl.multiple_of(i * step, 16), step))
        return carry
    lax.fori_loop(0, rows // step, one, 0)


def step_of(rows):
    for s in (48, 32, 16):
        if rows % s == 0:
            return s


class Sum:
    PER_CORE, HALF = 2, 2

    def __init__(self, place, src, out, scratch, first_row, rows, cols, sems, whole=True):
        (self.own, self.rc, self.rx, self.ry, self.rz, self.res, self.rf) = scratch
        self.p, self.src, self.out, self.sems = place, src, out, sems
        self.first, self.rows, self.cols, self.whole = first_row, rows, cols, whole
        self.at = 0
        self.open = []

    def sem(self):
        k = self.at
        self.at += 1
        return (self.sems.at[0, k], self.sems.at[1, k])

    def finish(self):
        for copy in self.open:
            copy.wait()
        self.open = []

    def p0(self):
        p, first = self.p, pl.ds(self.first, self.rows)
        if not self.whole:
            copy = pltpu.make_async_copy(self.src.at[first], self.own.at[p.chip], self.sem()[0])
            copy.start()
            self.open = [copy]
            return
        for order in (1, 0):
            chip = lax.rem(p.chip + order, 2)
            mate_part = 2 * chip + 1 - p.core
            own_part = 2 * chip + p.core
            self.open.append(send(self.src.at[mate_part, first], self.rc.at[chip], self.sem(), p.core_mate()))
            copy = pltpu.make_async_copy(self.src.at[own_part, first], self.own.at[chip], self.sem()[0])
            copy.start()
            self.open.append(copy)

    def add(self, chip, other):
        def body(rows):
            self.own[chip, rows, :] = (self.own[chip, rows, :].astype(F32) + other(rows).astype(F32)).astype(BF16)
        return body

    def p1(self):
        p = self.p
        if not self.whole:
            self.finish()
            return
        other = 1 - p.chip
        for copy in self.open[:2]:
            copy.wait()
        blockwise(self.rows, step_of(self.rows), self.add(other, lambda r: self.rc[other, r, :]))
        mine = send(self.own.at[other], self.rx, self.sem(), p.chip_mate())
        for copy in self.open[2:]:
            copy.wait()
        self.open = [mine]
        blockwise(self.rows, step_of(self.rows), self.add(p.chip, lambda r: self.rc[p.chip, r, :]))

    def p2(self):
        p, half = self.p, self.rows // 2
        self.finish()
        def both(at):
            def body(r):
                rows = rows_of(at + r.start, r.size)
                a = self.own[p.chip, rows, :].astype(F32)
                if self.whole:
                    a = a + self.rx[rows, :].astype(F32)
                self.own[p.chip, rows, :] = a.astype(BF16)
            return body
        if self.whole:
            blockwise(half, step_of(half), both((1 - p.y) * half))
        self.open = [send(self.own.at[p.chip, rows_of((1 - p.y) * half, half)], self.ry, self.sem(), p.y_mate())]
        if self.whole:
            blockwise(half, step_of(half), both(p.y * half))

    def p3(self):
        p, half, quarter = self.p, self.rows // 2, self.rows // 8
        self.finish()
        base = p.y * half
        def body(r):
            rows = rows_of(base + r.start, r.size)
            self.own[p.chip, rows, :] = (self.own[p.chip, rows, :].astype(F32) + self.ry[r, :].astype(F32)).astype(BF16)
        blockwise(half, step_of(half), body)
        for d in (2, 1, 3):
            z = p.z_of(d)
            self.open.append(
                send(self.own.at[p.chip, rows_of(base + z * quarter, quarter)], self.rz.at[4 - d - 1], self.sem(), p.z_mate(d))
            )

    def p4(self):
        p, half, quarter = self.p, self.rows // 2, self.rows // 8
        self.finish()
        base = p.y * half + p.z * quarter
        def body(r):
            rows = rows_of(base + r.start, r.size)
            t = self.own[p.chip, rows, :].astype(F32)
            for d in range(3):
                t = t + self.rz[d, r, :].astype(F32)
            self.res[rows, :] = t.astype(BF16)
        blockwise(quarter, step_of(quarter), body)
        far = p.n // 8
        mine = rows_of(base, quarter)
        if far > 1:
            copies = [send(self.res.at[mine], self.rf.at[far - d - 1], self.sem(), p.far_mate(d)) for d in range(1, far)]
            for copy in copies:
                copy.wait()
            def more(r):
                rows = rows_of(base + r.start, r.size)
                t = self.res[rows, :].astype(F32)
                for d in range(far - 1):
                    t = t + self.rf[d, r, :].astype(F32)
                self.res[rows, :] = t.astype(BF16)
            blockwise(quarter, step_of(quarter), more)
        for d in (2, 1, 3):
            self.open.append(send(self.res.at[mine], self.res.at[mine], self.sem(), p.z_mate(d)))

    def p5(self):
        p, half = self.p, self.rows // 2
        self.finish()
        mine = rows_of(p.y * half, half)
        self.open = [send(self.res.at[mine], self.res.at[mine], self.sem(), p.y_mate())]

    def p6(self):
        self.finish()
        def body(r):
            self.out[rows_of(self.first + r.start, r.size), :] = self.res[r, :].astype(F32)
        blockwise(self.rows, step_of(self.rows), body)

    def phase(self, k):
        [self.p0, self.p1, self.p2, self.p3, self.p4, self.p5, self.p6][k]()

    PHASES = 7


def scratch_of(rows, cols, n):
    V = lambda *s: pltpu.VMEM(s, BF16)
    return [V(2, rows, cols), V(2, rows, cols), V(rows, cols), V(rows // 2, cols), V(3, rows // 8, cols), V(rows, cols), V(max(n // 8 - 1, 1), rows // 8, cols)]


def sems_count(n):
    return 4 + 1 + 1 + 3 + 3 + 1 + n // 8


def ar_kernel(n, plan, n_in, *refs):
    ins, outs = refs[:n_in], refs[n_in:2 * n_in]
    scratch = refs[2 * n_in:]
    place = Place(n)
    greet(place.all_mates())
    sums = []
    sems = scratch[-1]
    for k, (arr, first, rows, cols, whole) in enumerate(plan):
        sums.append(Sum(place, ins[arr], outs[arr], scratch[7 * k:7 * k + 7], first, rows, cols, sems.at[k], whole))
    for tick in range(Sum.PHASES + len(sums) - 1):
        for k, one in enumerate(sums):
            if 0 <= tick - k < Sum.PHASES:
                one.phase(tick - k)


def all_sum(n, plan, arrays, out_shapes):
    n_in = len(arrays)
    scratch = []
    for (arr, first, rows, cols, whole) in plan:
        scratch += scratch_of(rows, cols, n)
    scratch.append(pltpu.SemaphoreType.DMA((len(plan), 2, sems_count(n))))
    return pl.pallas_call(
        functools.partial(ar_kernel, n, plan, n_in),
        out_shape=[jax.ShapeDtypeStruct(s, F32) for s in out_shapes],
        in_specs=[pl.BlockSpec(memory_space=pl.ANY)] * n_in,
        out_specs=[pl.BlockSpec(memory_space=pltpu.VMEM)] * n_in,
        scratch_shapes=scratch,
        compiler_params=pltpu.CompilerParams(collective_id=1, has_side_effects=True, vmem_limit_bytes=VMEM_LIMIT),
    )(*arrays)


def per_device(residual, documents, gain_one, gain_two, w_qkv, w_out, w_up, w_down, cotangent):
    seq_count = lax.axis_size("seq")
    place = lax.axis_index("seq")
    narrow = residual[0]
    tok = narrow.shape[0]
    width = w_out.shape[0]
    row = seq_count * tok
    heads = H // seq_count
    mine = heads * HD
    scale = 1.0 / math.sqrt(HD)

    h_one = crms_norm(narrow, gain_one).astype(BF16)
    h_all = lax.all_gather(h_one, "seq", axis=0, tiled=True)
    row_docs = lax.all_gather(documents[0], "seq", axis=0, tiled=True)
    w_mine = lax.dynamic_slice_in_dim(w_qkv.reshape(width, 3, width), place * mine, mine, axis=2)
    packed = jnp.dot(h_all, w_mine.reshape(width, 3 * mine), preferred_element_type=F32)
    packed = packed.astype(BF16)
    tail = slice(row - tok, row)
    prior, prior_docs = passed_along((packed[tail, mine:], row_docs[tail]), "batch", 1)
    kv = jnp.concatenate([prior, packed[:, mine:]], axis=0)
    docs_k = jnp.concatenate([prior_docs, row_docs])[:, None]
    docs_q = row_docs[None]

    def by_head(flat):
        return flat.reshape(flat.shape[0], heads, HD).transpose(1, 0, 2)

    q = by_head(packed[:, :mine] * jnp.bfloat16(scale))
    k = by_head(kv[:, :mine])
    v = by_head(kv[:, mine:])
    qT, kT, vT = q.swapaxes(1, 2), k.swapaxes(1, 2), v.swapaxes(1, 2)
    oT, lse = attend(k, qT, vT, docs_k, docs_q, tok)
    o_rows = oT.astype(BF16).transpose(2, 0, 1).reshape(row, mine)
    attended = lax.all_to_all(o_rows, "seq", split_axis=0, concat_axis=1, tiled=True)

    branch_one = jnp.dot(attended, w_out, preferred_element_type=F32)
    middle = narrow + shrink(branch_one)
    h_two = crms_norm(middle, gain_two).astype(BF16)
    up_proj = jnp.dot(h_two, w_up, preferred_element_type=F32)
    gelu_out = jax.nn.gelu(up_proj).astype(BF16)
    branch_two = jnp.dot(gelu_out, w_down, preferred_element_type=F32)
    new_residual = middle + shrink(branch_two)
    grad_new = cotangent[0]
    grad_two = shrink_back(grad_new).astype(BF16)
    grad_w_down = jnp.einsum("tf,td->fd", gelu_out, grad_two, preferred_element_type=F32)
    grad_gelu = jnp.einsum("td,fd->tf", grad_two, w_down, preferred_element_type=F32)
    _, gelu_pull = jax.vjp(jax.nn.gelu, up_proj)
    grad_up = gelu_pull(grad_gelu)[0].astype(BF16)
    grad_w_up = jnp.einsum("td,tf->df", h_two, grad_up, preferred_element_type=F32)
    grad_h_two = jnp.einsum("tf,df->td", grad_up, w_up, preferred_element_type=F32)
    _, norm_pull_two = jax.vjp(crms_norm, middle, gain_two)
    grad_middle_norm, _ = norm_pull_two(grad_h_two)
    grad_middle = grad_new + grad_middle_norm
    grad_one = shrink_back(grad_middle).astype(BF16)
    grad_w_out = jnp.einsum("td,te->de", attended, grad_one, preferred_element_type=F32)
    grad_attended = jnp.einsum("te,de->td", grad_one, w_out, preferred_element_type=F32)
    do_rows = lax.all_to_all(
        grad_attended.astype(BF16), "seq", split_axis=1, concat_axis=0, tiled=True
    )

    do = by_head(do_rows)
    doT = do.swapaxes(1, 2)
    dqT, dk, dv = attend_back(k, kT, v, q, qT, do, doT, oT, lse, docs_k, docs_q, tok)
    back_k, back_v = passed_along((dk[:, :tok].astype(BF16), dv[:, :tok].astype(BF16)), "batch", -1)

    def with_tail(own, back):
        return jnp.concatenate([own[:, tok:-tok], own[:, -tok:] + back.astype(F32)], axis=1)

    def rows_of(heads_first):
        return heads_first.transpose(1, 0, 2).reshape(row, mine).astype(BF16)

    grad_packed = jnp.concatenate(
        [
            rows_of(dqT.swapaxes(1, 2) * scale),
            rows_of(with_tail(dk, back_k)),
            rows_of(with_tail(dv, back_v)),
        ],
        axis=1,
    )
    grad_w_mine = jnp.einsum("td,tf->df", h_all, grad_packed, preferred_element_type=F32)
    grad_h_part = jnp.einsum(
        "tf,df->td", grad_packed, w_mine.reshape(width, 3 * mine), preferred_element_type=F32
    )
    grad_h_one = lax.psum_scatter(
        grad_h_part.astype(BF16), "seq", scatter_dimension=0, tiled=True
    ).astype(F32)
    _, norm_pull_one = jax.vjp(crms_norm, narrow, gain_one)
    grad_narrow_norm, _ = norm_pull_one(grad_h_one)
    residual_grad = grad_middle + grad_narrow_norm
    grad_w_rows = lax.all_to_all(
        grad_w_mine.astype(BF16), "seq", split_axis=0, concat_axis=0, tiled=True
    )
    share = width // seq_count
    parts = width // share

    def by_owner(grad, cut):
        split = grad.astype(BF16).reshape(seq_count, share, cut, grad.shape[1] // cut)
        return split.transpose(0, 2, 1, 3).reshape(seq_count, cut * share, grad.shape[1] // cut)

    n = lax.axis_size("batch")
    plan = [
        (0, 0, width // 2, width, True),
        (0, width // 2, width // 2, width, True),
        (1, 0, width // 2, width, True),
        (1, width // 2, width // 2, width, True),
        (2, 0, width // 2, width // 2, True),
        (3, 0, width, 3 * mine, False),
    ]
    sum_down, sum_up, sum_out, sum_qkv = all_sum(
        n,
        plan,
        (
            grad_w_down.astype(BF16).reshape(seq_count, width, width),
            by_owner(grad_w_up, parts),
            by_owner(grad_w_out, 2),
            grad_w_rows,
        ),
        [(width, width), (width, width), (width // 2, width // 2), (width, 3 * mine)],
    )
    sum_up = sum_up.reshape(parts, share, width).transpose(1, 0, 2).reshape(share, parts * width)
    sum_out = sum_out.reshape(2, share, width // 2).transpose(1, 0, 2).reshape(share, width)
    grad_w_qkv = (
        sum_qkv.reshape(seq_count, share, 3, mine)
        .transpose(1, 2, 0, 3)
        .reshape(share, 3 * width)
    )

    def gain_grad(w, total, gain):
        rows = lax.dynamic_slice_in_dim(w, place * share, share).astype(F32)
        mine_gain = lax.dynamic_slice_in_dim(gain, place * share, share)
        return jnp.sum(rows * total, axis=1) / mine_gain

    gain_one_out = gain_grad(w_qkv, grad_w_qkv, gain_one)
    gain_two_out = gain_grad(w_up, sum_up, gain_two)
    return (
        new_residual[None],
        residual_grad[None],
        gain_one_out,
        gain_two_out,
        grad_w_qkv,
        sum_out,
        sum_up,
        sum_down,
    )


def solution(mesh):
    placed = (
        P("batch", "seq", None),
        P("batch", "seq"),
        P(),
        P(),
        P(),
        P(),
        P(),
        P(),
        P("batch", "seq", None),
    )
    return jax.shard_map(
        per_device,
        mesh=mesh,
        in_specs=placed,
        out_specs=(
            P("batch", "seq", None),
            P("batch", "seq", None),
            P("seq"),
            P("seq"),
            P("seq", None),
            P("seq", None),
            P("seq", None),
            P("seq", None),
        ),
        check_vma=False,
    )
```

```python
import functools
import math

import jax
import jax.numpy as jnp
from jax import lax
from jax.experimental import pallas as pl
from jax.experimental.pallas import tpu as pltpu
from jax.sharding import PartitionSpec as P

H = 12
HD = 64
EPSILON = 1e-06
NEG = -1e30
F32, BF16 = jnp.float32, jnp.bfloat16
VMEM_LIMIT = 60 * 2**20


def passed_along(block, axis, distance):
    devices = range(lax.axis_size(axis))
    route = [((i - distance) % len(devices), i) for i in devices]
    return lax.ppermute(block, axis, route)


def expand(narrow):
    return jnp.concatenate([narrow, -jnp.sum(narrow, axis=-1, keepdims=True)], axis=-1)


def shrink(full_vec):
    return full_vec[..., :-1] - jnp.mean(full_vec, axis=-1, keepdims=True)


def shrink_back(grad_narrow):
    padded = jnp.concatenate([grad_narrow, jnp.zeros_like(grad_narrow[..., :1])], axis=-1)
    return padded - jnp.sum(grad_narrow, axis=-1, keepdims=True) / padded.shape[-1]


def crms_norm(narrow, gain_vec):
    full_vec = expand(narrow)
    return (
        gain_vec
        * full_vec
        * lax.rsqrt(jnp.mean(full_vec * full_vec, axis=-1, keepdims=True) + EPSILON)
    )


def dot(a, b):
    return lax.dot_general(a, b, (((1,), (0,)), ((), ())), preferred_element_type=F32)


def fwd_kernel(tok, blocks, heads, k_ref, qT_ref, vT_ref, start_ref, oT_ref, lse_ref):
    def head(h, carry):
        hr = pl.ds(pl.multiple_of(h * HD, HD), HD)
        for i in range(blocks):
            qs = slice(i * tok, (i + 1) * tok)
            qT = qT_ref[hr, qs]
            m = jnp.full((1, tok), NEG, F32)
            total = jnp.zeros((1, tok), F32)
            acc = jnp.zeros((HD, tok), F32)
            edge = i == 0 or i == blocks - 1
            for j in [0] * (i == 0) + list(range(1, i + 2)):
                ks = slice(j * tok, (j + 1) * tok)
                s = dot(k_ref[h, ks, :], qT)
                keep = None
                if edge or j <= 1 or j == i + 1:
                    at = lax.broadcasted_iota(jnp.int32, s.shape, 0) + j * tok
                if edge or j <= 1:
                    keep = at >= start_ref[:, qs]
                if j == i + 1:
                    until = lax.broadcasted_iota(jnp.int32, s.shape, 1) + (i + 1) * tok
                    keep = (at <= until) if keep is None else keep & (at <= until)
                if keep is not None:
                    s = jnp.where(keep, s, NEG)
                new_m = jnp.maximum(m, jnp.max(s, axis=0, keepdims=True))
                p = jnp.exp(s - new_m)
                shift = jnp.exp(m - new_m)
                total = total * shift + jnp.sum(p, axis=0, keepdims=True)
                acc = acc * shift + dot(vT_ref[hr, ks], p.astype(BF16))
                m = new_m
            oT_ref[hr, qs] = acc / total
            lse_ref[h, :, qs] = m + jnp.log(total)
        return carry

    lax.fori_loop(0, heads, head, 0)


def attend(k, qT, vT, start, tok):
    row = qT.shape[1]
    heads = k.shape[0]
    return pl.pallas_call(
        functools.partial(fwd_kernel, tok, row // tok, heads),
        out_shape=[
            jax.ShapeDtypeStruct(qT.shape, F32),
            jax.ShapeDtypeStruct((heads, 1, row), F32),
        ],
        compiler_params=pltpu.CompilerParams(vmem_limit_bytes=VMEM_LIMIT),
    )(k, qT, vT, start)


MESH = pl.DeviceIdType.MESH


class Place:
    def __init__(self, n):
        self.s = lax.axis_index("seq")
        self.b = lax.axis_index("batch")
        self.core = lax.rem(self.s, 2)
        self.chip = self.s // 2
        self.y = lax.rem(self.b, 2)
        self.z = lax.rem(self.b // 2, 4)
        self.far = self.b // 8
        self.n = n

    def core_mate(self):
        return (self.s + 1 - 2 * self.core, self.b)

    def chip_mate(self):
        return (self.s + 2 - 4 * self.chip, self.b)

    def cross_mate(self):
        return (3 - self.s, self.b)

    def y_mate(self):
        return (self.s, self.b + 1 - 2 * self.y)

    def z_of(self, d):
        return lax.rem(self.z + d, 4)

    def z_mate(self, d):
        return (self.s, self.b + 2 * (self.z_of(d) - self.z))

    def far_mate(self, d):
        f = lax.rem(self.far + d, self.n // 8)
        return (self.s, self.b + 8 * (f - self.far))

    def next_row(self):
        return (self.s, lax.rem(self.b + 1, self.n))

    def prior_row(self):
        return (self.s, lax.rem(self.b + self.n - 1, self.n))

    def all_mates(self):
        mates = [self.core_mate(), self.chip_mate(), self.cross_mate(), self.y_mate()]
        mates += [self.z_mate(d) for d in (1, 2, 3)]
        mates += [self.far_mate(d) for d in range(1, self.n // 8)]
        return mates + [self.next_row(), self.prior_row()]


def greet(mates):
    barrier = pltpu.get_barrier_semaphore()
    for mate in mates:
        pl.semaphore_signal(barrier, inc=1, device_id=mate, device_id_type=MESH)
    pl.semaphore_wait(barrier, len(mates))


class Copies:
    def __init__(self, sems):
        self.sems, self.made = sems, {}

    def remote(self, name, src, dst, mate):
        k = len(self.made)

        def make():
            return pltpu.make_async_remote_copy(
                src_ref=src(),
                dst_ref=dst(),
                send_sem=self.sems.at[0, k],
                recv_sem=self.sems.at[1, k],
                device_id=mate(),
                device_id_type=MESH,
            )

        self.made[name] = make

    def local(self, name, src, dst):
        k = len(self.made)

        def make():
            return pltpu.make_async_copy(src(), dst(), self.sems.at[0, k])

        self.made[name] = make

    def start(self, *names):
        for name in names:
            self.made[name]().start()

    def wait(self, *names):
        for name in names:
            self.made[name]().wait()

    def wait_recv(self, *names):
        for name in names:
            self.made[name]().wait_recv()

    def wait_send(self, *names):
        for name in names:
            self.made[name]().wait_send()


def rows_at(at, count):
    return pl.ds(pl.multiple_of(at, 16), count)


def blockwise(rows, body):
    step = next(s for s in (48, 32, 16) if rows % s == 0)

    def one(i, carry):
        body(i * step, step)
        return carry

    lax.fori_loop(0, rows // step, one, 0)


class Sum:
    def __init__(self, place, copies, name, mode, src, first, rows, cols, bufs, out):
        self.p, self.c, self.name, self.mode = place, copies, name, mode
        self.src, self.first, self.rows, self.cols, self.out = src, first, rows, cols, out
        if mode == "whole":
            self.own, self.ry, self.rz, self.res, self.rf, self.rc, self.rx = bufs
        else:
            self.own, self.ry, self.rz, self.res, self.rf = bufs
        self.mine = (lambda: self.own.at[self.p.chip]) if mode == "whole" else (lambda: self.own.at[0])
        self.define()

    def define(self):
        p, c, half, quarter, far = self.p, self.c, self.rows // 2, self.rows // 8, self.p.n // 8
        if self.mode == "whole":
            first = pl.ds(self.first, self.rows)
            for order in (1, 0):
                chip = lambda order=order: lax.rem(p.chip + order, 2)
                c.remote(
                    self.id(("core", order)),
                    lambda chip=chip: self.src.at[2 * chip() + 1 - p.core, first],
                    lambda chip=chip: self.rc.at[chip()],
                    p.core_mate,
                )
                c.local(
                    self.id(("own", order)),
                    lambda chip=chip: self.src.at[2 * chip() + p.core, first],
                    lambda chip=chip: self.own.at[chip()],
                )
            c.remote(self.id("x"), lambda: self.own.at[1 - p.chip], lambda: self.rx, p.chip_mate)
        other_half = lambda: self.mine().at[rows_at((1 - p.y) * half, half)]
        c.remote(self.id("y"), other_half, lambda: self.ry, p.y_mate)
        for d in (2, 1, 3):
            c.remote(
                self.id(("z", d)),
                lambda d=d: self.mine().at[rows_at(p.y * half + p.z_of(d) * quarter, quarter)],
                lambda d=d: self.rz.at[3 - d],
                lambda d=d: p.z_mate(d),
            )
        spot = lambda: self.res.at[rows_at(p.y * half + p.z * quarter, quarter)]
        for d in range(1, far):
            c.remote(
                self.id(("far", d)), spot, lambda d=d: self.rf.at[far - d - 1], lambda d=d: p.far_mate(d)
            )
        for d in (2, 1, 3):
            c.remote(self.id(("back z", d)), spot, spot, lambda d=d: p.z_mate(d))
        my_half = lambda: self.res.at[rows_at(p.y * half, half)]
        c.remote(self.id("back y"), my_half, my_half, p.y_mate)
        c.local(self.id("out"), lambda: self.res, lambda: self.out)

    @staticmethod
    def scratch(mode, rows, cols, n):
        def v(*s):
            return pltpu.VMEM(s, BF16)

        whole = mode == "whole"
        out = [v(2 if whole else 1, rows, cols), v(rows // 2, cols), v(3, rows // 8, cols), v(rows, cols)]
        out.append(v(max(n // 8 - 1, 1), rows // 8, cols))
        return out + ([v(2, rows, cols), v(rows, cols)] if whole else [])

    def id(self, what):
        return (self.name, what)

    def p0(self):
        for order in (1, 0):
            self.c.start(self.id(("core", order)), self.id(("own", order)))

    def add_core(self, chip):
        def body(at, step):
            rows = rows_at(at, step)
            total = self.own[chip, rows, :].astype(F32) + self.rc[chip, rows, :].astype(F32)
            self.own[chip, rows, :] = total.astype(BF16)

        blockwise(self.rows, body)

    def p1(self):
        p = self.p
        self.c.wait(self.id(("core", 1)), self.id(("own", 1)))
        self.add_core(1 - p.chip)
        self.c.start(self.id("x"))
        self.c.wait(self.id(("core", 0)), self.id(("own", 0)))
        self.add_core(p.chip)

    def add_x(self, first):
        def body(at, step):
            rows = rows_at(first + at, step)
            total = self.own[self.p.chip, rows, :].astype(F32) + self.rx[rows, :].astype(F32)
            self.own[self.p.chip, rows, :] = total.astype(BF16)

        blockwise(self.rows // 2, body)

    def p2(self):
        p, half = self.p, self.rows // 2
        if self.mode == "whole":
            self.c.wait(self.id("x"))
            self.add_x((1 - p.y) * half)
        self.c.start(self.id("y"))
        if self.mode == "whole":
            self.add_x(p.y * half)

    def p3(self):
        p, half = self.p, self.rows // 2
        self.c.wait(self.id("y"))
        own = self.mine()

        def body(at, step):
            rows = rows_at(p.y * half + at, step)
            total = own[rows, :].astype(F32) + self.ry[rows_at(at, step), :].astype(F32)
            own[rows, :] = total.astype(BF16)

        blockwise(half, body)
        self.c.start(*[self.id(("z", d)) for d in (2, 1, 3)])

    def p4(self):
        p, half, quarter = self.p, self.rows // 2, self.rows // 8
        self.c.wait(*[self.id(("z", d)) for d in (1, 2, 3)])
        own = self.mine()
        base = p.y * half + p.z * quarter

        def body(at, step):
            rows = rows_at(base + at, step)
            total = own[rows, :].astype(F32)
            for d in range(3):
                total = total + self.rz[d, rows_at(at, step), :].astype(F32)
            self.res[rows, :] = total.astype(BF16)

        blockwise(quarter, body)
        far = p.n // 8
        if far > 1:
            self.c.start(*[self.id(("far", d)) for d in range(1, far)])
            self.c.wait(*[self.id(("far", d)) for d in range(1, far)])

            def more(at, step):
                rows = rows_at(base + at, step)
                total = self.res[rows, :].astype(F32)
                for d in range(far - 1):
                    total = total + self.rf[d, rows_at(at, step), :].astype(F32)
                self.res[rows, :] = total.astype(BF16)

            blockwise(quarter, more)
        self.c.start(*[self.id(("back z", d)) for d in (2, 1, 3)])

    def p5(self):
        self.c.wait(*[self.id(("back z", d)) for d in (1, 2, 3)])
        self.c.start(self.id("back y"))

    def p6(self):
        self.c.wait(self.id("back y"))
        self.c.start(self.id("out"))

    def p7(self):
        self.c.wait(self.id("out"))


def dot_nt(a, b):
    return lax.dot_general(a, b, (((1,), (1,)), ((), ())), preferred_element_type=F32)


def dot_tn(a, b):
    return lax.dot_general(a, b, (((0,), (0,)), ((), ())), preferred_element_type=F32)


BACK_IN = ("doT", "k", "v", "kT", "qT", "oT", "lse", "start", "h", "w")


def back_kernel(n, tok, blocks, heads, chunks, *refs):
    refs = list(refs)
    take = lambda count: [refs.pop(0) for _ in range(count)]
    hbm = dict(zip(BACK_IN, take(len(BACK_IN))))
    grads = take(3)
    sums_out, qkv_out, grad_h_out = take(3), take(1)[0], take(1)[0]
    vm = dict(zip(BACK_IN, take(len(BACK_IN))))
    dkT, dvT, delta, dP, prior_out, prior_in, dws, g_stage, g_core, g_x, g_acc = take(11)
    per = [take(7) for _ in chunks]
    per_qkv = [take(5) for _ in range(heads)]
    sems = refs.pop(0)
    hd = HD
    row = blocks * tok
    mine = heads * hd
    place = Place(n)
    c = Copies(sems)
    for name in BACK_IN:
        c.local(name, lambda name=name: hbm[name], lambda name=name: vm[name])
    c.start(*BACK_IN)
    greet(place.all_mates())
    sums = []
    for k, (arr, first, rows, cols) in enumerate(chunks):
        out = sums_out[arr].at[pl.ds(first, rows)]
        sums.append(Sum(place, c, ("g", k), "whole", grads[arr], first, rows, cols, per[k], out))
    qkv = [Sum(place, c, ("q", k), "share", None, 0, blocks * mine, mine, per_qkv[k], qkv_out.at[k]) for k in range(heads)]

    for k in range(heads):
        for what, mate in (("cross", place.cross_mate), ("chip", place.chip_mate), ("core", place.core_mate)):
            c.remote(
                ("dw", k, what),
                lambda k=k, mate=mate: dws.at[k, rows_at(mate()[0] * mine, mine)],
                lambda k=k: qkv[k].own.at[0, rows_at(place.s * mine, mine)],
                mate,
            )
        c.local(
            ("dw", k, "own"),
            lambda k=k: dws.at[k, rows_at(place.s * mine, mine)],
            lambda k=k: qkv[k].own.at[0, rows_at(place.s * mine, mine)],
        )
        c.remote(("prior", k), lambda k=k: prior_out.at[k], lambda k=k: prior_in.at[k], place.prior_row)
    for order in (1, 0):
        c.remote(("gh", order), lambda order=order: g_stage.at[order], lambda order=order: g_core.at[order], place.core_mate)
    c.remote(("gh", "x"), lambda: g_stage.at[1], lambda: g_x, place.chip_mate)

    sums[0].p0()
    sums[1].p0()
    dqT = vm["oT"]
    doT, kk, vv, kT, qT, lse, start = (vm[x] for x in ("doT", "k", "v", "kT", "qT", "lse", "start"))
    c.wait(*BACK_IN)
    sums[0].p1()
    sums[2].p0()
    sums[1].p1()

    def make_delta(h, carry):
        rows = pl.ds(pl.multiple_of(h * hd, hd), hd)
        delta[h] = jnp.sum(doT[rows, :].astype(F32) * vm["oT"][rows, :], axis=0, keepdims=True)
        return carry

    lax.fori_loop(0, heads, make_delta, 0)
    dqT[...] = jnp.zeros_like(dqT)
    dkT[...] = jnp.zeros_like(dkT)
    dvT[...] = jnp.zeros_like(dvT)

    def pair(h, q0, qw, k0, kw, causal, use_start):
        hr = pl.ds(pl.multiple_of(h * hd, hd), hd)
        qs, ks = pl.ds(pl.multiple_of(q0, 128), qw), pl.ds(pl.multiple_of(k0, 128), kw)
        q_blk, do_blk = qT[hr, qs], doT[hr, qs]
        s = dot(kk[h, ks, :], q_blk)
        p = jnp.exp(s - lse[h, :, qs])
        keep = None
        if use_start or causal:
            at = lax.broadcasted_iota(jnp.int32, s.shape, 0) + k0
            if use_start:
                keep = at >= start[:, qs]
            if causal:
                until = lax.broadcasted_iota(jnp.int32, s.shape, 1) + (q0 + tok)
                keep = (at <= until) if keep is None else keep & (at <= until)
            p = jnp.where(keep, p, 0.0)
        dp = dot(vv[h, ks, :], do_blk)
        ds = (p * (dp - delta[h, :, qs])).astype(BF16)
        dvT[hr, ks] += dot_nt(do_blk, p.astype(BF16))
        dkT[hr, ks] += dot_nt(q_blk, ds)
        dqT[hr, qs] += dot(kT[hr, ks], ds)

    def full(first, last):
        def run(h):
            def one(t, carry):
                i = jnp.where(t == 0, 0, jnp.where(t <= 3, 3, jnp.where(t <= 5, 2, 1)))
                j = jnp.where(t == 0, 0, jnp.where(t <= 3, t, jnp.where(t <= 5, t - 3, 1)))
                pair(h, i * tok, tok, j * tok, tok, False, True)
                return carry

            lax.fori_loop(first, last, one, 0)

        return run

    def send_prior(h):
        hr = pl.ds(pl.multiple_of(h * hd, hd), hd)
        prior_out[h, 0:hd, :] = dkT[hr, 0:tok].astype(BF16)
        prior_out[h, hd : 2 * hd, :] = dvT[hr, 0:tok].astype(BF16)

    def diagonal(h):
        sub = tok // 2

        def one(i, carry):
            pair(h, i * tok, tok, (i + 1) * tok, sub, True, True)
            pair(h, i * tok + sub, sub, (i + 1) * tok + sub, sub, True, True)
            return carry

        lax.fori_loop(0, blocks, one, 0)

    def close(h):
        hr = pl.ds(pl.multiple_of(h * hd, hd), hd)
        last = pl.ds(row, tok)
        dkT[hr, last] += prior_in[h, 0:hd, :].astype(F32)
        dvT[hr, last] += prior_in[h, hd : 2 * hd, :].astype(F32)
        base = h * 3 * hd
        for k, (src, scale) in enumerate(((dqT, 1.0 / math.sqrt(hd)), (dkT, None), (dvT, None))):
            val = src[hr, :] * scale if scale else src[hr, tok:]
            dP[pl.ds(pl.multiple_of(base + k * hd, hd), hd), :] = val.astype(BF16)
        dw = dot(dP[pl.ds(pl.multiple_of(base, hd), 3 * hd), :], vm["h"][...])
        dws[h] = dw.T.astype(BF16)

    DW = ("cross", "chip", "core", "own")

    def send_dw(k):
        c.start(*[("dw", k, what) for what in DW])

    def dw_here(k):
        c.wait(*[("dw", k, what) for what in DW])

    def at_head(h, *todo):
        for k, steps in enumerate(todo):
            if steps:
                @pl.when(h == k)
                def _():
                    for step in steps:
                        step()

    def prior_send(k):
        return lambda: c.start(("prior", k))

    def head(h, carry):
        full(0, 1)(h)
        send_prior(h)
        at_head(h, *[[prior_send(k)] for k in range(heads)])
        full(1, 4)(h)
        at_head(h, [sums[3].p0], [sums[0].p3], [sums[1].p3, sums[0].p6])
        full(4, 7)(h)
        at_head(h, [sums[4].p0], [sums[0].p4], [sums[1].p4])
        diagonal(h)
        at_head(h, [sums[0].p2, sums[2].p1], [sums[0].p5, sums[1].p2, sums[3].p1], [sums[1].p5, sums[2].p2, sums[4].p1])
        at_head(h, *[[lambda k=k: c.wait(("prior", k))] for k in range(heads)])
        close(h)
        at_head(
            h,
            [lambda: send_dw(0)],
            [lambda: send_dw(1), lambda: dw_here(0), qkv[0].p2],
            [lambda: send_dw(2), lambda: dw_here(1), qkv[1].p2],
        )
        return carry

    lax.fori_loop(0, heads, head, 0)

    def grad_h_part(owner):
        cols = pl.ds(pl.multiple_of(owner * tok, tok), tok)
        return dot_tn(dP[:, cols], vm["w"][...])

    def core_grad(order):
        chip = lax.rem(place.chip + order, 2)
        g_stage[order] = grad_h_part(2 * chip + 1 - place.core).astype(BF16)
        c.start(("gh", order))

    core_grad(1)
    sums[2].p3()
    core_grad(0)
    g_acc[...] = grad_h_part(2 * (1 - place.chip) + place.core)
    c.wait_recv(("gh", 1))
    c.wait_send(("gh", 1))
    g_stage[1] = (g_acc[...] + g_core[1].astype(F32)).astype(BF16)
    c.start(("gh", "x"))
    qkv[0].p3()
    g_acc[...] = grad_h_part(2 * place.chip + place.core)
    c.wait(("gh", 0))
    g_acc[...] += g_core[0].astype(F32)
    sums[1].p6()
    dw_here(2)
    qkv[2].p2()
    qkv[1].p3()
    qkv[0].p4()
    sums[2].p4()
    sums[3].p2()
    qkv[2].p3()
    qkv[1].p4()
    qkv[0].p5()
    sums[2].p5()
    sums[3].p3()
    qkv[2].p4()
    qkv[1].p5()
    qkv[0].p6()
    sums[4].p2()
    sums[3].p4()
    qkv[2].p5()
    qkv[1].p6()
    sums[2].p6()
    sums[4].p3()
    sums[3].p5()
    qkv[2].p6()
    sums[4].p4()
    c.wait(("gh", "x"))
    grad_h_out[...] = g_acc[...] + g_x[...].astype(F32)
    sums[4].p5()
    sums[3].p6()
    sums[4].p6()
    for one in sums + qkv:
        one.p7()


def back_pass(n, tok, chunks, ins, grads, sums_shapes):
    heads = ins[1].shape[0]
    row = ins[4].shape[1]
    width = ins[8].shape[1]
    mine = heads * HD
    v = lambda *s, t=BF16: pltpu.VMEM(s, t)
    scratch = [pltpu.VMEM(a.shape, a.dtype) for a in ins]
    scratch += [
        v(mine, row + tok, t=F32), v(mine, row + tok, t=F32), v(heads, 1, row, t=F32), v(3 * mine, row),
        v(heads, 2 * HD, tok), v(heads, 2 * HD, tok), v(heads, width, mine),
        v(2, tok, width), v(2, tok, width), v(tok, width), v(tok, width, t=F32),
    ]
    copies = len(ins) + 4 * heads + 6 + heads
    for _, _, rows, cols in chunks:
        scratch += Sum.scratch("whole", rows, cols, n)
        copies += 16 + n // 8
    for _ in range(heads):
        scratch += Sum.scratch("share", row // tok * mine, mine, n)
        copies += 16 + n // 8
    scratch.append(pltpu.SemaphoreType.DMA((2, copies)))
    hbm = pl.BlockSpec(memory_space=pl.ANY)
    return pl.pallas_call(
        functools.partial(back_kernel, n, tok, row // tok, heads, chunks),
        out_shape=[jax.ShapeDtypeStruct(s, BF16) for s in sums_shapes]
        + [jax.ShapeDtypeStruct((heads, row // tok * mine, mine), BF16), jax.ShapeDtypeStruct((tok, width), F32)],
        in_specs=[hbm] * (len(ins) + len(grads)),
        out_specs=[hbm] * 4 + [pl.BlockSpec(memory_space=pltpu.VMEM)],
        scratch_shapes=scratch,
        compiler_params=pltpu.CompilerParams(collective_id=1, has_side_effects=True, vmem_limit_bytes=VMEM_LIMIT),
    )(*ins, *grads)


def run_starts(docs):
    at = jnp.arange(docs.shape[0], dtype=jnp.int32)
    fresh = jnp.concatenate([jnp.ones((1,), bool), docs[1:] != docs[:-1]])
    return lax.cummax(jnp.where(fresh, at, 0))


def per_device(residual, documents, gain_one, gain_two, w_qkv, w_out, w_up, w_down, cotangent):
    seq_count = lax.axis_size("seq")
    n = lax.axis_size("batch")
    place = lax.axis_index("seq")
    narrow = residual[0]
    tok = narrow.shape[0]
    width = w_out.shape[0]
    row = seq_count * tok
    heads = H // seq_count
    mine = heads * HD
    share = width // seq_count
    parts = w_up.shape[1] // width

    h_one = crms_norm(narrow, gain_one).astype(BF16)
    h_all = lax.all_gather(h_one, "seq", axis=0, tiled=True)
    row_docs = lax.all_gather(documents[0], "seq", axis=0, tiled=True)
    w_mine = lax.dynamic_index_in_dim(
        w_qkv.reshape(width, 3, seq_count, heads, HD), place, axis=2, keepdims=False
    )
    w_mine = w_mine.transpose(2, 1, 3, 0)
    packed = jnp.einsum("hcdw,tw->chdt", w_mine, h_all, preferred_element_type=F32).astype(BF16)
    q = packed[0] * jnp.bfloat16(1.0 / math.sqrt(HD))
    tail = slice(row - tok, row)
    prior, prior_docs = passed_along((packed[1:, :, :, tail], row_docs[tail]), "batch", 1)
    kv = jnp.concatenate([prior, packed[1:]], axis=3)
    start = run_starts(jnp.concatenate([prior_docs, row_docs]))[None, tok:]
    k, v = kv[0].swapaxes(1, 2), kv[1].swapaxes(1, 2)
    qT, kT, vT = q.reshape(mine, row), kv[0].reshape(mine, row + tok), kv[1].reshape(mine, row + tok)
    oT, lse = attend(k, qT, vT, start, tok)
    attended_T = lax.all_to_all(oT.astype(BF16), "seq", split_axis=1, concat_axis=0, tiled=True)
    attended = attended_T.T

    branch_one = jnp.dot(attended, w_out, preferred_element_type=F32)
    middle = narrow + shrink(branch_one)
    h_two = crms_norm(middle, gain_two).astype(BF16)
    up_proj = jnp.dot(h_two, w_up, preferred_element_type=F32)
    gelu_out = jax.nn.gelu(up_proj).astype(BF16)
    branch_two = jnp.dot(gelu_out, w_down, preferred_element_type=F32)
    new_residual = middle + shrink(branch_two)
    grad_new = cotangent[0]
    grad_two = shrink_back(grad_new).astype(BF16)
    grad_w_down = jnp.einsum("tf,td->fd", gelu_out, grad_two, preferred_element_type=F32)
    grad_gelu = jnp.einsum("td,fd->tf", grad_two, w_down, preferred_element_type=F32)
    _, gelu_pull = jax.vjp(jax.nn.gelu, up_proj)
    grad_up = gelu_pull(grad_gelu)[0].astype(BF16)
    grad_w_up = jnp.einsum("td,tf->df", h_two, grad_up, preferred_element_type=F32)
    grad_h_two = jnp.einsum("tf,df->td", grad_up, w_up, preferred_element_type=F32)
    _, norm_pull_two = jax.vjp(crms_norm, middle, gain_two)
    grad_middle_norm, _ = norm_pull_two(grad_h_two)
    grad_middle = grad_new + grad_middle_norm
    grad_one = shrink_back(grad_middle).astype(BF16)
    grad_w_out = jnp.einsum("td,te->de", attended, grad_one, preferred_element_type=F32)
    grad_attended_T = jnp.einsum("te,de->dt", grad_one, w_out, preferred_element_type=F32)
    doT = lax.all_to_all(
        grad_attended_T.astype(BF16), "seq", split_axis=0, concat_axis=1, tiled=True
    )

    def by_owner(grad, cut):
        split = grad.astype(BF16).reshape(seq_count, share, cut, grad.shape[1] // cut)
        return split.transpose(0, 2, 1, 3).reshape(seq_count, cut * share, grad.shape[1] // cut)

    chunks = [
        (0, 0, width // 2, width),
        (0, width // 2, width // 2, width),
        (1, 0, width // 2, width),
        (1, width // 2, width // 2, width),
        (2, 0, width // 2, width // 2),
    ]
    w_rows = w_mine.reshape(3 * mine, width)
    sum_down, sum_up, sum_out, sum_qkv, grad_h_one = back_pass(
        n,
        tok,
        chunks,
        (doT, k, v, kT, qT, oT, lse, start, h_all, w_rows),
        (grad_w_down.astype(BF16).reshape(seq_count, -1, width), by_owner(grad_w_up, parts), by_owner(grad_w_out, 2)),
        [(parts * share, width), (parts * share, width), (2 * share, width // 2)],
    )
    _, norm_pull_one = jax.vjp(crms_norm, narrow, gain_one)
    grad_narrow_norm, _ = norm_pull_one(grad_h_one)
    residual_grad = grad_middle + grad_narrow_norm
    sum_down = sum_down.astype(F32)
    sum_up = sum_up.astype(F32).reshape(parts, share, width).transpose(1, 0, 2).reshape(share, -1)
    sum_out = sum_out.astype(F32).reshape(2, share, -1).transpose(1, 0, 2).reshape(share, width)
    sum_qkv = sum_qkv.astype(F32).reshape(heads, seq_count, share, 3, HD)
    grad_w_qkv = sum_qkv.transpose(2, 3, 1, 0, 4).reshape(share, 3 * width)

    def gain_grad(w, total, gain):
        rows = lax.dynamic_slice_in_dim(w, place * share, share).astype(F32)
        mine_gain = lax.dynamic_slice_in_dim(gain, place * share, share)
        return jnp.sum(rows * total, axis=1) / mine_gain

    return (
        new_residual[None],
        residual_grad[None],
        gain_grad(w_qkv, grad_w_qkv, gain_one),
        gain_grad(w_up, sum_up, gain_two),
        grad_w_qkv,
        sum_out,
        sum_up,
        sum_down,
    )


def solution(mesh):
    placed = (
        P("batch", "seq", None),
        P("batch", "seq"),
        P(),
        P(),
        P(),
        P(),
        P(),
        P(),
        P("batch", "seq", None),
    )
    return jax.shard_map(
        per_device,
        mesh=mesh,
        in_specs=placed,
        out_specs=(
            P("batch", "seq", None),
            P("batch", "seq", None),
            P("seq"),
            P("seq"),
            P("seq", None),
            P("seq", None),
            P("seq", None),
            P("seq", None),
        ),
        check_vma=False,
    )
```

```python
import functools
import math

import jax
import jax.numpy as jnp
from jax import lax
from jax.experimental import pallas as pl
from jax.experimental.pallas import tpu as pltpu
from jax.sharding import PartitionSpec as P

H = 12
HD = 64
EPSILON = 1e-06
NEG = -1e30
F32, BF16 = jnp.float32, jnp.bfloat16
VMEM_LIMIT = 60 * 2**20


def dot(a, b):
    return lax.dot_general(a, b, (((1,), (0,)), ((), ())), preferred_element_type=F32)


def dot_nt(a, b):
    return lax.dot_general(a, b, (((1,), (1,)), ((), ())), preferred_element_type=F32)


def dot_tn(a, b):
    return lax.dot_general(a, b, (((0,), (0,)), ((), ())), preferred_element_type=F32)


def expand(narrow):
    return jnp.concatenate([narrow, -jnp.sum(narrow, axis=0, keepdims=True)], axis=0)


def shrink(full_vec):
    return full_vec[:-1] - jnp.mean(full_vec, axis=0, keepdims=True)


def shrink_back(grad_narrow):
    padded = jnp.concatenate([grad_narrow, jnp.zeros_like(grad_narrow[:1])], axis=0)
    return padded - jnp.sum(grad_narrow, axis=0, keepdims=True) / padded.shape[0]


def root(full_vec):
    return lax.rsqrt(jnp.mean(full_vec * full_vec, axis=0, keepdims=True) + EPSILON)


def norm_back(narrow, gain, grad_h):
    full_vec = expand(narrow)
    r = root(full_vec)
    scaled = gain * grad_h
    grad_full = r * (scaled - full_vec * (r * r * jnp.mean(scaled * full_vec, axis=0, keepdims=True)))
    return grad_full[:-1] - grad_full[-1:]


def column(gain_ref):
    return jnp.broadcast_to(gain_ref[...], (8, gain_ref.shape[1])).T[:, 0:1]


MESH = pl.DeviceIdType.MESH


class Place:
    def __init__(self, n):
        self.s = lax.axis_index("seq")
        self.b = lax.axis_index("batch")
        self.core = lax.rem(self.s, 2)
        self.chip = self.s // 2
        self.y = lax.rem(self.b, 2)
        self.z = lax.rem(self.b // 2, 4)
        self.far = self.b // 8
        self.n = n

    def core_mate(self):
        return (self.s + 1 - 2 * self.core, self.b)

    def chip_mate(self):
        return (self.s + 2 - 4 * self.chip, self.b)

    def cross_mate(self):
        return (3 - self.s, self.b)

    def y_mate(self):
        return (self.s, self.b + 1 - 2 * self.y)

    def z_of(self, d):
        return lax.rem(self.z + d, 4)

    def z_mate(self, d):
        return (self.s, self.b + 2 * (self.z_of(d) - self.z))

    def far_mate(self, d):
        f = lax.rem(self.far + d, self.n // 8)
        return (self.s, self.b + 8 * (f - self.far))

    def next_row(self):
        return (self.s, lax.rem(self.b + 1, self.n))

    def prior_row(self):
        return (self.s, lax.rem(self.b + self.n - 1, self.n))

    def all_mates(self):
        mates = [self.core_mate(), self.chip_mate(), self.cross_mate(), self.y_mate()]
        mates += [self.z_mate(d) for d in (1, 2, 3)]
        mates += [self.far_mate(d) for d in range(1, self.n // 8)]
        return mates + [self.next_row(), self.prior_row()]


def greet(mates):
    barrier = pltpu.get_barrier_semaphore()
    for mate in mates:
        pl.semaphore_signal(barrier, inc=1, device_id=mate, device_id_type=MESH)
    pl.semaphore_wait(barrier, len(mates))


class Copies:
    def __init__(self, sems):
        self.sems, self.made = sems, {}

    def remote(self, name, src, dst, mate):
        k = len(self.made)

        def make():
            return pltpu.make_async_remote_copy(
                src_ref=src(),
                dst_ref=dst(),
                send_sem=self.sems.at[0, k],
                recv_sem=self.sems.at[1, k],
                device_id=mate(),
                device_id_type=MESH,
            )

        self.made[name] = make

    def local(self, name, src, dst):
        k = len(self.made)

        def make():
            return pltpu.make_async_copy(src(), dst(), self.sems.at[0, k])

        self.made[name] = make

    def start(self, *names):
        for name in names:
            self.made[name]().start()

    def wait(self, *names):
        for name in names:
            self.made[name]().wait()

    def wait_recv(self, *names):
        for name in names:
            self.made[name]().wait_recv()

    def wait_send(self, *names):
        for name in names:
            self.made[name]().wait_send()


def rows_at(at, count):
    return pl.ds(pl.multiple_of(at, 16), count)


def blockwise(rows, body):
    step = next(s for s in (48, 32, 16) if rows % s == 0)

    def one(i, carry):
        body(i * step, step)
        return carry

    lax.fori_loop(0, rows // step, one, 0)


class Sum:
    def __init__(self, place, copies, name, mode, src, first, rows, cols, bufs, out):
        self.p, self.c, self.name, self.mode = place, copies, name, mode
        self.src, self.first, self.rows, self.cols, self.out = src, first, rows, cols, out
        self.own, self.ry, self.rz, self.res, self.rf = bufs[:5]
        self.rc = bufs[5] if mode == "whole" else None
        self.rx = bufs[-1] if mode != "share" else None
        self.mine = (lambda: self.own.at[self.p.chip]) if mode == "whole" else (lambda: self.own.at[0])
        self.define()

    def define(self):
        p, c, half, quarter, far = self.p, self.c, self.rows // 2, self.rows // 8, self.p.n // 8
        if self.mode == "whole":
            first = pl.ds(self.first, self.rows)
            for order in (1, 0):
                chip = lambda order=order: lax.rem(p.chip + order, 2)
                c.remote(
                    self.id(("core", order)),
                    lambda chip=chip: self.src.at[2 * chip() + 1 - p.core, first],
                    lambda chip=chip: self.rc.at[chip()],
                    p.core_mate,
                )
                c.local(
                    self.id(("own", order)),
                    lambda chip=chip: self.src.at[2 * chip() + p.core, first],
                    lambda chip=chip: self.own.at[chip()],
                )
            c.remote(self.id("x"), lambda: self.own.at[1 - p.chip], lambda: self.rx, p.chip_mate)
        elif self.mode == "pair":
            c.remote(self.id("x"), lambda: self.src.at[1 - p.chip], lambda: self.rx, p.chip_mate)
            c.local(self.id("own"), lambda: self.src.at[p.chip], lambda: self.own.at[0])
        elif self.src is not None:
            c.local(self.id("own"), lambda: self.src, lambda: self.own.at[0])
        other_half = lambda: self.mine().at[rows_at((1 - p.y) * half, half)]
        c.remote(self.id("y"), other_half, lambda: self.ry, p.y_mate)
        for d in (2, 1, 3):
            c.remote(
                self.id(("z", d)),
                lambda d=d: self.mine().at[rows_at(p.y * half + p.z_of(d) * quarter, quarter)],
                lambda d=d: self.rz.at[3 - d],
                lambda d=d: p.z_mate(d),
            )
        spot = lambda: self.res.at[rows_at(p.y * half + p.z * quarter, quarter)]
        for d in range(1, far):
            c.remote(
                self.id(("far", d)), spot, lambda d=d: self.rf.at[far - d - 1], lambda d=d: p.far_mate(d)
            )
        for d in (2, 1, 3):
            c.remote(self.id(("back z", d)), spot, spot, lambda d=d: p.z_mate(d))
        my_half = lambda: self.res.at[rows_at(p.y * half, half)]
        c.remote(self.id("back y"), my_half, my_half, p.y_mate)
        for k, (src, dst) in enumerate(self.out):
            c.local(self.id(("out", k)), lambda src=src: self.res.at[src], lambda dst=dst: dst)

    @staticmethod
    def scratch(mode, rows, cols, n):
        def v(*s):
            return pltpu.VMEM(s, BF16)

        whole = mode == "whole"
        out = [v(2 if whole else 1, rows, cols), v(rows // 2, cols), v(3, rows // 8, cols), v(rows, cols)]
        out.append(v(max(n // 8 - 1, 1), rows // 8, cols))
        out += [v(2, rows, cols)] if whole else []
        return out + ([v(rows, cols)] if mode != "share" else [])

    def id(self, what):
        return (self.name, what)

    def p0(self):
        if self.mode == "pair":
            self.c.start(self.id("x"), self.id("own"))
        elif self.mode == "share" and self.src is not None:
            self.c.start(self.id("own"))
        if self.mode != "whole":
            return
        for order in (1, 0):
            self.c.start(self.id(("core", order)), self.id(("own", order)))

    def add_core(self, chip):
        def body(at, step):
            rows = rows_at(at, step)
            total = self.own[chip, rows, :].astype(F32) + self.rc[chip, rows, :].astype(F32)
            self.own[chip, rows, :] = total.astype(BF16)

        blockwise(self.rows, body)

    def p1(self):
        p = self.p
        self.c.wait(self.id(("core", 1)), self.id(("own", 1)))
        self.add_core(1 - p.chip)
        self.c.start(self.id("x"))
        self.c.wait(self.id(("core", 0)), self.id(("own", 0)))
        self.add_core(p.chip)

    def add_x(self, first):
        own = self.mine()

        def body(at, step):
            rows = rows_at(first + at, step)
            own[rows, :] = (own[rows, :].astype(F32) + self.rx[rows, :].astype(F32)).astype(BF16)

        blockwise(self.rows // 2, body)

    def p2(self):
        p, half = self.p, self.rows // 2
        if self.mode == "pair" or self.mode == "share" and self.src is not None:
            self.c.wait(self.id("own"))
        if self.mode != "share":
            self.c.wait(self.id("x"))
            self.add_x((1 - p.y) * half)
        self.c.start(self.id("y"))
        if self.mode != "share":
            self.add_x(p.y * half)

    def p3(self):
        p, half = self.p, self.rows // 2
        self.c.wait(self.id("y"))
        own = self.mine()

        def body(at, step):
            rows = rows_at(p.y * half + at, step)
            total = own[rows, :].astype(F32) + self.ry[rows_at(at, step), :].astype(F32)
            own[rows, :] = total.astype(BF16)

        blockwise(half, body)
        self.c.start(*[self.id(("z", d)) for d in (2, 1, 3)])

    def p4(self):
        p, half, quarter = self.p, self.rows // 2, self.rows // 8
        self.c.wait(*[self.id(("z", d)) for d in (1, 2, 3)])
        own = self.mine()
        base = p.y * half + p.z * quarter

        def body(at, step):
            rows = rows_at(base + at, step)
            total = own[rows, :].astype(F32)
            for d in range(3):
                total = total + self.rz[d, rows_at(at, step), :].astype(F32)
            self.res[rows, :] = total.astype(BF16)

        blockwise(quarter, body)
        far = p.n // 8
        if far > 1:
            self.c.start(*[self.id(("far", d)) for d in range(1, far)])
            self.c.wait(*[self.id(("far", d)) for d in range(1, far)])

            def more(at, step):
                rows = rows_at(base + at, step)
                total = self.res[rows, :].astype(F32)
                for d in range(far - 1):
                    total = total + self.rf[d, rows_at(at, step), :].astype(F32)
                self.res[rows, :] = total.astype(BF16)

            blockwise(quarter, more)
        self.c.start(*[self.id(("back z", d)) for d in (2, 1, 3)])

    def p5(self):
        self.c.wait(*[self.id(("back z", d)) for d in (1, 2, 3)])
        self.c.start(self.id("back y"))

    def p6(self):
        self.c.wait(self.id("back y"))
        self.c.start(*[self.id(("out", k)) for k in range(len(self.out))])

    def p7(self):
        self.c.wait(*[self.id(("out", k)) for k in range(len(self.out))])


def fore_kernel(n, tok, blocks, heads, *refs):
    x, gain, docs, w = refs[:4]
    attT_o, hT_o, kT_o, qT_o, oT_o, lse_o, start_o, k_o, v_o, wm_o = refs[4:14]
    xs, ws, wm, hT, docs_all, prior_docs, start, kT, vT, qT, kk, vv, acc, m_ref, l_ref, lse, stage, sems = refs[14:]
    width = xs.shape[0] + 1
    row = blocks * tok
    mine = heads * HD
    p = Place(n)
    c = Copies(sems)
    mates = {"core": p.core_mate, "chip": p.chip_mate, "cross": p.cross_mate}
    block = lambda at: pl.ds(pl.multiple_of(at * tok, tok), tok)
    here = lambda: block(p.s)
    c.local("x", lambda: x.at[:, 0, :], lambda: xs)
    c.local("w", lambda: w, lambda: ws)
    c.local("docs", lambda: docs, lambda: docs_all.at[:, here()])
    for name, mate in mates.items():
        c.remote(("docs", name), lambda: docs, lambda: docs_all.at[:, here()], mate)
    last = pl.ds(row - tok, tok)
    c.remote("prior docs", lambda: docs_all.at[:, last], lambda: prior_docs, p.next_row)
    c.remote("h core", lambda: hT.at[:, here()], lambda: hT.at[:, here()], p.core_mate)
    half = tok // 2
    for k in range(2):
        piece = lambda s, k=k: hT.at[:, pl.ds(pl.multiple_of(s * tok + k * half, half), half)]
        c.remote(("h chip", k), lambda piece=piece: piece(p.s), lambda piece=piece: piece(p.s), p.chip_mate)
        other = lambda piece=piece: piece(p.chip_mate()[0])
        c.remote(("h on", k), other, other, p.core_mate)
    end = pl.ds(row, tok)
    c.remote("prior k", lambda: kT.at[:, end], lambda: kT.at[:, 0:tok], p.next_row)
    c.remote("prior v", lambda: vT.at[:, end], lambda: vT.at[:, 0:tok], p.next_row)
    for h in range(heads):
        spot = lambda h=h: attT_o.at[pl.ds(pl.multiple_of(p.s * mine + h * HD, HD), HD)]
        for name, mate in mates.items():
            src = lambda h=h, mate=mate: stage.at[pl.ds(h * HD, HD), block(mate()[0])]
            c.remote(("att", h, name), src, spot, mate)
        c.local(("att", h, "own"), lambda h=h: stage.at[pl.ds(h * HD, HD), here()], spot)
    outs = {"hT": (hT, hT_o), "kT": (kT, kT_o), "qT": (qT, qT_o), "oT": (acc, oT_o), "lse": (lse, lse_o)}
    outs.update({"start": (start, start_o), "k": (kk, k_o), "v": (vv, v_o), "wm": (wm, wm_o)})
    for name, (src, dst) in outs.items():
        c.local(("out", name), lambda src=src: src, lambda dst=dst: dst)

    c.start("x", "docs", "w")
    greet([p.core_mate(), p.chip_mate(), p.cross_mate(), p.next_row(), p.prior_row()])
    c.start(*[("docs", name) for name in mates])
    c.wait("x")
    full_vec = expand(xs[...])
    hT[:, here()] = (column(gain) * full_vec * root(full_vec)).astype(BF16)
    c.start(("h chip", 0), "h core")
    c.start(("h chip", 1))

    c.wait("w")
    for s in range(blocks):
        @pl.when(p.s == s)
        def _():
            for h in range(heads):
                for k in range(3):
                    at = k * width + s * mine + h * HD
                    to = (h * 3 + k) * HD
                    wm[:, to : to + HD] = ws[:, at : at + HD]

    c.wait("docs", *[("docs", name) for name in mates])
    c.start("prior docs")
    ids = jnp.broadcast_to(docs_all[...], (8, row))
    pos = lax.broadcasted_iota(jnp.int32, (8, row), 1)
    since = jnp.where((ids != pltpu.roll(ids, 1, 1)) | (pos == 0), pos, 0)
    hop = 1
    while hop < row:
        since = jnp.maximum(since, jnp.where(pos >= hop, pltpu.roll(since, hop, 1), 0))
        hop *= 2
    start[...] = since[0:1] + tok
    m_ref[...] = jnp.full(m_ref.shape, NEG, F32)
    l_ref[...] = jnp.zeros(l_ref.shape, F32)
    acc[...] = jnp.zeros(acc.shape, F32)

    def natural(keys_at):
        keys = pl.ds(pl.multiple_of(keys_at, tok), tok)
        for h in range(heads):
            kk[h, keys, :] = kT[h * HD : (h + 1) * HD, keys].T
            vv[h, keys, :] = vT[h * HD : (h + 1) * HD, keys].T

    def project(at):
        packed = dot_tn(wm[...], hT[:, block(at)]).astype(BF16)
        keys = pl.ds(pl.multiple_of((at + 1) * tok, tok), tok)
        for h in range(heads):
            to, base = slice(h * HD, (h + 1) * HD), h * 3 * HD
            qT[to, block(at)] = packed[base : base + HD] * jnp.bfloat16(1.0 / math.sqrt(HD))
            kT[to, keys] = packed[base + HD : base + 2 * HD]
            vT[to, keys] = packed[base + 2 * HD : base + 3 * HD]
        natural((at + 1) * tok)

    def pair(h, q0, qw, k0, kw, causal):
        hr = pl.ds(pl.multiple_of(h * HD, HD), HD)
        qs, ks = pl.ds(pl.multiple_of(q0, 128), qw), pl.ds(pl.multiple_of(k0, 128), kw)
        s = dot(kk[h, ks, :], qT[hr, qs])
        at = lax.broadcasted_iota(jnp.int32, s.shape, 0) + k0
        keep = at >= start[:, qs]
        if causal:
            until = lax.broadcasted_iota(jnp.int32, s.shape, 1) + (q0 + tok)
            keep = keep & (at <= until)
        s = jnp.where(keep, s, NEG)
        m = m_ref[h, :, qs]
        new_m = jnp.maximum(m, jnp.max(s, axis=0, keepdims=True))
        e = jnp.exp(s - new_m)
        shift = jnp.exp(m - new_m)
        m_ref[h, :, qs] = new_m
        l_ref[h, :, qs] = l_ref[h, :, qs] * shift + jnp.sum(e, axis=0, keepdims=True)
        acc[hr, qs] = acc[hr, qs] * shift + dot(vT[hr, ks], e.astype(BF16))

    def within(h, first):
        def one(t, carry):
            at = (first + t) * tok
            pair(h, at, tok, at + tok, half, True)
            pair(h, at + half, half, at + tok + half, half, True)
            return carry

        lax.fori_loop(0, 2, one, 0)

    def finish(h, i):
        hr, qs = pl.ds(pl.multiple_of(h * HD, HD), HD), block(i)
        out = acc[hr, qs] / l_ref[h, :, qs]
        acc[hr, qs] = out
        stage[hr, qs] = out.astype(BF16)
        lse[h, :, qs] = m_ref[h, :, qs] + jnp.log(l_ref[h, :, qs])

    def send_att(h, zero):
        for name, mate in list(mates.items()) + [("own", lambda: (p.s,))]:
            @pl.when((mate()[0] == 0) == zero)
            def _():
                c.start(("att", h, name))

    near, far = 2 * p.chip, 2 * (1 - p.chip)
    c.wait_recv("h core")

    def project_near(t, carry):
        project(near + t)
        return carry

    lax.fori_loop(0, 2, project_near, 0)

    @pl.when(p.chip == 1)
    def _():
        c.start("prior k", "prior v")

    def first(h, carry):
        within(h, near)
        pair(h, (near + 1) * tok, tok, (near + 1) * tok, tok, False)
        return carry

    lax.fori_loop(0, heads, first, 0)
    for k in range(2):
        c.wait_recv(("h chip", k))
        c.start(("h on", k))
    project(p.chip_mate()[0])
    c.wait_recv(("h on", 0), ("h on", 1))
    project(p.cross_mate()[0])

    @pl.when(p.chip == 0)
    def _():
        c.start("prior k", "prior v")

    def second(h, carry):
        within(h, far)
        pair(h, (far + 1) * tok, tok, (far + 1) * tok, tok, False)

        def cross(t, carry):
            pair(h, (2 + t // 2) * tok, tok, (1 + t % 2) * tok, tok, False)
            return carry

        lax.fori_loop(0, 4, cross, 0)
        lax.fori_loop(1, blocks, lambda i, carry: (finish(h, i), carry)[1], 0)
        for k in range(heads):
            @pl.when(h == k)
            def _():
                send_att(k, False)
        return carry

    lax.fori_loop(0, heads, second, 0)
    c.wait_recv("prior docs")
    from_doc = docs_all[:, 0:1]
    at = lax.broadcasted_iota(jnp.int32, (1, tok), 1)
    run = jnp.max(jnp.where(prior_docs[...] != from_doc, at + 1, 0), axis=1, keepdims=True)
    start[:, 0:tok] = jnp.where(start[:, 0:tok] == tok, run, start[:, 0:tok])
    c.wait_recv("prior k", "prior v")
    natural(0)

    def third(h, carry):
        pair(h, 0, tok, 0, tok, False)
        finish(h, 0)
        for k in range(heads):
            @pl.when(h == k)
            def _():
                send_att(k, True)
        return carry

    lax.fori_loop(0, heads, third, 0)
    c.start(*[("out", name) for name in outs])
    c.wait_send("h core", ("h chip", 0), ("h chip", 1), ("h on", 0), ("h on", 1), "prior docs", "prior k", "prior v")
    for h in range(heads):
        c.wait(*[("att", h, name) for name in list(mates) + ["own"]])
    c.wait(*[("out", name) for name in outs])


def fore_pass(n, tok, blocks, x, gain, docs, w):
    width, heads = w.shape[0], H // blocks
    row, mine = blocks * tok, heads * HD
    v = lambda *s, t=BF16: pltpu.VMEM(s, t)
    o = lambda *s, t=BF16: jax.ShapeDtypeStruct(s, t)
    hbm = pl.BlockSpec(memory_space=pl.ANY)
    scratch = [
        v(width - 1, tok, t=F32), v(width, 3 * width), v(width, 3 * mine), v(width, row),
        v(1, row, t=jnp.int32), v(1, tok, t=jnp.int32), v(1, row, t=jnp.int32),
        v(mine, row + tok), v(mine, row + tok), v(mine, row), v(heads, row + tok, HD), v(heads, row + tok, HD),
        v(mine, row, t=F32), v(heads, 1, row, t=F32), v(heads, 1, row, t=F32), v(heads, 1, row, t=F32), v(mine, row),
        pltpu.SemaphoreType.DMA((2, 24 + 4 * heads)),
    ]
    return pl.pallas_call(
        functools.partial(fore_kernel, n, tok, blocks, heads),
        out_shape=[
            o(width, tok), o(width, row), o(mine, row + tok), o(mine, row), o(mine, row, t=F32), o(heads, 1, row, t=F32),
            o(1, row, t=jnp.int32), o(heads, row + tok, HD), o(heads, row + tok, HD), o(width, 3 * mine),
        ],
        in_specs=[hbm, pl.BlockSpec(memory_space=pltpu.VMEM), hbm, hbm],
        out_specs=[hbm] * 10,
        scratch_shapes=scratch,
        compiler_params=pltpu.CompilerParams(collective_id=0, has_side_effects=True, vmem_limit_bytes=VMEM_LIMIT),
    )(x, gain, docs, w)


def gelu_both(v, grad):
    rate = math.sqrt(2.0 / math.pi)
    square = v * v
    th = jnp.tanh(rate * v * (1.0 + 0.044715 * square))
    up = 0.5 * (1.0 + th)
    slope = up + 0.5 * v * (1.0 - th * th) * (rate * (1.0 + 3.0 * 0.044715 * square))
    return (v * up).astype(BF16), (grad * slope).astype(BF16)


def mid_kernel(n, blocks, *refs):
    x, cot, attT, gain, w_out, w_up, w_down = refs[:7]
    new_o, gm_o, doT_o, gu_o, go_o, share_o, pair_o = refs[7:14]
    xs, cs, at, wo, wu, wd, mid, h2, g2, g1, geluT, gupT, b2, gh, dw, rc, rx, ga, gu, go, sems = refs[14:]
    tok, width = xs.shape[1], xs.shape[0] + 1
    parts = wu.shape[1] // width
    share = width // blocks
    p = Place(n)
    c = Copies(sems)
    mates = {"cross": p.cross_mate, "chip": p.chip_mate, "core": p.core_mate}
    c.local("att", lambda: attT, lambda: at)
    c.local("wo", lambda: w_out, lambda: wo)
    c.local("x", lambda: x.at[:, 0, :], lambda: xs)
    c.local("cot", lambda: cot.at[:, 0, :], lambda: cs)
    c.local("wu", lambda: w_up, lambda: wu)
    c.local("wd", lambda: w_down, lambda: wd)
    c.remote("core 0", lambda: dw.at[0], lambda: rc.at[0], p.core_mate)
    c.remote("core 1", lambda: dw.at[2], lambda: rc.at[1], p.core_mate)
    part = width // 2
    c.remote("chip", lambda: dw.at[1, 0:part], lambda: rx, p.chip_mate)
    there = lambda: doT_o.at[:, pl.ds(pl.multiple_of(p.s * tok, tok), tok)]
    for name, mate in mates.items():
        c.remote(("ga", name), lambda mate=mate: ga.at[rows_at(mate()[0] * share, share)], there, mate)
    c.local(("ga", "own"), lambda: ga.at[rows_at(p.s * share, share)], there)
    c.local("new out", lambda: xs, lambda: new_o.at[:, 0, :])
    c.local("gm", lambda: cs, lambda: gm_o)
    for k in range(parts):
        c.local(("gu", k), lambda k=k: gu.at[:, pl.ds(k * share, share)], lambda k=k: gu_o.at[:, pl.ds(k * share, share)])
    c.local("go", lambda: go, lambda: go_o)
    c.local("share", lambda: dw.at[3, 0:part], lambda: share_o)
    c.local("pair 0", lambda: dw.at[1, part:width], lambda: pair_o.at[1 - p.chip])
    c.local("pair 1", lambda: dw.at[3, part:width], lambda: pair_o.at[p.chip])

    c.start("att", "wo", "x", "cot", "wu", "wd")
    greet([p.core_mate(), p.chip_mate(), p.cross_mate()])
    c.wait("att", "wo")
    branch_one = dot_tn(wo[...], at[...])
    c.wait("x")
    mid[...] = xs[...] + shrink(branch_one)
    full_vec = expand(mid[...])
    gain_col = column(gain)
    h2[...] = (gain_col * full_vec * root(full_vec)).astype(BF16)
    c.wait("cot")
    g2[...] = shrink_back(cs[...]).astype(BF16)
    b2[...] = jnp.zeros_like(b2)
    gh[...] = jnp.zeros_like(gh)
    c.wait("wu", "wd")

    def add(dst, src, rows):
        def body(first, step):
            r = rows_at(first, step)
            dw[dst, r, :] = (dw[dst, r, :].astype(F32) + src[r, :].astype(F32)).astype(BF16)

        blockwise(rows, body)

    def piece(t, carry):
        s = jnp.where(t == 0, p.cross_mate()[0], jnp.where(t == 1, p.chip_mate()[0], jnp.where(t == 2, p.core_mate()[0], p.s)))
        its = pl.ds(pl.multiple_of(s * width, width), width)
        up = dot_tn(wu[:, its], h2[...])
        grad_gelu = dot(wd[its, :], g2[...])
        gelu, grad_up = gelu_both(up, grad_gelu)
        geluT[...] = gelu
        gupT[its, :] = grad_up
        dw[t] = dot_nt(geluT[...], g2[...]).astype(BF16)

        @pl.when(t == 0)
        def _():
            c.start("core 0")

        @pl.when(t == 2)
        def _():
            c.start("core 1")

        b2[...] += dot_tn(wd[its, :], geluT[...])
        gh[...] += dot(wu[:, its], gupT[its, :])

        @pl.when(t == 1)
        def _():
            c.wait_recv("core 0")
            add(1, rc.at[0], width)
            c.start("chip")

        return carry

    lax.fori_loop(0, parts, piece, 0)
    grad_middle = cs[...] + norm_back(mid[...], gain_col, gh[...])
    cs[...] = grad_middle
    g1[...] = shrink_back(grad_middle).astype(BF16)
    ga[...] = dot(wo[...], g1[...]).astype(BF16)
    c.start(*[("ga", name) for name in list(mates) + ["own"]])
    c.start("gm")
    xs[...] = mid[...] + shrink(b2[...])
    c.start("new out")

    def up_grad(k, carry):
        its = pl.ds(pl.multiple_of(k * width, width), width)
        grad = dot_nt(h2[...], gupT[its, :]).astype(BF16)
        for s in range(blocks):
            gu[s, rows_at(k * share, share), :] = grad[s * share : (s + 1) * share]
        return carry

    lax.fori_loop(0, parts, up_grad, 0)
    c.start(*[("gu", k) for k in range(parts)])
    out_grad = dot_nt(at[...], g1[...]).astype(BF16)
    for s in range(blocks):
        for k in range(2):
            go[s, k * share : (k + 1) * share, :] = out_grad[s * share : (s + 1) * share, k * part : (k + 1) * part]
    c.start("go")
    c.wait_recv("core 1")
    add(3, rc.at[1], width)
    c.start("pair 0", "pair 1")
    c.wait("chip")
    add(3, rx, part)
    c.start("share")
    c.wait_send("core 0", "core 1")
    c.wait(*[("ga", name) for name in list(mates) + ["own"]])
    c.wait("gm", "new out", "go", "share", "pair 0", "pair 1", *[("gu", k) for k in range(parts)])


def mid_pass(n, blocks, x, cot, attT, gain, w_out, w_up, w_down):
    width, tok = attT.shape
    parts, share = w_up.shape[1] // width, width // blocks
    v = lambda *s, t=BF16: pltpu.VMEM(s, t)
    o = lambda *s, t=BF16: jax.ShapeDtypeStruct(s, t)
    hbm = pl.BlockSpec(memory_space=pl.ANY)
    scratch = [
        v(width - 1, tok, t=F32), v(width - 1, tok, t=F32), v(width, tok), v(width, width), v(*w_up.shape), v(*w_down.shape),
        v(width - 1, tok, t=F32), v(width, tok), v(width, tok), v(width, tok), v(width, tok), v(w_up.shape[1], tok),
        v(width, tok, t=F32), v(width, tok, t=F32), v(4, width, width), v(2, width, width), v(width // 2, width),
        v(width, tok), v(blocks, parts * share, width), v(blocks, 2 * share, width // 2),
        pltpu.SemaphoreType.DMA((2, 32)),
    ]
    return pl.pallas_call(
        functools.partial(mid_kernel, n, blocks),
        out_shape=[
            o(width - 1, 1, tok, t=F32), o(width - 1, tok, t=F32), o(share, blocks * tok), o(blocks, parts * share, width),
            o(blocks, 2 * share, width // 2), o(width // 2, width), o(2, width // 2, width),
        ],
        in_specs=[hbm, hbm, hbm, pl.BlockSpec(memory_space=pltpu.VMEM), hbm, hbm, hbm],
        out_specs=[hbm] * 7,
        scratch_shapes=scratch,
        compiler_params=pltpu.CompilerParams(collective_id=2, has_side_effects=True, vmem_limit_bytes=VMEM_LIMIT),
    )(x, cot, attT, gain, w_out, w_up, w_down)


BACK_IN = ("doT", "k", "v", "kT", "qT", "oT", "lse", "start", "hT", "wm", "x", "gm")
DW = ("cross", "chip", "core", "own")


def back_kernel(n, tok, blocks, heads, parts, *refs):
    refs = list(refs)
    take = lambda count: [refs.pop(0) for _ in range(count)]
    hbm = dict(zip(BACK_IN, take(len(BACK_IN))))
    share_d, pair_d, gu, go, w_qkv, w_up, gain = take(7)
    down_o, up_o, out_o, qkv_o, gain_one_o, gain_two_o, rg_o = take(7)
    vm = dict(zip(BACK_IN, take(len(BACK_IN))))
    dkT, dvT, delta, dP, prior_out, prior_in, dws, g_stage, g_core, g_x, g_acc, qkv_v, wq_rows, wu_rows = take(14)
    p, hd, row = Place(n), HD, blocks * tok
    mine, width = heads * hd, blocks * heads * hd
    share, part = width // blocks, width // 2
    rows_out = lambda ref, at, count: ref.at[pl.ds(at, count)]
    per_part = part // share

    def up_outs(k):
        return [
            (pl.ds(j * share, share), up_o.at[:, pl.ds((k * per_part + j) * width, width)]) for j in range(per_part)
        ]

    plans = [
        ("d0", "share", share_d, 0, part, width, [(pl.ds(0, part), rows_out(down_o, 0, part))]),
        ("d1", "pair", pair_d, 0, part, width, [(pl.ds(0, part), rows_out(down_o, part, part))]),
    ]
    for k in range(parts // per_part):
        plans.append((("u", k), "whole", gu, k * part, part, width, up_outs(k)))
    out_parts = [(pl.ds(k * share, share), out_o.at[:, pl.ds(k * part, part)]) for k in range(2)]
    plans.append(("o", "whole", go, 0, 2 * share, part, out_parts))
    for k in range(heads):
        plans.append((("q", k), "share", None, 0, row // tok * mine, mine, []))
    bufs = [take(len(Sum.scratch(plan[1], 16, 128, n))) for plan in plans]
    sems = refs.pop(0)
    c = Copies(sems)
    for name in BACK_IN:
        src = (lambda: hbm["x"].at[:, 0, :]) if name == "x" else (lambda name=name: hbm[name])
        c.local(name, src, lambda name=name: vm[name])
    c.local("wq rows", lambda: w_qkv.at[rows_at(p.s * share, share)], lambda: wq_rows)
    c.local("wu rows", lambda: w_up.at[rows_at(p.s * share, share)], lambda: wu_rows)
    sums = [Sum(p, c, plan[0], plan[1], plan[2], plan[3], plan[4], plan[5], buf, plan[6]) for plan, buf in zip(plans, bufs)]
    d0, d1, u0, u1, o, qkv = sums[0], sums[1], sums[2], sums[3], sums[4], sums[5:]
    for k in range(heads):
        spot = lambda k=k: qkv[k].own.at[0, rows_at(p.s * mine, mine)]
        for what, mate in (("cross", p.cross_mate), ("chip", p.chip_mate), ("core", p.core_mate)):
            c.remote(("dw", k, what), lambda k=k, mate=mate: dws.at[k, rows_at(mate()[0] * mine, mine)], spot, mate)
        c.local(("dw", k, "own"), lambda k=k: dws.at[k, rows_at(p.s * mine, mine)], spot)
        c.remote(("prior", k), lambda k=k: prior_out.at[k], lambda k=k: prior_in.at[k], p.prior_row)
    for order in (1, 0):
        c.remote(("gh", order), lambda order=order: g_stage.at[order], lambda order=order: g_core.at[order], p.core_mate)
    c.remote(("gh", "x"), lambda: g_stage.at[1], lambda: g_x, p.chip_mate)
    c.local("rg", lambda: vm["gm"], lambda: rg_o.at[:, 0, :])
    c.local("qkv", lambda: qkv_v, lambda: qkv_o)

    first = BACK_IN[:8]
    c.start(*first)
    greet(p.all_mates())
    d1.p0()
    d0.p0()
    u0.p0()
    c.start(*BACK_IN[8:], "wq rows", "wu rows")
    d0.p2()
    u0.p1()
    u1.p0()
    o.p0()
    c.wait(*first)
    dqT = vm["oT"]
    doT, kk, vv, kT, qT, lse, start = (vm[x] for x in ("doT", "k", "v", "kT", "qT", "lse", "start"))

    def make_delta(h, carry):
        rows = pl.ds(pl.multiple_of(h * hd, hd), hd)
        delta[h] = jnp.sum(doT[rows, :].astype(F32) * vm["oT"][rows, :], axis=0, keepdims=True)
        return carry

    lax.fori_loop(0, heads, make_delta, 0)
    dqT[...] = jnp.zeros_like(dqT)
    dkT[...] = jnp.zeros_like(dkT)
    dvT[...] = jnp.zeros_like(dvT)

    def pair(h, q0, qw, k0, kw, causal):
        hr = pl.ds(pl.multiple_of(h * hd, hd), hd)
        qs, ks = pl.ds(pl.multiple_of(q0, 128), qw), pl.ds(pl.multiple_of(k0, 128), kw)
        q_blk, do_blk = qT[hr, qs], doT[hr, qs]
        s = dot(kk[h, ks, :], q_blk)
        e = jnp.exp(s - lse[h, :, qs])
        at = lax.broadcasted_iota(jnp.int32, s.shape, 0) + k0
        keep = at >= start[:, qs]
        if causal:
            until = lax.broadcasted_iota(jnp.int32, s.shape, 1) + (q0 + tok)
            keep = keep & (at <= until)
        e = jnp.where(keep, e, 0.0)
        dp = dot(vv[h, ks, :], do_blk)
        ds = (e * (dp - delta[h, :, qs])).astype(BF16)
        dvT[hr, ks] += dot_nt(do_blk, e.astype(BF16))
        dkT[hr, ks] += dot_nt(q_blk, ds)
        dqT[hr, qs] += dot(kT[hr, ks], ds)

    def full(h, first, last):
        def one(t, carry):
            i = jnp.where(t == 0, 0, jnp.where(t <= 3, 3, jnp.where(t <= 5, 2, 1)))
            j = jnp.where(t == 0, 0, jnp.where(t <= 3, t, jnp.where(t <= 5, t - 3, 1)))
            pair(h, i * tok, tok, j * tok, tok, False)
            return carry

        lax.fori_loop(first, last, one, 0)

    def diagonal(h):
        sub = tok // 2

        def one(i, carry):
            pair(h, i * tok, tok, (i + 1) * tok, sub, True)
            pair(h, i * tok + sub, sub, (i + 1) * tok + sub, sub, True)
            return carry

        lax.fori_loop(0, blocks, one, 0)

    def fill_prior(h):
        hr = pl.ds(pl.multiple_of(h * hd, hd), hd)
        prior_out[h, 0:hd, :] = dkT[hr, 0:tok].astype(BF16)
        prior_out[h, hd : 2 * hd, :] = dvT[hr, 0:tok].astype(BF16)

    def close(h):
        hr = pl.ds(pl.multiple_of(h * hd, hd), hd)
        last = pl.ds(row, tok)
        dkT[hr, last] += prior_in[h, 0:hd, :].astype(F32)
        dvT[hr, last] += prior_in[h, hd : 2 * hd, :].astype(F32)
        base = h * 3 * hd
        for k, (src, at) in enumerate(((dqT, 0), (dkT, tok), (dvT, tok))):
            val = src[hr, at:]
            val = val * (1.0 / math.sqrt(hd)) if k == 0 else val
            dP[pl.ds(pl.multiple_of(base + k * hd, hd), hd), :] = val.astype(BF16)
        dws[h] = dot_nt(vm["hT"][...], dP[pl.ds(pl.multiple_of(base, hd), 3 * hd), :]).astype(BF16)

    def send_dw(k):
        return lambda: c.start(*[("dw", k, what) for what in DW])

    def dw_here(k):
        return lambda: c.wait(*[("dw", k, what) for what in DW])

    def at_head(h, *todo):
        for k, steps in enumerate(todo):
            if steps:
                @pl.when(h == k)
                def _():
                    for step in steps:
                        step()

    def head(h, carry):
        full(h, 0, 1)
        fill_prior(h)
        at_head(h, *[[lambda k=k: c.start(("prior", k))] for k in range(heads)])
        full(h, 1, 4)
        at_head(h, [d0.p3, u1.p1], [d0.p6, d1.p4, u0.p2], [d1.p6, u0.p4, u1.p2])
        full(h, 4, 7)
        at_head(h, [d0.p4], [d1.p5, u0.p3], [u0.p5, u1.p3])
        diagonal(h)
        at_head(h, [d1.p2, d0.p5], [o.p1], [u0.p6])
        at_head(h, *[[lambda k=k: c.wait(("prior", k))] for k in range(heads)])
        if heads:
            at_head(h, [lambda: c.wait("hT", "wm")])
        close(h)
        at_head(h, [send_dw(0), d1.p3], [send_dw(1), dw_here(0), qkv[0].p2], [send_dw(2), dw_here(1), qkv[1].p2])
        return carry

    lax.fori_loop(0, heads, head, 0)

    def grad_h_part(owner):
        return dot(vm["wm"][...], dP[:, pl.ds(pl.multiple_of(owner * tok, tok), tok)])

    def core_grad(order):
        chip = lax.rem(p.chip + order, 2)
        g_stage[order] = grad_h_part(2 * chip + 1 - p.core).astype(BF16)
        c.start(("gh", order))

    core_grad(1)
    core_grad(0)
    g_acc[...] = grad_h_part(2 * (1 - p.chip) + p.core)
    c.wait(("gh", 1))
    g_stage[1] = (g_acc[...] + g_core[1].astype(F32)).astype(BF16)
    c.start(("gh", "x"))
    qkv[0].p3()
    u1.p4()
    g_acc[...] = grad_h_part(2 * p.chip + p.core)
    c.wait(("gh", 0))
    g_acc[...] += g_core[0].astype(F32)
    dw_here(2)()
    qkv[2].p2()
    qkv[1].p3()
    qkv[0].p4()
    o.p2()
    u1.p5()
    qkv[2].p3()
    qkv[1].p4()
    qkv[0].p5()
    o.p3()
    qkv[2].p4()
    qkv[1].p5()
    u1.p6()
    o.p4()
    qkv[2].p5()
    qkv[0].p6()
    qkv[1].p6()
    o.p5()
    c.wait("x", "gm", ("gh", "x"))
    gain_col = column(gain)
    vm["gm"][...] += norm_back(vm["x"][...], gain_col, g_acc[...] + g_x[...].astype(F32))
    c.start("rg")
    c.wait("wq rows", "wu rows")
    total = jnp.zeros((share, 1), F32)
    for k, one in enumerate((u0, u1)):
        for j in range(per_part):
            cols = slice((k * per_part + j) * width, (k * per_part + j + 1) * width)
            prod = one.res[j * share : (j + 1) * share, :].astype(F32) * wu_rows[:, cols].astype(F32)
            total = total + jnp.sum(prod, axis=1, keepdims=True)
    gain_two_o[...] = jnp.broadcast_to(total, gain_two_o.shape)
    qkv[2].p6()
    total = jnp.zeros((share, 1), F32)
    for k in range(3):
        for s in range(blocks):
            cells = [q.res[s * share : (s + 1) * share, k * hd : (k + 1) * hd] for q in qkv]
            cells = jnp.concatenate(cells, axis=1).astype(F32)
            cols = slice(k * width + s * mine, k * width + (s + 1) * mine)
            qkv_v[:, cols] = cells
            total = total + jnp.sum(cells * wq_rows[:, cols].astype(F32), axis=1, keepdims=True)
    gain_one_o[...] = jnp.broadcast_to(total, gain_one_o.shape)
    c.start("qkv")
    o.p6()
    for one in sums:
        one.p7()
    c.wait("qkv", "rg")


def back_pass(n, tok, blocks, ins, share_d, pair_d, gu, go, w_qkv, w_up, gain):
    heads = ins[1].shape[0]
    row = blocks * tok
    width = ins[8].shape[0]
    mine = heads * HD
    parts, share, part = w_up.shape[1] // width, width // blocks, width // 2
    v = lambda *s, t=BF16: pltpu.VMEM(s, t)
    o = lambda *s, t=BF16: jax.ShapeDtypeStruct(s, t)
    scratch = [v(width - 1, tok, t=F32) if name == "x" else pltpu.VMEM(a.shape, a.dtype) for name, a in zip(BACK_IN, ins)]
    scratch += [
        v(mine, row + tok, t=F32), v(mine, row + tok, t=F32), v(heads, 1, row, t=F32), v(3 * mine, row),
        v(heads, 2 * HD, tok), v(heads, 2 * HD, tok), v(heads, width, mine),
        v(2, width, tok), v(2, width, tok), v(width, tok), v(width, tok, t=F32), v(share, 3 * width, t=F32),
        v(share, 3 * width), v(share, w_up.shape[1]),
    ]
    modes = [("share", part, width), ("pair", part, width), ("whole", part, width), ("whole", part, width)]
    modes += [("whole", 2 * share, part)] + [("share", blocks * mine, mine)] * heads
    copies = len(ins) + 5 * heads + 8
    for mode, rows, cols in modes:
        scratch += Sum.scratch(mode, rows, cols, n)
        copies += 16 + n // 8
    scratch.append(pltpu.SemaphoreType.DMA((2, copies)))
    hbm = pl.BlockSpec(memory_space=pl.ANY)
    vmem = pl.BlockSpec(memory_space=pltpu.VMEM)
    return pl.pallas_call(
        functools.partial(back_kernel, n, tok, blocks, heads, parts),
        out_shape=[
            o(width, width), o(share, parts * width), o(share, width), o(share, 3 * width, t=F32),
            o(share, 128, t=F32), o(share, 128, t=F32), o(width - 1, 1, tok, t=F32),
        ],
        in_specs=[hbm] * (len(ins) + 6) + [vmem],
        out_specs=[hbm] * 4 + [vmem, vmem, hbm],
        scratch_shapes=scratch,
        compiler_params=pltpu.CompilerParams(collective_id=1, has_side_effects=True, vmem_limit_bytes=VMEM_LIMIT),
    )(*ins, share_d, pair_d, gu, go, w_qkv, w_up, gain)


def per_device(residual, documents, gain_one, gain_two, w_qkv, w_out, w_up, w_down, cotangent):
    blocks = lax.axis_size("seq")
    n = lax.axis_size("batch")
    place = lax.axis_index("seq")
    tok, width = residual.shape[1], w_out.shape[0]
    share = width // blocks
    x = jnp.transpose(residual, (2, 0, 1))
    cot = jnp.transpose(cotangent, (2, 0, 1))
    attT, hT, kT, qT, oT, lse, start, k, v, w_mine = fore_pass(n, tok, blocks, x, gain_one[None], documents, w_qkv)
    new, grad_middle, doT, grad_up, grad_out, down_share, down_pair = mid_pass(
        n, blocks, x, cot, attT, gain_two[None], w_out, w_up, w_down
    )
    sum_down, sum_up, sum_out, sum_qkv, one, two, grad_x = back_pass(
        n, tok, blocks, (doT, k, v, kT, qT, oT, lse, start, hT, w_mine, x, grad_middle),
        down_share, down_pair, grad_up, grad_out, w_qkv, w_up, gain_one[None],
    )

    def gain_grad(total, gain):
        return total[:, 0] / lax.dynamic_slice_in_dim(gain, place * share, share)

    return (
        jnp.transpose(new, (1, 2, 0)),
        jnp.transpose(grad_x, (1, 2, 0)),
        gain_grad(one, gain_one),
        gain_grad(two, gain_two),
        sum_qkv,
        sum_out.astype(F32),
        sum_up.astype(F32),
        sum_down.astype(F32),
    )


def solution(mesh):
    placed = (
        P("batch", "seq", None),
        P("batch", "seq"),
        P(),
        P(),
        P(),
        P(),
        P(),
        P(),
        P("batch", "seq", None),
    )
    return jax.shard_map(
        per_device,
        mesh=mesh,
        in_specs=placed,
        out_specs=(
            P("batch", "seq", None),
            P("batch", "seq", None),
            P("seq"),
            P("seq"),
            P("seq", None),
            P("seq", None),
            P("seq", None),
            P("seq", None),
        ),
        check_vma=False,
    )
```

```python
import functools
import math

import jax
import jax.numpy as jnp
from jax import lax
from jax.experimental import pallas as pl
from jax.experimental.pallas import tpu as pltpu
from jax.sharding import PartitionSpec as P

H = 12
HD = 64
EPSILON = 1e-06
NEG = -1e30
F32, BF16 = jnp.float32, jnp.bfloat16
VMEM_LIMIT = 62 * 2**20


def dot(a, b):
    return lax.dot_general(a, b, (((1,), (0,)), ((), ())), preferred_element_type=F32)


def dot_nt(a, b):
    return lax.dot_general(a, b, (((1,), (1,)), ((), ())), preferred_element_type=F32)


def dot_tn(a, b):
    return lax.dot_general(a, b, (((0,), (0,)), ((), ())), preferred_element_type=F32)


def expand(narrow):
    return jnp.concatenate([narrow, -jnp.sum(narrow, axis=0, keepdims=True)], axis=0)


def shrink(full_vec):
    return full_vec[:-1] - jnp.mean(full_vec, axis=0, keepdims=True)


def shrink_back(grad_narrow):
    padded = jnp.concatenate([grad_narrow, jnp.zeros_like(grad_narrow[:1])], axis=0)
    return padded - jnp.sum(grad_narrow, axis=0, keepdims=True) / padded.shape[0]


def root(full_vec):
    return lax.rsqrt(jnp.mean(full_vec * full_vec, axis=0, keepdims=True) + EPSILON)


def norm_back(narrow, gain, grad_h):
    full_vec = expand(narrow)
    r = root(full_vec)
    scaled = gain * grad_h
    grad_full = r * (scaled - full_vec * (r * r * jnp.mean(scaled * full_vec, axis=0, keepdims=True)))
    return grad_full[:-1] - grad_full[-1:]


def column(gain_ref):
    return jnp.broadcast_to(gain_ref[...].reshape(1, gain_ref.shape[0]), (8, gain_ref.shape[0])).T[:, 0:1]


MESH = pl.DeviceIdType.MESH


class Place:
    def __init__(self, n):
        self.s = lax.axis_index("seq")
        self.b = lax.axis_index("batch")
        self.core = lax.rem(self.s, 2)
        self.chip = self.s // 2
        self.y = lax.rem(self.b, 2)
        self.z = lax.rem(self.b // 2, 4)
        self.far = self.b // 8
        self.n = n

    def core_mate(self):
        return (self.s + 1 - 2 * self.core, self.b)

    def chip_mate(self):
        return (self.s + 2 - 4 * self.chip, self.b)

    def cross_mate(self):
        return (3 - self.s, self.b)

    def y_mate(self):
        return (self.s, self.b + 1 - 2 * self.y)

    def z_of(self, d):
        return lax.rem(self.z + d, 4)

    def z_mate(self, d):
        return (self.s, self.b + 2 * (self.z_of(d) - self.z))

    def z_pair(self, bit):
        here = lax.rem(self.z // bit, 2)
        return (self.s, self.b + 2 * bit * (1 - 2 * here))

    def far_mate(self, d):
        f = lax.rem(self.far + d, self.n // 8)
        return (self.s, self.b + 8 * (f - self.far))

    def next_row(self):
        return (self.s, lax.rem(self.b + 1, self.n))

    def prior_row(self):
        return (self.s, lax.rem(self.b + self.n - 1, self.n))

    def all_mates(self):
        mates = [self.core_mate(), self.chip_mate(), self.cross_mate(), self.y_mate()]
        mates += [self.z_mate(d) for d in (1, 2, 3)]
        mates += [self.far_mate(d) for d in range(1, self.n // 8)]
        return mates + [self.next_row(), self.prior_row()]


def greet(mates):
    barrier = pltpu.get_barrier_semaphore()
    for mate in mates:
        pl.semaphore_signal(barrier, inc=1, device_id=mate, device_id_type=MESH)
    pl.semaphore_wait(barrier, len(mates))


class Copies:
    def __init__(self, sems):
        self.sems, self.made = sems, {}

    def remote(self, name, src, dst, mate):
        k = len(self.made)

        def make():
            return pltpu.make_async_remote_copy(
                src_ref=src(),
                dst_ref=dst(),
                send_sem=self.sems.at[0, k],
                recv_sem=self.sems.at[1, k],
                device_id=mate(),
                device_id_type=MESH,
            )

        assert name not in self.made
        self.made[name] = make

    def local(self, name, src, dst):
        k = len(self.made)

        def make():
            return pltpu.make_async_copy(src(), dst(), self.sems.at[0, k])

        assert name not in self.made
        self.made[name] = make

    def start(self, *names):
        for name in names:
            self.made[name]().start()

    def wait(self, *names):
        for name in names:
            self.made[name]().wait()

    def wait_recv(self, *names):
        for name in names:
            self.made[name]().wait_recv()

    def wait_send(self, *names):
        for name in names:
            self.made[name]().wait_send()


def rows_at(at, count):
    return pl.ds(pl.multiple_of(at, 16), count)


def blockwise(rows, body):
    step = next(s for s in (48, 32, 16) if rows % s == 0)

    def one(i, carry):
        body(i * step, step)
        return carry

    lax.fori_loop(0, rows // step, one, 0)


class Sum:
    def __init__(self, place, copies, name, mode, far_z, src, first, rows, cols, bufs, out):
        self.p, self.c, self.name, self.mode, self.far_z = place, copies, name, mode, far_z
        self.src, self.first, self.rows, self.cols, self.out = src, first, rows, cols, out
        bufs = list(bufs)
        self.full = bufs.pop(0) if out else None
        self.own, self.ry, self.rz, self.res, self.rf = bufs[:5]
        self.rc = bufs[5] if mode in "xy" else None
        self.rx = bufs[-1] if mode != "share" else None
        self.mine = (lambda: self.own.at[self.p.chip]) if mode in "xy" else (lambda: self.own.at[0])
        self.define()

    @staticmethod
    def scratch(mode, far_z, rows, cols, n, full):
        def v(*s):
            return pltpu.VMEM(s, BF16)

        half, spot = rows // 2, rows // (8 if far_z else 4)
        out = [v(2 if mode in "xy" else 1, rows, cols), v(2 if mode == "y" else 1, half, cols)]
        out += [v(3 if far_z else 2, spot, cols), v(rows, cols), v(n // 8 if n > 8 else 1, spot if n > 8 else 16, cols)]
        if mode in "xy":
            out.append(v(2, rows, cols))
        if mode != "share":
            out.append(v(rows if mode == "x" else half, cols))
        return [pltpu.VMEM((rows, cols), F32)] + out if full else out

    def id(self, what):
        return (self.name, what)

    def at_half(self, y):
        return rows_at(y * (self.rows // 2), self.rows // 2)

    def at_spot(self):
        p, half = self.p, self.rows // 2
        if self.far_z:
            return rows_at(p.y * half + p.z * (half // 4), half // 4)
        return rows_at(p.y * half + lax.rem(p.z, 2) * (half // 2), half // 2)

    def define(self):
        p, c, half, far = self.p, self.c, self.rows // 2, self.p.n // 8
        if self.mode in "xy":
            first = pl.ds(self.first, self.rows)
            for order in (1, 0):
                chip = lambda order=order: lax.rem(p.chip + order, 2)
                c.remote(
                    self.id(("core", order)),
                    lambda chip=chip: self.src.at[2 * chip() + 1 - p.core, first],
                    lambda chip=chip: self.rc.at[chip()],
                    p.core_mate,
                )
                c.local(
                    self.id(("own", order)),
                    lambda chip=chip: self.src.at[2 * chip() + p.core, first],
                    lambda chip=chip: self.own.at[chip()],
                )
        other = lambda: self.own.at[1 - p.chip]
        if self.mode == "x":
            c.remote(self.id("x"), other, lambda: self.rx, p.chip_mate)
        if self.mode == "y":
            c.remote(self.id("y1"), lambda: other().at[self.at_half(1 - p.y)], lambda: self.ry.at[1], p.y_mate)
            c.remote(self.id("x"), lambda: other().at[self.at_half(p.y)], lambda: self.rx, p.chip_mate)
        if self.mode == "share" and self.src is not None:
            c.local(self.id("own"), lambda: self.src, lambda: self.own.at[0])
        if self.mode == "half":
            c.remote(self.id("x"), lambda: self.src.at[1 - p.chip], lambda: self.rx, p.chip_mate)
            c.local(self.id("own"), lambda: self.src.at[p.chip], lambda: self.own.at[0, self.at_half(p.y)])
        else:
            c.remote(self.id("y"), lambda: self.mine().at[self.at_half(1 - p.y)], lambda: self.ry.at[0], p.y_mate)
        spot = lambda: self.res.at[self.at_spot()]
        if self.far_z:
            for d in (2, 1, 3):
                c.remote(
                    self.id(("z", d)),
                    lambda d=d: self.mine().at[rows_at(p.y * half + p.z_of(d) * (half // 4), half // 4)],
                    lambda d=d: self.rz.at[3 - d],
                    lambda d=d: p.z_mate(d),
                )
                c.remote(self.id(("back z", d)), spot, spot, lambda d=d: p.z_mate(d))
        else:
            away = lambda: rows_at(p.y * half + (1 - lax.rem(p.z, 2)) * (half // 2), half // 2)
            c.remote(self.id("z1"), lambda: self.mine().at[away()], lambda: self.rz.at[0], lambda: p.z_pair(1))
            c.remote(self.id("z2"), lambda: self.mine().at[self.at_spot()], lambda: self.rz.at[1], lambda: p.z_pair(2))
            c.remote(self.id("back z1"), spot, spot, lambda: p.z_pair(1))
        for d in range(1, far):
            c.remote(self.id(("far", d)), lambda: self.rf.at[p.far], lambda: self.rf.at[p.far], lambda d=d: p.far_mate(d))
        my_half = lambda: self.res.at[self.at_half(p.y)]
        c.remote(self.id("back y"), my_half, my_half, p.y_mate)
        for k, (src, dst) in enumerate(self.out):
            c.local(self.id(("out", k)), lambda src=src: self.full.at[src], lambda dst=dst: dst)

    def add(self, dst, at, rows, *others):
        def body(first, step):
            here = rows_at(at + first, step)
            total = dst[here, :].astype(F32)
            for other, offset in others:
                total = total + other[rows_at(offset + first, step), :].astype(F32)
            dst[here, :] = total.astype(BF16)

        blockwise(rows, body)

    def p0(self):
        if self.mode == "half":
            self.c.start(self.id("x"), self.id("own"))
        if self.mode == "share":
            self.c.start(self.id("own"))
        if self.mode in "xy":
            for order in (1, 0):
                self.c.start(self.id(("core", order)), self.id(("own", order)))

    def p1(self):
        self.c.wait(self.id(("core", 1)), self.id(("own", 1)))
        other = 1 - self.p.chip
        self.add(self.own.at[other], 0, self.rows, (self.rc.at[other], 0))
        self.c.start(self.id("x" if self.mode == "x" else "y1"))

    def p1b(self):
        self.c.wait(self.id(("core", 0)), self.id(("own", 0)))
        self.add(self.mine(), 0, self.rows, (self.rc.at[self.p.chip], 0))
        if self.mode == "y":
            self.c.start(self.id("y"))

    def p2(self):
        p, half = self.p, self.rows // 2
        if self.mode == "y":
            self.c.wait(self.id("y1"))
            self.add(self.own.at[1 - p.chip], p.y * half, half, (self.ry.at[1], 0))
            self.c.start(self.id("x"))
            return
        if self.mode == "x":
            self.c.wait(self.id("x"))
            self.add(self.mine(), (1 - p.y) * half, half, (self.rx, (1 - p.y) * half))
        if self.mode == "share" and self.src is not None:
            self.c.wait(self.id("own"))
        self.c.start(self.id("y"))

    def p3(self):
        p, half, more = self.p, self.rows // 2, []
        if self.mode != "half":
            self.c.wait(self.id("y"))
            more.append((self.ry.at[0], 0))
        if self.mode == "x":
            more.append((self.rx, p.y * half))
        if self.mode in ("y", "half"):
            self.c.wait(self.id("x"))
            more.append((self.rx, 0))
        if self.mode == "half":
            self.c.wait(self.id("own"))
        self.add(self.mine(), p.y * half, half, *more)
        self.c.start(*([self.id(("z", d)) for d in (2, 1, 3)] if self.far_z else [self.id("z1")]))

    def total(self, *others):
        p = self.p
        spot, rows = self.at_spot(), self.at_spot().size
        own, far = self.mine(), p.n // 8

        def body(first, step):
            here = rows_at(spot.start + first, step)
            there = rows_at(first, step)
            total = own[here, :].astype(F32)
            for other in others:
                total = total + other[there, :].astype(F32)
            if far > 1:
                self.rf[p.far, there, :] = total.astype(BF16)
            else:
                self.res[here, :] = total.astype(BF16)

        blockwise(rows, body)
        if far > 1:
            self.c.start(*[self.id(("far", d)) for d in range(1, far)])
            self.c.wait(*[self.id(("far", d)) for d in range(1, far)])

            def more(first, step):
                there = rows_at(first, step)
                total = self.rf[0, there, :].astype(F32)
                for k in range(1, far):
                    total = total + self.rf[k, there, :].astype(F32)
                self.res[rows_at(spot.start + first, step), :] = total.astype(BF16)

            blockwise(rows, more)

    def p4(self):
        if self.far_z:
            self.c.wait(*[self.id(("z", d)) for d in (1, 2, 3)])
            self.total(*[self.rz.at[d] for d in range(3)])
            self.c.start(*[self.id(("back z", d)) for d in (2, 1, 3)])
            return
        self.c.wait(self.id("z1"))
        spot = self.at_spot()
        self.add(self.mine(), spot.start, spot.size, (self.rz.at[0], 0))
        self.c.start(self.id("z2"))

    def p4b(self):
        if not self.far_z:
            self.c.wait(self.id("z2"))
            self.total(self.rz.at[1])
            self.c.start(self.id("back z1"))

    def p5(self):
        self.c.wait(*([self.id(("back z", d)) for d in (1, 2, 3)] if self.far_z else [self.id("back z1")]))
        self.c.start(self.id("back y"))

    def p6(self):
        self.c.wait(self.id("back y"))
        if not self.out:
            return

        def body(first, step):
            here = rows_at(first, step)
            self.full[here, :] = self.res[here, :].astype(F32)

        blockwise(self.rows, body)
        self.c.start(*[self.id(("out", k)) for k in range(len(self.out))])

    def p7(self):
        self.c.wait(*[self.id(("out", k)) for k in range(len(self.out))])


def fore_kernel(n, tok, blocks, heads, *refs):
    x, gain, docs, w = refs[:4]
    attT_o, hT_o, kT_o, qT_o, oT_o, lse_o, start_o, k_o, v_o, wm_o = refs[4:14]
    xs, ws, wm, hT, docs_all, prior_docs, start, kT, vT, qT, kk, vv, acc, m_ref, l_ref, lse, stage, sems = refs[14:]
    width = xs.shape[0] + 1
    row = blocks * tok
    mine = heads * HD
    p = Place(n)
    c = Copies(sems)
    mates = {"core": p.core_mate, "chip": p.chip_mate, "cross": p.cross_mate}
    block = lambda at: pl.ds(pl.multiple_of(at * tok, tok), tok)
    here = lambda: block(p.s)
    c.local("x", lambda: x.at[:, 0, :], lambda: xs)
    c.local("w", lambda: w, lambda: ws)
    c.local("docs", lambda: docs, lambda: docs_all.at[:, here()])
    for name, mate in mates.items():
        c.remote(("docs", name), lambda: docs, lambda: docs_all.at[:, here()], mate)
    last = pl.ds(row - tok, tok)
    c.remote("prior docs", lambda: docs_all.at[:, last], lambda: prior_docs, p.next_row)
    c.remote("h core", lambda: hT.at[:, here()], lambda: hT.at[:, here()], p.core_mate)
    half = tok // 2
    for k in range(2):
        piece = lambda s, k=k: hT.at[:, pl.ds(pl.multiple_of(s * tok + k * half, half), half)]
        c.remote(("h chip", k), lambda piece=piece: piece(p.s), lambda piece=piece: piece(p.s), p.chip_mate)
        other = lambda piece=piece: piece(p.chip_mate()[0])
        c.remote(("h on", k), other, other, p.core_mate)
    end = pl.ds(row, tok)
    c.remote("prior k", lambda: kT.at[:, end], lambda: kT.at[:, 0:tok], p.next_row)
    c.remote("prior v", lambda: vT.at[:, end], lambda: vT.at[:, 0:tok], p.next_row)
    for h in range(heads):
        spot = lambda h=h: attT_o.at[pl.ds(pl.multiple_of(p.s * mine + h * HD, HD), HD)]
        for name, mate in mates.items():
            src = lambda h=h, mate=mate: stage.at[pl.ds(h * HD, HD), block(mate()[0])]
            c.remote(("att", h, name), src, spot, mate)
        c.local(("att", h, "own"), lambda h=h: stage.at[pl.ds(h * HD, HD), here()], spot)
    outs = {"hT": (hT, hT_o), "kT": (kT, kT_o), "qT": (qT, qT_o), "oT": (acc, oT_o), "lse": (lse, lse_o)}
    outs.update({"start": (start, start_o), "k": (kk, k_o), "v": (vv, v_o), "wm": (wm, wm_o)})
    for name, (src, dst) in outs.items():
        c.local(("out", name), lambda src=src: src, lambda dst=dst: dst)

    c.start("x", "docs", "w")
    greet([p.core_mate(), p.chip_mate(), p.cross_mate(), p.next_row(), p.prior_row()])
    c.start(*[("docs", name) for name in mates])
    c.wait("x")
    full_vec = expand(xs[...])
    hT[:, here()] = (column(gain) * full_vec * root(full_vec)).astype(BF16)
    c.start(("h chip", 0), "h core")
    c.start(("h chip", 1))

    c.wait("w")
    for s in range(blocks):
        @pl.when(p.s == s)
        def _():
            for h in range(heads):
                for k in range(3):
                    at = k * width + s * mine + h * HD
                    to = (h * 3 + k) * HD
                    wm[:, to : to + HD] = ws[:, at : at + HD]

    c.wait("docs", *[("docs", name) for name in mates])
    c.start("prior docs")
    ids = jnp.broadcast_to(docs_all[...], (8, row))
    pos = lax.broadcasted_iota(jnp.int32, (8, row), 1)
    since = jnp.where((ids != pltpu.roll(ids, 1, 1)) | (pos == 0), pos, 0)
    hop = 1
    while hop < row:
        since = jnp.maximum(since, jnp.where(pos >= hop, pltpu.roll(since, hop, 1), 0))
        hop *= 2
    start[...] = since[0:1] + tok
    m_ref[...] = jnp.full(m_ref.shape, NEG, F32)
    l_ref[...] = jnp.zeros(l_ref.shape, F32)
    acc[...] = jnp.zeros(acc.shape, F32)

    def natural(keys_at):
        keys = pl.ds(pl.multiple_of(keys_at, tok), tok)
        for h in range(heads):
            kk[h, keys, :] = kT[h * HD : (h + 1) * HD, keys].T
            vv[h, keys, :] = vT[h * HD : (h + 1) * HD, keys].T

    def project(at):
        packed = dot_tn(wm[...], hT[:, block(at)]).astype(BF16)
        keys = pl.ds(pl.multiple_of((at + 1) * tok, tok), tok)
        for h in range(heads):
            to, base = slice(h * HD, (h + 1) * HD), h * 3 * HD
            qT[to, block(at)] = packed[base : base + HD] * jnp.bfloat16(1.0 / math.sqrt(HD))
            kT[to, keys] = packed[base + HD : base + 2 * HD]
            vT[to, keys] = packed[base + 2 * HD : base + 3 * HD]
        natural((at + 1) * tok)

    def pair(h, i, j, size, causal):
        hr = pl.ds(pl.multiple_of(h * HD, HD), HD)
        qs, ks = (pl.ds(pl.multiple_of(at * tok, tok), size) for at in (i, j))
        s = dot(kk[h, ks, :], qT[hr, qs])
        at = lax.broadcasted_iota(jnp.int32, s.shape, 0)
        keep = at >= start[:, qs] - j * tok
        if causal:
            keep = keep & (at <= lax.broadcasted_iota(jnp.int32, s.shape, 1))
        s = jnp.where(keep, s, NEG)
        m = m_ref[h, :, qs]
        new_m = jnp.maximum(m, jnp.max(s, axis=0, keepdims=True))
        e = jnp.exp(s - new_m)
        shift = jnp.exp(m - new_m)
        m_ref[h, :, qs] = new_m
        l_ref[h, :, qs] = l_ref[h, :, qs] * shift + jnp.sum(e, axis=0, keepdims=True)
        acc[hr, qs] = acc[hr, qs] * shift + dot(vT[hr, ks], e.astype(BF16))

    def finish(h, i):
        hr, qs = pl.ds(pl.multiple_of(h * HD, HD), HD), block(i)
        out = acc[hr, qs] / l_ref[h, :, qs]
        acc[hr, qs] = out
        stage[hr, qs] = out.astype(BF16)
        lse[h, :, qs] = m_ref[h, :, qs] + jnp.log(l_ref[h, :, qs])

    def send_att(h, zero):
        for name, mate in list(mates.items()) + [("own", lambda: (p.s,))]:
            @pl.when((mate()[0] == 0) == zero)
            def _():
                c.start(("att", h, name))

    near, far = 2 * p.chip, 2 * (1 - p.chip)
    c.wait_recv("h core")

    def project_near(t, carry):
        project(near + t)
        return carry

    lax.fori_loop(0, 2, project_near, 0)

    @pl.when(p.chip == 1)
    def _():
        c.start("prior k", "prior v")

    def first(h, carry):
        pair(h, near, near + 1, 2 * tok, True)
        return carry

    lax.fori_loop(0, heads, first, 0)
    for k in range(2):
        c.wait_recv(("h chip", k))
        c.start(("h on", k))
    project(p.chip_mate()[0])
    c.wait_recv(("h on", 0), ("h on", 1))
    project(p.cross_mate()[0])

    @pl.when(p.chip == 0)
    def _():
        c.start("prior k", "prior v")

    def second(h, carry):
        pair(h, far, far + 1, 2 * tok, True)
        pair(h, 2, 1, 2 * tok, False)
        lax.fori_loop(1, blocks, lambda i, carry: (finish(h, i), carry)[1], 0)
        for k in range(heads):
            @pl.when(h == k)
            def _():
                send_att(k, False)
        return carry

    lax.fori_loop(0, heads, second, 0)
    c.wait_recv("prior docs")
    from_doc = docs_all[:, 0:1]
    at = lax.broadcasted_iota(jnp.int32, (1, tok), 1)
    run = jnp.max(jnp.where(prior_docs[...] != from_doc, at + 1, 0), axis=1, keepdims=True)
    start[:, 0:tok] = jnp.where(start[:, 0:tok] == tok, run, start[:, 0:tok])
    c.wait_recv("prior k", "prior v")
    natural(0)

    def third(h, carry):
        pair(h, 0, 0, tok, False)
        finish(h, 0)
        for k in range(heads):
            @pl.when(h == k)
            def _():
                send_att(k, True)
        return carry

    lax.fori_loop(0, heads, third, 0)
    c.start(*[("out", name) for name in outs])
    c.wait_send("h core", ("h chip", 0), ("h chip", 1), ("h on", 0), ("h on", 1), "prior docs", "prior k", "prior v")
    for h in range(heads):
        c.wait(*[("att", h, name) for name in list(mates) + ["own"]])
    c.wait(*[("out", name) for name in outs])


def fore_pass(n, tok, blocks, x, gain, docs, w):
    width, heads = w.shape[0], H // blocks
    row, mine = blocks * tok, heads * HD
    v = lambda *s, t=BF16: pltpu.VMEM(s, t)
    o = lambda *s, t=BF16: jax.ShapeDtypeStruct(s, t)
    hbm = pl.BlockSpec(memory_space=pl.ANY)
    scratch = [
        v(width - 1, tok, t=F32), v(width, 3 * width), v(width, 3 * mine), v(width, row),
        v(1, row, t=jnp.int32), v(1, tok, t=jnp.int32), v(1, row, t=jnp.int32),
        v(mine, row + tok), v(mine, row + tok), v(mine, row), v(heads, row + tok, HD), v(heads, row + tok, HD),
        v(mine, row, t=F32), v(heads, 1, row, t=F32), v(heads, 1, row, t=F32), v(heads, 1, row, t=F32), v(mine, row),
        pltpu.SemaphoreType.DMA((2, 24 + 4 * heads)),
    ]
    return pl.pallas_call(
        functools.partial(fore_kernel, n, tok, blocks, heads),
        out_shape=[
            o(width, tok), o(width, row), o(mine, row + tok), o(mine, row), o(mine, row, t=F32), o(heads, 1, row, t=F32),
            o(1, row, t=jnp.int32), o(heads, row + tok, HD), o(heads, row + tok, HD), o(width, 3 * mine),
        ],
        in_specs=[hbm, pl.BlockSpec(memory_space=pltpu.VMEM), hbm, hbm],
        out_specs=[hbm] * 10,
        scratch_shapes=scratch,
        compiler_params=pltpu.CompilerParams(collective_id=0, has_side_effects=True, vmem_limit_bytes=VMEM_LIMIT),
    )(x, gain, docs, w)


def gelu_both(v, grad):
    rate = math.sqrt(2.0 / math.pi)
    square = v * v
    th = jnp.tanh(rate * v * (1.0 + 0.044715 * square))
    up = 0.5 * (1.0 + th)
    slope = up + 0.5 * v * (1.0 - th * th) * (rate * (1.0 + 3.0 * 0.044715 * square))
    return (v * up).astype(BF16), (grad * slope).astype(BF16)


def mid_kernel(n, blocks, *refs):
    x, cot, attT, gain, w_out, w_up, w_down = refs[:7]
    new_o, gm_o, doT_o, gu_o, go_o, half_o, share_o = refs[7:14]
    xs, cs, at, wo, wu, wd, mid, h2, g2, g1, geluT, gupT, b2, gh, dw, rc, ry, rx, ga, gu, go, sems = refs[14:]
    tok, width = xs.shape[1], xs.shape[0] + 1
    parts = wu.shape[1] // width
    share = width // blocks
    p = Place(n)
    c = Copies(sems)
    mates = {"cross": p.cross_mate, "chip": p.chip_mate, "core": p.core_mate}
    c.local("att", lambda: attT, lambda: at)
    c.local("wo", lambda: w_out, lambda: wo)
    c.local("x", lambda: x.at[:, 0, :], lambda: xs)
    c.local("cot", lambda: cot.at[:, 0, :], lambda: cs)
    c.local("wu", lambda: w_up, lambda: wu)
    c.local("wd", lambda: w_down, lambda: wd)
    c.remote("core 0", lambda: dw.at[0], lambda: rc.at[0], p.core_mate)
    c.remote("core 1", lambda: dw.at[2], lambda: rc.at[1], p.core_mate)
    part = width // 2
    fourth = part // 2
    low = lambda y: rows_at(y * fourth, fourth)
    for t in range(2):
        c.remote(("y", t), lambda t=t: dw.at[2 * t + 1, low(1 - p.y)], lambda t=t: ry.at[t], p.y_mate)
        dst = lambda t=t: half_o.at[1 - p.chip if t == 0 else p.chip]
        c.local(("half", t), lambda t=t: dw.at[2 * t + 1, low(p.y)], dst)
    high = pl.ds(part, part)
    c.remote("chip", lambda: dw.at[1, high], lambda: rx, p.chip_mate)
    c.local("share", lambda: dw.at[3, high], lambda: share_o)
    there = lambda: doT_o.at[:, pl.ds(pl.multiple_of(p.s * tok, tok), tok)]
    for name, mate in mates.items():
        c.remote(("ga", name), lambda mate=mate: ga.at[rows_at(mate()[0] * share, share)], there, mate)
    c.local(("ga", "own"), lambda: ga.at[rows_at(p.s * share, share)], there)
    c.local("new out", lambda: xs, lambda: new_o.at[:, 0, :])
    c.local("gm", lambda: cs, lambda: gm_o)
    for k in range(parts):
        c.local(("gu", k), lambda k=k: gu.at[:, pl.ds(k * share, share)], lambda k=k: gu_o.at[:, pl.ds(k * share, share)])
    c.local("go", lambda: go, lambda: go_o)

    c.start("att", "wo", "x", "cot", "wu", "wd")
    greet([p.core_mate(), p.chip_mate(), p.cross_mate(), p.y_mate()])
    c.wait("att", "wo")
    branch_one = dot_tn(wo[...], at[...])
    c.wait("x")
    mid[...] = xs[...] + shrink(branch_one)
    full_vec = expand(mid[...])
    gain_col = column(gain)
    h2[...] = (gain_col * full_vec * root(full_vec)).astype(BF16)
    c.wait("cot")
    g2[...] = shrink_back(cs[...]).astype(BF16)
    b2[...] = jnp.zeros_like(b2)
    gh[...] = jnp.zeros_like(gh)
    c.wait("wu", "wd")

    def add(dst, at, src, rows):
        def body(first, step):
            r = rows_at(at + first, step)
            dw[dst, r, :] = (dw[dst, r, :].astype(F32) + src[rows_at(first, step), :].astype(F32)).astype(BF16)

        blockwise(rows, body)

    def chip_sum(t):
        c.wait_recv(f"core {t}")
        add(2 * t + 1, 0, rc.at[t], width)
        c.start(("y", t), *(["chip"] if t == 0 else []))

    def y_sum(t):
        c.wait(("y", t))
        add(2 * t + 1, p.y * fourth, ry.at[t], fourth)
        c.start(("half", t))

    def piece(t, carry):
        s = jnp.where(t == 0, p.cross_mate()[0], jnp.where(t == 1, p.chip_mate()[0], jnp.where(t == 2, p.core_mate()[0], p.s)))
        its = pl.ds(pl.multiple_of(s * width, width), width)
        up = dot_tn(wu[:, its], h2[...])
        grad_gelu = dot(wd[its, :], g2[...])
        gelu, grad_up = gelu_both(up, grad_gelu)
        geluT[...] = gelu
        gupT[its, :] = grad_up
        dw[t] = dot_nt(geluT[...], g2[...]).astype(BF16)

        @pl.when(t == 0)
        def _():
            c.start("core 0")

        @pl.when(t == 2)
        def _():
            c.start("core 1")

        b2[...] += dot_tn(wd[its, :], geluT[...])
        gh[...] += dot(wu[:, its], gupT[its, :])

        @pl.when(t == 1)
        def _():
            chip_sum(0)

        return carry

    lax.fori_loop(0, parts, piece, 0)
    chip_sum(1)
    grad_middle = cs[...] + norm_back(mid[...], gain_col, gh[...])
    cs[...] = grad_middle
    g1[...] = shrink_back(grad_middle).astype(BF16)
    ga[...] = dot(wo[...], g1[...]).astype(BF16)
    c.start(*[("ga", name) for name in list(mates) + ["own"]])
    c.start("gm")
    xs[...] = mid[...] + shrink(b2[...])
    c.start("new out")

    def up_grad(k, carry):
        its = pl.ds(pl.multiple_of(k * width, width), width)
        grad = dot_nt(h2[...], gupT[its, :]).astype(BF16)
        for s in range(blocks):
            gu[s, rows_at(k * share, share), :] = grad[s * share : (s + 1) * share]
        return carry

    lax.fori_loop(0, parts, up_grad, 0)
    c.start(*[("gu", k) for k in range(parts)])
    out_grad = dot_nt(at[...], g1[...]).astype(BF16)
    for s in range(blocks):
        for k in range(2):
            go[s, k * share : (k + 1) * share, :] = out_grad[s * share : (s + 1) * share, k * part : (k + 1) * part]
    c.start("go")
    c.wait("chip")
    add(3, part, rx, part)
    c.start("share")
    y_sum(0)
    y_sum(1)
    c.wait_send("core 0", "core 1")
    c.wait(*[("ga", name) for name in list(mates) + ["own"]])
    c.wait("gm", "new out", "go", "share", ("half", 0), ("half", 1), *[("gu", k) for k in range(parts)])


def mid_pass(n, blocks, x, cot, attT, gain, w_out, w_up, w_down):
    width, tok = attT.shape
    parts, share = w_up.shape[1] // width, width // blocks
    v = lambda *s, t=BF16: pltpu.VMEM(s, t)
    o = lambda *s, t=BF16: jax.ShapeDtypeStruct(s, t)
    hbm = pl.BlockSpec(memory_space=pl.ANY)
    scratch = [
        v(width - 1, tok, t=F32), v(width - 1, tok, t=F32), v(width, tok), v(width, width), v(*w_up.shape), v(*w_down.shape),
        v(width - 1, tok, t=F32), v(width, tok), v(width, tok), v(width, tok), v(width, tok), v(w_up.shape[1], tok),
        v(width, tok, t=F32), v(width, tok, t=F32), v(4, width, width), v(2, width, width), v(2, width // 4, width), v(width // 2, width),
        v(width, tok), v(blocks, parts * share, width), v(blocks, 2 * share, width // 2),
        pltpu.SemaphoreType.DMA((2, 32)),
    ]
    return pl.pallas_call(
        functools.partial(mid_kernel, n, blocks),
        out_shape=[
            o(width - 1, 1, tok, t=F32), o(width - 1, tok, t=F32), o(share, blocks * tok), o(blocks, parts * share, width),
            o(blocks, 2 * share, width // 2), o(2, width // 4, width), o(width // 2, width),
        ],
        in_specs=[hbm, hbm, hbm, pl.BlockSpec(memory_space=pltpu.VMEM), hbm, hbm, hbm],
        out_specs=[hbm] * 7,
        scratch_shapes=scratch,
        compiler_params=pltpu.CompilerParams(collective_id=2, has_side_effects=True, vmem_limit_bytes=VMEM_LIMIT),
    )(x, cot, attT, gain, w_out, w_up, w_down)


BACK_IN = ("doT", "k", "v", "kT", "qT", "oT", "lse", "start", "hT", "wm", "x", "gm")
DW = ("cross", "chip", "core", "own")
Q_HEADS = ((0, 1), (2,))
U_MODES = ("x", "x")
O_MODE = "y"
FAR_Z = {"d": True, "u": False, "o": False, "q": False}
PLAN = {
    "start": {
        (): ["d0.p0", "u1.p0", "u0.p0", "d1.p0", "o.p0"],
    },
    "ready": {
        (): ["u1.p1", "d1.p2"],
    },
    "prior": {
        (0,): ["u1.p1b", "u0.p1"],
        (1,): ["u0.p1b", "o.p1", "d0.p3", "o.p1b"],
    },
    "full": {
        (0, 1): ["d1.p3"],
        (1, 2): ["d0.p4"],
        (2, 2): ["o.p3"],
        (2, 5): ["d0.p5"],
    },
    "close": {
        (0,): ["u1.p2", "o.p2"],
        (1,): ["dw0", "u1.p3", "d1.p4", "u0.p2"],
        (2,): ["dw1", "gh1", "gh0", "o.p4", "d0.p6", "d1.p5", "ghA"],
    },
    "diagonal": {
        (2, 1): ["u1.p4"],
        (2, 2): ["u0.p3"],
        (2, 3): ["q0.p2"],
    },
    "end": {
        (): ["ghx", "ghB", "q1.p2", "ghC", "u1.p4b", "u0.p4", "q0.p3", "o.p4b", "u1.p5", "d1.p6", "q0.p4", "u0.p4b", "q1.p3", "o.p5", "final", "u1.p6", "q0.p4b", "u0.p5", "o.p6", "q1.p4", "q0.p5", "u0.p6", "q1.p4b", "q1.p5", "q0.p6", "q1.p6"],
    },
}


def back_sums(n, width, share, part, mine):
    half = [("d%d" % k, ("half", "share")[k], n > 8 or FAR_Z["d"], k, 0, part, width) for k in range(2)]
    up = [("u%d" % k, U_MODES[k], n > 8 or FAR_Z["u"], 0, k * part, part, width) for k in range(2)]
    out = [("o", O_MODE, n > 8 or FAR_Z["o"], 1, 0, 2 * share, part)]
    return half + up + out + [
        ("q%d" % k, "share", n > 8 or FAR_Z["q"], None, 0, width // share * mine, mine * len(hs)) for k, hs in enumerate(Q_HEADS)
    ]


def back_kernel(n, tok, blocks, heads, parts, *refs):
    refs = list(refs)
    take = lambda count: [refs.pop(0) for _ in range(count)]
    hbm = dict(zip(BACK_IN, take(len(BACK_IN))))
    down_half, down_share, gu, go, w_qkv, w_up, gain_one, gain_two = take(8)
    down_o, up_o, out_o, qkv_o, gain_one_o, gain_two_o, rg_o = take(7)
    vm = dict(zip(BACK_IN, take(len(BACK_IN))))
    dkT, dvT, delta, dP, prior_out, prior_in, g_stage, g_core, g_x, g_acc, qkv_v, wq_rows, wu_rows, gcol = take(14)
    dws = take(len(Q_HEADS))
    p, hd, row = Place(n), HD, blocks * tok
    mine, width = heads * hd, blocks * heads * hd
    share, part = width // blocks, width // 2
    per_part = part // share
    outs = {"d%d" % k: [(pl.ds(0, part), down_o.at[pl.ds(k * part, part)])] for k in range(2)}
    for k in range(2):
        outs["u%d" % k] = [
            (pl.ds(j * share, share), up_o.at[:, pl.ds((k * per_part + j) * width, width)]) for j in range(per_part)
        ]
    outs["o"] = [(pl.ds(k * share, share), out_o.at[:, pl.ds(k * part, part)]) for k in range(2)]
    plans = back_sums(n, width, share, part, mine)
    bufs = [take(len(Sum.scratch(q[1], q[2], 16, 128, n, q[0] in outs))) for q in plans]
    c = Copies(refs.pop(0))
    for name in BACK_IN:
        src = (lambda: hbm["x"].at[:, 0, :]) if name == "x" else (lambda name=name: hbm[name])
        c.local(name, src, lambda name=name: vm[name])
    c.local("wq rows", lambda: w_qkv.at[rows_at(p.s * share, share)], lambda: wq_rows)
    c.local("wu rows", lambda: w_up.at[rows_at(p.s * share, share)], lambda: wu_rows)
    sums = {}
    for (name, mode, far_z, arr, first, rows, cols), buf in zip(plans, bufs):
        src = None if arr is None else ((down_half, down_share) if name[0] == "d" else (gu, go))[arr]
        sums[name] = Sum(p, c, name, mode, far_z, src, first, rows, cols, buf, outs.get(name, []))
    qkv = [sums["q%d" % k] for k in range(len(Q_HEADS))]
    for k, own in enumerate(qkv):
        spot = lambda own=own: own.own.at[0, rows_at(p.s * mine, mine)]
        for what, mate in (("cross", p.cross_mate), ("chip", p.chip_mate), ("core", p.core_mate)):
            c.remote(("dw", k, what), lambda k=k, mate=mate: dws[k].at[rows_at(mate()[0] * mine, mine)], spot, mate)
        c.local(("dw", k, "own"), lambda k=k: dws[k].at[rows_at(p.s * mine, mine)], spot)
    for k in range(heads):
        c.remote(("prior", k), lambda k=k: prior_out.at[k], lambda k=k: prior_in.at[k], p.prior_row)
    for order in (1, 0):
        c.remote(("gh", order), lambda order=order: g_stage.at[order], lambda order=order: g_core.at[order], p.core_mate)
    c.remote(("gh", "x"), lambda: g_stage.at[1], lambda: g_x, p.chip_mate)
    c.local("rg", lambda: vm["gm"], lambda: rg_o.at[:, 0, :])
    c.local("qkv", lambda: qkv_v, lambda: qkv_o)

    def grad_h_part(owner):
        return dot(vm["wm"][...], dP[:, pl.ds(pl.multiple_of(owner * tok, tok), tok)])

    def core_grad(order):
        chip = lax.rem(p.chip + order, 2)
        g_stage[order] = grad_h_part(2 * chip + 1 - p.core).astype(BF16)
        c.start(("gh", order))

    def keep_grad(order):
        chip = lax.rem(p.chip + order, 2)
        g_acc[...] = grad_h_part(2 * chip + p.core)

    def chip_grad():
        c.wait(("gh", 1))
        g_stage[1] = (g_acc[...] + g_core[1].astype(F32)).astype(BF16)
        c.start(("gh", "x"))

    def own_grad():
        c.wait(("gh", 0))
        g_acc[...] += g_core[0].astype(F32)

    def input_grad():
        c.wait("x", "gm", ("gh", "x"))
        vm["gm"][...] += norm_back(vm["x"][...], column(gain_one), g_acc[...] + g_x[...].astype(F32))
        c.start("rg")

    def send_dw(k):
        rows = slice(Q_HEADS[k][0] * 3 * hd, (Q_HEADS[k][-1] + 1) * 3 * hd)
        dws[k][...] = dot_nt(vm["hT"][...], dP[rows, :]).astype(BF16)
        c.start(*[("dw", k, what) for what in DW])

    steps = {"gh1": lambda: core_grad(1), "gh0": lambda: core_grad(0), "ghA": lambda: keep_grad(1), "ghx": chip_grad}
    steps.update({"ghB": lambda: keep_grad(0), "ghC": own_grad, "final": input_grad})
    for name, one in sums.items():
        for phase in ("p0", "p1", "p1b", "p2", "p3", "p4", "p4b", "p5", "p6"):
            steps[name + "." + phase] = getattr(one, phase)
    for k in range(len(Q_HEADS)):
        steps["dw%d" % k] = lambda k=k: send_dw(k)
        steps["q%d.p2" % k] = lambda k=k: (c.wait(*[("dw", k, what) for what in DW]), qkv[k].p2())

    def steps_at(place, **now):
        for at, names in PLAN.get(place, {}).items():
            same = None
            for want, have in zip(at, now.values()):
                same = (have == want) if same is None else same & (have == want)

            def run():
                for name in names:
                    steps[name]()

            run() if same is None else pl.when(same)(run)

    first = BACK_IN[:8]
    c.start(*first)
    greet(p.all_mates())
    steps_at("start")
    c.start(*BACK_IN[8:], "wq rows", "wu rows")
    c.wait(*first)
    dqT = vm["oT"]
    doT, kk, vv, kT, qT, lse, start = (vm[x] for x in ("doT", "k", "v", "kT", "qT", "lse", "start"))

    def make_delta(h, carry):
        rows = pl.ds(pl.multiple_of(h * hd, hd), hd)
        delta[h] = jnp.sum(doT[rows, :].astype(F32) * vm["oT"][rows, :], axis=0, keepdims=True)
        return carry

    lax.fori_loop(0, heads, make_delta, 0)
    dqT[...] = jnp.zeros_like(dqT)
    dkT[...] = jnp.zeros_like(dkT)
    dvT[...] = jnp.zeros_like(dvT)
    steps_at("ready")

    def pair(h, i, j, causal):
        hr = pl.ds(pl.multiple_of(h * hd, hd), hd)
        qs, ks = (pl.ds(pl.multiple_of(at * tok, tok), tok) for at in (i, j))
        q_blk, do_blk = qT[hr, qs], doT[hr, qs]
        s = dot(kk[h, ks, :], q_blk)
        e = jnp.exp(s - lse[h, :, qs])
        at = lax.broadcasted_iota(jnp.int32, s.shape, 0)
        keep = at >= start[:, qs] - j * tok
        if causal:
            keep = keep & (at <= lax.broadcasted_iota(jnp.int32, s.shape, 1))
        e = jnp.where(keep, e, 0.0)
        dp = dot(vv[h, ks, :], do_blk)
        ds = (e * (dp - delta[h, :, qs])).astype(BF16)
        dvT[hr, ks] += dot_nt(do_blk, e.astype(BF16))
        dkT[hr, ks] += dot_nt(q_blk, ds)
        dqT[hr, qs] += dot(kT[hr, ks], ds)

    def prior(h, carry):
        pair(h, 0, 0, False)
        hr = pl.ds(pl.multiple_of(h * hd, hd), hd)
        prior_out[h, 0:hd, :] = dkT[hr, 0:tok].astype(BF16)
        prior_out[h, hd : 2 * hd, :] = dvT[hr, 0:tok].astype(BF16)
        for k in range(heads):
            @pl.when(h == k)
            def _():
                c.start(("prior", k))
        steps_at("prior", h=h)
        return carry

    lax.fori_loop(0, heads, prior, 0)

    def close(h):
        hr = pl.ds(pl.multiple_of(h * hd, hd), hd)
        last = pl.ds(row, tok)
        dkT[hr, last] += prior_in[h, 0:hd, :].astype(F32)
        dvT[hr, last] += prior_in[h, hd : 2 * hd, :].astype(F32)
        base = h * 3 * hd
        for k, (src, at) in enumerate(((dqT, 0), (dkT, tok), (dvT, tok))):
            val = src[hr, at:]
            val = val * (1.0 / math.sqrt(hd)) if k == 0 else val
            dP[pl.ds(pl.multiple_of(base + k * hd, hd), hd), :] = val.astype(BF16)

    def head(h, carry):
        def full(t, carry):
            i = jnp.where(t < 3, 3, jnp.where(t < 5, 2, 1))
            j = jnp.where(t < 3, t + 1, jnp.where(t < 5, t - 2, 1))
            pair(h, i, j, False)
            steps_at("full", h=h, t=t)
            return carry

        lax.fori_loop(0, 6, full, 0)

        def diagonal(i, carry):
            pair(h, i, i + 1, True)
            steps_at("diagonal", h=h, i=i)
            return carry

        lax.fori_loop(0, blocks, diagonal, 0)
        for k in range(heads):
            @pl.when(h == k)
            def _():
                if k == 0:
                    c.wait("hT", "wm")
                c.wait(("prior", k))
        close(h)
        steps_at("close", h=h)
        return carry

    lax.fori_loop(0, heads, head, 0)
    steps_at("end")

    def row_of(col):
        return jnp.broadcast_to(col, (share, 128)).T[0:1, :]

    def my_gain(gain):
        gcol[...] = column(gain)
        return gcol[pl.ds(pl.multiple_of(p.s * share, share), share), :]

    c.wait("wq rows", "wu rows")
    total = jnp.zeros((share, 1), F32)
    for k in range(2):
        for j in range(per_part):
            cols = slice((k * per_part + j) * width, (k * per_part + j + 1) * width)
            prod = sums["u%d" % k].full[j * share : (j + 1) * share, :] * wu_rows[:, cols].astype(F32)
            total = total + jnp.sum(prod, axis=1, keepdims=True)
    gain_two_o[...] = row_of(total / my_gain(gain_two))
    total = jnp.zeros((share, 1), F32)
    for k in range(3):
        for s in range(blocks):
            cells = []
            for own, hs in zip(qkv, Q_HEADS):
                for h in range(len(hs)):
                    at = (h * 3 + k) * hd
                    cells.append(own.res[s * share : (s + 1) * share, at : at + hd])
            cells = jnp.concatenate(cells, axis=1).astype(F32)
            cols = slice(k * width + s * mine, k * width + (s + 1) * mine)
            qkv_v[:, cols] = cells
            total = total + jnp.sum(cells * wq_rows[:, cols].astype(F32), axis=1, keepdims=True)
    gain_one_o[...] = row_of(total / my_gain(gain_one))
    c.start("qkv")
    for one in sums.values():
        one.p7()
    c.wait("qkv", "rg")


def back_pass(n, tok, blocks, ins, down_half, down_share, gu, go, w_qkv, w_up, gain_one, gain_two):
    heads = ins[1].shape[0]
    row = blocks * tok
    width = ins[8].shape[0]
    mine = heads * HD
    parts, share, part = w_up.shape[1] // width, width // blocks, width // 2
    v = lambda *s, t=BF16: pltpu.VMEM(s, t)
    o = lambda *s: jax.ShapeDtypeStruct(s, F32)
    scratch = [v(width - 1, tok, t=F32) if name == "x" else pltpu.VMEM(a.shape, a.dtype) for name, a in zip(BACK_IN, ins)]
    scratch += [
        v(mine, row + tok, t=F32), v(mine, row + tok, t=F32), v(heads, 1, row, t=F32), v(3 * mine, row),
        v(heads, 2 * HD, tok), v(heads, 2 * HD, tok),
        v(2, width, tok), v(2, width, tok), v(width, tok), v(width, tok, t=F32), v(share, 3 * width, t=F32),
        v(share, 3 * width), v(share, w_up.shape[1]), v(width, 1, t=F32),
    ]
    scratch += [v(width, mine * len(hs)) for hs in Q_HEADS]
    copies = len(ins) + 5 * heads + 8
    for name, mode, far_z, _, _, rows, cols in back_sums(n, width, share, part, mine):
        scratch += Sum.scratch(mode, far_z, rows, cols, n, name[0] != "q")
        copies += 17 + n // 8
    scratch.append(pltpu.SemaphoreType.DMA((2, copies)))
    hbm = pl.BlockSpec(memory_space=pl.ANY)
    vmem = pl.BlockSpec(memory_space=pltpu.VMEM)
    return pl.pallas_call(
        functools.partial(back_kernel, n, tok, blocks, heads, parts),
        out_shape=[
            o(width, width), o(share, parts * width), o(share, width), o(share, 3 * width),
            o(1, share), o(1, share), o(width - 1, 1, tok),
        ],
        in_specs=[hbm] * (len(ins) + 6) + [vmem, vmem],
        out_specs=[hbm] * 4 + [vmem, vmem, hbm],
        scratch_shapes=scratch,
        compiler_params=pltpu.CompilerParams(collective_id=1, has_side_effects=True, vmem_limit_bytes=VMEM_LIMIT),
    )(*ins, down_half, down_share, gu, go, w_qkv, w_up, gain_one, gain_two)


def per_device(residual, documents, gain_one, gain_two, w_qkv, w_out, w_up, w_down, cotangent):
    blocks = lax.axis_size("seq")
    n = lax.axis_size("batch")
    tok = residual.shape[1]
    x = jnp.transpose(residual, (2, 0, 1))
    cot = jnp.transpose(cotangent, (2, 0, 1))
    attT, hT, kT, qT, oT, lse, start, k, v, w_mine = fore_pass(n, tok, blocks, x, gain_one, documents, w_qkv)
    new, grad_middle, doT, grad_up, grad_out, down_half, down_share = mid_pass(
        n, blocks, x, cot, attT, gain_two, w_out, w_up, w_down
    )
    sum_down, sum_up, sum_out, sum_qkv, one, two, grad_x = back_pass(
        n, tok, blocks, (doT, k, v, kT, qT, oT, lse, start, hT, w_mine, x, grad_middle),
        down_half, down_share, grad_up, grad_out, w_qkv, w_up, gain_one, gain_two,
    )
    new, grad_x = jnp.transpose(new, (1, 2, 0)), jnp.transpose(grad_x, (1, 2, 0))
    return (new, grad_x, one[0], two[0], sum_qkv, sum_out, sum_up, sum_down)


def solution(mesh):
    placed = (
        P("batch", "seq", None),
        P("batch", "seq"),
        P(),
        P(),
        P(),
        P(),
        P(),
        P(),
        P("batch", "seq", None),
    )
    return jax.shard_map(
        per_device,
        mesh=mesh,
        in_specs=placed,
        out_specs=(
            P("batch", "seq", None),
            P("batch", "seq", None),
            P("seq"),
            P("seq"),
            P("seq", None),
            P("seq", None),
            P("seq", None),
            P("seq", None),
        ),
        check_vma=False,
    )
```

```python
import functools
import math

import jax
import jax.numpy as jnp
from jax import lax
from jax.experimental import pallas as pl
from jax.experimental.pallas import tpu as pltpu
from jax.sharding import PartitionSpec as P

H = 12
HD = 64
EPSILON = 1e-06
NEG = -1e30
F32, BF16 = jnp.float32, jnp.bfloat16
VMEM_LIMIT = 62 * 2**20


def dot(a, b):
    return lax.dot_general(a, b, (((1,), (0,)), ((), ())), preferred_element_type=F32)


def dot_nt(a, b):
    return lax.dot_general(a, b, (((1,), (1,)), ((), ())), preferred_element_type=F32)


def dot_tn(a, b):
    return lax.dot_general(a, b, (((0,), (0,)), ((), ())), preferred_element_type=F32)


def expand(narrow):
    return jnp.concatenate([narrow, -jnp.sum(narrow, axis=0, keepdims=True)], axis=0)


def shrink(full_vec):
    return full_vec[:-1] - jnp.mean(full_vec, axis=0, keepdims=True)


def shrink_back(grad_narrow):
    padded = jnp.concatenate([grad_narrow, jnp.zeros_like(grad_narrow[:1])], axis=0)
    return padded - jnp.sum(grad_narrow, axis=0, keepdims=True) / padded.shape[0]


def root(full_vec):
    return lax.rsqrt(jnp.mean(full_vec * full_vec, axis=0, keepdims=True) + EPSILON)


def norm_back(narrow, gain, grad_h):
    full_vec = expand(narrow)
    r = root(full_vec)
    scaled = gain * grad_h
    grad_full = r * (scaled - full_vec * (r * r * jnp.mean(scaled * full_vec, axis=0, keepdims=True)))
    return grad_full[:-1] - grad_full[-1:]


def column(gain_ref):
    return jnp.broadcast_to(gain_ref[...].reshape(1, gain_ref.shape[0]), (8, gain_ref.shape[0])).T[:, 0:1]


MESH = pl.DeviceIdType.MESH


class Place:
    def __init__(self, n):
        self.s = lax.axis_index("seq")
        self.b = lax.axis_index("batch")
        self.core = lax.rem(self.s, 2)
        self.chip = self.s // 2
        self.y = lax.rem(self.b, 2)
        self.z = lax.rem(self.b // 2, 4)
        self.far = self.b // 8
        self.n = n

    def core_mate(self):
        return (self.s + 1 - 2 * self.core, self.b)

    def chip_mate(self):
        return (self.s + 2 - 4 * self.chip, self.b)

    def cross_mate(self):
        return (3 - self.s, self.b)

    def y_mate(self):
        return (self.s, self.b + 1 - 2 * self.y)

    def z_of(self, d):
        return lax.rem(self.z + d, 4)

    def z_mate(self, d):
        return (self.s, self.b + 2 * (self.z_of(d) - self.z))

    def z_pair(self, bit):
        here = lax.rem(self.z // bit, 2)
        return (self.s, self.b + 2 * bit * (1 - 2 * here))

    def far_mate(self, d):
        f = lax.rem(self.far + d, self.n // 8)
        return (self.s, self.b + 8 * (f - self.far))

    def next_row(self):
        return (self.s, lax.rem(self.b + 1, self.n))

    def prior_row(self):
        return (self.s, lax.rem(self.b + self.n - 1, self.n))

    def all_mates(self):
        mates = [self.core_mate(), self.chip_mate(), self.cross_mate(), self.y_mate()]
        mates += [self.z_mate(d) for d in (1, 2, 3)]
        mates += [self.far_mate(d) for d in range(1, self.n // 8)]
        return mates + [self.next_row(), self.prior_row()]


def greet(mates):
    barrier = pltpu.get_barrier_semaphore()
    for mate in mates:
        pl.semaphore_signal(barrier, inc=1, device_id=mate, device_id_type=MESH)
    pl.semaphore_wait(barrier, len(mates))


class Copies:
    def __init__(self, sems):
        self.sems, self.made = sems, {}

    def remote(self, name, src, dst, mate):
        k = len(self.made)

        def make():
            return pltpu.make_async_remote_copy(
                src_ref=src(),
                dst_ref=dst(),
                send_sem=self.sems.at[0, k],
                recv_sem=self.sems.at[1, k],
                device_id=mate(),
                device_id_type=MESH,
            )

        assert name not in self.made
        self.made[name] = make

    def local(self, name, src, dst):
        k = len(self.made)

        def make():
            return pltpu.make_async_copy(src(), dst(), self.sems.at[0, k])

        assert name not in self.made
        self.made[name] = make

    def start(self, *names):
        for name in names:
            self.made[name]().start()

    def wait(self, *names):
        for name in names:
            self.made[name]().wait()

    def wait_recv(self, *names):
        for name in names:
            self.made[name]().wait_recv()

    def wait_send(self, *names):
        for name in names:
            self.made[name]().wait_send()


def rows_at(at, count):
    return pl.ds(pl.multiple_of(at, 16), count)


def blockwise(rows, body):
    step = next(s for s in (48, 32, 16) if rows % s == 0)

    def one(i, carry):
        body(i * step, step)
        return carry

    lax.fori_loop(0, rows // step, one, 0)


PAIRS, QUARTERS, PAIRS_Z = range(3)


class Sum:
    def __init__(self, place, copies, name, mode, way, src, first, rows, cols, bufs, out):
        self.p, self.c, self.name, self.mode, self.way = place, copies, name, mode, way
        bits = [(place.y, place.y_mate), (lax.rem(place.z, 2), lambda: place.z_pair(1))]
        (self.one, self.one_mate), (self.two, self.two_mate) = bits[::-1] if way == PAIRS_Z else bits
        self.src, self.first, self.rows, self.cols, self.out = src, first, rows, cols, out
        bufs = list(bufs)
        self.own, self.ry, self.rz, self.res, self.rf = bufs[:5]
        self.rc = bufs[5] if mode in "xy" else None
        self.rx = bufs[-1] if mode not in ("share", "ready") else None
        self.mine = (lambda: self.own.at[self.p.chip]) if mode in "xy" else (lambda: self.own.at[0])
        self.define()

    @staticmethod
    def scratch(mode, way, rows, cols, n):
        def v(*s):
            return pltpu.VMEM(s, BF16)

        half, spot = rows // 2, rows // (8 if way == QUARTERS else 4)
        out = [v(2 if mode in "xy" else 1, rows, cols), v(2 if mode == "y" else 1, half, cols)]
        out += [v(3 if way == QUARTERS else 2, spot, cols), v(rows, cols), v(n // 8 if n > 8 else 1, spot if n > 8 else 16, cols)]
        if mode in "xy":
            out.append(v(2, rows, cols))
        if mode not in ("share", "ready"):
            out.append(v(rows if mode == "x" else half, cols))
        return out

    def id(self, what):
        return (self.name, what)

    def at_half(self, one):
        return rows_at(one * (self.rows // 2), self.rows // 2)

    def at_spot(self):
        p, half = self.p, self.rows // 2
        if self.way == QUARTERS:
            return rows_at(p.y * half + p.z * (half // 4), half // 4)
        return rows_at(self.one * half + self.two * (half // 2), half // 2)

    def define(self):
        p, c, half, far = self.p, self.c, self.rows // 2, self.p.n // 8
        if self.mode in "xy":
            first = pl.ds(self.first, self.rows)
            for order in (1, 0):
                chip = lambda order=order: lax.rem(p.chip + order, 2)
                c.remote(
                    self.id(("core", order)),
                    lambda chip=chip: self.src.at[2 * chip() + 1 - p.core, first],
                    lambda chip=chip: self.rc.at[chip()],
                    p.core_mate,
                )
                c.local(
                    self.id(("own", order)),
                    lambda chip=chip: self.src.at[2 * chip() + p.core, first],
                    lambda chip=chip: self.own.at[chip()],
                )
        other = lambda: self.own.at[1 - p.chip]
        if self.mode == "x":
            c.remote(self.id("x"), other, lambda: self.rx, p.chip_mate)
        if self.mode == "y":
            c.remote(self.id("y1"), lambda: other().at[self.at_half(1 - self.one)], lambda: self.ry.at[1], self.one_mate)
            c.remote(self.id("x"), lambda: other().at[self.at_half(self.one)], lambda: self.rx, p.chip_mate)
        if self.mode == "ready":
            c.local(self.id("own"), lambda: self.src, lambda: self.own.at[0, self.at_half(self.one)])
        if self.mode == "half":
            c.remote(self.id("x"), lambda: self.src.at[1 - p.chip], lambda: self.rx, p.chip_mate)
            c.local(self.id("own"), lambda: self.src.at[p.chip], lambda: self.own.at[0, self.at_half(self.one)])
        elif self.mode != "ready":
            c.remote(self.id("y"), lambda: self.mine().at[self.at_half(1 - self.one)], lambda: self.ry.at[0], self.one_mate)
        spot = lambda: self.res.at[self.at_spot()]
        if self.way == QUARTERS:
            for d in (2, 1, 3):
                c.remote(
                    self.id(("z", d)),
                    lambda d=d: self.mine().at[rows_at(p.y * half + p.z_of(d) * (half // 4), half // 4)],
                    lambda d=d: self.rz.at[3 - d],
                    lambda d=d: p.z_mate(d),
                )
                c.remote(self.id(("back z", d)), spot, spot, lambda d=d: p.z_mate(d))
        else:
            away = lambda: rows_at(self.one * half + (1 - self.two) * (half // 2), half // 2)
            c.remote(self.id("z1"), lambda: self.mine().at[away()], lambda: self.rz.at[0], self.two_mate)
            c.remote(self.id("z2"), lambda: self.mine().at[self.at_spot()], lambda: self.rz.at[1], lambda: p.z_pair(2))
            c.remote(self.id("back z1"), spot, spot, self.two_mate)
        for d in range(1, far):
            c.remote(self.id(("far", d)), lambda: self.rf.at[p.far], lambda: self.rf.at[p.far], lambda d=d: p.far_mate(d))
        my_half = lambda: self.res.at[self.at_half(self.one)]
        c.remote(self.id("back y"), my_half, my_half, self.one_mate)
        for k, (src, dst) in enumerate(self.out):
            c.local(self.id(("out", k)), lambda src=src: self.res.at[src], lambda dst=dst: dst)

    def add(self, dst, at, rows, *others):
        def body(first, step):
            here = rows_at(at + first, step)
            total = dst[here, :].astype(F32)
            for other, offset in others:
                total = total + other[rows_at(offset + first, step), :].astype(F32)
            dst[here, :] = total.astype(BF16)

        blockwise(rows, body)

    def p0(self):
        if self.mode == "half":
            self.c.start(self.id("x"), self.id("own"))
        if self.mode == "ready":
            self.c.start(self.id("own"))
        if self.mode in "xy":
            for order in (1, 0):
                self.c.start(self.id(("core", order)), self.id(("own", order)))

    def p1(self):
        self.c.wait(self.id(("core", 1)), self.id(("own", 1)))
        other = 1 - self.p.chip
        self.add(self.own.at[other], 0, self.rows, (self.rc.at[other], 0))
        self.c.start(self.id("x" if self.mode == "x" else "y1"))

    def p1b(self):
        self.c.wait(self.id(("core", 0)), self.id(("own", 0)))
        self.add(self.mine(), 0, self.rows, (self.rc.at[self.p.chip], 0))
        if self.mode == "y":
            self.c.start(self.id("y"))

    def p2(self):
        half = self.rows // 2
        if self.mode == "y":
            self.c.wait(self.id("y1"))
            self.add(self.own.at[1 - self.p.chip], self.one * half, half, (self.ry.at[1], 0))
            self.c.start(self.id("x"))
            return
        if self.mode == "x":
            self.c.wait(self.id("x"))
            self.add(self.mine(), (1 - self.one) * half, half, (self.rx, (1 - self.one) * half))
        self.c.start(self.id("y"))

    def p3(self):
        half, more = self.rows // 2, []
        if self.mode not in ("half", "ready"):
            self.c.wait(self.id("y"))
            more.append((self.ry.at[0], 0))
        if self.mode == "x":
            more.append((self.rx, self.one * half))
        if self.mode in ("y", "half"):
            self.c.wait(self.id("x"))
            more.append((self.rx, 0))
        if self.mode in ("half", "ready"):
            self.c.wait(self.id("own"))
        self.add(self.mine(), self.one * half, half, *more)
        self.c.start(*([self.id(("z", d)) for d in (2, 1, 3)] if self.way == QUARTERS else [self.id("z1")]))

    def total(self, *others):
        p = self.p
        spot, rows = self.at_spot(), self.at_spot().size
        own, far = self.mine(), p.n // 8

        def body(first, step):
            here = rows_at(spot.start + first, step)
            there = rows_at(first, step)
            total = own[here, :].astype(F32)
            for other in others:
                total = total + other[there, :].astype(F32)
            if far > 1:
                self.rf[p.far, there, :] = total.astype(BF16)
            else:
                self.res[here, :] = total.astype(BF16)

        blockwise(rows, body)
        if far > 1:
            self.c.start(*[self.id(("far", d)) for d in range(1, far)])
            self.c.wait(*[self.id(("far", d)) for d in range(1, far)])

            def more(first, step):
                there = rows_at(first, step)
                total = self.rf[0, there, :].astype(F32)
                for k in range(1, far):
                    total = total + self.rf[k, there, :].astype(F32)
                self.res[rows_at(spot.start + first, step), :] = total.astype(BF16)

            blockwise(rows, more)

    def p4(self):
        if self.way == QUARTERS:
            self.c.wait(*[self.id(("z", d)) for d in (1, 2, 3)])
            self.total(*[self.rz.at[d] for d in range(3)])
            self.c.start(*[self.id(("back z", d)) for d in (2, 1, 3)])
            return
        self.c.wait(self.id("z1"))
        spot = self.at_spot()
        self.add(self.mine(), spot.start, spot.size, (self.rz.at[0], 0))
        self.c.start(self.id("z2"))

    def p4b(self):
        if not self.way == QUARTERS:
            self.c.wait(self.id("z2"))
            self.total(self.rz.at[1])
            self.c.start(self.id("back z1"))

    def p5(self):
        self.c.wait(*([self.id(("back z", d)) for d in (1, 2, 3)] if self.way == QUARTERS else [self.id("back z1")]))
        self.c.start(self.id("back y"))

    def p6(self):
        self.c.wait(self.id("back y"))
        self.c.start(*[self.id(("out", k)) for k in range(len(self.out))])

    def p7(self):
        self.c.wait(*[self.id(("out", k)) for k in range(len(self.out))])

    def phase(self, k):
        (self.p0, self.p1, self.p1b, self.p2, self.p3, self.p4, self.p4b, self.p5, self.p6)[k]()


PRIOR_KV = (("prior k", 0), ("prior k", 1), ("prior v", 0), ("prior v", 1))


def fore_kernel(n, tok, blocks, heads, *refs):
    x, gain, docs, w = refs[:4]
    attT_o, hT_o, kT_o, qT_o, oT_o, lse_o, start_o, k_o, v_o, wm_o = refs[4:14]
    xs, ws, wm, hT, docs_all, prior_docs, start, kT, vT, qT, kk, vv, acc, m_ref, l_ref, lse, stage, sems = refs[14:]
    width = xs.shape[0] + 1
    row = blocks * tok
    mine = heads * HD
    p = Place(n)
    c = Copies(sems)
    mates = {"core": p.core_mate, "chip": p.chip_mate, "cross": p.cross_mate}
    block = lambda at: pl.ds(pl.multiple_of(at * tok, tok), tok)
    here = lambda: block(p.s)
    c.local("w", lambda: w, lambda: ws)
    c.local("docs", lambda: docs, lambda: docs_all.at[:, here()])
    for name, mate in mates.items():
        c.remote(("docs", name), lambda: docs, lambda: docs_all.at[:, here()], mate)
    last = pl.ds(row - tok, tok)
    c.remote("prior docs", lambda: docs_all.at[:, last], lambda: prior_docs, p.next_row)
    c.remote("h core", lambda: hT.at[:, here()], lambda: hT.at[:, here()], p.core_mate)
    half = tok // 2
    for k in range(2):
        c.local(("x", k), lambda k=k: x.at[:, 0, pl.ds(k * half, half)], lambda k=k: xs.at[:, pl.ds(k * half, half)])
        piece = lambda s, k=k: hT.at[:, pl.ds(pl.multiple_of(s * tok + k * half, half), half)]
        c.remote(("h chip", k), lambda piece=piece: piece(p.s), lambda piece=piece: piece(p.s), p.chip_mate)
        other = lambda piece=piece: piece(p.chip_mate()[0])
        c.remote(("h on", k), other, other, p.core_mate)
    for k in range(2):
        end, to = pl.ds(row + k * half, half), pl.ds(k * half, half)
        c.remote(("prior k", k), lambda end=end: kT.at[:, end], lambda to=to: kT.at[:, to], p.next_row)
        c.remote(("prior v", k), lambda end=end: vT.at[:, end], lambda to=to: vT.at[:, to], p.next_row)
    for h in range(heads):
        spot = lambda h=h: attT_o.at[pl.ds(pl.multiple_of(p.s * mine + h * HD, HD), HD)]
        for name, mate in mates.items():
            src = lambda h=h, mate=mate: stage.at[pl.ds(h * HD, HD), block(mate()[0])]
            c.remote(("att", h, name), src, spot, mate)
        c.local(("att", h, "own"), lambda h=h: stage.at[pl.ds(h * HD, HD), here()], spot)
    outs = {"hT": (hT, hT_o), "kT": (kT, kT_o), "qT": (qT, qT_o), "oT": (acc, oT_o), "lse": (lse, lse_o)}
    outs.update({"start": (start, start_o), "k": (kk, k_o), "v": (vv, v_o), "wm": (wm, wm_o)})
    for name, (src, dst) in outs.items():
        c.local(("out", name), lambda src=src: src, lambda dst=dst: dst)

    c.start(("x", 0), ("x", 1), "docs", "w")
    greet([p.core_mate(), p.chip_mate(), p.cross_mate(), p.next_row(), p.prior_row()])
    c.start(*[("docs", name) for name in mates])
    gain_col = column(gain)
    for k in range(2):
        c.wait(("x", k))
        full_vec = expand(xs[:, k * half : (k + 1) * half])
        mine_now = pl.ds(pl.multiple_of(p.s * tok + k * half, half), half)
        hT[:, mine_now] = (gain_col * full_vec * root(full_vec)).astype(BF16)
        c.start(("h chip", k))
    c.start("h core")

    c.wait("w")
    for s in range(blocks):
        @pl.when(p.s == s)
        def _():
            for h in range(heads):
                for k in range(3):
                    at = k * width + s * mine + h * HD
                    to = (h * 3 + k) * HD
                    wm[:, to : to + HD] = ws[:, at : at + HD]

    c.wait("docs", *[("docs", name) for name in mates])
    c.start("prior docs")
    ids = jnp.broadcast_to(docs_all[...], (8, row))
    pos = lax.broadcasted_iota(jnp.int32, (8, row), 1)
    since = jnp.where((ids != pltpu.roll(ids, 1, 1)) | (pos == 0), pos, 0)
    hop = 1
    while hop < row:
        since = jnp.maximum(since, jnp.where(pos >= hop, pltpu.roll(since, hop, 1), 0))
        hop *= 2
    start[...] = since[0:1] + tok
    m_ref[...] = jnp.full(m_ref.shape, NEG, F32)
    l_ref[...] = jnp.zeros(l_ref.shape, F32)
    acc[...] = jnp.zeros(acc.shape, F32)

    def natural(keys_at, count):
        keys = pl.ds(pl.multiple_of(keys_at, 128), count)
        for h in range(heads):
            kk[h, keys, :] = kT[h * HD : (h + 1) * HD, keys].T
            vv[h, keys, :] = vT[h * HD : (h + 1) * HD, keys].T

    def project(at, count):
        own, keys = pl.ds(pl.multiple_of(at, 128), count), pl.ds(pl.multiple_of(at + tok, 128), count)
        packed = dot_tn(wm[...], hT[:, own]).astype(BF16)
        for h in range(heads):
            to, base = slice(h * HD, (h + 1) * HD), h * 3 * HD
            qT[to, own] = packed[base : base + HD] * jnp.bfloat16(1.0 / math.sqrt(HD))
            kT[to, keys] = packed[base + HD : base + 2 * HD]
            vT[to, keys] = packed[base + 2 * HD : base + 3 * HD]
        natural(at + tok, count)

    def pair(h, q0, qw, k0, kw, causal):
        hr = pl.ds(pl.multiple_of(h * HD, HD), HD)
        qs, ks = pl.ds(pl.multiple_of(q0, 128), qw), pl.ds(pl.multiple_of(k0 + tok, 128), kw)
        s = dot(kk[h, ks, :], qT[hr, qs])
        at = lax.broadcasted_iota(jnp.int32, s.shape, 0)
        keep = at >= start[:, qs] - (k0 + tok)
        if causal:
            keep = keep & (at <= lax.broadcasted_iota(jnp.int32, s.shape, 1))
        s = jnp.where(keep, s, NEG)
        m = m_ref[h, :, qs]
        new_m = jnp.maximum(m, jnp.max(s, axis=0, keepdims=True))
        e = jnp.exp(s - new_m)
        shift = jnp.exp(m - new_m)
        m_ref[h, :, qs] = new_m
        l_ref[h, :, qs] = l_ref[h, :, qs] * shift + jnp.sum(e, axis=0, keepdims=True)
        acc[hr, qs] = acc[hr, qs] * shift + dot(vT[hr, ks], e.astype(BF16))

    def finish(h, i):
        hr, qs = pl.ds(pl.multiple_of(h * HD, HD), HD), block(i)
        out = acc[hr, qs] / l_ref[h, :, qs]
        acc[hr, qs] = out
        stage[hr, qs] = out.astype(BF16)
        lse[h, :, qs] = m_ref[h, :, qs] + jnp.log(l_ref[h, :, qs])

    def send_att(h, zero):
        for name, mate in list(mates.items()) + [("own", lambda: (p.s,))]:
            @pl.when((mate()[0] == 0) == zero)
            def _():
                c.start(("att", h, name))

    pair_rows = 2 * tok
    near, far = pair_rows * p.chip, pair_rows * (1 - p.chip)
    c.wait_recv("h core")
    lax.fori_loop(0, 2, lambda t, carry: (project(near + t * tok, tok), carry)[1], 0)

    def send_prior(k):
        c.start(("prior k", k), ("prior v", k))

    @pl.when(p.chip == 1)
    def _():
        send_prior(0)
        send_prior(1)

    lax.fori_loop(0, heads, lambda h, carry: (pair(h, near, pair_rows, near, pair_rows, True), carry)[1], 0)

    def far_half(k):
        c.wait_recv(("h chip", k))
        c.start(("h on", k))
        project(p.chip_mate()[0] * tok + k * half, half)
        c.wait_recv(("h on", k))
        project(p.cross_mate()[0] * tok + k * half, half)

        def queries(h, carry):
            for i in range(2):
                pair(h, pair_rows + i * tok + k * half, half, 0, pair_rows, False)
            return carry

        def keys(h, carry):
            for i in range(2):
                pair(h, pair_rows, pair_rows, i * tok + k * half, half, False)
            return carry

        @pl.when(p.chip == 0)
        def _():
            send_prior(k)
            lax.fori_loop(0, heads, queries, 0)

        @pl.when(p.chip == 1)
        def _():
            lax.fori_loop(0, heads, keys, 0)

    far_half(0)
    far_half(1)

    def second(h, carry):
        pair(h, far, pair_rows, far, pair_rows, True)
        lax.fori_loop(1, blocks, lambda i, carry: (finish(h, i), carry)[1], 0)
        for k in range(heads):
            @pl.when(h == k)
            def _():
                send_att(k, False)
        return carry

    lax.fori_loop(0, heads, second, 0)
    c.wait_recv("prior docs")
    from_doc = docs_all[:, 0:1]
    at = lax.broadcasted_iota(jnp.int32, (1, tok), 1)
    run = jnp.max(jnp.where(prior_docs[...] != from_doc, at + 1, 0), axis=1, keepdims=True)
    start[:, 0:tok] = jnp.where(start[:, 0:tok] == tok, run, start[:, 0:tok])
    c.wait_recv(*PRIOR_KV)
    natural(0, tok)

    def third(h, carry):
        pair(h, 0, tok, -tok, tok, False)
        finish(h, 0)
        for k in range(heads):
            @pl.when(h == k)
            def _():
                send_att(k, True)
        return carry

    lax.fori_loop(0, heads, third, 0)
    c.start(*[("out", name) for name in outs])
    c.wait_send("h core", ("h chip", 0), ("h chip", 1), ("h on", 0), ("h on", 1), "prior docs", *PRIOR_KV)
    for h in range(heads):
        c.wait(*[("att", h, name) for name in list(mates) + ["own"]])
    c.wait(*[("out", name) for name in outs])


def fore_pass(n, tok, blocks, x, gain, docs, w):
    width, heads = w.shape[0], H // blocks
    row, mine = blocks * tok, heads * HD
    v = lambda *s, t=BF16: pltpu.VMEM(s, t)
    o = lambda *s, t=BF16: jax.ShapeDtypeStruct(s, t)
    hbm = pl.BlockSpec(memory_space=pl.ANY)
    scratch = [
        v(width - 1, tok, t=F32), v(width, 3 * width), v(width, 3 * mine), v(width, row),
        v(1, row, t=jnp.int32), v(1, tok, t=jnp.int32), v(1, row, t=jnp.int32),
        v(mine, row + tok), v(mine, row + tok), v(mine, row), v(heads, row + tok, HD), v(heads, row + tok, HD),
        v(mine, row, t=F32), v(heads, 1, row, t=F32), v(heads, 1, row, t=F32), v(heads, 1, row, t=F32), v(mine, row),
        pltpu.SemaphoreType.DMA((2, 27 + 4 * heads)),
    ]
    return pl.pallas_call(
        functools.partial(fore_kernel, n, tok, blocks, heads),
        out_shape=[
            o(width, tok), o(width, row), o(mine, row + tok), o(mine, row), o(mine, row, t=F32), o(heads, 1, row, t=F32),
            o(1, row, t=jnp.int32), o(heads, row + tok, HD), o(heads, row + tok, HD), o(width, 3 * mine),
        ],
        in_specs=[hbm, pl.BlockSpec(memory_space=pltpu.VMEM), hbm, hbm],
        out_specs=[hbm] * 10,
        scratch_shapes=scratch,
        compiler_params=pltpu.CompilerParams(collective_id=0, has_side_effects=True, vmem_limit_bytes=VMEM_LIMIT),
    )(x, gain, docs, w)


def gelu_both(v, grad):
    rate = math.sqrt(2.0 / math.pi)
    square = v * v
    th = jnp.tanh(rate * v * (1.0 + 0.044715 * square))
    up = 0.5 * (1.0 + th)
    slope = up + 0.5 * v * (1.0 - th * th) * (rate * (1.0 + 3.0 * 0.044715 * square))
    return (v * up).astype(BF16), (grad * slope).astype(BF16)


def mid_kernel(n, blocks, *refs):
    x, cot, attT, gain, w_out, w_up, w_down = refs[:7]
    new_o, gm_o, doT_o, gu_o, go_o, half_o, ready_o = refs[7:14]
    xs, cs, at, wo, wu, wd, mid, h2, g2, g1, geluT, gupT, b2, gh, dw, rc, ry, rx, ga, gu, go, sems = refs[14:]
    tok, width = xs.shape[1], xs.shape[0] + 1
    parts = wu.shape[1] // width
    share = width // blocks
    p = Place(n)
    c = Copies(sems)
    mates = {"cross": p.cross_mate, "chip": p.chip_mate, "core": p.core_mate}
    c.local("att", lambda: attT, lambda: at)
    c.local("wo", lambda: w_out, lambda: wo)
    c.local("x", lambda: x.at[:, 0, :], lambda: xs)
    c.local("cot", lambda: cot.at[:, 0, :], lambda: cs)
    c.local("wu", lambda: w_up, lambda: wu)
    c.local("wd", lambda: w_down, lambda: wd)
    c.remote("core 0", lambda: dw.at[0], lambda: rc.at[0], p.core_mate)
    c.remote("core 1", lambda: dw.at[2], lambda: rc.at[1], p.core_mate)
    part = width // 2
    fourth = part // 2
    low = lambda y: rows_at(y * fourth, fourth)
    for t in range(2):
        c.remote(("y", t), lambda t=t: dw.at[2 * t + 1, low(1 - p.y)], lambda t=t: ry.at[t], p.y_mate)
        dst = lambda t=t: half_o.at[1 - p.chip if t == 0 else p.chip]
        c.local(("half", t), lambda t=t: dw.at[2 * t + 1, low(p.y)], dst)
    high = pl.ds(part, part)
    c.remote("chip", lambda: dw.at[1, high], lambda: rx, p.chip_mate)
    later = lambda y: rows_at(part + y * fourth, fourth)
    c.remote(("y", 2), lambda: dw.at[3, later(1 - p.y)], lambda: ry.at[2], p.y_mate)
    c.local("ready", lambda: dw.at[3, later(p.y)], lambda: ready_o)
    there = lambda: doT_o.at[:, pl.ds(pl.multiple_of(p.s * tok, tok), tok)]
    for name, mate in mates.items():
        c.remote(("ga", name), lambda mate=mate: ga.at[rows_at(mate()[0] * share, share)], there, mate)
    c.local(("ga", "own"), lambda: ga.at[rows_at(p.s * share, share)], there)
    c.local("new out", lambda: xs, lambda: new_o.at[:, 0, :])
    c.local("gm", lambda: cs, lambda: gm_o)
    for k in range(parts):
        c.local(("gu", k), lambda k=k: gu.at[:, pl.ds(k * share, share)], lambda k=k: gu_o.at[:, pl.ds(k * share, share)])
    c.local("go", lambda: go, lambda: go_o)

    c.start("att", "wo", "x", "cot", "wu", "wd")
    greet([p.core_mate(), p.chip_mate(), p.cross_mate(), p.y_mate()])
    c.wait("att", "wo")
    branch_one = dot_tn(wo[...], at[...])
    c.wait("x")
    mid[...] = xs[...] + shrink(branch_one)
    full_vec = expand(mid[...])
    gain_col = column(gain)
    h2[...] = (gain_col * full_vec * root(full_vec)).astype(BF16)
    c.wait("cot")
    g2[...] = shrink_back(cs[...]).astype(BF16)
    b2[...] = jnp.zeros_like(b2)
    gh[...] = jnp.zeros_like(gh)
    c.wait("wu", "wd")

    def add(dst, at, src, rows):
        def body(first, step):
            r = rows_at(at + first, step)
            dw[dst, r, :] = (dw[dst, r, :].astype(F32) + src[rows_at(first, step), :].astype(F32)).astype(BF16)

        blockwise(rows, body)

    def chip_sum(t):
        c.wait_recv(f"core {t}")
        add(2 * t + 1, 0, rc.at[t], width)
        c.start(("y", t), *(["chip"] if t == 0 else []))

    def y_sum(t):
        c.wait(("y", t))
        add(2 * t + 1, p.y * fourth, ry.at[t], fourth)
        c.start(("half", t))

    def piece(t, carry):
        s = jnp.where(t == 0, p.cross_mate()[0], jnp.where(t == 1, p.chip_mate()[0], jnp.where(t == 2, p.core_mate()[0], p.s)))
        its = pl.ds(pl.multiple_of(s * width, width), width)
        up = dot_tn(wu[:, its], h2[...])
        grad_gelu = dot(wd[its, :], g2[...])
        gelu, grad_up = gelu_both(up, grad_gelu)
        geluT[...] = gelu
        gupT[its, :] = grad_up
        dw[t] = dot_nt(geluT[...], g2[...]).astype(BF16)

        @pl.when(t == 0)
        def _():
            c.start("core 0")

        @pl.when(t == 2)
        def _():
            c.start("core 1")

        b2[...] += dot_tn(wd[its, :], geluT[...])
        gh[...] += dot(wu[:, its], gupT[its, :])

        @pl.when(t == 1)
        def _():
            chip_sum(0)

        return carry

    lax.fori_loop(0, parts, piece, 0)
    chip_sum(1)
    grad_middle = cs[...] + norm_back(mid[...], gain_col, gh[...])
    cs[...] = grad_middle
    g1[...] = shrink_back(grad_middle).astype(BF16)
    ga[...] = dot(wo[...], g1[...]).astype(BF16)
    c.start(*[("ga", name) for name in list(mates) + ["own"]])
    c.start("gm")
    xs[...] = mid[...] + shrink(b2[...])
    c.start("new out")

    def up_grad(k, carry):
        its = pl.ds(pl.multiple_of(k * width, width), width)
        grad = dot_nt(h2[...], gupT[its, :]).astype(BF16)
        for s in range(blocks):
            gu[s, rows_at(k * share, share), :] = grad[s * share : (s + 1) * share]
        return carry

    lax.fori_loop(0, parts // 2, up_grad, 0)
    c.wait("chip")
    add(3, part, rx, part)
    c.start(("y", 2))
    lax.fori_loop(parts // 2, parts, up_grad, 0)
    c.start(*[("gu", k) for k in range(parts)])
    out_grad = dot_nt(at[...], g1[...]).astype(BF16)
    for s in range(blocks):
        for k in range(2):
            go[s, k * share : (k + 1) * share, :] = out_grad[s * share : (s + 1) * share, k * part : (k + 1) * part]
    c.start("go")
    y_sum(0)
    y_sum(1)
    c.wait(("y", 2))
    add(3, part + p.y * fourth, ry.at[2], fourth)
    c.start("ready")
    c.wait_send("core 0", "core 1")
    c.wait(*[("ga", name) for name in list(mates) + ["own"]])
    c.wait("gm", "new out", "go", "ready", ("half", 0), ("half", 1), *[("gu", k) for k in range(parts)])


def mid_pass(n, blocks, x, cot, attT, gain, w_out, w_up, w_down):
    width, tok = attT.shape
    parts, share = w_up.shape[1] // width, width // blocks
    v = lambda *s, t=BF16: pltpu.VMEM(s, t)
    o = lambda *s, t=BF16: jax.ShapeDtypeStruct(s, t)
    hbm = pl.BlockSpec(memory_space=pl.ANY)
    scratch = [
        v(width - 1, tok, t=F32), v(width - 1, tok, t=F32), v(width, tok), v(width, width), v(*w_up.shape), v(*w_down.shape),
        v(width - 1, tok, t=F32), v(width, tok), v(width, tok), v(width, tok), v(width, tok), v(w_up.shape[1], tok),
        v(width, tok, t=F32), v(width, tok, t=F32), v(4, width, width), v(2, width, width), v(3, width // 4, width), v(width // 2, width),
        v(width, tok), v(blocks, parts * share, width), v(blocks, 2 * share, width // 2),
        pltpu.SemaphoreType.DMA((2, 32)),
    ]
    return pl.pallas_call(
        functools.partial(mid_kernel, n, blocks),
        out_shape=[
            o(width - 1, 1, tok, t=F32), o(width - 1, tok, t=F32), o(share, blocks * tok), o(blocks, parts * share, width),
            o(blocks, 2 * share, width // 2), o(2, width // 4, width), o(width // 4, width),
        ],
        in_specs=[hbm, hbm, hbm, pl.BlockSpec(memory_space=pltpu.VMEM), hbm, hbm, hbm],
        out_specs=[hbm] * 7,
        scratch_shapes=scratch,
        compiler_params=pltpu.CompilerParams(collective_id=2, has_side_effects=True, vmem_limit_bytes=VMEM_LIMIT),
    )(x, cot, attT, gain, w_out, w_up, w_down)


BACK_IN = ("doT", "k", "v", "kT", "qT", "oT", "lse", "start", "hT", "wm", "x", "gm")
DW = ("cross", "chip", "core", "own")
D0, D1, U0, U1, O, Q0, Q1, GRAD_H, SEND = range(9)
Q_HEADS = ((0, 1), (2,))
U_MODES = ("x", "x")
O_MODE = "y"
WAYS = (PAIRS, PAIRS, PAIRS, PAIRS, PAIRS, PAIRS_Z, PAIRS)
START, READY, PRIOR, FULL, DIAGONAL, CLOSE, END = range(7)
PLAN = {
    START: {
        (): [(D0, 0), (U1, 0), (U0, 0), (D1, 0), (O, 0)],
    },
    READY: {
        (): [(U1, 1), (D1, 4)],
    },
    PRIOR: {
        (0,): [(U1, 2)],
        (1,): [(U0, 1), (U0, 2)],
        (2,): [(D0, 4), (D1, 5), (O, 1), (O, 2)],
    },
    FULL: {
        (1, 0): [(D0, 5), (U1, 3), (O, 3)],
        (2, 1): [(D0, 6), (U0, 3), (D1, 7)],
        (2, 4): [(U1, 5), (O, 4)],
    },
    DIAGONAL: {
        (1, 0): [(D1, 6)],
        (2, 1): [(D0, 7)],
    },
    CLOSE: {
        (1,): [(U1, 4), (SEND, 0)],
        (2,): [(Q0, 3), (SEND, 1), (GRAD_H, 0), (U0, 4), (GRAD_H, 1), (GRAD_H, 2), (O, 5), (U1, 6)],
    },
    END: {
        (): [(GRAD_H, 3), (Q1, 3), (D1, 8), (GRAD_H, 4), (GRAD_H, 5), (Q0, 4), (U0, 5), (D0, 8),
            (O, 6), (Q1, 4), (U1, 7), (Q0, 5), (O, 7), (U0, 6), (Q1, 5), (GRAD_H, 6),
            (U1, 8), (O, 8), (Q0, 6), (U0, 7), (Q1, 6), (Q0, 7), (Q1, 7), (U0, 8),
            (Q0, 8), (Q1, 8)],
    },
}


def folds(cols):
    return 2 if cols % 128 else 1


def back_sums(n, width, share, part):
    way = lambda k: QUARTERS if n > 8 else WAYS[k]
    half = [(D0 + k, ("half", "ready")[k], way(D0 + k), k, 0, part, width) for k in range(2)]
    up = [(U0 + k, U_MODES[k], way(U0 + k), 0, k * part, part, width) for k in range(2)]
    sums = half + up + [(O, O_MODE, way(O), 1, 0, 2 * share, part)]
    for k, hs in enumerate(Q_HEADS):
        cols = share * len(hs)
        sums.append((Q0 + k, "share", way(Q0 + k), None, 0, width // folds(cols), cols * folds(cols)))
    return sums


def back_kernel(n, tok, blocks, heads, parts, *refs):
    refs = list(refs)
    take = lambda count: [refs.pop(0) for _ in range(count)]
    hbm = dict(zip(BACK_IN, take(len(BACK_IN))))
    down_half, down_ready, gu, go, gain_one = take(5)
    down_o, up_o, out_o, rg_o = take(4)
    qkv_o = take(len(Q_HEADS))
    vm = dict(zip(BACK_IN, take(len(BACK_IN))))
    dkT, dvT, delta, dP, prior_out, prior_in, g_stage, g_core, g_x, g_acc = take(10)
    dws = take(len(Q_HEADS))
    p, hd, row = Place(n), HD, blocks * tok
    mine, width = heads * hd, blocks * heads * hd
    share, part = width // blocks, width // 2
    per_part = part // share
    outs = {D0 + k: [(pl.ds(0, part), down_o.at[pl.ds(k * part, part)])] for k in range(2)}
    for k in range(2):
        outs[U0 + k] = [
            (pl.ds(j * share, share), up_o.at[:, pl.ds((k * per_part + j) * width, width)]) for j in range(per_part)
        ]
    outs[O] = [(pl.ds(k * share, share), out_o.at[:, pl.ds(k * part, part)]) for k in range(2)]
    for k in range(len(Q_HEADS)):
        outs[Q0 + k] = [(pl.ds(0, qkv_o[k].shape[0]), qkv_o[k])]
    plans = back_sums(n, width, share, part)
    bufs = [take(len(Sum.scratch(q[1], q[2], 16, 128, n))) for q in plans]
    c = Copies(refs.pop(0))
    for name in BACK_IN:
        src = (lambda: hbm["x"].at[:, 0, :]) if name == "x" else (lambda name=name: hbm[name])
        c.local(name, src, lambda name=name: vm[name])
    sums = {}
    for (name, mode, way, arr, first, rows, cols), buf in zip(plans, bufs):
        src = None if arr is None else ((down_half, down_ready) if name < U0 else (gu, go))[arr]
        sums[name] = Sum(p, c, name, mode, way, src, first, rows, cols, buf, outs[name])
    qkv = [sums[Q0 + k] for k in range(len(Q_HEADS))]
    for k, one in enumerate(qkv):
        count = one.rows // blocks
        block = lambda ref, s, count=count: ref.at[rows_at(s * count, count)]
        spot = lambda one=one, block=block: block(one.own.at[0], p.s)
        for what, mate in (("cross", p.cross_mate), ("chip", p.chip_mate), ("core", p.core_mate)):
            c.remote(("dw", k, what), lambda k=k, mate=mate, block=block: block(dws[k], mate()[0]), spot, mate)
        c.local(("dw", k, "own"), lambda k=k, block=block: block(dws[k], p.s), spot)
    for k in range(heads):
        c.remote(("prior", k), lambda k=k: prior_out.at[k], lambda k=k: prior_in.at[k], p.prior_row)
    for order in (1, 0):
        c.remote(("gh", order), lambda order=order: g_stage.at[order], lambda order=order: g_core.at[order], p.core_mate)
    c.remote(("gh", "x"), lambda: g_stage.at[1], lambda: g_x, p.chip_mate)
    c.local("rg", lambda: vm["gm"], lambda: rg_o.at[:, 0, :])

    def grad_h_part(owner):
        return dot(vm["wm"][...], dP[:, pl.ds(pl.multiple_of(owner * tok, tok), tok)])

    def core_grad(order):
        chip = lax.rem(p.chip + order, 2)
        g_stage[order] = grad_h_part(2 * chip + 1 - p.core).astype(BF16)
        c.start(("gh", order))

    def keep_grad(order):
        chip = lax.rem(p.chip + order, 2)
        g_acc[...] = grad_h_part(2 * chip + p.core)

    def chip_grad():
        c.wait(("gh", 1))
        g_stage[1] = (g_acc[...] + g_core[1].astype(F32)).astype(BF16)
        c.start(("gh", "x"))

    def own_grad():
        c.wait(("gh", 0))
        g_acc[...] += g_core[0].astype(F32)

    def input_grad():
        c.wait("x", "gm", ("gh", "x"))
        vm["gm"][...] += norm_back(vm["x"][...], column(gain_one), g_acc[...] + g_x[...].astype(F32))
        c.start("rg")

    def send_dw(k):
        rows = slice(Q_HEADS[k][0] * 3 * hd, (Q_HEADS[k][-1] + 1) * 3 * hd)
        grad = dot_nt(vm["hT"][...], dP[rows, :]).astype(BF16)
        fold = folds(grad.shape[1])
        count = share // fold
        for s in range(blocks):
            cells = [grad[s * share + f * count : s * share + (f + 1) * count] for f in range(fold)]
            dws[k][s * count : (s + 1) * count, :] = jnp.concatenate(cells, axis=1)
        c.start(*[("dw", k, what) for what in DW])

    special = {GRAD_H: [lambda: core_grad(1), lambda: core_grad(0), lambda: keep_grad(1), chip_grad, lambda: keep_grad(0)]}
    special[GRAD_H] += [own_grad, input_grad]
    special[SEND] = [lambda k=k: send_dw(k) for k in range(len(Q_HEADS))]

    def step(which, phase):
        if which in special:
            special[which][phase]()
            return
        if which >= Q0 and phase == 3:
            c.wait(*[("dw", which - Q0, what) for what in DW])
        sums[which].phase(phase)

    def steps_at(place, *now):
        for at, names in PLAN.get(place, {}).items():
            same = None
            for want, have in zip(at, now):
                same = (have == want) if same is None else same & (have == want)

            def run():
                for which, phase in names:
                    step(which, phase)

            run() if same is None else pl.when(same)(run)

    first = BACK_IN[:8]
    c.start(*first)
    greet(p.all_mates())
    steps_at(START)
    c.start(*BACK_IN[8:])
    c.wait(*first)
    dqT = vm["oT"]
    doT, kk, vv, kT, qT, lse, start = (vm[x] for x in ("doT", "k", "v", "kT", "qT", "lse", "start"))

    def make_delta(h, carry):
        rows = pl.ds(pl.multiple_of(h * hd, hd), hd)
        delta[h] = jnp.sum(doT[rows, :].astype(F32) * vm["oT"][rows, :], axis=0, keepdims=True)
        return carry

    lax.fori_loop(0, heads, make_delta, 0)
    dqT[...] = jnp.zeros_like(dqT)
    dkT[...] = jnp.zeros_like(dkT)
    dvT[...] = jnp.zeros_like(dvT)
    steps_at(READY)

    def pair(h, i, j, causal):
        hr = pl.ds(pl.multiple_of(h * hd, hd), hd)
        qs, ks = (pl.ds(pl.multiple_of(at * tok, tok), tok) for at in (i, j))
        q_blk, do_blk = qT[hr, qs], doT[hr, qs]
        s = dot(kk[h, ks, :], q_blk)
        e = jnp.exp(s - lse[h, :, qs])
        at = lax.broadcasted_iota(jnp.int32, s.shape, 0)
        keep = at >= start[:, qs] - j * tok
        if causal:
            keep = keep & (at <= lax.broadcasted_iota(jnp.int32, s.shape, 1))
        e = jnp.where(keep, e, 0.0)
        dp = dot(vv[h, ks, :], do_blk)
        ds = (e * (dp - delta[h, :, qs])).astype(BF16)
        dvT[hr, ks] += dot_nt(do_blk, e.astype(BF16))
        dkT[hr, ks] += dot_nt(q_blk, ds)
        dqT[hr, qs] += dot(kT[hr, ks], ds)

    def prior(h, carry):
        pair(h, 0, 0, False)
        hr = pl.ds(pl.multiple_of(h * hd, hd), hd)
        prior_out[h, 0:hd, :] = dkT[hr, 0:tok].astype(BF16)
        prior_out[h, hd : 2 * hd, :] = dvT[hr, 0:tok].astype(BF16)
        for k in range(heads):
            @pl.when(h == k)
            def _():
                c.start(("prior", k))
        steps_at(PRIOR, h)
        return carry

    lax.fori_loop(0, heads, prior, 0)

    def close(h):
        hr = pl.ds(pl.multiple_of(h * hd, hd), hd)
        last = pl.ds(row, tok)
        dkT[hr, last] += prior_in[h, 0:hd, :].astype(F32)
        dvT[hr, last] += prior_in[h, hd : 2 * hd, :].astype(F32)
        base = h * 3 * hd
        for k, (src, at) in enumerate(((dqT, 0), (dkT, tok), (dvT, tok))):
            val = src[hr, at:]
            val = val * (1.0 / math.sqrt(hd)) if k == 0 else val
            dP[pl.ds(pl.multiple_of(base + k * hd, hd), hd), :] = val.astype(BF16)

    def head(h, carry):
        def full(t, carry):
            i = jnp.where(t < 3, 3, jnp.where(t < 5, 2, 1))
            j = jnp.where(t < 3, t + 1, jnp.where(t < 5, t - 2, 1))
            pair(h, i, j, False)
            steps_at(FULL, h, t)
            return carry

        lax.fori_loop(0, 6, full, 0)

        def diagonal(i, carry):
            pair(h, i, i + 1, True)
            steps_at(DIAGONAL, h, i)
            return carry

        lax.fori_loop(0, blocks, diagonal, 0)
        for k in range(heads):
            @pl.when(h == k)
            def _():
                if k == 0:
                    c.wait("hT", "wm")
                c.wait(("prior", k))
        close(h)
        steps_at(CLOSE, h)
        return carry

    lax.fori_loop(0, heads, head, 0)
    steps_at(END)

    for one in sums.values():
        one.p7()
    c.wait("rg")


def back_pass(n, tok, blocks, ins, down_half, down_ready, gu, go, gain, parts):
    heads = ins[1].shape[0]
    row = blocks * tok
    width = ins[8].shape[0]
    mine = heads * HD
    share, part = width // blocks, width // 2
    v = lambda *s, t=BF16: pltpu.VMEM(s, t)
    o = lambda *s, t=BF16: jax.ShapeDtypeStruct(s, t)
    scratch = [v(width - 1, tok, t=F32) if name == "x" else pltpu.VMEM(a.shape, a.dtype) for name, a in zip(BACK_IN, ins)]
    scratch += [
        v(mine, row + tok, t=F32), v(mine, row + tok, t=F32), v(heads, 1, row, t=F32), v(3 * mine, row),
        v(heads, 2 * HD, tok), v(heads, 2 * HD, tok),
        v(2, width, tok), v(2, width, tok), v(width, tok), v(width, tok, t=F32),
    ]
    sums = back_sums(n, width, share, part)
    scratch += [v(*one[5:]) for one in sums[Q0:]]
    copies = len(ins) + 5 * heads + 8
    for _, mode, way, _, _, rows, cols in sums:
        scratch += Sum.scratch(mode, way, rows, cols, n)
        copies += 17 + n // 8
    scratch.append(pltpu.SemaphoreType.DMA((2, copies)))
    hbm = pl.BlockSpec(memory_space=pl.ANY)
    vmem = pl.BlockSpec(memory_space=pltpu.VMEM)
    return pl.pallas_call(
        functools.partial(back_kernel, n, tok, blocks, heads, parts),
        out_shape=[o(width, width), o(share, parts * width), o(share, width), o(width - 1, 1, tok, t=F32)]
        + [o(*one[5:]) for one in sums[Q0:]],
        in_specs=[hbm] * (len(ins) + 4) + [vmem],
        out_specs=[hbm] * (4 + len(Q_HEADS)),
        scratch_shapes=scratch,
        compiler_params=pltpu.CompilerParams(collective_id=1, has_side_effects=True, vmem_limit_bytes=VMEM_LIMIT),
    )(*ins, down_half, down_ready, gu, go, gain)


def last_kernel(blocks, *refs):
    new, rg, down, up, out, w_qkv, w_up, gain_one, gain_two = refs[:9]
    q_in = refs[9 : 9 + len(Q_HEADS)]
    refs = refs[9 + len(Q_HEADS) :]
    new_o, rg_o, gain_one_o, gain_two_o, qkv_o, out_o, up_o, down_o = refs[:8]
    down_v, up_v, out_v, wq, wu, gcol, down_f, up_f, out_f, qkv_f, x_v, sems = refs[8:19] + refs[-1:]
    q_v = refs[19:-1]
    s = lax.axis_index("seq")
    share, width = out_v.shape
    mine, hd = width // blocks, HD
    c = Copies(sems)
    my_rows = lambda ref: ref.at[rows_at(s * share, share)]
    loads = list(zip(q_in, q_v)) + [(my_rows(w_qkv), wq), (up, up_v), (down, down_v), (out, out_v), (my_rows(w_up), wu)]
    for k, (src, dst) in enumerate(loads):
        c.local(("in", k), lambda src=src: src, lambda dst=dst: dst)
    for k, (src, dst) in enumerate(((up_f, up_o), (down_f, down_o), (out_f, out_o), (qkv_f, qkv_o))):
        c.local(("out", k), lambda src=src: src, lambda dst=dst: dst)
    for k, (src, dst) in enumerate(((new, new_o), (rg, rg_o))):
        c.local(("x in", k), lambda k=k, src=src: src.at[:, 0, :], lambda k=k: x_v.at[k])
        c.local(("x out", k), lambda k=k: x_v.at[k], lambda k=k, dst=dst: dst.at[:, 0, :])
    at = len(q_in)
    c.start(*[("in", k) for k in range(at + 2)], ("x in", 0), ("x in", 1), *[("in", k) for k in range(at + 2, len(loads))])

    def row_of(col):
        return jnp.broadcast_to(col, (share, 128)).T[0:1, :]

    def my_gain(gain):
        gcol[...] = column(gain)
        return gcol[pl.ds(pl.multiple_of(s * share, share), share), :]

    c.wait(*[("in", k) for k in range(at + 1)])
    total = jnp.zeros((share, 1), F32)
    for k in range(3):
        for o in range(blocks):
            cells = []
            for src, hs in zip(q_v, Q_HEADS):
                fold, cols = folds(share * len(hs)), share * len(hs)
                rows = slice(o * share // fold, (o + 1) * share // fold)
                for h in range(len(hs)):
                    lanes = [f * cols + (h * 3 + k) * hd for f in range(fold)]
                    cells.append(jnp.concatenate([src[rows, lane : lane + hd] for lane in lanes], axis=0))
            cells = jnp.concatenate(cells, axis=1).astype(F32)
            cols = slice(k * width + o * mine, k * width + (o + 1) * mine)
            qkv_f[:, cols] = cells
            total = total + jnp.sum(cells * wq[:, cols].astype(F32), axis=1, keepdims=True)
    c.start(("out", 3))
    for k, (src, dst) in enumerate(((up_v, up_f), (down_v, down_f), (out_v, out_f))):
        c.wait(("in", at + 1 + k))
        dst[...] = src[...].astype(F32)
        c.start(("out", k))
        if k < 2:
            c.wait(("x in", k))
            c.start(("x out", k))
    c.wait(("in", at + 4))
    gain_two_o[...] = row_of(jnp.sum(up_f[...] * wu[...].astype(F32), axis=1, keepdims=True) / my_gain(gain_two))
    gain_one_o[...] = row_of(total / my_gain(gain_one))
    c.wait(("x out", 0), ("x out", 1), *[("out", k) for k in range(4)])


def last_pass(blocks, new, rg, down, up, out, qs, w_qkv, w_up, gain_one, gain_two):
    share, width = out.shape
    v = lambda *s, t=BF16: pltpu.VMEM(s, t)
    f = lambda *s: jax.ShapeDtypeStruct(s, F32)
    hbm = pl.BlockSpec(memory_space=pl.ANY)
    vmem = pl.BlockSpec(memory_space=pltpu.VMEM)
    scratch = [
        v(*down.shape), v(*up.shape), v(*out.shape), v(share, 3 * width), v(*up.shape), v(width, 1, t=F32),
        v(*down.shape, t=F32), v(*up.shape, t=F32), v(*out.shape, t=F32), v(share, 3 * width, t=F32),
        v(2, new.shape[0], new.shape[2], t=F32),
    ]
    scratch += [v(*q.shape) for q in qs] + [pltpu.SemaphoreType.DMA((1, 20))]
    return pl.pallas_call(
        functools.partial(last_kernel, blocks),
        out_shape=[f(*new.shape), f(*rg.shape), f(1, share), f(1, share), f(share, 3 * width), f(*out.shape), f(*up.shape), f(*down.shape)],
        in_specs=[hbm] * 7 + [vmem] * 2 + [hbm] * len(qs),
        out_specs=[hbm, hbm, vmem, vmem] + [hbm] * 4,
        scratch_shapes=scratch,
        compiler_params=pltpu.CompilerParams(vmem_limit_bytes=VMEM_LIMIT),
    )(new, rg, down, up, out, w_qkv, w_up, gain_one, gain_two, *qs)


def per_device(residual, documents, gain_one, gain_two, w_qkv, w_out, w_up, w_down, cotangent):
    blocks = lax.axis_size("seq")
    n = lax.axis_size("batch")
    tok = residual.shape[1]
    x = jnp.transpose(residual, (2, 0, 1))
    cot = jnp.transpose(cotangent, (2, 0, 1))
    attT, hT, kT, qT, oT, lse, start, k, v, w_mine = fore_pass(n, tok, blocks, x, gain_one, documents, w_qkv)
    new, grad_middle, doT, grad_up, grad_out, down_half, down_ready = mid_pass(
        n, blocks, x, cot, attT, gain_two, w_out, w_up, w_down
    )
    sum_down, sum_up, sum_out, grad_x, *sum_qkv = back_pass(
        n, tok, blocks, (doT, k, v, kT, qT, oT, lse, start, hT, w_mine, x, grad_middle),
        down_half, down_ready, grad_up, grad_out, gain_one, w_up.shape[1] // w_up.shape[0],
    )
    new, grad_x, one, two, sum_qkv, sum_out, sum_up, sum_down = last_pass(
        blocks, new, grad_x, sum_down, sum_up, sum_out, sum_qkv, w_qkv, w_up, gain_one, gain_two
    )
    new, grad_x = jnp.transpose(new, (1, 2, 0)), jnp.transpose(grad_x, (1, 2, 0))
    return (new, grad_x, one[0], two[0], sum_qkv, sum_out, sum_up, sum_down)


def solution(mesh):
    placed = (
        P("batch", "seq", None),
        P("batch", "seq"),
        P(),
        P(),
        P(),
        P(),
        P(),
        P(),
        P("batch", "seq", None),
    )
    return jax.shard_map(
        per_device,
        mesh=mesh,
        in_specs=placed,
        out_specs=(
            P("batch", "seq", None),
            P("batch", "seq", None),
            P("seq"),
            P("seq"),
            P("seq", None),
            P("seq", None),
            P("seq", None),
            P("seq", None),
        ),
        check_vma=False,
    )
```

```python
import functools
import math

import jax
import jax.numpy as jnp
from jax import lax
from jax.experimental import pallas as pl
from jax.experimental.pallas import tpu as pltpu
from jax.sharding import PartitionSpec as P

H = 12
HD = 64
EPSILON = 1e-06
NEG = -1e30
F32, BF16 = jnp.float32, jnp.bfloat16
VMEM_LIMIT = 62 * 2**20


def dot(a, b):
    return lax.dot_general(a, b, (((1,), (0,)), ((), ())), preferred_element_type=F32)


def dot_nt(a, b):
    return lax.dot_general(a, b, (((1,), (1,)), ((), ())), preferred_element_type=F32)


def dot_tn(a, b):
    return lax.dot_general(a, b, (((0,), (0,)), ((), ())), preferred_element_type=F32)


def expand(narrow):
    return jnp.concatenate([narrow, -jnp.sum(narrow, axis=0, keepdims=True)], axis=0)


def shrink(full_vec):
    return full_vec[:-1] - jnp.mean(full_vec, axis=0, keepdims=True)


def shrink_back(grad_narrow):
    padded = jnp.concatenate([grad_narrow, jnp.zeros_like(grad_narrow[:1])], axis=0)
    return padded - jnp.sum(grad_narrow, axis=0, keepdims=True) / padded.shape[0]


def root(full_vec):
    return lax.rsqrt(jnp.mean(full_vec * full_vec, axis=0, keepdims=True) + EPSILON)


def norm_back(narrow, gain, grad_h):
    full_vec = expand(narrow)
    r = root(full_vec)
    scaled = gain * grad_h
    grad_full = r * (scaled - full_vec * (r * r * jnp.mean(scaled * full_vec, axis=0, keepdims=True)))
    return grad_full[:-1] - grad_full[-1:]


def column(gain_ref):
    return jnp.broadcast_to(gain_ref[...].reshape(1, gain_ref.shape[0]), (8, gain_ref.shape[0])).T[:, 0:1]


MESH = pl.DeviceIdType.MESH


class Place:
    def __init__(self, n):
        self.s = lax.axis_index("seq")
        self.b = lax.axis_index("batch")
        self.core = lax.rem(self.s, 2)
        self.chip = self.s // 2
        self.y = lax.rem(self.b, 2)
        self.z = lax.rem(self.b // 2, 4)
        self.far = self.b // 8
        self.n = n

    def core_mate(self):
        return (self.s + 1 - 2 * self.core, self.b)

    def chip_mate(self):
        return (self.s + 2 - 4 * self.chip, self.b)

    def cross_mate(self):
        return (3 - self.s, self.b)

    def y_mate(self):
        return (self.s, self.b + 1 - 2 * self.y)

    def z_of(self, d):
        return lax.rem(self.z + d, 4)

    def z_mate(self, d):
        return (self.s, self.b + 2 * (self.z_of(d) - self.z))

    def z_pair(self, bit):
        here = lax.rem(self.z // bit, 2)
        return (self.s, self.b + 2 * bit * (1 - 2 * here))

    def far_mate(self, d):
        f = lax.rem(self.far + d, self.n // 8)
        return (self.s, self.b + 8 * (f - self.far))

    def next_row(self):
        return (self.s, lax.rem(self.b + 1, self.n))

    def prior_row(self):
        return (self.s, lax.rem(self.b + self.n - 1, self.n))

    def all_mates(self):
        mates = [self.core_mate(), self.chip_mate(), self.cross_mate(), self.y_mate()]
        mates += [self.z_mate(d) for d in (1, 2, 3)]
        mates += [self.far_mate(d) for d in range(1, self.n // 8)]
        return mates + [self.next_row(), self.prior_row()]


def greet(mates):
    barrier = pltpu.get_barrier_semaphore()
    for mate in mates:
        pl.semaphore_signal(barrier, inc=1, device_id=mate, device_id_type=MESH)
    pl.semaphore_wait(barrier, len(mates))


class Copies:
    def __init__(self, sems):
        self.sems, self.made = sems, {}

    def remote(self, name, src, dst, mate):
        k = len(self.made)

        def make():
            return pltpu.make_async_remote_copy(
                src_ref=src(),
                dst_ref=dst(),
                send_sem=self.sems.at[0, k],
                recv_sem=self.sems.at[1, k],
                device_id=mate(),
                device_id_type=MESH,
            )

        assert name not in self.made
        self.made[name] = make

    def local(self, name, src, dst):
        k = len(self.made)

        def make():
            return pltpu.make_async_copy(src(), dst(), self.sems.at[0, k])

        assert name not in self.made
        self.made[name] = make

    def start(self, *names):
        for name in names:
            self.made[name]().start()

    def wait(self, *names):
        for name in names:
            self.made[name]().wait()

    def wait_recv(self, *names):
        for name in names:
            self.made[name]().wait_recv()

    def wait_send(self, *names):
        for name in names:
            self.made[name]().wait_send()


def rows_at(at, count):
    return pl.ds(pl.multiple_of(at, 16), count)


def blockwise(rows, body):
    step = next(s for s in (48, 32, 16) if rows % s == 0)

    def one(i, carry):
        body(i * step, step)
        return carry

    lax.fori_loop(0, rows // step, one, 0)


PAIRS, QUARTERS, PAIRS_Z = range(3)


class Sum:
    def __init__(self, place, copies, name, mode, way, src, first, rows, cols, bufs, out):
        self.p, self.c, self.name, self.mode, self.way = place, copies, name, mode, way
        bits = [(place.y, place.y_mate), (lax.rem(place.z, 2), lambda: place.z_pair(1))]
        (self.one, self.one_mate), (self.two, self.two_mate) = bits[::-1] if way == PAIRS_Z else bits
        self.src, self.first, self.rows, self.cols, self.out = src, first, rows, cols, out
        bufs = list(bufs)
        self.own, self.ry, self.rz, self.res, self.rf = bufs[:5]
        self.rc = bufs[5] if mode in "xy" else None
        self.rx = bufs[-1] if mode not in ("share", "ready") else None
        self.mine = (lambda: self.own.at[self.p.chip]) if mode in "xy" else (lambda: self.own.at[0])
        self.define()

    @staticmethod
    def scratch(mode, way, rows, cols, n):
        def v(*s):
            return pltpu.VMEM(s, BF16)

        half, spot = rows // 2, rows // (8 if way == QUARTERS else 4)
        out = [v(2 if mode in "xy" else 1, rows, cols), v(2 if mode == "y" else 1, half, cols)]
        out += [v(3 if way == QUARTERS else 2, spot, cols), v(rows, cols), v(n // 8 if n > 8 else 1, spot if n > 8 else 16, cols)]
        if mode in "xy":
            out.append(v(2, rows, cols))
        if mode not in ("share", "ready"):
            out.append(v(rows if mode == "x" else half, cols))
        return out

    def id(self, what):
        return (self.name, what)

    def at_half(self, one):
        return rows_at(one * (self.rows // 2), self.rows // 2)

    def at_spot(self):
        p, half = self.p, self.rows // 2
        if self.way == QUARTERS:
            return rows_at(p.y * half + p.z * (half // 4), half // 4)
        return rows_at(self.one * half + self.two * (half // 2), half // 2)

    def define(self):
        p, c, half, far = self.p, self.c, self.rows // 2, self.p.n // 8
        if self.mode in "xy":
            first = pl.ds(self.first, self.rows)
            for order in (1, 0):
                chip = lambda order=order: lax.rem(p.chip + order, 2)
                c.remote(
                    self.id(("core", order)),
                    lambda chip=chip: self.src.at[2 * chip() + 1 - p.core, first],
                    lambda chip=chip: self.rc.at[chip()],
                    p.core_mate,
                )
                c.local(
                    self.id(("own", order)),
                    lambda chip=chip: self.src.at[2 * chip() + p.core, first],
                    lambda chip=chip: self.own.at[chip()],
                )
        other = lambda: self.own.at[1 - p.chip]
        if self.mode == "x":
            c.remote(self.id("x"), other, lambda: self.rx, p.chip_mate)
        if self.mode == "y":
            c.remote(self.id("y1"), lambda: other().at[self.at_half(1 - self.one)], lambda: self.ry.at[1], self.one_mate)
            c.remote(self.id("x"), lambda: other().at[self.at_half(self.one)], lambda: self.rx, p.chip_mate)
        if self.mode == "ready":
            c.local(self.id("own"), lambda: self.src, lambda: self.own.at[0, self.at_half(self.one)])
        if self.mode == "half":
            c.remote(self.id("x"), lambda: self.src.at[1 - p.chip], lambda: self.rx, p.chip_mate)
            c.local(self.id("own"), lambda: self.src.at[p.chip], lambda: self.own.at[0, self.at_half(self.one)])
        elif self.mode != "ready":
            c.remote(self.id("y"), lambda: self.mine().at[self.at_half(1 - self.one)], lambda: self.ry.at[0], self.one_mate)
        spot = lambda: self.res.at[self.at_spot()]
        if self.way == QUARTERS:
            for d in (2, 1, 3):
                c.remote(
                    self.id(("z", d)),
                    lambda d=d: self.mine().at[rows_at(p.y * half + p.z_of(d) * (half // 4), half // 4)],
                    lambda d=d: self.rz.at[3 - d],
                    lambda d=d: p.z_mate(d),
                )
                c.remote(self.id(("bz", d)), spot, spot, lambda d=d: p.z_mate(d))
        else:
            away = lambda: rows_at(self.one * half + (1 - self.two) * (half // 2), half // 2)
            c.remote(self.id("z1"), lambda: self.mine().at[away()], lambda: self.rz.at[0], self.two_mate)
            c.remote(self.id("z2"), lambda: self.mine().at[self.at_spot()], lambda: self.rz.at[1], lambda: p.z_pair(2))
            c.remote(self.id("bz1"), spot, spot, self.two_mate)
        for d in range(1, far):
            c.remote(self.id(("far", d)), lambda: self.rf.at[p.far], lambda: self.rf.at[p.far], lambda d=d: p.far_mate(d))
        my_half = lambda: self.res.at[self.at_half(self.one)]
        c.remote(self.id("by"), my_half, my_half, self.one_mate)
        for k, (src, dst) in enumerate(self.out):
            c.local(self.id(("out", k)), lambda src=src: self.res.at[src], lambda dst=dst: dst)

    def add(self, dst, at, rows, *others):
        def body(first, step):
            here = rows_at(at + first, step)
            total = dst[here, :].astype(F32)
            for other, offset in others:
                total = total + other[rows_at(offset + first, step), :].astype(F32)
            dst[here, :] = total.astype(BF16)

        blockwise(rows, body)

    def p0(self):
        if self.mode == "half":
            self.c.start(self.id("x"), self.id("own"))
        if self.mode == "ready":
            self.c.start(self.id("own"))
        if self.mode in "xy":
            for order in (1, 0):
                self.c.start(self.id(("core", order)), self.id(("own", order)))

    def p1(self):
        self.c.wait(self.id(("core", 1)), self.id(("own", 1)))
        other = 1 - self.p.chip
        self.add(self.own.at[other], 0, self.rows, (self.rc.at[other], 0))
        self.c.start(self.id("x" if self.mode == "x" else "y1"))

    def p1b(self):
        self.c.wait(self.id(("core", 0)), self.id(("own", 0)))
        self.add(self.mine(), 0, self.rows, (self.rc.at[self.p.chip], 0))
        if self.mode == "y":
            self.c.start(self.id("y"))

    def p2(self):
        half = self.rows // 2
        if self.mode == "y":
            self.c.wait(self.id("y1"))
            self.add(self.own.at[1 - self.p.chip], self.one * half, half, (self.ry.at[1], 0))
            self.c.start(self.id("x"))
            return
        if self.mode == "x":
            self.c.wait(self.id("x"))
            self.add(self.mine(), (1 - self.one) * half, half, (self.rx, (1 - self.one) * half))
        self.c.start(self.id("y"))

    def p3(self):
        half, more = self.rows // 2, []
        if self.mode not in ("half", "ready"):
            self.c.wait(self.id("y"))
            more.append((self.ry.at[0], 0))
        if self.mode == "x":
            more.append((self.rx, self.one * half))
        if self.mode in ("y", "half"):
            self.c.wait(self.id("x"))
            more.append((self.rx, 0))
        if self.mode in ("half", "ready"):
            self.c.wait(self.id("own"))
        self.add(self.mine(), self.one * half, half, *more)
        self.c.start(*([self.id(("z", d)) for d in (2, 1, 3)] if self.way == QUARTERS else [self.id("z1")]))

    def total(self, *others):
        p = self.p
        spot, rows = self.at_spot(), self.at_spot().size
        own, far = self.mine(), p.n // 8

        def body(first, step):
            here = rows_at(spot.start + first, step)
            there = rows_at(first, step)
            total = own[here, :].astype(F32)
            for other in others:
                total = total + other[there, :].astype(F32)
            if far > 1:
                self.rf[p.far, there, :] = total.astype(BF16)
            else:
                self.res[here, :] = total.astype(BF16)

        blockwise(rows, body)
        if far > 1:
            self.c.start(*[self.id(("far", d)) for d in range(1, far)])
            self.c.wait(*[self.id(("far", d)) for d in range(1, far)])

            def more(first, step):
                there = rows_at(first, step)
                total = self.rf[0, there, :].astype(F32)
                for k in range(1, far):
                    total = total + self.rf[k, there, :].astype(F32)
                self.res[rows_at(spot.start + first, step), :] = total.astype(BF16)

            blockwise(rows, more)

    def p4(self):
        if self.way == QUARTERS:
            self.c.wait(*[self.id(("z", d)) for d in (1, 2, 3)])
            self.total(*[self.rz.at[d] for d in range(3)])
            self.c.start(*[self.id(("bz", d)) for d in (2, 1, 3)])
            return
        self.c.wait(self.id("z1"))
        spot = self.at_spot()
        self.add(self.mine(), spot.start, spot.size, (self.rz.at[0], 0))
        self.c.start(self.id("z2"))

    def p4b(self):
        if not self.way == QUARTERS:
            self.c.wait(self.id("z2"))
            self.total(self.rz.at[1])
            self.c.start(self.id("bz1"))

    def p5(self):
        self.c.wait(*([self.id(("bz", d)) for d in (1, 2, 3)] if self.way == QUARTERS else [self.id("bz1")]))
        self.c.start(self.id("by"))

    def p6(self):
        self.c.wait(self.id("by"))
        self.c.start(*[self.id(("out", k)) for k in range(len(self.out))])

    def p7(self):
        self.c.wait(*[self.id(("out", k)) for k in range(len(self.out))])

    def phase(self, k):
        (self.p0, self.p1, self.p1b, self.p2, self.p3, self.p4, self.p4b, self.p5, self.p6)[k]()


PRIOR_KV = (("pk", 0), ("pk", 1), ("pv", 0), ("pv", 1))


def fore_kernel(n, tok, blocks, heads, *refs):
    x, gain, docs, w, cot, w_down = refs[:6]
    attT_o, hT_o, kT_o, qT_o, oT_o, lse_o, start_o, k_o, v_o, wm_o, gg_o, g2_o = refs[6:18]
    xs, ws, wm, hT, docs_all, prior_docs, start, kT, vT, qT, kk, vv, acc, m_ref, l_ref, lse, stage, cs, wd, gg, g2, sems = refs[18:]
    width = xs.shape[0] + 1
    row = blocks * tok
    mine = heads * HD
    p = Place(n)
    c = Copies(sems)
    mates = {"core": p.core_mate, "chip": p.chip_mate, "cross": p.cross_mate}
    block = lambda at: pl.ds(pl.multiple_of(at * tok, tok), tok)
    here = lambda: block(p.s)
    c.local("w", lambda: w, lambda: ws)
    c.local("cot", lambda: cot.at[:, 0, :], lambda: cs)
    c.local("wd", lambda: w_down, lambda: wd)
    c.local("gg", lambda: gg, lambda: gg_o)
    c.local("g2", lambda: g2, lambda: g2_o)
    c.local("docs", lambda: docs, lambda: docs_all.at[:, here()])
    for name, mate in mates.items():
        c.remote(("docs", name), lambda: docs, lambda: docs_all.at[:, here()], mate)
    last = pl.ds(row - tok, tok)
    c.remote("old docs", lambda: docs_all.at[:, last], lambda: prior_docs, p.next_row)
    c.remote("hc", lambda: hT.at[:, here()], lambda: hT.at[:, here()], p.core_mate)
    half = tok // 2
    for k in range(2):
        c.local(("x", k), lambda k=k: x.at[:, 0, pl.ds(k * half, half)], lambda k=k: xs.at[:, pl.ds(k * half, half)])
        piece = lambda s, k=k: hT.at[:, pl.ds(pl.multiple_of(s * tok + k * half, half), half)]
        c.remote(("hx", k), lambda piece=piece: piece(p.s), lambda piece=piece: piece(p.s), p.chip_mate)
        other = lambda piece=piece: piece(p.chip_mate()[0])
        c.remote(("ho", k), other, other, p.core_mate)
    for k in range(2):
        end, to = pl.ds(row + k * half, half), pl.ds(k * half, half)
        c.remote(("pk", k), lambda end=end: kT.at[:, end], lambda to=to: kT.at[:, to], p.next_row)
        c.remote(("pv", k), lambda end=end: vT.at[:, end], lambda to=to: vT.at[:, to], p.next_row)
    for h in range(heads):
        spot = lambda h=h: attT_o.at[pl.ds(pl.multiple_of(p.s * mine + h * HD, HD), HD)]
        for name, mate in mates.items():
            src = lambda h=h, mate=mate: stage.at[pl.ds(h * HD, HD), block(mate()[0])]
            c.remote(("att", h, name), src, spot, mate)
        c.local(("att", h, "own"), lambda h=h: stage.at[pl.ds(h * HD, HD), here()], spot)
    outs = {"hT": (hT, hT_o), "kT": (kT, kT_o), "qT": (qT, qT_o), "oT": (acc, oT_o), "lse": (lse, lse_o)}
    outs.update({"start": (start, start_o), "k": (kk, k_o), "v": (vv, v_o), "wm": (wm, wm_o)})
    for name, (src, dst) in outs.items():
        c.local(("out", name), lambda src=src: src, lambda dst=dst: dst)

    c.start(("x", 0), ("x", 1), "docs", "w")
    greet([p.core_mate(), p.chip_mate(), p.cross_mate(), p.next_row(), p.prior_row()])
    c.start(*[("docs", name) for name in mates])
    gain_col = column(gain)
    for k in range(2):
        c.wait(("x", k))
        full_vec = expand(xs[:, k * half : (k + 1) * half])
        mine_now = pl.ds(pl.multiple_of(p.s * tok + k * half, half), half)
        hT[:, mine_now] = (gain_col * full_vec * root(full_vec)).astype(BF16)
        c.start(("hx", k))
    c.start("hc", "cot", "wd")

    c.wait("w")
    for s in range(blocks):
        @pl.when(p.s == s)
        def _():
            for h in range(heads):
                for k in range(3):
                    at = k * width + s * mine + h * HD
                    to = (h * 3 + k) * HD
                    wm[:, to : to + HD] = ws[:, at : at + HD]

    c.wait("docs", *[("docs", name) for name in mates])
    c.start("old docs")
    ids = jnp.broadcast_to(docs_all[...], (8, row))
    pos = lax.broadcasted_iota(jnp.int32, (8, row), 1)
    since = jnp.where((ids != pltpu.roll(ids, 1, 1)) | (pos == 0), pos, 0)
    hop = 1
    while hop < row:
        since = jnp.maximum(since, jnp.where(pos >= hop, pltpu.roll(since, hop, 1), 0))
        hop *= 2
    start[...] = since[0:1] + tok
    m_ref[...] = jnp.full(m_ref.shape, NEG, F32)
    l_ref[...] = jnp.zeros(l_ref.shape, F32)
    acc[...] = jnp.zeros(acc.shape, F32)

    def natural(keys_at, count):
        keys = pl.ds(pl.multiple_of(keys_at, 128), count)
        for h in range(heads):
            kk[h, keys, :] = kT[h * HD : (h + 1) * HD, keys].T
            vv[h, keys, :] = vT[h * HD : (h + 1) * HD, keys].T

    def project(at, count):
        own, keys = pl.ds(pl.multiple_of(at, 128), count), pl.ds(pl.multiple_of(at + tok, 128), count)
        packed = dot_tn(wm[...], hT[:, own]).astype(BF16)
        for h in range(heads):
            to, base = slice(h * HD, (h + 1) * HD), h * 3 * HD
            qT[to, own] = packed[base : base + HD] * jnp.bfloat16(1.0 / math.sqrt(HD))
            kT[to, keys] = packed[base + HD : base + 2 * HD]
            vT[to, keys] = packed[base + 2 * HD : base + 3 * HD]
        natural(at + tok, count)

    def pair(h, q0, qw, k0, kw, causal):
        hr = pl.ds(pl.multiple_of(h * HD, HD), HD)
        qs, ks = pl.ds(pl.multiple_of(q0, 128), qw), pl.ds(pl.multiple_of(k0 + tok, 128), kw)
        s = dot(kk[h, ks, :], qT[hr, qs])
        at = lax.broadcasted_iota(jnp.int32, s.shape, 0)
        keep = at >= start[:, qs] - (k0 + tok)
        if causal:
            keep = keep & (at <= lax.broadcasted_iota(jnp.int32, s.shape, 1))
        s = jnp.where(keep, s, NEG)
        m = m_ref[h, :, qs]
        new_m = jnp.maximum(m, jnp.max(s, axis=0, keepdims=True))
        e = jnp.exp(s - new_m)
        shift = jnp.exp(m - new_m)
        m_ref[h, :, qs] = new_m
        l_ref[h, :, qs] = l_ref[h, :, qs] * shift + jnp.sum(e, axis=0, keepdims=True)
        acc[hr, qs] = acc[hr, qs] * shift + dot(vT[hr, ks], e.astype(BF16))

    def finish(h, i):
        hr, qs = pl.ds(pl.multiple_of(h * HD, HD), HD), block(i)
        out = acc[hr, qs] / l_ref[h, :, qs]
        acc[hr, qs] = out
        stage[hr, qs] = out.astype(BF16)
        lse[h, :, qs] = m_ref[h, :, qs] + jnp.log(l_ref[h, :, qs])

    def send_att(h, zero):
        for name, mate in list(mates.items()) + [("own", lambda: (p.s,))]:
            @pl.when((mate()[0] == 0) == zero)
            def _():
                c.start(("att", h, name))

    pair_rows = 2 * tok
    near, far = pair_rows * p.chip, pair_rows * (1 - p.chip)
    c.wait_recv("hc")
    lax.fori_loop(0, 2, lambda t, carry: (project(near + t * tok, tok), carry)[1], 0)

    def send_prior(k):
        c.start(("pk", k), ("pv", k))

    @pl.when(p.chip == 1)
    def _():
        send_prior(0)
        send_prior(1)

    lax.fori_loop(0, heads, lambda h, carry: (pair(h, near, pair_rows, near, pair_rows, True), carry)[1], 0)

    def far_half(k):
        c.wait_recv(("hx", k))
        c.start(("ho", k))
        project(p.chip_mate()[0] * tok + k * half, half)
        c.wait_recv(("ho", k))
        project(p.cross_mate()[0] * tok + k * half, half)

        def queries(h, carry):
            for i in range(2):
                pair(h, pair_rows + i * tok + k * half, half, 0, pair_rows, False)
            return carry

        def keys(h, carry):
            for i in range(2):
                pair(h, pair_rows, pair_rows, i * tok + k * half, half, False)
            return carry

        @pl.when(p.chip == 0)
        def _():
            send_prior(k)
            lax.fori_loop(0, heads, queries, 0)

        @pl.when(p.chip == 1)
        def _():
            lax.fori_loop(0, heads, keys, 0)

    c.wait("cot", "wd")
    g2[...] = shrink_back(cs[...]).astype(BF16)
    c.start("g2")

    def grad_gelu(t, carry):
        its = pl.ds(pl.multiple_of(t * width, width), width)
        gg[its, :] = dot(wd[its, :], g2[...]).astype(BF16)
        return carry

    lax.fori_loop(0, wd.shape[0] // width, grad_gelu, 0)
    c.start("gg")
    far_half(0)
    far_half(1)

    def second(h, carry):
        pair(h, far, pair_rows, far, pair_rows, True)
        lax.fori_loop(1, blocks, lambda i, carry: (finish(h, i), carry)[1], 0)
        for k in range(heads):
            @pl.when(h == k)
            def _():
                send_att(k, False)
        return carry

    lax.fori_loop(0, heads, second, 0)
    c.wait_recv("old docs")
    from_doc = docs_all[:, 0:1]
    at = lax.broadcasted_iota(jnp.int32, (1, tok), 1)
    run = jnp.max(jnp.where(prior_docs[...] != from_doc, at + 1, 0), axis=1, keepdims=True)
    start[:, 0:tok] = jnp.where(start[:, 0:tok] == tok, run, start[:, 0:tok])
    c.wait_recv(*PRIOR_KV)
    natural(0, tok)

    def third(h, carry):
        pair(h, 0, tok, -tok, tok, False)
        finish(h, 0)
        for k in range(heads):
            @pl.when(h == k)
            def _():
                send_att(k, True)
        return carry

    lax.fori_loop(0, heads, third, 0)
    c.start(*[("out", name) for name in outs])
    c.wait_send("hc", ("hx", 0), ("hx", 1), ("ho", 0), ("ho", 1), "old docs", *PRIOR_KV)
    for h in range(heads):
        c.wait(*[("att", h, name) for name in list(mates) + ["own"]])
    c.wait("gg", "g2", *[("out", name) for name in outs])


def fore_pass(n, tok, blocks, x, gain, docs, w, cot, w_down):
    width, heads = w.shape[0], H // blocks
    row, mine = blocks * tok, heads * HD
    v = lambda *s, t=BF16: pltpu.VMEM(s, t)
    o = lambda *s, t=BF16: jax.ShapeDtypeStruct(s, t)
    hbm = pl.BlockSpec(memory_space=pl.ANY)
    scratch = [
        v(width - 1, tok, t=F32), v(width, 3 * width), v(width, 3 * mine), v(width, row),
        v(1, row, t=jnp.int32), v(1, tok, t=jnp.int32), v(1, row, t=jnp.int32),
        v(mine, row + tok), v(mine, row + tok), v(mine, row), v(heads, row + tok, HD), v(heads, row + tok, HD),
        v(mine, row, t=F32), v(heads, 1, row, t=F32), v(heads, 1, row, t=F32), v(heads, 1, row, t=F32), v(mine, row),
        v(width - 1, tok, t=F32), v(*w_down.shape), v(w_down.shape[0], tok), v(width, tok),
        pltpu.SemaphoreType.DMA((2, 31 + 4 * heads)),
    ]
    return pl.pallas_call(
        functools.partial(fore_kernel, n, tok, blocks, heads),
        out_shape=[
            o(width, tok), o(width, row), o(mine, row + tok), o(mine, row), o(mine, row, t=F32), o(heads, 1, row, t=F32),
            o(1, row, t=jnp.int32), o(heads, row + tok, HD), o(heads, row + tok, HD), o(width, 3 * mine),
            o(w_down.shape[0], tok), o(width, tok),
        ],
        in_specs=[hbm, pl.BlockSpec(memory_space=pltpu.VMEM)] + [hbm] * 4,
        out_specs=[hbm] * 12,
        scratch_shapes=scratch,
        compiler_params=pltpu.CompilerParams(collective_id=0, has_side_effects=True, vmem_limit_bytes=VMEM_LIMIT),
    )(x, gain, docs, w, cot, w_down)


def gelu_both(v, grad):
    rate = math.sqrt(2.0 / math.pi)
    square = v * v
    th = jnp.tanh(rate * v * (1.0 + 0.044715 * square))
    up = 0.5 * (1.0 + th)
    slope = up + 0.5 * v * (1.0 - th * th) * (rate * (1.0 + 3.0 * 0.044715 * square))
    return (v * up).astype(BF16), (grad * slope).astype(BF16)


def mid_kernel(n, blocks, *refs):
    x, cot, attT, gain, w_out, w_up, w_down, gg_in, g2_in = refs[:9]
    new_o, gm_o, doT_o, gu_o, go_o, half_o, ready_o = refs[9:16]
    xs, cs, at, wo, wu, wd, mid, h2, g2, g1, gg, geluT, gupT, dw, rc, ry, rx, ga, gu, go, sems = refs[16:]
    tok, width = xs.shape[1], xs.shape[0] + 1
    parts = wu.shape[1] // width
    share = width // blocks
    p = Place(n)
    c = Copies(sems)
    mates = {"cross": p.cross_mate, "chip": p.chip_mate, "core": p.core_mate}
    c.local("att", lambda: attT, lambda: at)
    c.local("wo", lambda: w_out, lambda: wo)
    c.local("x", lambda: x.at[:, 0, :], lambda: xs)
    c.local("cot", lambda: cot.at[:, 0, :], lambda: cs)
    c.local("wu", lambda: w_up, lambda: wu)
    c.local("wd", lambda: w_down, lambda: wd)
    c.local("gg", lambda: gg_in, lambda: gg)
    c.local("g2", lambda: g2_in, lambda: g2)
    c.remote(("core", 0), lambda: dw.at[0], lambda: rc.at[0], p.core_mate)
    c.remote(("core", 1), lambda: dw.at[2], lambda: rc.at[1], p.core_mate)
    part = width // 2
    fourth = part // 2
    low = lambda y: rows_at(y * fourth, fourth)
    for t in range(2):
        c.remote(("y", t), lambda t=t: dw.at[2 * t + 1, low(1 - p.y)], lambda t=t: ry.at[t], p.y_mate)
        dst = lambda t=t: half_o.at[1 - p.chip if t == 0 else p.chip]
        c.local(("half", t), lambda t=t: dw.at[2 * t + 1, low(p.y)], dst)
    high = pl.ds(part, part)
    c.remote("chip", lambda: dw.at[1, high], lambda: rx, p.chip_mate)
    later = lambda y: rows_at(part + y * fourth, fourth)
    c.remote(("y", 2), lambda: dw.at[3, later(1 - p.y)], lambda: ry.at[2], p.y_mate)
    c.local("ready", lambda: dw.at[3, later(p.y)], lambda: ready_o)
    there = lambda: doT_o.at[:, pl.ds(pl.multiple_of(p.s * tok, tok), tok)]
    for name, mate in mates.items():
        c.remote(("ga", name), lambda mate=mate: ga.at[rows_at(mate()[0] * share, share)], there, mate)
    c.local(("ga", "own"), lambda: ga.at[rows_at(p.s * share, share)], there)
    c.local("new", lambda: xs, lambda: new_o.at[:, 0, :])
    c.local("gm", lambda: cs, lambda: gm_o)
    for k in range(parts):
        c.local(("gu", k), lambda k=k: gu.at[:, pl.ds(k * share, share)], lambda k=k: gu_o.at[:, pl.ds(k * share, share)])
    c.local("go", lambda: go, lambda: go_o)

    c.start("att", "wo", "x", "wu", "gg", "g2", "cot", "wd")
    greet([p.core_mate(), p.chip_mate(), p.cross_mate(), p.y_mate()])
    c.wait("att", "wo")
    branch_one = dot_tn(wo[...], at[...])
    c.wait("x")
    mid[...] = xs[...] + shrink(branch_one)
    full_vec = expand(mid[...])
    gain_col = column(gain)
    h2[...] = (gain_col * full_vec * root(full_vec)).astype(BF16)
    c.wait("wu", "gg", "g2")

    def add(dst, at, src, rows):
        def body(first, step):
            r = rows_at(at + first, step)
            dw[dst, r, :] = (dw[dst, r, :].astype(F32) + src[rows_at(first, step), :].astype(F32)).astype(BF16)

        blockwise(rows, body)

    def chip_sum(t):
        c.wait_recv(("core", t))
        add(2 * t + 1, 0, rc.at[t], width)
        c.start(("y", t), *(["chip"] if t == 0 else []))

    def y_sum(t):
        c.wait(("y", t))
        add(2 * t + 1, p.y * fourth, ry.at[t], fourth)
        c.start(("half", t))

    def piece(t, carry):
        s = jnp.where(t == 0, p.cross_mate()[0], jnp.where(t == 1, p.chip_mate()[0], jnp.where(t == 2, p.core_mate()[0], p.s)))
        its = pl.ds(pl.multiple_of(s * width, width), width)
        gelu, grad_up = gelu_both(dot_tn(wu[:, its], h2[...]), gg[its, :].astype(F32))
        geluT[its, :] = gelu
        gupT[its, :] = grad_up
        dw[t] = dot_nt(geluT[its, :], g2[...]).astype(BF16)

        @pl.when(t == 0)
        def _():
            c.start(("core", 0))

        @pl.when(t == 2)
        def _():
            c.start(("core", 1))

        @pl.when(t == 1)
        def _():
            chip_sum(0)

        return carry

    lax.fori_loop(0, parts, piece, 0)
    chip_sum(1)
    grad_h = dot(wu[...], gupT[...])
    c.wait("cot")
    grad_middle = cs[...] + norm_back(mid[...], gain_col, grad_h)
    cs[...] = grad_middle
    g1[...] = shrink_back(grad_middle).astype(BF16)
    ga[...] = dot(wo[...], g1[...]).astype(BF16)
    c.start(*[("ga", name) for name in list(mates) + ["own"]])
    c.start("gm")
    def up_grad(k, carry):
        its = pl.ds(pl.multiple_of(k * width, width), width)
        grad = dot_nt(h2[...], gupT[its, :]).astype(BF16)
        for s in range(blocks):
            gu[s, rows_at(k * share, share), :] = grad[s * share : (s + 1) * share]
        return carry

    lax.fori_loop(0, parts // 2, up_grad, 0)
    c.wait("chip")
    add(3, part, rx, part)
    c.start(("y", 2))
    lax.fori_loop(parts // 2, parts, up_grad, 0)
    c.start(*[("gu", k) for k in range(parts)])
    out_grad = dot_nt(at[...], g1[...]).astype(BF16)
    for s in range(blocks):
        for k in range(2):
            go[s, k * share : (k + 1) * share, :] = out_grad[s * share : (s + 1) * share, k * part : (k + 1) * part]
    c.start("go")
    c.wait("wd")
    xs[...] = mid[...] + shrink(dot_tn(wd[...], geluT[...]))
    c.start("new")
    y_sum(0)
    y_sum(1)
    c.wait(("y", 2))
    add(3, part + p.y * fourth, ry.at[2], fourth)
    c.start("ready")
    c.wait_send(("core", 0), ("core", 1))
    c.wait(*[("ga", name) for name in list(mates) + ["own"]])
    c.wait("gm", "new", "go", "ready", ("half", 0), ("half", 1), *[("gu", k) for k in range(parts)])


def mid_pass(n, blocks, x, cot, attT, gain, w_out, w_up, w_down, gg, g2):
    width, tok = attT.shape
    parts, share = w_up.shape[1] // width, width // blocks
    v = lambda *s, t=BF16: pltpu.VMEM(s, t)
    o = lambda *s, t=BF16: jax.ShapeDtypeStruct(s, t)
    hbm = pl.BlockSpec(memory_space=pl.ANY)
    scratch = [
        v(width - 1, tok, t=F32), v(width - 1, tok, t=F32), v(width, tok), v(width, width), v(*w_up.shape), v(*w_down.shape),
        v(width - 1, tok, t=F32), v(width, tok), v(width, tok), v(width, tok), v(*gg.shape), v(*gg.shape), v(*gg.shape), v(4, width, width), v(2, width, width), v(3, width // 4, width), v(width // 2, width),
        v(width, tok), v(blocks, parts * share, width), v(blocks, 2 * share, width // 2),
        pltpu.SemaphoreType.DMA((2, 32)),
    ]
    return pl.pallas_call(
        functools.partial(mid_kernel, n, blocks),
        out_shape=[
            o(width - 1, 1, tok, t=F32), o(width - 1, tok, t=F32), o(share, blocks * tok), o(blocks, parts * share, width),
            o(blocks, 2 * share, width // 2), o(2, width // 4, width), o(width // 4, width),
        ],
        in_specs=[hbm] * 3 + [pl.BlockSpec(memory_space=pltpu.VMEM)] + [hbm] * 5,
        out_specs=[hbm] * 7,
        scratch_shapes=scratch,
        compiler_params=pltpu.CompilerParams(collective_id=2, has_side_effects=True, vmem_limit_bytes=VMEM_LIMIT),
    )(x, cot, attT, gain, w_out, w_up, w_down, gg, g2)


BACK_IN = ("doT", "k", "v", "kT", "qT", "oT", "lse", "start", "hT", "wm", "x", "gm")
DW = ("cross", "chip", "core", "own")
D0, D1, U0, U1, O, Q0, Q1, GRAD_H, SEND = range(9)
Q_HEADS = ((0, 1), (2,))
U_MODES = ("x", "x")
O_MODE = "y"
WAYS = (PAIRS, PAIRS, PAIRS, PAIRS, PAIRS, PAIRS_Z, PAIRS)
START, READY, PRIOR, FULL, DIAGONAL, CLOSE, END = range(7)
PLAN = {
    START: {
        (): [(D0, 0), (U1, 0), (U0, 0), (D1, 0), (O, 0)],
    },
    READY: {
        (): [(U1, 1), (D1, 4)],
    },
    PRIOR: {
        (0,): [(U1, 2)],
        (1,): [(U0, 1), (U0, 2)],
        (2,): [(D0, 4), (D1, 5), (O, 1), (O, 2)],
    },
    FULL: {
        (1, 0): [(D0, 5), (U1, 3), (O, 3)],
        (2, 1): [(D0, 6), (U0, 3), (D1, 7)],
        (2, 4): [(U1, 5), (O, 4)],
    },
    DIAGONAL: {
        (1, 0): [(D1, 6)],
        (2, 1): [(D0, 7)],
    },
    CLOSE: {
        (1,): [(U1, 4), (SEND, 0)],
        (2,): [(Q0, 3), (SEND, 1), (GRAD_H, 0), (U0, 4), (GRAD_H, 1), (GRAD_H, 2), (O, 5), (U1, 6)],
    },
    END: {
        (): [(GRAD_H, 3), (Q1, 3), (D1, 8), (GRAD_H, 4), (GRAD_H, 5), (Q0, 4), (U0, 5), (D0, 8),
            (O, 6), (Q1, 4), (U1, 7), (Q0, 5), (O, 7), (U0, 6), (Q1, 5), (GRAD_H, 6),
            (U1, 8), (O, 8), (Q0, 6), (U0, 7), (Q1, 6), (Q0, 7), (Q1, 7), (U0, 8),
            (Q0, 8), (Q1, 8)],
    },
}


def folds(cols):
    return 2 if cols % 128 else 1


def back_sums(n, width, share, part):
    way = lambda k: QUARTERS if n > 8 else WAYS[k]
    half = [(D0 + k, ("half", "ready")[k], way(D0 + k), k, 0, part, width) for k in range(2)]
    up = [(U0 + k, U_MODES[k], way(U0 + k), 0, k * part, part, width) for k in range(2)]
    sums = half + up + [(O, O_MODE, way(O), 1, 0, 2 * share, part)]
    for k, hs in enumerate(Q_HEADS):
        cols = share * len(hs)
        sums.append((Q0 + k, "share", way(Q0 + k), None, 0, width // folds(cols), cols * folds(cols)))
    return sums


def back_kernel(n, tok, blocks, heads, parts, *refs):
    refs = list(refs)
    take = lambda count: [refs.pop(0) for _ in range(count)]
    hbm = dict(zip(BACK_IN, take(len(BACK_IN))))
    down_half, down_ready, gu, go, gain_one = take(5)
    down_o, up_o, out_o, rg_o = take(4)
    qkv_o = take(len(Q_HEADS))
    vm = dict(zip(BACK_IN, take(len(BACK_IN))))
    dkT, dvT, delta, dP, prior_out, prior_in, g_stage, g_core, g_x, g_acc = take(10)
    dws = take(len(Q_HEADS))
    p, hd, row = Place(n), HD, blocks * tok
    mine, width = heads * hd, blocks * heads * hd
    share, part = width // blocks, width // 2
    per_part = part // share
    outs = {D0 + k: [(pl.ds(0, part), down_o.at[pl.ds(k * part, part)])] for k in range(2)}
    for k in range(2):
        outs[U0 + k] = [
            (pl.ds(j * share, share), up_o.at[:, pl.ds((k * per_part + j) * width, width)]) for j in range(per_part)
        ]
    outs[O] = [(pl.ds(k * share, share), out_o.at[:, pl.ds(k * part, part)]) for k in range(2)]
    for k in range(len(Q_HEADS)):
        outs[Q0 + k] = [(pl.ds(0, qkv_o[k].shape[0]), qkv_o[k])]
    plans = back_sums(n, width, share, part)
    bufs = [take(len(Sum.scratch(q[1], q[2], 16, 128, n))) for q in plans]
    c = Copies(refs.pop(0))
    for name in BACK_IN:
        src = (lambda: hbm["x"].at[:, 0, :]) if name == "x" else (lambda name=name: hbm[name])
        c.local(name, src, lambda name=name: vm[name])
    sums = {}
    for (name, mode, way, arr, first, rows, cols), buf in zip(plans, bufs):
        src = None if arr is None else ((down_half, down_ready) if name < U0 else (gu, go))[arr]
        sums[name] = Sum(p, c, name, mode, way, src, first, rows, cols, buf, outs[name])
    qkv = [sums[Q0 + k] for k in range(len(Q_HEADS))]
    for k, one in enumerate(qkv):
        count = one.rows // blocks
        block = lambda ref, s, count=count: ref.at[rows_at(s * count, count)]
        spot = lambda one=one, block=block: block(one.own.at[0], p.s)
        for what, mate in (("cross", p.cross_mate), ("chip", p.chip_mate), ("core", p.core_mate)):
            c.remote(("dw", k, what), lambda k=k, mate=mate, block=block: block(dws[k], mate()[0]), spot, mate)
        c.local(("dw", k, "own"), lambda k=k, block=block: block(dws[k], p.s), spot)
    for k in range(heads):
        c.remote(("prior", k), lambda k=k: prior_out.at[k], lambda k=k: prior_in.at[k], p.prior_row)
    for order in (1, 0):
        c.remote(("gh", order), lambda order=order: g_stage.at[order], lambda order=order: g_core.at[order], p.core_mate)
    c.remote(("gh", "x"), lambda: g_stage.at[1], lambda: g_x, p.chip_mate)
    c.local("rg", lambda: vm["gm"], lambda: rg_o.at[:, 0, :])

    def grad_h_part(owner):
        return dot(vm["wm"][...], dP[:, pl.ds(pl.multiple_of(owner * tok, tok), tok)])

    def core_grad(order):
        chip = lax.rem(p.chip + order, 2)
        g_stage[order] = grad_h_part(2 * chip + 1 - p.core).astype(BF16)
        c.start(("gh", order))

    def keep_grad(order):
        chip = lax.rem(p.chip + order, 2)
        g_acc[...] = grad_h_part(2 * chip + p.core)

    def chip_grad():
        c.wait(("gh", 1))
        g_stage[1] = (g_acc[...] + g_core[1].astype(F32)).astype(BF16)
        c.start(("gh", "x"))

    def own_grad():
        c.wait(("gh", 0))
        g_acc[...] += g_core[0].astype(F32)

    def input_grad():
        c.wait("x", "gm", ("gh", "x"))
        vm["gm"][...] += norm_back(vm["x"][...], column(gain_one), g_acc[...] + g_x[...].astype(F32))
        c.start("rg")

    def send_dw(k):
        rows = slice(Q_HEADS[k][0] * 3 * hd, (Q_HEADS[k][-1] + 1) * 3 * hd)
        grad = dot_nt(vm["hT"][...], dP[rows, :]).astype(BF16)
        fold = folds(grad.shape[1])
        count = share // fold
        for s in range(blocks):
            cells = [grad[s * share + f * count : s * share + (f + 1) * count] for f in range(fold)]
            dws[k][s * count : (s + 1) * count, :] = jnp.concatenate(cells, axis=1)
        c.start(*[("dw", k, what) for what in DW])

    special = {GRAD_H: [lambda: core_grad(1), lambda: core_grad(0), lambda: keep_grad(1), chip_grad, lambda: keep_grad(0)]}
    special[GRAD_H] += [own_grad, input_grad]
    special[SEND] = [lambda k=k: send_dw(k) for k in range(len(Q_HEADS))]

    def step(which, phase):
        if which in special:
            special[which][phase]()
            return
        if which >= Q0 and phase == 3:
            c.wait(*[("dw", which - Q0, what) for what in DW])
        sums[which].phase(phase)

    def steps_at(place, *now):
        for at, names in PLAN.get(place, {}).items():
            same = None
            for want, have in zip(at, now):
                same = (have == want) if same is None else same & (have == want)

            def run():
                for which, phase in names:
                    step(which, phase)

            run() if same is None else pl.when(same)(run)

    first = BACK_IN[:8]
    c.start(*first)
    greet(p.all_mates())
    steps_at(START)
    c.start(*BACK_IN[8:])
    c.wait(*first)
    dqT = vm["oT"]
    doT, kk, vv, kT, qT, lse, start = (vm[x] for x in ("doT", "k", "v", "kT", "qT", "lse", "start"))

    def make_delta(h, carry):
        rows = pl.ds(pl.multiple_of(h * hd, hd), hd)
        delta[h] = jnp.sum(doT[rows, :].astype(F32) * vm["oT"][rows, :], axis=0, keepdims=True)
        return carry

    lax.fori_loop(0, heads, make_delta, 0)
    dqT[...] = jnp.zeros_like(dqT)
    dkT[...] = jnp.zeros_like(dkT)
    dvT[...] = jnp.zeros_like(dvT)
    steps_at(READY)

    def pair(h, i, j, causal):
        hr = pl.ds(pl.multiple_of(h * hd, hd), hd)
        qs, ks = (pl.ds(pl.multiple_of(at * tok, tok), tok) for at in (i, j))
        q_blk, do_blk = qT[hr, qs], doT[hr, qs]
        s = dot(kk[h, ks, :], q_blk)
        e = jnp.exp(s - lse[h, :, qs])
        at = lax.broadcasted_iota(jnp.int32, s.shape, 0)
        keep = at >= start[:, qs] - j * tok
        if causal:
            keep = keep & (at <= lax.broadcasted_iota(jnp.int32, s.shape, 1))
        e = jnp.where(keep, e, 0.0)
        dp = dot(vv[h, ks, :], do_blk)
        ds = (e * (dp - delta[h, :, qs])).astype(BF16)
        dvT[hr, ks] += dot_nt(do_blk, e.astype(BF16))
        dkT[hr, ks] += dot_nt(q_blk, ds)
        dqT[hr, qs] += dot(kT[hr, ks], ds)

    def prior(h, carry):
        pair(h, 0, 0, False)
        hr = pl.ds(pl.multiple_of(h * hd, hd), hd)
        prior_out[h, 0:hd, :] = dkT[hr, 0:tok].astype(BF16)
        prior_out[h, hd : 2 * hd, :] = dvT[hr, 0:tok].astype(BF16)
        for k in range(heads):
            @pl.when(h == k)
            def _():
                c.start(("prior", k))
        steps_at(PRIOR, h)
        return carry

    lax.fori_loop(0, heads, prior, 0)

    def close(h):
        hr = pl.ds(pl.multiple_of(h * hd, hd), hd)
        last = pl.ds(row, tok)
        dkT[hr, last] += prior_in[h, 0:hd, :].astype(F32)
        dvT[hr, last] += prior_in[h, hd : 2 * hd, :].astype(F32)
        base = h * 3 * hd
        for k, (src, at) in enumerate(((dqT, 0), (dkT, tok), (dvT, tok))):
            val = src[hr, at:]
            val = val * (1.0 / math.sqrt(hd)) if k == 0 else val
            dP[pl.ds(pl.multiple_of(base + k * hd, hd), hd), :] = val.astype(BF16)

    def head(h, carry):
        def full(t, carry):
            i = jnp.where(t < 3, 3, jnp.where(t < 5, 2, 1))
            j = jnp.where(t < 3, t + 1, jnp.where(t < 5, t - 2, 1))
            pair(h, i, j, False)
            steps_at(FULL, h, t)
            return carry

        lax.fori_loop(0, 6, full, 0)

        def diagonal(i, carry):
            pair(h, i, i + 1, True)
            steps_at(DIAGONAL, h, i)
            return carry

        lax.fori_loop(0, blocks, diagonal, 0)
        for k in range(heads):
            @pl.when(h == k)
            def _():
                if k == 0:
                    c.wait("hT", "wm")
                c.wait(("prior", k))
        close(h)
        steps_at(CLOSE, h)
        return carry

    lax.fori_loop(0, heads, head, 0)
    steps_at(END)

    for one in sums.values():
        one.p7()
    c.wait("rg")


def back_pass(n, tok, blocks, ins, down_half, down_ready, gu, go, gain, parts):
    heads = ins[1].shape[0]
    row = blocks * tok
    width = ins[8].shape[0]
    mine = heads * HD
    share, part = width // blocks, width // 2
    v = lambda *s, t=BF16: pltpu.VMEM(s, t)
    o = lambda *s, t=BF16: jax.ShapeDtypeStruct(s, t)
    scratch = [v(width - 1, tok, t=F32) if name == "x" else pltpu.VMEM(a.shape, a.dtype) for name, a in zip(BACK_IN, ins)]
    scratch += [
        v(mine, row + tok, t=F32), v(mine, row + tok, t=F32), v(heads, 1, row, t=F32), v(3 * mine, row),
        v(heads, 2 * HD, tok), v(heads, 2 * HD, tok),
        v(2, width, tok), v(2, width, tok), v(width, tok), v(width, tok, t=F32),
    ]
    sums = back_sums(n, width, share, part)
    scratch += [v(*one[5:]) for one in sums[Q0:]]
    copies = len(ins) + 5 * heads + 8
    for _, mode, way, _, _, rows, cols in sums:
        scratch += Sum.scratch(mode, way, rows, cols, n)
        copies += 17 + n // 8
    scratch.append(pltpu.SemaphoreType.DMA((2, copies)))
    hbm = pl.BlockSpec(memory_space=pl.ANY)
    vmem = pl.BlockSpec(memory_space=pltpu.VMEM)
    return pl.pallas_call(
        functools.partial(back_kernel, n, tok, blocks, heads, parts),
        out_shape=[o(width, width), o(share, parts * width), o(share, width), o(width - 1, 1, tok, t=F32)]
        + [o(*one[5:]) for one in sums[Q0:]],
        in_specs=[hbm] * (len(ins) + 4) + [vmem],
        out_specs=[hbm] * (4 + len(Q_HEADS)),
        scratch_shapes=scratch,
        compiler_params=pltpu.CompilerParams(collective_id=1, has_side_effects=True, vmem_limit_bytes=VMEM_LIMIT),
    )(*ins, down_half, down_ready, gu, go, gain)


def last_kernel(blocks, *refs):
    new, rg, down, up, out, w_qkv, w_up, gain_one, gain_two = refs[:9]
    q_in = refs[9 : 9 + len(Q_HEADS)]
    refs = refs[9 + len(Q_HEADS) :]
    new_o, rg_o, gain_one_o, gain_two_o, qkv_o, out_o, up_o, down_o = refs[:8]
    down_v, up_v, out_v, wq, wu, gcol, down_f, up_f, out_f, qkv_f, x_v, sems = refs[8:19] + refs[-1:]
    q_v = refs[19:-1]
    s = lax.axis_index("seq")
    share, width = out_v.shape
    mine, hd = width // blocks, HD
    c = Copies(sems)
    my_rows = lambda ref: ref.at[rows_at(s * share, share)]
    loads = list(zip(q_in, q_v)) + [(my_rows(w_qkv), wq), (up, up_v), (down, down_v), (out, out_v), (my_rows(w_up), wu)]
    for k, (src, dst) in enumerate(loads):
        c.local(("in", k), lambda src=src: src, lambda dst=dst: dst)
    for k, (src, dst) in enumerate(((up_f, up_o), (down_f, down_o), (out_f, out_o), (qkv_f, qkv_o))):
        c.local(("out", k), lambda src=src: src, lambda dst=dst: dst)
    for k, (src, dst) in enumerate(((new, new_o), (rg, rg_o))):
        c.local(("x in", k), lambda k=k, src=src: src.at[:, 0, :], lambda k=k: x_v.at[k])
        c.local(("x out", k), lambda k=k: x_v.at[k], lambda k=k, dst=dst: dst.at[:, 0, :])
    at = len(q_in)
    c.start(*[("in", k) for k in range(at + 2)], ("x in", 0), ("x in", 1), *[("in", k) for k in range(at + 2, len(loads))])

    def row_of(col):
        return jnp.broadcast_to(col, (share, 128)).T[0:1, :]

    def my_gain(gain):
        gcol[...] = column(gain)
        return gcol[pl.ds(pl.multiple_of(s * share, share), share), :]

    c.wait(*[("in", k) for k in range(at + 1)])
    total = jnp.zeros((share, 1), F32)
    for k in range(3):
        for o in range(blocks):
            cells = []
            for src, hs in zip(q_v, Q_HEADS):
                fold, cols = folds(share * len(hs)), share * len(hs)
                rows = slice(o * share // fold, (o + 1) * share // fold)
                for h in range(len(hs)):
                    lanes = [f * cols + (h * 3 + k) * hd for f in range(fold)]
                    cells.append(jnp.concatenate([src[rows, lane : lane + hd] for lane in lanes], axis=0))
            cells = jnp.concatenate(cells, axis=1).astype(F32)
            cols = slice(k * width + o * mine, k * width + (o + 1) * mine)
            qkv_f[:, cols] = cells
            total = total + jnp.sum(cells * wq[:, cols].astype(F32), axis=1, keepdims=True)
    c.start(("out", 3))
    for k, (src, dst) in enumerate(((up_v, up_f), (down_v, down_f), (out_v, out_f))):
        c.wait(("in", at + 1 + k))
        dst[...] = src[...].astype(F32)
        c.start(("out", k))
        if k < 2:
            c.wait(("x in", k))
            c.start(("x out", k))
    c.wait(("in", at + 4))
    gain_two_o[...] = row_of(jnp.sum(up_f[...] * wu[...].astype(F32), axis=1, keepdims=True) / my_gain(gain_two))
    gain_one_o[...] = row_of(total / my_gain(gain_one))
    c.wait(("x out", 0), ("x out", 1), *[("out", k) for k in range(4)])


def last_pass(blocks, new, rg, down, up, out, qs, w_qkv, w_up, gain_one, gain_two):
    share, width = out.shape
    v = lambda *s, t=BF16: pltpu.VMEM(s, t)
    f = lambda *s: jax.ShapeDtypeStruct(s, F32)
    hbm = pl.BlockSpec(memory_space=pl.ANY)
    vmem = pl.BlockSpec(memory_space=pltpu.VMEM)
    scratch = [
        v(*down.shape), v(*up.shape), v(*out.shape), v(share, 3 * width), v(*up.shape), v(width, 1, t=F32),
        v(*down.shape, t=F32), v(*up.shape, t=F32), v(*out.shape, t=F32), v(share, 3 * width, t=F32),
        v(2, new.shape[0], new.shape[2], t=F32),
    ]
    scratch += [v(*q.shape) for q in qs] + [pltpu.SemaphoreType.DMA((1, 20))]
    return pl.pallas_call(
        functools.partial(last_kernel, blocks),
        out_shape=[f(*new.shape), f(*rg.shape), f(1, share), f(1, share), f(share, 3 * width), f(*out.shape), f(*up.shape), f(*down.shape)],
        in_specs=[hbm] * 7 + [vmem] * 2 + [hbm] * len(qs),
        out_specs=[hbm, hbm, vmem, vmem] + [hbm] * 4,
        scratch_shapes=scratch,
        compiler_params=pltpu.CompilerParams(vmem_limit_bytes=VMEM_LIMIT),
    )(new, rg, down, up, out, w_qkv, w_up, gain_one, gain_two, *qs)


def per_device(residual, documents, gain_one, gain_two, w_qkv, w_out, w_up, w_down, cotangent):
    blocks = lax.axis_size("seq")
    n = lax.axis_size("batch")
    tok = residual.shape[1]
    x = jnp.transpose(residual, (2, 0, 1))
    cot = jnp.transpose(cotangent, (2, 0, 1))
    attT, hT, kT, qT, oT, lse, start, k, v, w_mine, grad_gelu, grad_two = fore_pass(
        n, tok, blocks, x, gain_one, documents, w_qkv, cot, w_down
    )
    new, grad_middle, doT, grad_up, grad_out, down_half, down_ready = mid_pass(
        n, blocks, x, cot, attT, gain_two, w_out, w_up, w_down, grad_gelu, grad_two
    )
    sum_down, sum_up, sum_out, grad_x, *sum_qkv = back_pass(
        n, tok, blocks, (doT, k, v, kT, qT, oT, lse, start, hT, w_mine, x, grad_middle),
        down_half, down_ready, grad_up, grad_out, gain_one, w_up.shape[1] // w_up.shape[0],
    )
    new, grad_x, one, two, sum_qkv, sum_out, sum_up, sum_down = last_pass(
        blocks, new, grad_x, sum_down, sum_up, sum_out, sum_qkv, w_qkv, w_up, gain_one, gain_two
    )
    new, grad_x = jnp.transpose(new, (1, 2, 0)), jnp.transpose(grad_x, (1, 2, 0))
    return (new, grad_x, one[0], two[0], sum_qkv, sum_out, sum_up, sum_down)


def solution(mesh):
    placed = (
        P("batch", "seq", None),
        P("batch", "seq"),
        P(),
        P(),
        P(),
        P(),
        P(),
        P(),
        P("batch", "seq", None),
    )
    return jax.shard_map(
        per_device,
        mesh=mesh,
        in_specs=placed,
        out_specs=(
            P("batch", "seq", None),
            P("batch", "seq", None),
            P("seq"),
            P("seq"),
            P("seq", None),
            P("seq", None),
            P("seq", None),
            P("seq", None),
        ),
        check_vma=False,
    )
```

```python
import functools
import math

import jax
import jax.numpy as jnp
from jax import lax
from jax.experimental import pallas as pl
from jax.experimental.pallas import tpu as pltpu
from jax.sharding import PartitionSpec as P

H = 12
HD = 64
EPSILON = 1e-06
NEG = -1e30
F32, BF16 = jnp.float32, jnp.bfloat16
VMEM_LIMIT = 62 * 2**20


def dot(a, b):
    return lax.dot_general(a, b, (((1,), (0,)), ((), ())), preferred_element_type=F32)


def dot_nt(a, b):
    return lax.dot_general(a, b, (((1,), (1,)), ((), ())), preferred_element_type=F32)


def dot_tn(a, b):
    return lax.dot_general(a, b, (((0,), (0,)), ((), ())), preferred_element_type=F32)


def expand(narrow):
    return jnp.concatenate([narrow, -jnp.sum(narrow, axis=0, keepdims=True)], axis=0)


def shrink(full_vec):
    return full_vec[:-1] - jnp.mean(full_vec, axis=0, keepdims=True)


def shrink_back(grad_narrow):
    padded = jnp.concatenate([grad_narrow, jnp.zeros_like(grad_narrow[:1])], axis=0)
    return padded - jnp.sum(grad_narrow, axis=0, keepdims=True) / padded.shape[0]


def root(full_vec):
    return lax.rsqrt(jnp.mean(full_vec * full_vec, axis=0, keepdims=True) + EPSILON)


def norm_back(narrow, gain, grad_h):
    full_vec = expand(narrow)
    r = root(full_vec)
    scaled = gain * grad_h
    grad_full = r * (scaled - full_vec * (r * r * jnp.mean(scaled * full_vec, axis=0, keepdims=True)))
    return grad_full[:-1] - grad_full[-1:]


def column(gain_ref):
    return jnp.broadcast_to(gain_ref[...].reshape(1, gain_ref.shape[0]), (8, gain_ref.shape[0])).T[:, 0:1]


MESH = pl.DeviceIdType.MESH


class Place:
    def __init__(self, n):
        self.s = lax.axis_index("seq")
        self.b = lax.axis_index("batch")
        self.core = lax.rem(self.s, 2)
        self.chip = self.s // 2
        self.y = lax.rem(self.b, 2)
        self.z = lax.rem(self.b // 2, 4)
        self.far = self.b // 8
        self.n = n

    def core_mate(self):
        return (self.s + 1 - 2 * self.core, self.b)

    def chip_mate(self):
        return (self.s + 2 - 4 * self.chip, self.b)

    def cross_mate(self):
        return (3 - self.s, self.b)

    def y_mate(self):
        return (self.s, self.b + 1 - 2 * self.y)

    def z_of(self, d):
        return lax.rem(self.z + d, 4)

    def z_mate(self, d):
        return (self.s, self.b + 2 * (self.z_of(d) - self.z))

    def z_pair(self, bit):
        here = lax.rem(self.z // bit, 2)
        return (self.s, self.b + 2 * bit * (1 - 2 * here))

    def far_mate(self, d):
        f = lax.rem(self.far + d, self.n // 8)
        return (self.s, self.b + 8 * (f - self.far))

    def next_row(self):
        return (self.s, lax.rem(self.b + 1, self.n))

    def prior_row(self):
        return (self.s, lax.rem(self.b + self.n - 1, self.n))

    def all_mates(self):
        mates = [self.core_mate(), self.chip_mate(), self.cross_mate(), self.y_mate()]
        mates += [self.z_mate(d) for d in (1, 2, 3)]
        mates += [self.far_mate(d) for d in range(1, self.n // 8)]
        return mates + [self.next_row(), self.prior_row()]


def greet(mates):
    barrier = pltpu.get_barrier_semaphore()
    for mate in mates:
        pl.semaphore_signal(barrier, inc=1, device_id=mate, device_id_type=MESH)
    pl.semaphore_wait(barrier, len(mates))


class Copies:
    def __init__(self, sems):
        self.sems, self.made = sems, {}

    def remote(self, name, src, dst, mate):
        k = len(self.made)

        def make():
            return pltpu.make_async_remote_copy(
                src_ref=src(),
                dst_ref=dst(),
                send_sem=self.sems.at[0, k],
                recv_sem=self.sems.at[1, k],
                device_id=mate(),
                device_id_type=MESH,
            )

        assert name not in self.made
        self.made[name] = make

    def local(self, name, src, dst):
        k = len(self.made)

        def make():
            return pltpu.make_async_copy(src(), dst(), self.sems.at[0, k])

        assert name not in self.made
        self.made[name] = make

    def start(self, *names):
        for name in names:
            self.made[name]().start()

    def wait(self, *names):
        for name in names:
            self.made[name]().wait()

    def wait_recv(self, *names):
        for name in names:
            self.made[name]().wait_recv()

    def wait_send(self, *names):
        for name in names:
            self.made[name]().wait_send()


def rows_at(at, count):
    return pl.ds(pl.multiple_of(at, 16), count)


def blockwise(rows, body):
    step = next(s for s in (48, 32, 16) if rows % s == 0)

    def one(i, carry):
        body(i * step, step)
        return carry

    lax.fori_loop(0, rows // step, one, 0)


PAIRS, QUARTERS, PAIRS_Z = range(3)


class Sum:
    def __init__(self, place, copies, name, mode, way, src, first, rows, cols, bufs, out):
        self.p, self.c, self.name, self.mode, self.way = place, copies, name, mode, way
        bits = [(place.y, place.y_mate), (lax.rem(place.z, 2), lambda: place.z_pair(1))]
        (self.one, self.one_mate), (self.two, self.two_mate) = bits[::-1] if way == PAIRS_Z else bits
        self.src, self.first, self.rows, self.cols, self.out = src, first, rows, cols, out
        bufs = list(bufs)
        self.own, self.ry, self.rz, self.res, self.rf = bufs[:5]
        self.rc = bufs[5] if mode in "xy" else None
        self.rx = bufs[-1] if mode not in ("share", "ready") else None
        self.mine = (lambda: self.own.at[self.p.chip]) if mode in "xy" else (lambda: self.own.at[0])
        self.define()

    @staticmethod
    def scratch(mode, way, rows, cols, n):
        def v(*s):
            return pltpu.VMEM(s, BF16)

        half, spot = rows // 2, rows // (8 if way == QUARTERS else 4)
        out = [v(2 if mode in "xy" else 1, rows, cols), v(2 if mode == "y" else 1, half, cols)]
        out += [v(3 if way == QUARTERS else 2, spot, cols), v(rows, cols), v(n // 8 if n > 8 else 1, spot if n > 8 else 16, cols)]
        if mode in "xy":
            out.append(v(2, rows, cols))
        if mode not in ("share", "ready"):
            out.append(v(rows if mode == "x" else half, cols))
        return out

    def id(self, what):
        return (self.name, what)

    def at_half(self, one):
        return rows_at(one * (self.rows // 2), self.rows // 2)

    def at_spot(self):
        p, half = self.p, self.rows // 2
        if self.way == QUARTERS:
            return rows_at(p.y * half + p.z * (half // 4), half // 4)
        return rows_at(self.one * half + self.two * (half // 2), half // 2)

    def define(self):
        p, c, half, far = self.p, self.c, self.rows // 2, self.p.n // 8
        if self.mode in "xy":
            first = pl.ds(self.first, self.rows)
            for order in (1, 0):
                chip = lambda order=order: lax.rem(p.chip + order, 2)
                c.remote(
                    self.id(("core", order)),
                    lambda chip=chip: self.src.at[2 * chip() + 1 - p.core, first],
                    lambda chip=chip: self.rc.at[chip()],
                    p.core_mate,
                )
                c.local(
                    self.id(("own", order)),
                    lambda chip=chip: self.src.at[2 * chip() + p.core, first],
                    lambda chip=chip: self.own.at[chip()],
                )
        other = lambda: self.own.at[1 - p.chip]
        if self.mode == "x":
            c.remote(self.id("x"), other, lambda: self.rx, p.chip_mate)
        if self.mode == "y":
            c.remote(self.id("y1"), lambda: other().at[self.at_half(1 - self.one)], lambda: self.ry.at[1], self.one_mate)
            c.remote(self.id("x"), lambda: other().at[self.at_half(self.one)], lambda: self.rx, p.chip_mate)
        if self.mode == "ready":
            c.local(self.id("own"), lambda: self.src, lambda: self.own.at[0, self.at_half(self.one)])
        if self.mode == "half":
            c.remote(self.id("x"), lambda: self.src.at[1 - p.chip], lambda: self.rx, p.chip_mate)
            c.local(self.id("own"), lambda: self.src.at[p.chip], lambda: self.own.at[0, self.at_half(self.one)])
        elif self.mode != "ready":
            c.remote(self.id("y"), lambda: self.mine().at[self.at_half(1 - self.one)], lambda: self.ry.at[0], self.one_mate)
        spot = lambda: self.res.at[self.at_spot()]
        if self.way == QUARTERS:
            for d in (2, 1, 3):
                c.remote(
                    self.id(("z", d)),
                    lambda d=d: self.mine().at[rows_at(p.y * half + p.z_of(d) * (half // 4), half // 4)],
                    lambda d=d: self.rz.at[3 - d],
                    lambda d=d: p.z_mate(d),
                )
                c.remote(self.id(("bz", d)), spot, spot, lambda d=d: p.z_mate(d))
        else:
            away = lambda: rows_at(self.one * half + (1 - self.two) * (half // 2), half // 2)
            c.remote(self.id("z1"), lambda: self.mine().at[away()], lambda: self.rz.at[0], self.two_mate)
            c.remote(self.id("z2"), lambda: self.mine().at[self.at_spot()], lambda: self.rz.at[1], lambda: p.z_pair(2))
            c.remote(self.id("bz1"), spot, spot, self.two_mate)
        for d in range(1, far):
            c.remote(self.id(("far", d)), lambda: self.rf.at[p.far], lambda: self.rf.at[p.far], lambda d=d: p.far_mate(d))
        my_half = lambda: self.res.at[self.at_half(self.one)]
        c.remote(self.id("by"), my_half, my_half, self.one_mate)
        for k, (src, dst) in enumerate(self.out):
            c.local(self.id(("out", k)), lambda src=src: self.res.at[src], lambda dst=dst: dst)

    def add(self, dst, at, rows, *others):
        def body(first, step):
            here = rows_at(at + first, step)
            total = dst[here, :].astype(F32)
            for other, offset in others:
                total = total + other[rows_at(offset + first, step), :].astype(F32)
            dst[here, :] = total.astype(BF16)

        blockwise(rows, body)

    def p0(self):
        if self.mode == "half":
            self.c.start(self.id("x"), self.id("own"))
        if self.mode == "ready":
            self.c.start(self.id("own"))
        if self.mode in "xy":
            for order in (1, 0):
                self.c.start(self.id(("core", order)), self.id(("own", order)))

    def p1(self):
        self.c.wait(self.id(("core", 1)), self.id(("own", 1)))
        other = 1 - self.p.chip
        self.add(self.own.at[other], 0, self.rows, (self.rc.at[other], 0))
        self.c.start(self.id("x" if self.mode == "x" else "y1"))

    def p1b(self):
        self.c.wait(self.id(("core", 0)), self.id(("own", 0)))
        self.add(self.mine(), 0, self.rows, (self.rc.at[self.p.chip], 0))
        if self.mode == "y":
            self.c.start(self.id("y"))

    def p2(self):
        half = self.rows // 2
        if self.mode == "y":
            self.c.wait(self.id("y1"))
            self.add(self.own.at[1 - self.p.chip], self.one * half, half, (self.ry.at[1], 0))
            self.c.start(self.id("x"))
            return
        if self.mode == "x":
            self.c.wait(self.id("x"))
            self.add(self.mine(), (1 - self.one) * half, half, (self.rx, (1 - self.one) * half))
        self.c.start(self.id("y"))

    def p3(self):
        half, more = self.rows // 2, []
        if self.mode not in ("half", "ready"):
            self.c.wait(self.id("y"))
            more.append((self.ry.at[0], 0))
        if self.mode == "x":
            more.append((self.rx, self.one * half))
        if self.mode in ("y", "half"):
            self.c.wait(self.id("x"))
            more.append((self.rx, 0))
        if self.mode in ("half", "ready"):
            self.c.wait(self.id("own"))
        self.add(self.mine(), self.one * half, half, *more)
        self.c.start(*([self.id(("z", d)) for d in (2, 1, 3)] if self.way == QUARTERS else [self.id("z1")]))

    def total(self, *others):
        p = self.p
        spot, rows = self.at_spot(), self.at_spot().size
        own, far = self.mine(), p.n // 8

        def body(first, step):
            here = rows_at(spot.start + first, step)
            there = rows_at(first, step)
            total = own[here, :].astype(F32)
            for other in others:
                total = total + other[there, :].astype(F32)
            if far > 1:
                self.rf[p.far, there, :] = total.astype(BF16)
            else:
                self.res[here, :] = total.astype(BF16)

        blockwise(rows, body)
        if far > 1:
            self.c.start(*[self.id(("far", d)) for d in range(1, far)])
            self.c.wait(*[self.id(("far", d)) for d in range(1, far)])

            def more(first, step):
                there = rows_at(first, step)
                total = self.rf[0, there, :].astype(F32)
                for k in range(1, far):
                    total = total + self.rf[k, there, :].astype(F32)
                self.res[rows_at(spot.start + first, step), :] = total.astype(BF16)

            blockwise(rows, more)

    def p4(self):
        if self.way == QUARTERS:
            self.c.wait(*[self.id(("z", d)) for d in (1, 2, 3)])
            self.total(*[self.rz.at[d] for d in range(3)])
            self.c.start(*[self.id(("bz", d)) for d in (2, 1, 3)])
            return
        self.c.wait(self.id("z1"))
        spot = self.at_spot()
        self.add(self.mine(), spot.start, spot.size, (self.rz.at[0], 0))
        self.c.start(self.id("z2"))

    def p4b(self):
        if not self.way == QUARTERS:
            self.c.wait(self.id("z2"))
            self.total(self.rz.at[1])
            self.c.start(self.id("bz1"))

    def p5(self):
        self.c.wait(*([self.id(("bz", d)) for d in (1, 2, 3)] if self.way == QUARTERS else [self.id("bz1")]))
        self.c.start(self.id("by"))

    def p6(self):
        self.c.wait(self.id("by"))
        self.c.start(*[self.id(("out", k)) for k in range(len(self.out))])

    def p7(self):
        self.c.wait(*[self.id(("out", k)) for k in range(len(self.out))])

    def phase(self, k):
        (self.p0, self.p1, self.p1b, self.p2, self.p3, self.p4, self.p4b, self.p5, self.p6)[k]()


PRIOR_KV = (("pk", 0), ("pk", 1), ("pv", 0), ("pv", 1))


def fore_kernel(n, tok, blocks, heads, *refs):
    x, gain, docs, w, cot, w_down = refs[:6]
    attT_o, hT_o, kT_o, qT_o, oT_o, lse_o, start_o, k_o, v_o, wm_o, gg_o, g2_o = refs[6:18]
    xs, ws, wm, hT, docs_all, prior_docs, start, kT, vT, qT, kk, vv, acc, m_ref, l_ref, lse, stage, cs, wd, gg, g2, sems = refs[18:]
    width = xs.shape[0] + 1
    row = blocks * tok
    mine = heads * HD
    p = Place(n)
    c = Copies(sems)
    mates = {"core": p.core_mate, "chip": p.chip_mate, "cross": p.cross_mate}
    block = lambda at: pl.ds(pl.multiple_of(at * tok, tok), tok)
    here = lambda: block(p.s)
    c.local("w", lambda: w, lambda: ws)
    c.local("cot", lambda: cot.at[:, 0, :], lambda: cs)
    c.local("wd", lambda: w_down, lambda: wd)
    c.local("gg", lambda: gg, lambda: gg_o)
    c.local("g2", lambda: g2, lambda: g2_o)
    c.local("docs", lambda: docs, lambda: docs_all.at[:, here()])
    for name, mate in mates.items():
        c.remote(("docs", name), lambda: docs, lambda: docs_all.at[:, here()], mate)
    last = pl.ds(row - tok, tok)
    c.remote("old docs", lambda: docs_all.at[:, last], lambda: prior_docs, p.next_row)
    c.remote("hc", lambda: hT.at[:, here()], lambda: hT.at[:, here()], p.core_mate)
    half = tok // 2
    for k in range(2):
        c.local(("x", k), lambda k=k: x.at[:, 0, pl.ds(k * half, half)], lambda k=k: xs.at[:, pl.ds(k * half, half)])
        piece = lambda s, k=k: hT.at[:, pl.ds(pl.multiple_of(s * tok + k * half, half), half)]
        c.remote(("hx", k), lambda piece=piece: piece(p.s), lambda piece=piece: piece(p.s), p.chip_mate)
        other = lambda piece=piece: piece(p.chip_mate()[0])
        c.remote(("ho", k), other, other, p.core_mate)
    for k in range(2):
        end, to = pl.ds(row + k * half, half), pl.ds(k * half, half)
        c.remote(("pk", k), lambda end=end: kT.at[:, end], lambda to=to: kT.at[:, to], p.next_row)
        c.remote(("pv", k), lambda end=end: vT.at[:, end], lambda to=to: vT.at[:, to], p.next_row)
    for h in range(heads):
        spot = lambda h=h: attT_o.at[pl.ds(pl.multiple_of(p.s * mine + h * HD, HD), HD)]
        for name, mate in mates.items():
            src = lambda h=h, mate=mate: stage.at[pl.ds(h * HD, HD), block(mate()[0])]
            c.remote(("att", h, name), src, spot, mate)
        c.local(("att", h, "own"), lambda h=h: stage.at[pl.ds(h * HD, HD), here()], spot)
    outs = {"hT": (hT, hT_o), "kT": (kT, kT_o), "qT": (qT, qT_o), "oT": (acc, oT_o), "lse": (lse, lse_o)}
    outs.update({"start": (start, start_o), "k": (kk, k_o), "v": (vv, v_o), "wm": (wm, wm_o)})
    for name, (src, dst) in outs.items():
        c.local(("out", name), lambda src=src: src, lambda dst=dst: dst)

    c.start(("x", 0), ("x", 1), "docs", "w")
    greet([p.core_mate(), p.chip_mate(), p.cross_mate(), p.next_row(), p.prior_row()])
    c.start(*[("docs", name) for name in mates])
    gain_col = column(gain)
    for k in range(2):
        c.wait(("x", k))
        full_vec = expand(xs[:, k * half : (k + 1) * half])
        mine_now = pl.ds(pl.multiple_of(p.s * tok + k * half, half), half)
        hT[:, mine_now] = (gain_col * full_vec * root(full_vec)).astype(BF16)
        c.start(("hx", k))
    c.start("hc", "cot", "wd")

    c.wait("w")
    for s in range(blocks):
        @pl.when(p.s == s)
        def _():
            for h in range(heads):
                for k in range(3):
                    at = k * width + s * mine + h * HD
                    to = (h * 3 + k) * HD
                    wm[:, to : to + HD] = ws[:, at : at + HD]

    c.wait("docs", *[("docs", name) for name in mates])
    c.start("old docs")
    ids = jnp.broadcast_to(docs_all[...], (8, row))
    pos = lax.broadcasted_iota(jnp.int32, (8, row), 1)
    since = jnp.where((ids != pltpu.roll(ids, 1, 1)) | (pos == 0), pos, 0)
    hop = 1
    while hop < row:
        since = jnp.maximum(since, jnp.where(pos >= hop, pltpu.roll(since, hop, 1), 0))
        hop *= 2
    start[...] = since[0:1] + tok
    m_ref[...] = jnp.full(m_ref.shape, NEG, F32)
    l_ref[...] = jnp.zeros(l_ref.shape, F32)
    acc[...] = jnp.zeros(acc.shape, F32)

    def natural(keys_at, count):
        keys = pl.ds(pl.multiple_of(keys_at, 128), count)
        for h in range(heads):
            kk[h, keys, :] = kT[h * HD : (h + 1) * HD, keys].T
            vv[h, keys, :] = vT[h * HD : (h + 1) * HD, keys].T

    def project(at, count):
        own, keys = pl.ds(pl.multiple_of(at, 128), count), pl.ds(pl.multiple_of(at + tok, 128), count)
        packed = dot_tn(wm[...], hT[:, own]).astype(BF16)
        for h in range(heads):
            to, base = slice(h * HD, (h + 1) * HD), h * 3 * HD
            qT[to, own] = packed[base : base + HD] * jnp.bfloat16(1.0 / math.sqrt(HD))
            kT[to, keys] = packed[base + HD : base + 2 * HD]
            vT[to, keys] = packed[base + 2 * HD : base + 3 * HD]
        natural(at + tok, count)

    def pair(h, q0, qw, k0, kw, causal):
        hr = pl.ds(pl.multiple_of(h * HD, HD), HD)
        qs, ks = pl.ds(pl.multiple_of(q0, 128), qw), pl.ds(pl.multiple_of(k0 + tok, 128), kw)
        s = dot(kk[h, ks, :], qT[hr, qs])
        at = lax.broadcasted_iota(jnp.int32, s.shape, 0)
        keep = at >= start[:, qs] - (k0 + tok)
        if causal:
            keep = keep & (at <= lax.broadcasted_iota(jnp.int32, s.shape, 1))
        s = jnp.where(keep, s, NEG)
        m = m_ref[h, :, qs]
        new_m = jnp.maximum(m, jnp.max(s, axis=0, keepdims=True))
        e = jnp.exp(s - new_m)
        shift = jnp.exp(m - new_m)
        m_ref[h, :, qs] = new_m
        l_ref[h, :, qs] = l_ref[h, :, qs] * shift + jnp.sum(e, axis=0, keepdims=True)
        acc[hr, qs] = acc[hr, qs] * shift + dot(vT[hr, ks], e.astype(BF16))

    def finish(h, i):
        hr, qs = pl.ds(pl.multiple_of(h * HD, HD), HD), block(i)
        out = acc[hr, qs] / l_ref[h, :, qs]
        acc[hr, qs] = out
        stage[hr, qs] = out.astype(BF16)
        lse[h, :, qs] = m_ref[h, :, qs] + jnp.log(l_ref[h, :, qs])

    def send_att(h, zero):
        for name, mate in list(mates.items()) + [("own", lambda: (p.s,))]:
            @pl.when((mate()[0] == 0) == zero)
            def _():
                c.start(("att", h, name))

    pair_rows = 2 * tok
    near, far = pair_rows * p.chip, pair_rows * (1 - p.chip)
    c.wait_recv("hc")
    lax.fori_loop(0, 2, lambda t, carry: (project(near + t * tok, tok), carry)[1], 0)

    def send_prior(k):
        c.start(("pk", k), ("pv", k))

    @pl.when(p.chip == 1)
    def _():
        send_prior(0)
        send_prior(1)

    lax.fori_loop(0, heads, lambda h, carry: (pair(h, near, pair_rows, near, pair_rows, True), carry)[1], 0)

    def far_half(k):
        c.wait_recv(("hx", k))
        c.start(("ho", k))
        project(p.chip_mate()[0] * tok + k * half, half)
        c.wait_recv(("ho", k))
        project(p.cross_mate()[0] * tok + k * half, half)

        def queries(t, carry):
            pair(t // 2, pair_rows + t % 2 * tok + k * half, half, 0, pair_rows, False)
            return carry

        def keys(t, carry):
            pair(t // 2, pair_rows, pair_rows, t % 2 * tok + k * half, half, False)
            return carry

        @pl.when(p.chip == 0)
        def _():
            send_prior(k)
            lax.fori_loop(0, 2 * heads, queries, 0)

        @pl.when(p.chip == 1)
        def _():
            lax.fori_loop(0, 2 * heads, keys, 0)

    c.wait("cot", "wd")
    g2[...] = shrink_back(cs[...]).astype(BF16)
    c.start("g2")

    def grad_gelu(t, carry):
        its = pl.ds(pl.multiple_of(t * width, width), width)
        gg[its, :] = dot(wd[its, :], g2[...]).astype(BF16)
        return carry

    lax.fori_loop(0, wd.shape[0] // width, grad_gelu, 0)
    c.start("gg")
    far_half(0)
    far_half(1)

    def second(h, carry):
        pair(h, far, pair_rows, far, pair_rows, True)
        lax.fori_loop(1, blocks, lambda i, carry: (finish(h, i), carry)[1], 0)
        for k in range(heads):
            @pl.when(h == k)
            def _():
                send_att(k, False)
        return carry

    lax.fori_loop(0, heads, second, 0)
    c.wait_recv("old docs")
    from_doc = docs_all[:, 0:1]
    at = lax.broadcasted_iota(jnp.int32, (1, tok), 1)
    run = jnp.max(jnp.where(prior_docs[...] != from_doc, at + 1, 0), axis=1, keepdims=True)
    start[:, 0:tok] = jnp.where(start[:, 0:tok] == tok, run, start[:, 0:tok])
    c.wait_recv(*PRIOR_KV)
    natural(0, tok)

    def third(h, carry):
        pair(h, 0, tok, -tok, tok, False)
        finish(h, 0)
        for k in range(heads):
            @pl.when(h == k)
            def _():
                send_att(k, True)
        return carry

    lax.fori_loop(0, heads, third, 0)
    c.start(*[("out", name) for name in outs])
    c.wait_send("hc", ("hx", 0), ("hx", 1), ("ho", 0), ("ho", 1), "old docs", *PRIOR_KV)
    for h in range(heads):
        c.wait(*[("att", h, name) for name in list(mates) + ["own"]])
    c.wait("gg", "g2", *[("out", name) for name in outs])


def fore_pass(n, tok, blocks, x, gain, docs, w, cot, w_down):
    width, heads = w.shape[0], H // blocks
    row, mine = blocks * tok, heads * HD
    v = lambda *s, t=BF16: pltpu.VMEM(s, t)
    o = lambda *s, t=BF16: jax.ShapeDtypeStruct(s, t)
    hbm = pl.BlockSpec(memory_space=pl.ANY)
    scratch = [
        v(width - 1, tok, t=F32), v(width, 3 * width), v(width, 3 * mine), v(width, row),
        v(1, row, t=jnp.int32), v(1, tok, t=jnp.int32), v(1, row, t=jnp.int32),
        v(mine, row + tok), v(mine, row + tok), v(mine, row), v(heads, row + tok, HD), v(heads, row + tok, HD),
        v(mine, row, t=F32), v(heads, 1, row, t=F32), v(heads, 1, row, t=F32), v(heads, 1, row, t=F32), v(mine, row),
        v(width - 1, tok, t=F32), v(*w_down.shape), v(w_down.shape[0], tok), v(width, tok),
        pltpu.SemaphoreType.DMA((2, 31 + 4 * heads)),
    ]
    return pl.pallas_call(
        functools.partial(fore_kernel, n, tok, blocks, heads),
        out_shape=[
            o(width, tok), o(width, row), o(mine, row + tok), o(mine, row), o(mine, row, t=F32), o(heads, 1, row, t=F32),
            o(1, row, t=jnp.int32), o(heads, row + tok, HD), o(heads, row + tok, HD), o(width, 3 * mine),
            o(w_down.shape[0], tok), o(width, tok),
        ],
        in_specs=[hbm, pl.BlockSpec(memory_space=pltpu.VMEM)] + [hbm] * 4,
        out_specs=[hbm] * 12,
        scratch_shapes=scratch,
        compiler_params=pltpu.CompilerParams(collective_id=0, has_side_effects=True, vmem_limit_bytes=VMEM_LIMIT),
    )(x, gain, docs, w, cot, w_down)


def gelu_both(v, grad):
    rate = math.sqrt(2.0 / math.pi)
    square = v * v
    th = jnp.tanh(rate * v * (1.0 + 0.044715 * square))
    up = 0.5 * (1.0 + th)
    slope = up + 0.5 * v * (1.0 - th * th) * (rate * (1.0 + 3.0 * 0.044715 * square))
    return (v * up).astype(BF16), (grad * slope).astype(BF16)


def mid_kernel(n, blocks, *refs):
    x, cot, attT, gain, w_out, w_up, w_down, gg_in, g2_in = refs[:9]
    new_o, gm_o, doT_o, gu_o, go_o, half_o, ready_o = refs[9:16]
    xs, cs, at, wo, wu, wd, mid, h2, g2, g1, gg, geluT, gupT, dw, rc, ry, rx, ga, gu, go, sems = refs[16:]
    tok, width = xs.shape[1], xs.shape[0] + 1
    parts = wu.shape[1] // width
    share = width // blocks
    p = Place(n)
    c = Copies(sems)
    mates = {"cross": p.cross_mate, "chip": p.chip_mate, "core": p.core_mate}
    c.local("att", lambda: attT, lambda: at)
    c.local("wo", lambda: w_out, lambda: wo)
    c.local("x", lambda: x.at[:, 0, :], lambda: xs)
    c.local("cot", lambda: cot.at[:, 0, :], lambda: cs)
    c.local("wu", lambda: w_up, lambda: wu)
    c.local("wd", lambda: w_down, lambda: wd)
    c.local("gg", lambda: gg_in, lambda: gg)
    c.local("g2", lambda: g2_in, lambda: g2)
    c.remote(("core", 0), lambda: dw.at[0], lambda: rc.at[0], p.core_mate)
    c.remote(("core", 1), lambda: dw.at[2], lambda: rc.at[1], p.core_mate)
    part = width // 2
    fourth = part // 2
    low = lambda y: rows_at(y * fourth, fourth)
    for t in range(2):
        c.remote(("y", t), lambda t=t: dw.at[2 * t + 1, low(1 - p.y)], lambda t=t: ry.at[t], p.y_mate)
        dst = lambda t=t: half_o.at[1 - p.chip if t == 0 else p.chip]
        c.local(("half", t), lambda t=t: dw.at[2 * t + 1, low(p.y)], dst)
    high = pl.ds(part, part)
    c.remote("chip", lambda: dw.at[1, high], lambda: rx, p.chip_mate)
    later = lambda y: rows_at(part + y * fourth, fourth)
    c.remote(("y", 2), lambda: dw.at[3, later(1 - p.y)], lambda: ry.at[2], p.y_mate)
    c.local("ready", lambda: dw.at[3, later(p.y)], lambda: ready_o)
    there = lambda: doT_o.at[:, pl.ds(pl.multiple_of(p.s * tok, tok), tok)]
    for name, mate in mates.items():
        c.remote(("ga", name), lambda mate=mate: ga.at[rows_at(mate()[0] * share, share)], there, mate)
    c.local(("ga", "own"), lambda: ga.at[rows_at(p.s * share, share)], there)
    c.local("new", lambda: xs, lambda: new_o.at[:, 0, :])
    c.local("gm", lambda: cs, lambda: gm_o)
    for k in range(parts):
        c.local(("gu", k), lambda k=k: gu.at[:, pl.ds(k * share, share)], lambda k=k: gu_o.at[:, pl.ds(k * share, share)])
    c.local("go", lambda: go, lambda: go_o)

    c.start("att", "wo", "x", "wu", "gg", "g2", "cot", "wd")
    greet([p.core_mate(), p.chip_mate(), p.cross_mate(), p.y_mate()])
    c.wait("att", "wo")
    branch_one = dot_tn(wo[...], at[...])
    c.wait("x")
    mid[...] = xs[...] + shrink(branch_one)
    full_vec = expand(mid[...])
    gain_col = column(gain)
    h2[...] = (gain_col * full_vec * root(full_vec)).astype(BF16)
    c.wait("wu", "gg", "g2")

    def add(dst, at, src, rows):
        def body(first, step):
            r = rows_at(at + first, step)
            dw[dst, r, :] = (dw[dst, r, :].astype(F32) + src[rows_at(first, step), :].astype(F32)).astype(BF16)

        blockwise(rows, body)

    def chip_sum(t):
        c.wait_recv(("core", t))
        add(2 * t + 1, 0, rc.at[t], width)
        c.start(("y", t), *(["chip"] if t == 0 else []))

    def y_sum(t):
        c.wait(("y", t))
        add(2 * t + 1, p.y * fourth, ry.at[t], fourth)
        c.start(("half", t))

    def piece(t, carry):
        s = jnp.where(t == 0, p.cross_mate()[0], jnp.where(t == 1, p.chip_mate()[0], jnp.where(t == 2, p.core_mate()[0], p.s)))
        its = pl.ds(pl.multiple_of(s * width, width), width)
        gelu, grad_up = gelu_both(dot_tn(wu[:, its], h2[...]), gg[its, :].astype(F32))
        geluT[its, :] = gelu
        gupT[its, :] = grad_up
        dw[t] = dot_nt(geluT[its, :], g2[...]).astype(BF16)

        @pl.when(t == 0)
        def _():
            c.start(("core", 0))

        @pl.when(t == 2)
        def _():
            c.start(("core", 1))

        @pl.when(t == 1)
        def _():
            chip_sum(0)

        return carry

    lax.fori_loop(0, parts, piece, 0)
    chip_sum(1)
    grad_h = dot(wu[...], gupT[...])
    c.wait("cot")
    grad_middle = cs[...] + norm_back(mid[...], gain_col, grad_h)
    cs[...] = grad_middle
    g1[...] = shrink_back(grad_middle).astype(BF16)
    ga[...] = dot(wo[...], g1[...]).astype(BF16)
    c.start(*[("ga", name) for name in list(mates) + ["own"]])
    c.start("gm")
    def up_grad(k, carry):
        its = pl.ds(pl.multiple_of(k * width, width), width)
        grad = dot_nt(h2[...], gupT[its, :]).astype(BF16)
        for s in range(blocks):
            gu[s, rows_at(k * share, share), :] = grad[s * share : (s + 1) * share]
        return carry

    lax.fori_loop(0, parts // 2, up_grad, 0)
    c.wait("chip")
    add(3, part, rx, part)
    c.start(("y", 2))
    lax.fori_loop(parts // 2, parts, up_grad, 0)
    c.start(*[("gu", k) for k in range(parts)])
    out_grad = dot_nt(at[...], g1[...]).astype(BF16)
    for s in range(blocks):
        for k in range(2):
            go[s, k * share : (k + 1) * share, :] = out_grad[s * share : (s + 1) * share, k * part : (k + 1) * part]
    c.start("go")
    c.wait("wd")
    xs[...] = mid[...] + shrink(dot_tn(wd[...], geluT[...]))
    c.start("new")
    y_sum(0)
    y_sum(1)
    c.wait(("y", 2))
    add(3, part + p.y * fourth, ry.at[2], fourth)
    c.start("ready")
    c.wait_send(("core", 0), ("core", 1))
    c.wait(*[("ga", name) for name in list(mates) + ["own"]])
    c.wait("gm", "new", "go", "ready", ("half", 0), ("half", 1), *[("gu", k) for k in range(parts)])


def mid_pass(n, blocks, x, cot, attT, gain, w_out, w_up, w_down, gg, g2):
    width, tok = attT.shape
    parts, share = w_up.shape[1] // width, width // blocks
    v = lambda *s, t=BF16: pltpu.VMEM(s, t)
    o = lambda *s, t=BF16: jax.ShapeDtypeStruct(s, t)
    hbm = pl.BlockSpec(memory_space=pl.ANY)
    scratch = [
        v(width - 1, tok, t=F32), v(width - 1, tok, t=F32), v(width, tok), v(width, width), v(*w_up.shape), v(*w_down.shape),
        v(width - 1, tok, t=F32), v(width, tok), v(width, tok), v(width, tok), v(*gg.shape), v(*gg.shape), v(*gg.shape), v(4, width, width), v(2, width, width), v(3, width // 4, width), v(width // 2, width),
        v(width, tok), v(blocks, parts * share, width), v(blocks, 2 * share, width // 2),
        pltpu.SemaphoreType.DMA((2, 32)),
    ]
    return pl.pallas_call(
        functools.partial(mid_kernel, n, blocks),
        out_shape=[
            o(width - 1, 1, tok, t=F32), o(width - 1, tok, t=F32), o(share, blocks * tok), o(blocks, parts * share, width),
            o(blocks, 2 * share, width // 2), o(2, width // 4, width), o(width // 4, width),
        ],
        in_specs=[hbm] * 3 + [pl.BlockSpec(memory_space=pltpu.VMEM)] + [hbm] * 5,
        out_specs=[hbm] * 7,
        scratch_shapes=scratch,
        compiler_params=pltpu.CompilerParams(collective_id=2, has_side_effects=True, vmem_limit_bytes=VMEM_LIMIT),
    )(x, cot, attT, gain, w_out, w_up, w_down, gg, g2)


BACK_IN = ("doT", "k", "v", "kT", "qT", "oT", "lse", "start", "hT", "wm", "x", "gm")
DW = ("cross", "chip", "core", "own")
D0, D1, U0, U1, O, Q0, Q1, GRAD_H, SEND = range(9)
Q_HEADS = ((0, 1), (2,))
U_MODES = ("x", "x")
O_MODE = "y"
WAYS = (PAIRS, PAIRS, PAIRS, PAIRS, PAIRS, PAIRS_Z, PAIRS)
START, READY, PRIOR, FULL, DIAGONAL, CLOSE, END = range(7)
PLAN = {
    START: {
        (): [(D0, 0), (U1, 0), (U0, 0), (D1, 0), (O, 0)],
    },
    READY: {
        (): [(U1, 1), (D1, 4)],
    },
    PRIOR: {
        (0,): [(U1, 2)],
        (1,): [(U0, 1), (U0, 2)],
        (2,): [(D0, 4), (D1, 5), (O, 1), (O, 2)],
    },
    FULL: {
        (1, 0): [(D0, 5), (U1, 3), (O, 3)],
        (2, 1): [(D0, 6), (U0, 3), (D1, 7)],
        (2, 4): [(U1, 5), (O, 4)],
    },
    DIAGONAL: {
        (1, 0): [(D1, 6)],
        (2, 1): [(D0, 7)],
    },
    CLOSE: {
        (1,): [(U1, 4), (SEND, 0)],
        (2,): [(Q0, 3), (SEND, 1), (GRAD_H, 0), (U0, 4), (GRAD_H, 1), (GRAD_H, 2), (O, 5), (U1, 6)],
    },
    END: {
        (): [(GRAD_H, 3), (Q1, 3), (D1, 8), (GRAD_H, 4), (GRAD_H, 5), (Q0, 4), (U0, 5), (D0, 8),
            (O, 6), (Q1, 4), (U1, 7), (Q0, 5), (O, 7), (U0, 6), (Q1, 5), (GRAD_H, 6),
            (U1, 8), (O, 8), (Q0, 6), (U0, 7), (Q1, 6), (Q0, 7), (Q1, 7), (U0, 8),
            (Q0, 8), (Q1, 8)],
    },
}


def folds(cols):
    return 2 if cols % 128 else 1


def back_sums(n, width, share, part):
    way = lambda k: QUARTERS if n > 8 else WAYS[k]
    half = [(D0 + k, ("half", "ready")[k], way(D0 + k), k, 0, part, width) for k in range(2)]
    up = [(U0 + k, U_MODES[k], way(U0 + k), 0, k * part, part, width) for k in range(2)]
    sums = half + up + [(O, O_MODE, way(O), 1, 0, 2 * share, part)]
    for k, hs in enumerate(Q_HEADS):
        cols = share * len(hs)
        sums.append((Q0 + k, "share", way(Q0 + k), None, 0, width // folds(cols), cols * folds(cols)))
    return sums


def back_kernel(n, tok, blocks, heads, parts, *refs):
    refs = list(refs)
    take = lambda count: [refs.pop(0) for _ in range(count)]
    hbm = dict(zip(BACK_IN, take(len(BACK_IN))))
    down_half, down_ready, gu, go, gain_one = take(5)
    down_o, up_o, out_o, rg_o = take(4)
    qkv_o = take(len(Q_HEADS))
    vm = dict(zip(BACK_IN, take(len(BACK_IN))))
    dkT, dvT, delta, dP, prior_out, prior_in, g_stage, g_core, g_x, g_acc = take(10)
    dws = take(len(Q_HEADS))
    p, hd, row = Place(n), HD, blocks * tok
    mine, width = heads * hd, blocks * heads * hd
    share, part = width // blocks, width // 2
    per_part = part // share
    outs = {D0 + k: [(pl.ds(0, part), down_o.at[pl.ds(k * part, part)])] for k in range(2)}
    for k in range(2):
        outs[U0 + k] = [
            (pl.ds(j * share, share), up_o.at[:, pl.ds((k * per_part + j) * width, width)]) for j in range(per_part)
        ]
    outs[O] = [(pl.ds(k * share, share), out_o.at[:, pl.ds(k * part, part)]) for k in range(2)]
    for k in range(len(Q_HEADS)):
        outs[Q0 + k] = [(pl.ds(0, qkv_o[k].shape[0]), qkv_o[k])]
    plans = back_sums(n, width, share, part)
    bufs = [take(len(Sum.scratch(q[1], q[2], 16, 128, n))) for q in plans]
    c = Copies(refs.pop(0))
    for name in BACK_IN:
        src = (lambda: hbm["x"].at[:, 0, :]) if name == "x" else (lambda name=name: hbm[name])
        c.local(name, src, lambda name=name: vm[name])
    sums = {}
    for (name, mode, way, arr, first, rows, cols), buf in zip(plans, bufs):
        src = None if arr is None else ((down_half, down_ready) if name < U0 else (gu, go))[arr]
        sums[name] = Sum(p, c, name, mode, way, src, first, rows, cols, buf, outs[name])
    qkv = [sums[Q0 + k] for k in range(len(Q_HEADS))]
    for k, one in enumerate(qkv):
        count = one.rows // blocks
        block = lambda ref, s, count=count: ref.at[rows_at(s * count, count)]
        spot = lambda one=one, block=block: block(one.own.at[0], p.s)
        for what, mate in (("cross", p.cross_mate), ("chip", p.chip_mate), ("core", p.core_mate)):
            c.remote(("dw", k, what), lambda k=k, mate=mate, block=block: block(dws[k], mate()[0]), spot, mate)
        c.local(("dw", k, "own"), lambda k=k, block=block: block(dws[k], p.s), spot)
    for k in range(heads):
        c.remote(("prior", k), lambda k=k: prior_out.at[k], lambda k=k: prior_in.at[k], p.prior_row)
    for order in (1, 0):
        c.remote(("gh", order), lambda order=order: g_stage.at[order], lambda order=order: g_core.at[order], p.core_mate)
    c.remote(("gh", "x"), lambda: g_stage.at[1], lambda: g_x, p.chip_mate)
    c.local("rg", lambda: vm["gm"], lambda: rg_o.at[:, 0, :])

    def grad_h_part(owner):
        return dot(vm["wm"][...], dP[:, pl.ds(pl.multiple_of(owner * tok, tok), tok)])

    def core_grad(order):
        chip = lax.rem(p.chip + order, 2)
        g_stage[order] = grad_h_part(2 * chip + 1 - p.core).astype(BF16)
        c.start(("gh", order))

    def keep_grad(order):
        chip = lax.rem(p.chip + order, 2)
        g_acc[...] = grad_h_part(2 * chip + p.core)

    def chip_grad():
        c.wait(("gh", 1))
        g_stage[1] = (g_acc[...] + g_core[1].astype(F32)).astype(BF16)
        c.start(("gh", "x"))

    def own_grad():
        c.wait(("gh", 0))
        g_acc[...] += g_core[0].astype(F32)

    def input_grad():
        c.wait("x", "gm", ("gh", "x"))
        vm["gm"][...] += norm_back(vm["x"][...], column(gain_one), g_acc[...] + g_x[...].astype(F32))
        c.start("rg")

    def send_dw(k):
        rows = slice(Q_HEADS[k][0] * 3 * hd, (Q_HEADS[k][-1] + 1) * 3 * hd)
        grad = dot_nt(vm["hT"][...], dP[rows, :]).astype(BF16)
        fold = folds(grad.shape[1])
        count = share // fold
        for s in range(blocks):
            cells = [grad[s * share + f * count : s * share + (f + 1) * count] for f in range(fold)]
            dws[k][s * count : (s + 1) * count, :] = jnp.concatenate(cells, axis=1)
        c.start(*[("dw", k, what) for what in DW])

    special = {GRAD_H: [lambda: core_grad(1), lambda: core_grad(0), lambda: keep_grad(1), chip_grad, lambda: keep_grad(0)]}
    special[GRAD_H] += [own_grad, input_grad]
    special[SEND] = [lambda k=k: send_dw(k) for k in range(len(Q_HEADS))]

    def step(which, phase):
        if which in special:
            special[which][phase]()
            return
        if which >= Q0 and phase == 3:
            c.wait(*[("dw", which - Q0, what) for what in DW])
        sums[which].phase(phase)

    def steps_at(place, *now):
        for at, names in PLAN.get(place, {}).items():
            same = None
            for want, have in zip(at, now):
                same = (have == want) if same is None else same & (have == want)

            def run():
                for which, phase in names:
                    step(which, phase)

            run() if same is None else pl.when(same)(run)

    first = BACK_IN[:8]
    c.start(*first)
    greet(p.all_mates())
    steps_at(START)
    c.start(*BACK_IN[8:])
    c.wait(*first)
    dqT = vm["oT"]
    doT, kk, vv, kT, qT, lse, start = (vm[x] for x in ("doT", "k", "v", "kT", "qT", "lse", "start"))

    def make_delta(h, carry):
        rows = pl.ds(pl.multiple_of(h * hd, hd), hd)
        delta[h] = jnp.sum(doT[rows, :].astype(F32) * vm["oT"][rows, :], axis=0, keepdims=True)
        return carry

    lax.fori_loop(0, heads, make_delta, 0)
    dqT[...] = jnp.zeros_like(dqT)
    dkT[...] = jnp.zeros_like(dkT)
    dvT[...] = jnp.zeros_like(dvT)
    steps_at(READY)

    def pair(h, i, j, causal):
        hr = pl.ds(pl.multiple_of(h * hd, hd), hd)
        qs, ks = (pl.ds(pl.multiple_of(at * tok, tok), tok) for at in (i, j))
        q_blk, do_blk = qT[hr, qs], doT[hr, qs]
        s = dot(kk[h, ks, :], q_blk)
        e = jnp.exp(s - lse[h, :, qs])
        at = lax.broadcasted_iota(jnp.int32, s.shape, 0)
        keep = at >= start[:, qs] - j * tok
        if causal:
            keep = keep & (at <= lax.broadcasted_iota(jnp.int32, s.shape, 1))
        e = jnp.where(keep, e, 0.0)
        dp = dot(vv[h, ks, :], do_blk)
        ds = (e * (dp - delta[h, :, qs])).astype(BF16)
        dvT[hr, ks] += dot_nt(do_blk, e.astype(BF16))
        dkT[hr, ks] += dot_nt(q_blk, ds)
        dqT[hr, qs] += dot(kT[hr, ks], ds)

    def prior(h, carry):
        pair(h, 0, 0, False)
        hr = pl.ds(pl.multiple_of(h * hd, hd), hd)
        prior_out[h, 0:hd, :] = dkT[hr, 0:tok].astype(BF16)
        prior_out[h, hd : 2 * hd, :] = dvT[hr, 0:tok].astype(BF16)
        for k in range(heads):
            @pl.when(h == k)
            def _():
                c.start(("prior", k))
        steps_at(PRIOR, h)
        return carry

    lax.fori_loop(0, heads, prior, 0)

    def close(h):
        hr = pl.ds(pl.multiple_of(h * hd, hd), hd)
        last = pl.ds(row, tok)
        dkT[hr, last] += prior_in[h, 0:hd, :].astype(F32)
        dvT[hr, last] += prior_in[h, hd : 2 * hd, :].astype(F32)
        base = h * 3 * hd
        for k, (src, at) in enumerate(((dqT, 0), (dkT, tok), (dvT, tok))):
            val = src[hr, at:]
            val = val * (1.0 / math.sqrt(hd)) if k == 0 else val
            dP[pl.ds(pl.multiple_of(base + k * hd, hd), hd), :] = val.astype(BF16)

    def head(h, carry):
        def full(t, carry):
            i = jnp.where(t < 3, 3, jnp.where(t < 5, 2, 1))
            j = jnp.where(t < 3, t + 1, jnp.where(t < 5, t - 2, 1))
            pair(h, i, j, False)
            steps_at(FULL, h, t)
            return carry

        lax.fori_loop(0, 6, full, 0)

        def diagonal(i, carry):
            pair(h, i, i + 1, True)
            steps_at(DIAGONAL, h, i)
            return carry

        lax.fori_loop(0, blocks, diagonal, 0)
        for k in range(heads):
            @pl.when(h == k)
            def _():
                if k == 0:
                    c.wait("hT", "wm")
                c.wait(("prior", k))
        close(h)
        steps_at(CLOSE, h)
        return carry

    lax.fori_loop(0, heads, head, 0)
    steps_at(END)

    for one in sums.values():
        one.p7()
    c.wait("rg")


def back_pass(n, tok, blocks, ins, down_half, down_ready, gu, go, gain, parts):
    heads = ins[1].shape[0]
    row = blocks * tok
    width = ins[8].shape[0]
    mine = heads * HD
    share, part = width // blocks, width // 2
    v = lambda *s, t=BF16: pltpu.VMEM(s, t)
    o = lambda *s, t=BF16: jax.ShapeDtypeStruct(s, t)
    scratch = [v(width - 1, tok, t=F32) if name == "x" else pltpu.VMEM(a.shape, a.dtype) for name, a in zip(BACK_IN, ins)]
    scratch += [
        v(mine, row + tok, t=F32), v(mine, row + tok, t=F32), v(heads, 1, row, t=F32), v(3 * mine, row),
        v(heads, 2 * HD, tok), v(heads, 2 * HD, tok),
        v(2, width, tok), v(2, width, tok), v(width, tok), v(width, tok, t=F32),
    ]
    sums = back_sums(n, width, share, part)
    scratch += [v(*one[5:]) for one in sums[Q0:]]
    copies = len(ins) + 5 * heads + 8
    for _, mode, way, _, _, rows, cols in sums:
        scratch += Sum.scratch(mode, way, rows, cols, n)
        copies += 17 + n // 8
    scratch.append(pltpu.SemaphoreType.DMA((2, copies)))
    hbm = pl.BlockSpec(memory_space=pl.ANY)
    vmem = pl.BlockSpec(memory_space=pltpu.VMEM)
    return pl.pallas_call(
        functools.partial(back_kernel, n, tok, blocks, heads, parts),
        out_shape=[o(width, width), o(share, parts * width), o(share, width), o(width - 1, 1, tok, t=F32)]
        + [o(*one[5:]) for one in sums[Q0:]],
        in_specs=[hbm] * (len(ins) + 4) + [vmem],
        out_specs=[hbm] * (4 + len(Q_HEADS)),
        scratch_shapes=scratch,
        compiler_params=pltpu.CompilerParams(collective_id=1, has_side_effects=True, vmem_limit_bytes=VMEM_LIMIT),
    )(*ins, down_half, down_ready, gu, go, gain)


def last_kernel(blocks, *refs):
    new, rg, down, up, out, w_qkv, w_up, gain_one, gain_two = refs[:9]
    q_in = refs[9 : 9 + len(Q_HEADS)]
    refs = refs[9 + len(Q_HEADS) :]
    new_o, rg_o, gain_one_o, gain_two_o, qkv_o, out_o, up_o, down_o = refs[:8]
    down_v, up_v, out_v, wq, wu, gcol, down_f, up_f, out_f, qkv_f, x_v, sems = refs[8:19] + refs[-1:]
    q_v = refs[19:-1]
    s = lax.axis_index("seq")
    share, width = out_v.shape
    mine, hd = width // blocks, HD
    c = Copies(sems)
    my_rows = lambda ref: ref.at[rows_at(s * share, share)]
    loads = list(zip(q_in, q_v)) + [(my_rows(w_qkv), wq), (up, up_v), (down, down_v), (out, out_v), (my_rows(w_up), wu)]
    for k, (src, dst) in enumerate(loads):
        c.local(("in", k), lambda src=src: src, lambda dst=dst: dst)
    for k, (src, dst) in enumerate(((up_f, up_o), (down_f, down_o), (out_f, out_o), (qkv_f, qkv_o))):
        c.local(("out", k), lambda src=src: src, lambda dst=dst: dst)
    for k, (src, dst) in enumerate(((new, new_o), (rg, rg_o))):
        c.local(("x in", k), lambda k=k, src=src: src.at[:, 0, :], lambda k=k: x_v.at[k])
        c.local(("x out", k), lambda k=k: x_v.at[k], lambda k=k, dst=dst: dst.at[:, 0, :])
    at = len(q_in)
    c.start(*[("in", k) for k in range(at + 2)], ("x in", 0), ("x in", 1), *[("in", k) for k in range(at + 2, len(loads))])

    def row_of(col):
        return jnp.broadcast_to(col, (share, 128)).T[0:1, :]

    def my_gain(gain):
        gcol[...] = column(gain)
        return gcol[pl.ds(pl.multiple_of(s * share, share), share), :]

    c.wait(*[("in", k) for k in range(at + 1)])
    total = jnp.zeros((share, 1), F32)
    for k in range(3):
        for o in range(blocks):
            cells = []
            for src, hs in zip(q_v, Q_HEADS):
                fold, cols = folds(share * len(hs)), share * len(hs)
                rows = slice(o * share // fold, (o + 1) * share // fold)
                for h in range(len(hs)):
                    lanes = [f * cols + (h * 3 + k) * hd for f in range(fold)]
                    cells.append(jnp.concatenate([src[rows, lane : lane + hd] for lane in lanes], axis=0))
            cells = jnp.concatenate(cells, axis=1).astype(F32)
            cols = slice(k * width + o * mine, k * width + (o + 1) * mine)
            qkv_f[:, cols] = cells
            total = total + jnp.sum(cells * wq[:, cols].astype(F32), axis=1, keepdims=True)
    c.start(("out", 3))
    for k, (src, dst) in enumerate(((up_v, up_f), (down_v, down_f), (out_v, out_f))):
        c.wait(("in", at + 1 + k))
        dst[...] = src[...].astype(F32)
        c.start(("out", k))
        if k < 2:
            c.wait(("x in", k))
            c.start(("x out", k))
    c.wait(("in", at + 4))
    gain_two_o[...] = row_of(jnp.sum(up_f[...] * wu[...].astype(F32), axis=1, keepdims=True) / my_gain(gain_two))
    gain_one_o[...] = row_of(total / my_gain(gain_one))
    c.wait(("x out", 0), ("x out", 1), *[("out", k) for k in range(4)])


def last_pass(blocks, new, rg, down, up, out, qs, w_qkv, w_up, gain_one, gain_two):
    share, width = out.shape
    v = lambda *s, t=BF16: pltpu.VMEM(s, t)
    f = lambda *s: jax.ShapeDtypeStruct(s, F32)
    hbm = pl.BlockSpec(memory_space=pl.ANY)
    vmem = pl.BlockSpec(memory_space=pltpu.VMEM)
    scratch = [
        v(*down.shape), v(*up.shape), v(*out.shape), v(share, 3 * width), v(*up.shape), v(width, 1, t=F32),
        v(*down.shape, t=F32), v(*up.shape, t=F32), v(*out.shape, t=F32), v(share, 3 * width, t=F32),
        v(2, new.shape[0], new.shape[2], t=F32),
    ]
    scratch += [v(*q.shape) for q in qs] + [pltpu.SemaphoreType.DMA((1, 20))]
    return pl.pallas_call(
        functools.partial(last_kernel, blocks),
        out_shape=[f(*new.shape), f(*rg.shape), f(1, share), f(1, share), f(share, 3 * width), f(*out.shape), f(*up.shape), f(*down.shape)],
        in_specs=[hbm] * 7 + [vmem] * 2 + [hbm] * len(qs),
        out_specs=[hbm, hbm, vmem, vmem] + [hbm] * 4,
        scratch_shapes=scratch,
        compiler_params=pltpu.CompilerParams(vmem_limit_bytes=VMEM_LIMIT),
    )(new, rg, down, up, out, w_qkv, w_up, gain_one, gain_two, *qs)


def per_device(residual, documents, gain_one, gain_two, w_qkv, w_out, w_up, w_down, cotangent):
    blocks = lax.axis_size("seq")
    n = lax.axis_size("batch")
    tok = residual.shape[1]
    x = jnp.transpose(residual, (2, 0, 1))
    cot = jnp.transpose(cotangent, (2, 0, 1))
    attT, hT, kT, qT, oT, lse, start, k, v, w_mine, grad_gelu, grad_two = fore_pass(
        n, tok, blocks, x, gain_one, documents, w_qkv, cot, w_down
    )
    new, grad_middle, doT, grad_up, grad_out, down_half, down_ready = mid_pass(
        n, blocks, x, cot, attT, gain_two, w_out, w_up, w_down, grad_gelu, grad_two
    )
    sum_down, sum_up, sum_out, grad_x, *sum_qkv = back_pass(
        n, tok, blocks, (doT, k, v, kT, qT, oT, lse, start, hT, w_mine, x, grad_middle),
        down_half, down_ready, grad_up, grad_out, gain_one, w_up.shape[1] // w_up.shape[0],
    )
    new, grad_x, one, two, sum_qkv, sum_out, sum_up, sum_down = last_pass(
        blocks, new, grad_x, sum_down, sum_up, sum_out, sum_qkv, w_qkv, w_up, gain_one, gain_two
    )
    new, grad_x = jnp.transpose(new, (1, 2, 0)), jnp.transpose(grad_x, (1, 2, 0))
    return (new, grad_x, one[0], two[0], sum_qkv, sum_out, sum_up, sum_down)


def solution(mesh):
    placed = (
        P("batch", "seq", None),
        P("batch", "seq"),
        P(),
        P(),
        P(),
        P(),
        P(),
        P(),
        P("batch", "seq", None),
    )
    return jax.shard_map(
        per_device,
        mesh=mesh,
        in_specs=placed,
        out_specs=(
            P("batch", "seq", None),
            P("batch", "seq", None),
            P("seq"),
            P("seq"),
            P("seq", None),
            P("seq", None),
            P("seq", None),
            P("seq", None),
        ),
        check_vma=False,
    )
```

```python
import functools
import math

import jax
import jax.numpy as jnp
from jax import lax
from jax.experimental import pallas as pl
from jax.experimental.pallas import tpu as pltpu
from jax.sharding import PartitionSpec as P

H = 12
HD = 64
EPSILON = 1e-06
NEG = -1e30
F32, BF16 = jnp.float32, jnp.bfloat16
VMEM_LIMIT = 62 * 2**20


def dot(a, b):
    return lax.dot_general(a, b, (((1,), (0,)), ((), ())), preferred_element_type=F32)


def dot_nt(a, b):
    return lax.dot_general(a, b, (((1,), (1,)), ((), ())), preferred_element_type=F32)


def dot_tn(a, b):
    return lax.dot_general(a, b, (((0,), (0,)), ((), ())), preferred_element_type=F32)


def expand(narrow):
    return jnp.concatenate([narrow, -jnp.sum(narrow, axis=0, keepdims=True)], axis=0)


def shrink(full_vec):
    return full_vec[:-1] - jnp.mean(full_vec, axis=0, keepdims=True)


def shrink_back(grad_narrow):
    padded = jnp.concatenate([grad_narrow, jnp.zeros_like(grad_narrow[:1])], axis=0)
    return padded - jnp.sum(grad_narrow, axis=0, keepdims=True) / padded.shape[0]


def root(full_vec):
    return lax.rsqrt(jnp.mean(full_vec * full_vec, axis=0, keepdims=True) + EPSILON)


def norm_back(narrow, gain, grad_h):
    full_vec = expand(narrow)
    r = root(full_vec)
    scaled = gain * grad_h
    grad_full = r * (scaled - full_vec * (r * r * jnp.mean(scaled * full_vec, axis=0, keepdims=True)))
    return grad_full[:-1] - grad_full[-1:]


def column(gain_ref):
    return jnp.broadcast_to(gain_ref[...].reshape(1, gain_ref.shape[0]), (8, gain_ref.shape[0])).T[:, 0:1]


MESH = pl.DeviceIdType.MESH


class Place:
    def __init__(self, n):
        self.s = lax.axis_index("seq")
        self.b = lax.axis_index("batch")
        self.core = lax.rem(self.s, 2)
        self.chip = self.s // 2
        self.y = lax.rem(self.b, 2)
        self.z = lax.rem(self.b // 2, 4)
        self.far = self.b // 8
        self.n = n

    def core_mate(self):
        return (self.s + 1 - 2 * self.core, self.b)

    def chip_mate(self):
        return (self.s + 2 - 4 * self.chip, self.b)

    def cross_mate(self):
        return (3 - self.s, self.b)

    def y_mate(self):
        return (self.s, self.b + 1 - 2 * self.y)

    def z_of(self, d):
        return lax.rem(self.z + d, 4)

    def z_mate(self, d):
        return (self.s, self.b + 2 * (self.z_of(d) - self.z))

    def z_pair(self, bit):
        here = lax.rem(self.z // bit, 2)
        return (self.s, self.b + 2 * bit * (1 - 2 * here))

    def far_mate(self, d):
        f = lax.rem(self.far + d, self.n // 8)
        return (self.s, self.b + 8 * (f - self.far))

    def next_row(self):
        return (self.s, lax.rem(self.b + 1, self.n))

    def prior_row(self):
        return (self.s, lax.rem(self.b + self.n - 1, self.n))

    def all_mates(self):
        mates = [self.core_mate(), self.chip_mate(), self.cross_mate(), self.y_mate()]
        mates += [self.z_mate(d) for d in (1, 2, 3)]
        mates += [self.far_mate(d) for d in range(1, self.n // 8)]
        return mates + [self.next_row(), self.prior_row()]


def greet(mates):
    barrier = pltpu.get_barrier_semaphore()
    for mate in mates:
        pl.semaphore_signal(barrier, inc=1, device_id=mate, device_id_type=MESH)
    pl.semaphore_wait(barrier, len(mates))


class Copies:
    def __init__(self, sems):
        self.sems, self.made = sems, {}

    def remote(self, name, src, dst, mate):
        k = len(self.made)

        def make():
            return pltpu.make_async_remote_copy(
                src_ref=src(),
                dst_ref=dst(),
                send_sem=self.sems.at[0, k],
                recv_sem=self.sems.at[1, k],
                device_id=mate(),
                device_id_type=MESH,
            )

        assert name not in self.made
        self.made[name] = make

    def local(self, name, src, dst):
        k = len(self.made)

        def make():
            return pltpu.make_async_copy(src(), dst(), self.sems.at[0, k])

        assert name not in self.made
        self.made[name] = make

    def start(self, *names):
        for name in names:
            self.made[name]().start()

    def wait(self, *names):
        for name in names:
            self.made[name]().wait()

    def wait_recv(self, *names):
        for name in names:
            self.made[name]().wait_recv()

    def wait_send(self, *names):
        for name in names:
            self.made[name]().wait_send()


def rows_at(at, count):
    return pl.ds(pl.multiple_of(at, 16), count)


def blockwise(rows, body):
    step = next(s for s in (48, 32, 16) if rows % s == 0)

    def one(i, carry):
        body(i * step, step)
        return carry

    lax.fori_loop(0, rows // step, one, 0)


PAIRS, QUARTERS, PAIRS_Z = range(3)


class Sum:
    def __init__(self, place, copies, name, mode, way, src, first, rows, cols, bufs, out):
        self.p, self.c, self.name, self.mode, self.way = place, copies, name, mode, way
        bits = [(place.y, place.y_mate), (lax.rem(place.z, 2), lambda: place.z_pair(1))]
        (self.one, self.one_mate), (self.two, self.two_mate) = bits[::-1] if way == PAIRS_Z else bits
        self.src, self.first, self.rows, self.cols, self.out = src, first, rows, cols, out
        bufs = list(bufs)
        self.own, self.ry, self.rz, self.res, self.rf = bufs[:5]
        self.rc = bufs[5] if mode in "xy" else None
        self.rx = bufs[-1] if mode not in ("share", "ready") else None
        self.mine = (lambda: self.own.at[self.p.chip]) if mode in "xy" else (lambda: self.own.at[0])
        self.define()

    @staticmethod
    def scratch(mode, way, rows, cols, n):
        def v(*s):
            return pltpu.VMEM(s, BF16)

        half, spot = rows // 2, rows // (8 if way == QUARTERS else 4)
        out = [v(2 if mode in "xy" else 1, rows, cols), v(2 if mode == "y" else 1, half, cols)]
        out += [v(3 if way == QUARTERS else 2, spot, cols), v(rows, cols), v(n // 8 if n > 8 else 1, spot if n > 8 else 16, cols)]
        if mode in "xy":
            out.append(v(2, rows, cols))
        if mode not in ("share", "ready"):
            out.append(v(rows if mode == "x" else half, cols))
        return out

    def id(self, what):
        return (self.name, what)

    def at_half(self, one):
        return rows_at(one * (self.rows // 2), self.rows // 2)

    def at_spot(self):
        p, half = self.p, self.rows // 2
        if self.way == QUARTERS:
            return rows_at(p.y * half + p.z * (half // 4), half // 4)
        return rows_at(self.one * half + self.two * (half // 2), half // 2)

    def define(self):
        p, c, half, far = self.p, self.c, self.rows // 2, self.p.n // 8
        if self.mode in "xy":
            first = pl.ds(self.first, self.rows)
            for order in (1, 0):
                chip = lambda order=order: lax.rem(p.chip + order, 2)
                c.remote(
                    self.id(("core", order)),
                    lambda chip=chip: self.src.at[2 * chip() + 1 - p.core, first],
                    lambda chip=chip: self.rc.at[chip()],
                    p.core_mate,
                )
                c.local(
                    self.id(("own", order)),
                    lambda chip=chip: self.src.at[2 * chip() + p.core, first],
                    lambda chip=chip: self.own.at[chip()],
                )
        other = lambda: self.own.at[1 - p.chip]
        if self.mode == "x":
            c.remote(self.id("x"), other, lambda: self.rx, p.chip_mate)
        if self.mode == "y":
            c.remote(self.id("y1"), lambda: other().at[self.at_half(1 - self.one)], lambda: self.ry.at[1], self.one_mate)
            c.remote(self.id("x"), lambda: other().at[self.at_half(self.one)], lambda: self.rx, p.chip_mate)
        if self.mode == "ready":
            c.local(self.id("own"), lambda: self.src, lambda: self.own.at[0, self.at_half(self.one)])
        if self.mode == "half":
            c.remote(self.id("x"), lambda: self.src.at[1 - p.chip], lambda: self.rx, p.chip_mate)
            c.local(self.id("own"), lambda: self.src.at[p.chip], lambda: self.own.at[0, self.at_half(self.one)])
        elif self.mode != "ready":
            c.remote(self.id("y"), lambda: self.mine().at[self.at_half(1 - self.one)], lambda: self.ry.at[0], self.one_mate)
        spot = lambda: self.res.at[self.at_spot()]
        if self.way == QUARTERS:
            for d in (2, 1, 3):
                c.remote(
                    self.id(("z", d)),
                    lambda d=d: self.mine().at[rows_at(p.y * half + p.z_of(d) * (half // 4), half // 4)],
                    lambda d=d: self.rz.at[3 - d],
                    lambda d=d: p.z_mate(d),
                )
                c.remote(self.id(("bz", d)), spot, spot, lambda d=d: p.z_mate(d))
        else:
            away = lambda: rows_at(self.one * half + (1 - self.two) * (half // 2), half // 2)
            c.remote(self.id("z1"), lambda: self.mine().at[away()], lambda: self.rz.at[0], self.two_mate)
            c.remote(self.id("z2"), lambda: self.mine().at[self.at_spot()], lambda: self.rz.at[1], lambda: p.z_pair(2))
            c.remote(self.id("bz1"), spot, spot, self.two_mate)
        for d in range(1, far):
            c.remote(self.id(("far", d)), lambda: self.rf.at[p.far], lambda: self.rf.at[p.far], lambda d=d: p.far_mate(d))
        my_half = lambda: self.res.at[self.at_half(self.one)]
        c.remote(self.id("by"), my_half, my_half, self.one_mate)
        for k, (src, dst) in enumerate(self.out):
            c.local(self.id(("out", k)), lambda src=src: self.res.at[src], lambda dst=dst: dst)

    def add(self, dst, at, rows, *others):
        def body(first, step):
            here = rows_at(at + first, step)
            total = dst[here, :].astype(F32)
            for other, offset in others:
                total = total + other[rows_at(offset + first, step), :].astype(F32)
            dst[here, :] = total.astype(BF16)

        blockwise(rows, body)

    def p0(self):
        if self.mode == "half":
            self.c.start(self.id("x"), self.id("own"))
        if self.mode == "ready":
            self.c.start(self.id("own"))
        if self.mode in "xy":
            for order in (1, 0):
                self.c.start(self.id(("core", order)), self.id(("own", order)))

    def p1(self):
        self.c.wait(self.id(("core", 1)), self.id(("own", 1)))
        other = 1 - self.p.chip
        self.add(self.own.at[other], 0, self.rows, (self.rc.at[other], 0))
        self.c.start(self.id("x" if self.mode == "x" else "y1"))

    def p1b(self):
        self.c.wait(self.id(("core", 0)), self.id(("own", 0)))
        self.add(self.mine(), 0, self.rows, (self.rc.at[self.p.chip], 0))
        if self.mode == "y":
            self.c.start(self.id("y"))

    def p2(self):
        half = self.rows // 2
        if self.mode == "y":
            self.c.wait(self.id("y1"))
            self.add(self.own.at[1 - self.p.chip], self.one * half, half, (self.ry.at[1], 0))
            self.c.start(self.id("x"))
            return
        if self.mode == "x":
            self.c.wait(self.id("x"))
            self.add(self.mine(), (1 - self.one) * half, half, (self.rx, (1 - self.one) * half))
        self.c.start(self.id("y"))

    def p3(self):
        half, more = self.rows // 2, []
        if self.mode not in ("half", "ready"):
            self.c.wait(self.id("y"))
            more.append((self.ry.at[0], 0))
        if self.mode == "x":
            more.append((self.rx, self.one * half))
        if self.mode in ("y", "half"):
            self.c.wait(self.id("x"))
            more.append((self.rx, 0))
        if self.mode in ("half", "ready"):
            self.c.wait(self.id("own"))
        self.add(self.mine(), self.one * half, half, *more)
        self.c.start(*([self.id(("z", d)) for d in (2, 1, 3)] if self.way == QUARTERS else [self.id("z1")]))

    def total(self, *others):
        p = self.p
        spot, rows = self.at_spot(), self.at_spot().size
        own, far = self.mine(), p.n // 8

        def body(first, step):
            here = rows_at(spot.start + first, step)
            there = rows_at(first, step)
            total = own[here, :].astype(F32)
            for other in others:
                total = total + other[there, :].astype(F32)
            if far > 1:
                self.rf[p.far, there, :] = total.astype(BF16)
            else:
                self.res[here, :] = total.astype(BF16)

        blockwise(rows, body)
        if far > 1:
            self.c.start(*[self.id(("far", d)) for d in range(1, far)])
            self.c.wait(*[self.id(("far", d)) for d in range(1, far)])

            def more(first, step):
                there = rows_at(first, step)
                total = self.rf[0, there, :].astype(F32)
                for k in range(1, far):
                    total = total + self.rf[k, there, :].astype(F32)
                self.res[rows_at(spot.start + first, step), :] = total.astype(BF16)

            blockwise(rows, more)

    def p4(self):
        if self.way == QUARTERS:
            self.c.wait(*[self.id(("z", d)) for d in (1, 2, 3)])
            self.total(*[self.rz.at[d] for d in range(3)])
            self.c.start(*[self.id(("bz", d)) for d in (2, 1, 3)])
            return
        self.c.wait(self.id("z1"))
        spot = self.at_spot()
        self.add(self.mine(), spot.start, spot.size, (self.rz.at[0], 0))
        self.c.start(self.id("z2"))

    def p4b(self):
        if not self.way == QUARTERS:
            self.c.wait(self.id("z2"))
            self.total(self.rz.at[1])
            self.c.start(self.id("bz1"))

    def p5(self):
        self.c.wait(*([self.id(("bz", d)) for d in (1, 2, 3)] if self.way == QUARTERS else [self.id("bz1")]))
        self.c.start(self.id("by"))

    def p6(self):
        self.c.wait(self.id("by"))
        self.c.start(*[self.id(("out", k)) for k in range(len(self.out))])

    def p7(self):
        self.c.wait(*[self.id(("out", k)) for k in range(len(self.out))])

    def phase(self, k):
        (self.p0, self.p1, self.p1b, self.p2, self.p3, self.p4, self.p4b, self.p5, self.p6)[k]()


PRIOR_KV = (("pk", 0), ("pk", 1), ("pv", 0), ("pv", 1))


def fore_kernel(n, tok, blocks, heads, *refs):
    x, gain, docs, w, cot, w_down = refs[:6]
    attT_o, hT_o, kT_o, qT_o, oT_o, lse_o, start_o, k_o, v_o, wm_o, gg_o, g2_o = refs[6:18]
    xs, ws, wm, hT, docs_all, prior_docs, start, kT, vT, qT, kk, vv, acc, m_ref, l_ref, lse, stage, cs, wd, gg, g2, sems = refs[18:]
    width = xs.shape[0] + 1
    row = blocks * tok
    mine = heads * HD
    p = Place(n)
    c = Copies(sems)
    mates = {"core": p.core_mate, "chip": p.chip_mate, "cross": p.cross_mate}
    block = lambda at: pl.ds(pl.multiple_of(at * tok, tok), tok)
    here = lambda: block(p.s)
    c.local("w", lambda: w, lambda: ws)
    c.local("cot", lambda: cot.at[:, 0, :], lambda: cs)
    c.local("wd", lambda: w_down, lambda: wd)
    c.local("gg", lambda: gg, lambda: gg_o)
    c.local("g2", lambda: g2, lambda: g2_o)
    c.local("docs", lambda: docs, lambda: docs_all.at[:, here()])
    for name, mate in mates.items():
        c.remote(("docs", name), lambda: docs, lambda: docs_all.at[:, here()], mate)
    last = pl.ds(row - tok, tok)
    c.remote("old docs", lambda: docs_all.at[:, last], lambda: prior_docs, p.next_row)
    c.remote("hc", lambda: hT.at[:, here()], lambda: hT.at[:, here()], p.core_mate)
    half = tok // 2
    for k in range(2):
        c.local(("x", k), lambda k=k: x.at[:, 0, pl.ds(k * half, half)], lambda k=k: xs.at[:, pl.ds(k * half, half)])
        piece = lambda s, k=k: hT.at[:, pl.ds(pl.multiple_of(s * tok + k * half, half), half)]
        c.remote(("hx", k), lambda piece=piece: piece(p.s), lambda piece=piece: piece(p.s), p.chip_mate)
        other = lambda piece=piece: piece(p.chip_mate()[0])
        c.remote(("ho", k), other, other, p.core_mate)
    for k in range(2):
        end, to = pl.ds(row + k * half, half), pl.ds(k * half, half)
        c.remote(("pk", k), lambda end=end: kT.at[:, end], lambda to=to: kT.at[:, to], p.next_row)
        c.remote(("pv", k), lambda end=end: vT.at[:, end], lambda to=to: vT.at[:, to], p.next_row)
    for h in range(heads):
        spot = lambda h=h: attT_o.at[pl.ds(pl.multiple_of(p.s * mine + h * HD, HD), HD)]
        for name, mate in mates.items():
            src = lambda h=h, mate=mate: stage.at[pl.ds(h * HD, HD), block(mate()[0])]
            c.remote(("att", h, name), src, spot, mate)
        c.local(("att", h, "own"), lambda h=h: stage.at[pl.ds(h * HD, HD), here()], spot)
    outs = {"hT": (hT, hT_o), "kT": (kT, kT_o), "qT": (qT, qT_o), "oT": (acc, oT_o), "lse": (lse, lse_o)}
    outs.update({"start": (start, start_o), "k": (kk, k_o), "v": (vv, v_o), "wm": (wm, wm_o)})
    for name, (src, dst) in outs.items():
        c.local(("out", name), lambda src=src: src, lambda dst=dst: dst)

    c.start(("x", 0), ("x", 1), "docs", "w")
    greet([p.core_mate(), p.chip_mate(), p.cross_mate(), p.next_row(), p.prior_row()])
    c.start(*[("docs", name) for name in mates])
    gain_col = column(gain)
    for k in range(2):
        c.wait(("x", k))
        full_vec = expand(xs[:, k * half : (k + 1) * half])
        mine_now = pl.ds(pl.multiple_of(p.s * tok + k * half, half), half)
        hT[:, mine_now] = (gain_col * full_vec * root(full_vec)).astype(BF16)
        c.start(("hx", k))
    c.start("hc", "cot", "wd")

    c.wait("w")
    for s in range(blocks):
        @pl.when(p.s == s)
        def _():
            for h in range(heads):
                for k in range(3):
                    at = k * width + s * mine + h * HD
                    to = (h * 3 + k) * HD
                    wm[:, to : to + HD] = ws[:, at : at + HD]

    c.wait("docs", *[("docs", name) for name in mates])
    c.start("old docs")
    ids = jnp.broadcast_to(docs_all[...], (8, row))
    pos = lax.broadcasted_iota(jnp.int32, (8, row), 1)
    since = jnp.where((ids != pltpu.roll(ids, 1, 1)) | (pos == 0), pos, 0)
    hop = 1
    while hop < row:
        since = jnp.maximum(since, jnp.where(pos >= hop, pltpu.roll(since, hop, 1), 0))
        hop *= 2
    start[...] = since[0:1] + tok
    m_ref[...] = jnp.full(m_ref.shape, NEG, F32)
    l_ref[...] = jnp.zeros(l_ref.shape, F32)
    acc[...] = jnp.zeros(acc.shape, F32)

    def natural(keys_at, count):
        keys = pl.ds(pl.multiple_of(keys_at, 128), count)
        for h in range(heads):
            kk[h, keys, :] = kT[h * HD : (h + 1) * HD, keys].T
            vv[h, keys, :] = vT[h * HD : (h + 1) * HD, keys].T

    def project(at, count):
        own, keys = pl.ds(pl.multiple_of(at, 128), count), pl.ds(pl.multiple_of(at + tok, 128), count)
        packed = dot_tn(wm[...], hT[:, own]).astype(BF16)
        for h in range(heads):
            to, base = slice(h * HD, (h + 1) * HD), h * 3 * HD
            qT[to, own] = packed[base : base + HD] * jnp.bfloat16(1.0 / math.sqrt(HD))
            kT[to, keys] = packed[base + HD : base + 2 * HD]
            vT[to, keys] = packed[base + 2 * HD : base + 3 * HD]
        natural(at + tok, count)

    def pair(h, q0, qw, k0, kw, causal):
        hr = pl.ds(pl.multiple_of(h * HD, HD), HD)
        qs, ks = pl.ds(pl.multiple_of(q0, 128), qw), pl.ds(pl.multiple_of(k0 + tok, 128), kw)
        s = dot(kk[h, ks, :], qT[hr, qs])
        at = lax.broadcasted_iota(jnp.int32, s.shape, 0)
        keep = at >= start[:, qs] - (k0 + tok)
        if causal:
            keep = keep & (at <= lax.broadcasted_iota(jnp.int32, s.shape, 1))
        s = jnp.where(keep, s, NEG)
        m = m_ref[h, :, qs]
        new_m = jnp.maximum(m, jnp.max(s, axis=0, keepdims=True))
        e = jnp.exp(s - new_m)
        shift = jnp.exp(m - new_m)
        m_ref[h, :, qs] = new_m
        l_ref[h, :, qs] = l_ref[h, :, qs] * shift + jnp.sum(e, axis=0, keepdims=True)
        acc[hr, qs] = acc[hr, qs] * shift + dot(vT[hr, ks], e.astype(BF16))

    def finish(h, i):
        hr, qs = pl.ds(pl.multiple_of(h * HD, HD), HD), block(i)
        out = acc[hr, qs] / l_ref[h, :, qs]
        acc[hr, qs] = out
        stage[hr, qs] = out.astype(BF16)
        lse[h, :, qs] = m_ref[h, :, qs] + jnp.log(l_ref[h, :, qs])

    def send_att(h, zero):
        for name, mate in list(mates.items()) + [("own", lambda: (p.s,))]:
            @pl.when((mate()[0] == 0) == zero)
            def _():
                c.start(("att", h, name))

    pair_rows = 2 * tok
    near, far = pair_rows * p.chip, pair_rows * (1 - p.chip)
    c.wait_recv("hc")
    lax.fori_loop(0, 2, lambda t, carry: (project(near + t * tok, tok), carry)[1], 0)

    def send_prior(k):
        c.start(("pk", k), ("pv", k))

    @pl.when(p.chip == 1)
    def _():
        send_prior(0)
        send_prior(1)

    lax.fori_loop(0, heads, lambda h, carry: (pair(h, near, pair_rows, near, pair_rows, True), carry)[1], 0)

    def far_half(k):
        c.wait_recv(("hx", k))
        c.start(("ho", k))
        project(p.chip_mate()[0] * tok + k * half, half)
        c.wait_recv(("ho", k))
        project(p.cross_mate()[0] * tok + k * half, half)

        def queries(t, carry):
            pair(t // 2, pair_rows + t % 2 * tok + k * half, half, 0, pair_rows, False)
            return carry

        def keys(t, carry):
            pair(t // 2, pair_rows, pair_rows, t % 2 * tok + k * half, half, False)
            return carry

        @pl.when(p.chip == 0)
        def _():
            send_prior(k)
            lax.fori_loop(0, 2 * heads, queries, 0)

        @pl.when(p.chip == 1)
        def _():
            lax.fori_loop(0, 2 * heads, keys, 0)

    c.wait("cot", "wd")
    g2[...] = shrink_back(cs[...]).astype(BF16)
    c.start("g2")

    def grad_gelu(t, carry):
        its = pl.ds(pl.multiple_of(t * width, width), width)
        gg[its, :] = dot(wd[its, :], g2[...]).astype(BF16)
        return carry

    lax.fori_loop(0, wd.shape[0] // width, grad_gelu, 0)
    c.start("gg")
    far_half(0)
    far_half(1)

    def second(h, carry):
        pair(h, far, pair_rows, far, pair_rows, True)
        lax.fori_loop(1, blocks, lambda i, carry: (finish(h, i), carry)[1], 0)
        for k in range(heads):
            @pl.when(h == k)
            def _():
                send_att(k, False)
        return carry

    lax.fori_loop(0, heads, second, 0)
    c.wait_recv("old docs")
    from_doc = docs_all[:, 0:1]
    at = lax.broadcasted_iota(jnp.int32, (1, tok), 1)
    run = jnp.max(jnp.where(prior_docs[...] != from_doc, at + 1, 0), axis=1, keepdims=True)
    start[:, 0:tok] = jnp.where(start[:, 0:tok] == tok, run, start[:, 0:tok])
    c.wait_recv(*PRIOR_KV)
    natural(0, tok)

    def third(h, carry):
        pair(h, 0, tok, -tok, tok, False)
        finish(h, 0)
        for k in range(heads):
            @pl.when(h == k)
            def _():
                send_att(k, True)
        return carry

    lax.fori_loop(0, heads, third, 0)
    c.start(*[("out", name) for name in outs])
    c.wait_send("hc", ("hx", 0), ("hx", 1), ("ho", 0), ("ho", 1), "old docs", *PRIOR_KV)
    for h in range(heads):
        c.wait(*[("att", h, name) for name in list(mates) + ["own"]])
    c.wait("gg", "g2", *[("out", name) for name in outs])


def fore_pass(n, tok, blocks, x, gain, docs, w, cot, w_down):
    width, heads = w.shape[0], H // blocks
    row, mine = blocks * tok, heads * HD
    v = lambda *s, t=BF16: pltpu.VMEM(s, t)
    o = lambda *s, t=BF16: jax.ShapeDtypeStruct(s, t)
    hbm = pl.BlockSpec(memory_space=pl.ANY)
    scratch = [
        v(width - 1, tok, t=F32), v(width, 3 * width), v(width, 3 * mine), v(width, row),
        v(1, row, t=jnp.int32), v(1, tok, t=jnp.int32), v(1, row, t=jnp.int32),
        v(mine, row + tok), v(mine, row + tok), v(mine, row), v(heads, row + tok, HD), v(heads, row + tok, HD),
        v(mine, row, t=F32), v(heads, 1, row, t=F32), v(heads, 1, row, t=F32), v(heads, 1, row, t=F32), v(mine, row),
        v(width - 1, tok, t=F32), v(*w_down.shape), v(w_down.shape[0], tok), v(width, tok),
        pltpu.SemaphoreType.DMA((2, 31 + 4 * heads)),
    ]
    return pl.pallas_call(
        functools.partial(fore_kernel, n, tok, blocks, heads),
        out_shape=[
            o(width, tok), o(width, row), o(mine, row + tok), o(mine, row), o(mine, row, t=F32), o(heads, 1, row, t=F32),
            o(1, row, t=jnp.int32), o(heads, row + tok, HD), o(heads, row + tok, HD), o(width, 3 * mine),
            o(w_down.shape[0], tok), o(width, tok),
        ],
        in_specs=[hbm, pl.BlockSpec(memory_space=pltpu.VMEM)] + [hbm] * 4,
        out_specs=[hbm] * 12,
        scratch_shapes=scratch,
        compiler_params=pltpu.CompilerParams(collective_id=0, has_side_effects=True, vmem_limit_bytes=VMEM_LIMIT),
    )(x, gain, docs, w, cot, w_down)


def gelu_both(v, grad):
    rate = math.sqrt(2.0 / math.pi)
    square = v * v
    th = jnp.tanh(rate * v * (1.0 + 0.044715 * square))
    up = 0.5 * (1.0 + th)
    slope = up + 0.5 * v * (1.0 - th * th) * (rate * (1.0 + 3.0 * 0.044715 * square))
    return (v * up).astype(BF16), (grad * slope).astype(BF16)


def mid_kernel(n, blocks, *refs):
    x, cot, attT, gain, w_out, w_up, w_down, gg_in, g2_in = refs[:9]
    new_o, gm_o, doT_o, gu_o, go_o, half_o, ready_o = refs[9:16]
    xs, cs, at, wo, wu, wd, mid, h2, g2, g1, gg, geluT, gupT, dw, rc, ry, rx, ga, gu, go, sems = refs[16:]
    tok, width = xs.shape[1], xs.shape[0] + 1
    parts = wu.shape[1] // width
    share = width // blocks
    p = Place(n)
    c = Copies(sems)
    mates = {"cross": p.cross_mate, "chip": p.chip_mate, "core": p.core_mate}
    c.local("att", lambda: attT, lambda: at)
    c.local("wo", lambda: w_out, lambda: wo)
    c.local("x", lambda: x.at[:, 0, :], lambda: xs)
    c.local("cot", lambda: cot.at[:, 0, :], lambda: cs)
    c.local("wu", lambda: w_up, lambda: wu)
    c.local("wd", lambda: w_down, lambda: wd)
    c.local("gg", lambda: gg_in, lambda: gg)
    c.local("g2", lambda: g2_in, lambda: g2)
    c.remote(("core", 0), lambda: dw.at[0], lambda: rc.at[0], p.core_mate)
    c.remote(("core", 1), lambda: dw.at[2], lambda: rc.at[1], p.core_mate)
    part = width // 2
    fourth = part // 2
    low = lambda y: rows_at(y * fourth, fourth)
    for t in range(2):
        c.remote(("y", t), lambda t=t: dw.at[2 * t + 1, low(1 - p.y)], lambda t=t: ry.at[t], p.y_mate)
        dst = lambda t=t: half_o.at[1 - p.chip if t == 0 else p.chip]
        c.local(("half", t), lambda t=t: dw.at[2 * t + 1, low(p.y)], dst)
    high = pl.ds(part, part)
    c.remote("chip", lambda: dw.at[1, high], lambda: rx, p.chip_mate)
    later = lambda y: rows_at(part + y * fourth, fourth)
    c.remote(("y", 2), lambda: dw.at[3, later(1 - p.y)], lambda: ry.at[2], p.y_mate)
    c.local("ready", lambda: dw.at[3, later(p.y)], lambda: ready_o)
    there = lambda: doT_o.at[:, pl.ds(pl.multiple_of(p.s * tok, tok), tok)]
    for name, mate in mates.items():
        c.remote(("ga", name), lambda mate=mate: ga.at[rows_at(mate()[0] * share, share)], there, mate)
    c.local(("ga", "own"), lambda: ga.at[rows_at(p.s * share, share)], there)
    c.local("new", lambda: xs, lambda: new_o.at[:, 0, :])
    c.local("gm", lambda: cs, lambda: gm_o)
    for k in range(parts):
        c.local(("gu", k), lambda k=k: gu.at[:, pl.ds(k * share, share)], lambda k=k: gu_o.at[:, pl.ds(k * share, share)])
    c.local("go", lambda: go, lambda: go_o)

    c.start("att", "wo", "x", "wu", "gg", "g2", "cot", "wd")
    greet([p.core_mate(), p.chip_mate(), p.cross_mate(), p.y_mate()])
    c.wait("att", "wo")
    branch_one = dot_tn(wo[...], at[...])
    c.wait("x")
    mid[...] = xs[...] + shrink(branch_one)
    full_vec = expand(mid[...])
    gain_col = column(gain)
    h2[...] = (gain_col * full_vec * root(full_vec)).astype(BF16)
    c.wait("wu", "gg", "g2")

    def add(dst, at, src, rows):
        def body(first, step):
            r = rows_at(at + first, step)
            dw[dst, r, :] = (dw[dst, r, :].astype(F32) + src[rows_at(first, step), :].astype(F32)).astype(BF16)

        blockwise(rows, body)

    def chip_sum(t):
        c.wait_recv(("core", t))
        add(2 * t + 1, 0, rc.at[t], width)
        c.start(("y", t), *(["chip"] if t == 0 else []))

    def y_sum(t):
        c.wait(("y", t))
        add(2 * t + 1, p.y * fourth, ry.at[t], fourth)
        c.start(("half", t))

    def piece(t, carry):
        s = jnp.where(t == 0, p.cross_mate()[0], jnp.where(t == 1, p.chip_mate()[0], jnp.where(t == 2, p.core_mate()[0], p.s)))
        its = pl.ds(pl.multiple_of(s * width, width), width)
        gelu, grad_up = gelu_both(dot_tn(wu[:, its], h2[...]), gg[its, :].astype(F32))
        geluT[its, :] = gelu
        gupT[its, :] = grad_up
        dw[t] = dot_nt(geluT[its, :], g2[...]).astype(BF16)

        @pl.when(t == 0)
        def _():
            c.start(("core", 0))

        @pl.when(t == 2)
        def _():
            c.start(("core", 1))

        @pl.when(t == 1)
        def _():
            chip_sum(0)

        return carry

    lax.fori_loop(0, parts, piece, 0)
    chip_sum(1)
    grad_h = dot(wu[...], gupT[...])
    c.wait("cot")
    grad_middle = cs[...] + norm_back(mid[...], gain_col, grad_h)
    cs[...] = grad_middle
    g1[...] = shrink_back(grad_middle).astype(BF16)
    ga[...] = dot(wo[...], g1[...]).astype(BF16)
    c.start(*[("ga", name) for name in list(mates) + ["own"]])
    c.start("gm")
    def up_grad(k, carry):
        its = pl.ds(pl.multiple_of(k * width, width), width)
        grad = dot_nt(h2[...], gupT[its, :]).astype(BF16)
        for s in range(blocks):
            gu[s, rows_at(k * share, share), :] = grad[s * share : (s + 1) * share]
        return carry

    lax.fori_loop(0, parts // 2, up_grad, 0)
    c.wait("chip")
    add(3, part, rx, part)
    c.start(("y", 2))
    lax.fori_loop(parts // 2, parts, up_grad, 0)
    c.start(*[("gu", k) for k in range(parts)])
    out_grad = dot_nt(at[...], g1[...]).astype(BF16)
    for s in range(blocks):
        for k in range(2):
            go[s, k * share : (k + 1) * share, :] = out_grad[s * share : (s + 1) * share, k * part : (k + 1) * part]
    c.start("go")
    c.wait("wd")
    xs[...] = mid[...] + shrink(dot_tn(wd[...], geluT[...]))
    c.start("new")
    y_sum(0)
    y_sum(1)
    c.wait(("y", 2))
    add(3, part + p.y * fourth, ry.at[2], fourth)
    c.start("ready")
    c.wait_send(("core", 0), ("core", 1))
    c.wait(*[("ga", name) for name in list(mates) + ["own"]])
    c.wait("gm", "new", "go", "ready", ("half", 0), ("half", 1), *[("gu", k) for k in range(parts)])


def mid_pass(n, blocks, x, cot, attT, gain, w_out, w_up, w_down, gg, g2):
    width, tok = attT.shape
    parts, share = w_up.shape[1] // width, width // blocks
    v = lambda *s, t=BF16: pltpu.VMEM(s, t)
    o = lambda *s, t=BF16: jax.ShapeDtypeStruct(s, t)
    hbm = pl.BlockSpec(memory_space=pl.ANY)
    scratch = [
        v(width - 1, tok, t=F32), v(width - 1, tok, t=F32), v(width, tok), v(width, width), v(*w_up.shape), v(*w_down.shape),
        v(width - 1, tok, t=F32), v(width, tok), v(width, tok), v(width, tok), v(*gg.shape), v(*gg.shape), v(*gg.shape), v(4, width, width), v(2, width, width), v(3, width // 4, width), v(width // 2, width),
        v(width, tok), v(blocks, parts * share, width), v(blocks, 2 * share, width // 2),
        pltpu.SemaphoreType.DMA((2, 32)),
    ]
    return pl.pallas_call(
        functools.partial(mid_kernel, n, blocks),
        out_shape=[
            o(width - 1, 1, tok, t=F32), o(width - 1, tok, t=F32), o(share, blocks * tok), o(blocks, parts * share, width),
            o(blocks, 2 * share, width // 2), o(2, width // 4, width), o(width // 4, width),
        ],
        in_specs=[hbm] * 3 + [pl.BlockSpec(memory_space=pltpu.VMEM)] + [hbm] * 5,
        out_specs=[hbm] * 7,
        scratch_shapes=scratch,
        compiler_params=pltpu.CompilerParams(collective_id=2, has_side_effects=True, vmem_limit_bytes=VMEM_LIMIT),
    )(x, cot, attT, gain, w_out, w_up, w_down, gg, g2)


BACK_IN = ("doT", "k", "v", "kT", "qT", "oT", "lse", "start", "hT", "wm", "x", "gm")
DW = ("cross", "chip", "core", "own")
D0, D1, U0, U1, O, Q0, Q1, GRAD_H, SEND = range(9)
Q_HEADS = ((0, 1), (2,))
U_MODES = ("x", "x")
O_MODE = "y"
WAYS = (PAIRS, PAIRS, PAIRS, PAIRS, PAIRS, PAIRS_Z, PAIRS)
START, READY, PRIOR, FULL, DIAGONAL, CLOSE, END = range(7)
PLAN = {
    START: {
        (): [(D0, 0), (U1, 0), (U0, 0), (D1, 0), (O, 0)],
    },
    READY: {
        (): [(U1, 1), (D1, 4)],
    },
    PRIOR: {
        (0,): [(U1, 2)],
        (1,): [(U0, 1), (U0, 2)],
        (2,): [(D0, 4), (D1, 5), (O, 1), (O, 2)],
    },
    FULL: {
        (1, 0): [(D0, 5), (U1, 3), (O, 3)],
        (2, 1): [(D0, 6), (U0, 3), (U1, 5), (D1, 7)],
        (2, 4): [(O, 4)],
    },
    DIAGONAL: {
        (1, 0): [(D1, 6)],
        (2, 1): [(D0, 7)],
    },
    CLOSE: {
        (1,): [(U1, 4), (SEND, 0)],
        (2,): [(Q0, 3), (SEND, 1), (U0, 4), (GRAD_H, 0), (GRAD_H, 1), (GRAD_H, 2), (O, 5), (U1, 6)],
    },
    END: {
        (): [(GRAD_H, 3), (Q1, 3), (D1, 8), (GRAD_H, 4), (O, 6), (GRAD_H, 5), (Q0, 4), (U0, 5),
            (D0, 8), (Q1, 4), (U1, 7), (Q0, 5), (O, 7), (U0, 6), (Q1, 5), (GRAD_H, 6),
            (U1, 8), (O, 8), (Q0, 6), (U0, 7), (Q1, 6), (Q0, 7), (Q1, 7), (U0, 8),
            (Q0, 8), (Q1, 8)],
    },
}


def folds(cols):
    return 2 if cols % 128 else 1


def back_sums(n, width, share, part):
    way = lambda k: QUARTERS if n > 8 else WAYS[k]
    half = [(D0 + k, ("half", "ready")[k], way(D0 + k), k, 0, part, width) for k in range(2)]
    up = [(U0 + k, U_MODES[k], way(U0 + k), 0, k * part, part, width) for k in range(2)]
    sums = half + up + [(O, O_MODE, way(O), 1, 0, 2 * share, part)]
    for k, hs in enumerate(Q_HEADS):
        cols = share * len(hs)
        sums.append((Q0 + k, "share", way(Q0 + k), None, 0, width // folds(cols), cols * folds(cols)))
    return sums


def back_kernel(n, tok, blocks, heads, parts, *refs):
    refs = list(refs)
    take = lambda count: [refs.pop(0) for _ in range(count)]
    hbm = dict(zip(BACK_IN, take(len(BACK_IN))))
    down_half, down_ready, gu, go, gain_one = take(5)
    down_o, up_o, out_o, rg_o = take(4)
    qkv_o = take(len(Q_HEADS))
    vm = dict(zip(BACK_IN, take(len(BACK_IN))))
    dkT, dvT, delta, dP, prior_out, prior_in, g_stage, g_core, g_x, g_acc = take(10)
    dws = take(len(Q_HEADS))
    p, hd, row = Place(n), HD, blocks * tok
    mine, width = heads * hd, blocks * heads * hd
    share, part = width // blocks, width // 2
    per_part = part // share
    outs = {D0 + k: [(pl.ds(0, part), down_o.at[pl.ds(k * part, part)])] for k in range(2)}
    for k in range(2):
        outs[U0 + k] = [
            (pl.ds(j * share, share), up_o.at[:, pl.ds((k * per_part + j) * width, width)]) for j in range(per_part)
        ]
    outs[O] = [(pl.ds(k * share, share), out_o.at[:, pl.ds(k * part, part)]) for k in range(2)]
    for k in range(len(Q_HEADS)):
        outs[Q0 + k] = [(pl.ds(0, qkv_o[k].shape[0]), qkv_o[k])]
    plans = back_sums(n, width, share, part)
    bufs = [take(len(Sum.scratch(q[1], q[2], 16, 128, n))) for q in plans]
    c = Copies(refs.pop(0))
    for name in BACK_IN:
        src = (lambda: hbm["x"].at[:, 0, :]) if name == "x" else (lambda name=name: hbm[name])
        c.local(name, src, lambda name=name: vm[name])
    sums = {}
    for (name, mode, way, arr, first, rows, cols), buf in zip(plans, bufs):
        src = None if arr is None else ((down_half, down_ready) if name < U0 else (gu, go))[arr]
        sums[name] = Sum(p, c, name, mode, way, src, first, rows, cols, buf, outs[name])
    qkv = [sums[Q0 + k] for k in range(len(Q_HEADS))]
    for k, one in enumerate(qkv):
        count = one.rows // blocks
        block = lambda ref, s, count=count: ref.at[rows_at(s * count, count)]
        spot = lambda one=one, block=block: block(one.own.at[0], p.s)
        for what, mate in (("cross", p.cross_mate), ("chip", p.chip_mate), ("core", p.core_mate)):
            c.remote(("dw", k, what), lambda k=k, mate=mate, block=block: block(dws[k], mate()[0]), spot, mate)
        c.local(("dw", k, "own"), lambda k=k, block=block: block(dws[k], p.s), spot)
    for k in range(heads):
        c.remote(("prior", k), lambda k=k: prior_out.at[k], lambda k=k: prior_in.at[k], p.prior_row)
    for order in (1, 0):
        c.remote(("gh", order), lambda order=order: g_stage.at[order], lambda order=order: g_core.at[order], p.core_mate)
    c.remote(("gh", "x"), lambda: g_stage.at[1], lambda: g_x, p.chip_mate)
    c.local("rg", lambda: vm["gm"], lambda: rg_o.at[:, 0, :])

    def grad_h_part(owner):
        return dot(vm["wm"][...], dP[:, pl.ds(pl.multiple_of(owner * tok, tok), tok)])

    def core_grad(order):
        chip = lax.rem(p.chip + order, 2)
        g_stage[order] = grad_h_part(2 * chip + 1 - p.core).astype(BF16)
        c.start(("gh", order))

    def keep_grad(order):
        chip = lax.rem(p.chip + order, 2)
        g_acc[...] = grad_h_part(2 * chip + p.core)

    def chip_grad():
        c.wait(("gh", 1))
        g_stage[1] = (g_acc[...] + g_core[1].astype(F32)).astype(BF16)
        c.start(("gh", "x"))

    def own_grad():
        c.wait(("gh", 0))
        g_acc[...] += g_core[0].astype(F32)

    def input_grad():
        c.wait("x", "gm", ("gh", "x"))
        vm["gm"][...] += norm_back(vm["x"][...], column(gain_one), g_acc[...] + g_x[...].astype(F32))
        c.start("rg")

    def send_dw(k):
        rows = slice(Q_HEADS[k][0] * 3 * hd, (Q_HEADS[k][-1] + 1) * 3 * hd)
        grad = dot_nt(vm["hT"][...], dP[rows, :]).astype(BF16)
        fold = folds(grad.shape[1])
        count = share // fold
        for s in range(blocks):
            cells = [grad[s * share + f * count : s * share + (f + 1) * count] for f in range(fold)]
            dws[k][s * count : (s + 1) * count, :] = jnp.concatenate(cells, axis=1)
        c.start(*[("dw", k, what) for what in DW])

    special = {GRAD_H: [lambda: core_grad(1), lambda: core_grad(0), lambda: keep_grad(1), chip_grad, lambda: keep_grad(0)]}
    special[GRAD_H] += [own_grad, input_grad]
    special[SEND] = [lambda k=k: send_dw(k) for k in range(len(Q_HEADS))]

    def step(which, phase):
        if which in special:
            special[which][phase]()
            return
        if which >= Q0 and phase == 3:
            c.wait(*[("dw", which - Q0, what) for what in DW])
        sums[which].phase(phase)

    def steps_at(place, *now):
        for at, names in PLAN.get(place, {}).items():
            same = None
            for want, have in zip(at, now):
                same = (have == want) if same is None else same & (have == want)

            def run():
                for which, phase in names:
                    step(which, phase)

            run() if same is None else pl.when(same)(run)

    first = BACK_IN[:8]
    c.start(*first)
    greet(p.all_mates())
    steps_at(START)
    c.start(*BACK_IN[8:])
    c.wait(*first)
    dqT = vm["oT"]
    doT, kk, vv, kT, qT, lse, start = (vm[x] for x in ("doT", "k", "v", "kT", "qT", "lse", "start"))

    def make_delta(h, carry):
        rows = pl.ds(pl.multiple_of(h * hd, hd), hd)
        delta[h] = jnp.sum(doT[rows, :].astype(F32) * vm["oT"][rows, :], axis=0, keepdims=True)
        return carry

    lax.fori_loop(0, heads, make_delta, 0)
    dqT[...] = jnp.zeros_like(dqT)
    dkT[...] = jnp.zeros_like(dkT)
    dvT[...] = jnp.zeros_like(dvT)
    steps_at(READY)

    def pair(h, i, j, causal):
        hr = pl.ds(pl.multiple_of(h * hd, hd), hd)
        qs, ks = (pl.ds(pl.multiple_of(at * tok, tok), tok) for at in (i, j))
        q_blk, do_blk = qT[hr, qs], doT[hr, qs]
        s = dot(kk[h, ks, :], q_blk)
        e = jnp.exp(s - lse[h, :, qs])
        at = lax.broadcasted_iota(jnp.int32, s.shape, 0)
        keep = at >= start[:, qs] - j * tok
        if causal:
            keep = keep & (at <= lax.broadcasted_iota(jnp.int32, s.shape, 1))
        e = jnp.where(keep, e, 0.0)
        dp = dot(vv[h, ks, :], do_blk)
        ds = (e * (dp - delta[h, :, qs])).astype(BF16)
        dvT[hr, ks] += dot_nt(do_blk, e.astype(BF16))
        dkT[hr, ks] += dot_nt(q_blk, ds)
        dqT[hr, qs] += dot(kT[hr, ks], ds)

    def prior(h, carry):
        pair(h, 0, 0, False)
        hr = pl.ds(pl.multiple_of(h * hd, hd), hd)
        prior_out[h, 0:hd, :] = dkT[hr, 0:tok].astype(BF16)
        prior_out[h, hd : 2 * hd, :] = dvT[hr, 0:tok].astype(BF16)
        for k in range(heads):
            @pl.when(h == k)
            def _():
                c.start(("prior", k))
        steps_at(PRIOR, h)
        return carry

    lax.fori_loop(0, heads, prior, 0)

    def close(h):
        hr = pl.ds(pl.multiple_of(h * hd, hd), hd)
        last = pl.ds(row, tok)
        dkT[hr, last] += prior_in[h, 0:hd, :].astype(F32)
        dvT[hr, last] += prior_in[h, hd : 2 * hd, :].astype(F32)
        base = h * 3 * hd
        for k, (src, at) in enumerate(((dqT, 0), (dkT, tok), (dvT, tok))):
            val = src[hr, at:]
            val = val * (1.0 / math.sqrt(hd)) if k == 0 else val
            dP[pl.ds(pl.multiple_of(base + k * hd, hd), hd), :] = val.astype(BF16)

    def head(h, carry):
        def full(t, carry):
            i = jnp.where(t < 3, 3, jnp.where(t < 5, 2, 1))
            j = jnp.where(t < 3, t + 1, jnp.where(t < 5, t - 2, 1))
            pair(h, i, j, False)
            steps_at(FULL, h, t)
            return carry

        lax.fori_loop(0, 6, full, 0)

        def diagonal(i, carry):
            pair(h, i, i + 1, True)
            steps_at(DIAGONAL, h, i)
            return carry

        lax.fori_loop(0, blocks, diagonal, 0)
        for k in range(heads):
            @pl.when(h == k)
            def _():
                if k == 0:
                    c.wait("hT", "wm")
                c.wait(("prior", k))
        close(h)
        steps_at(CLOSE, h)
        return carry

    lax.fori_loop(0, heads, head, 0)
    steps_at(END)

    for one in sums.values():
        one.p7()
    c.wait("rg")


def back_pass(n, tok, blocks, ins, down_half, down_ready, gu, go, gain, parts):
    heads = ins[1].shape[0]
    row = blocks * tok
    width = ins[8].shape[0]
    mine = heads * HD
    share, part = width // blocks, width // 2
    v = lambda *s, t=BF16: pltpu.VMEM(s, t)
    o = lambda *s, t=BF16: jax.ShapeDtypeStruct(s, t)
    scratch = [v(width - 1, tok, t=F32) if name == "x" else pltpu.VMEM(a.shape, a.dtype) for name, a in zip(BACK_IN, ins)]
    scratch += [
        v(mine, row + tok, t=F32), v(mine, row + tok, t=F32), v(heads, 1, row, t=F32), v(3 * mine, row),
        v(heads, 2 * HD, tok), v(heads, 2 * HD, tok),
        v(2, width, tok), v(2, width, tok), v(width, tok), v(width, tok, t=F32),
    ]
    sums = back_sums(n, width, share, part)
    scratch += [v(*one[5:]) for one in sums[Q0:]]
    copies = len(ins) + 5 * heads + 8
    for _, mode, way, _, _, rows, cols in sums:
        scratch += Sum.scratch(mode, way, rows, cols, n)
        copies += 17 + n // 8
    scratch.append(pltpu.SemaphoreType.DMA((2, copies)))
    hbm = pl.BlockSpec(memory_space=pl.ANY)
    vmem = pl.BlockSpec(memory_space=pltpu.VMEM)
    return pl.pallas_call(
        functools.partial(back_kernel, n, tok, blocks, heads, parts),
        out_shape=[o(width, width), o(share, parts * width), o(share, width), o(width - 1, 1, tok, t=F32)]
        + [o(*one[5:]) for one in sums[Q0:]],
        in_specs=[hbm] * (len(ins) + 4) + [vmem],
        out_specs=[hbm] * (4 + len(Q_HEADS)),
        scratch_shapes=scratch,
        compiler_params=pltpu.CompilerParams(collective_id=1, has_side_effects=True, vmem_limit_bytes=VMEM_LIMIT),
    )(*ins, down_half, down_ready, gu, go, gain)


def last_kernel(blocks, *refs):
    new, rg, down, up, out, w_qkv, w_up, gain_one, gain_two = refs[:9]
    q_in = refs[9 : 9 + len(Q_HEADS)]
    refs = refs[9 + len(Q_HEADS) :]
    new_o, rg_o, gain_one_o, gain_two_o, qkv_o, out_o, up_o, down_o = refs[:8]
    down_v, up_v, out_v, wq, wu, gcol, down_f, up_f, out_f, qkv_f, x_v, sems = refs[8:19] + refs[-1:]
    q_v = refs[19:-1]
    s = lax.axis_index("seq")
    share, width = out_v.shape
    mine, hd = width // blocks, HD
    c = Copies(sems)
    my_rows = lambda ref: ref.at[rows_at(s * share, share)]
    loads = list(zip(q_in, q_v)) + [(my_rows(w_qkv), wq), (up, up_v), (down, down_v), (out, out_v), (my_rows(w_up), wu)]
    for k, (src, dst) in enumerate(loads):
        c.local(("in", k), lambda src=src: src, lambda dst=dst: dst)
    for k, (src, dst) in enumerate(((up_f, up_o), (down_f, down_o), (out_f, out_o), (qkv_f, qkv_o))):
        c.local(("out", k), lambda src=src: src, lambda dst=dst: dst)
    for k, (src, dst) in enumerate(((new, new_o), (rg, rg_o))):
        c.local(("x in", k), lambda k=k, src=src: src.at[:, 0, :], lambda k=k: x_v.at[k])
        c.local(("x out", k), lambda k=k: x_v.at[k], lambda k=k, dst=dst: dst.at[:, 0, :])
    at = len(q_in)
    c.start(*[("in", k) for k in range(at + 2)], ("x in", 0), ("x in", 1), *[("in", k) for k in range(at + 2, len(loads))])

    def row_of(col):
        return jnp.broadcast_to(col, (share, 128)).T[0:1, :]

    def my_gain(gain):
        gcol[...] = column(gain)
        return gcol[pl.ds(pl.multiple_of(s * share, share), share), :]

    c.wait(*[("in", k) for k in range(at + 1)])
    total = jnp.zeros((share, 1), F32)
    for k in range(3):
        for o in range(blocks):
            cells = []
            for src, hs in zip(q_v, Q_HEADS):
                fold, cols = folds(share * len(hs)), share * len(hs)
                rows = slice(o * share // fold, (o + 1) * share // fold)
                for h in range(len(hs)):
                    lanes = [f * cols + (h * 3 + k) * hd for f in range(fold)]
                    cells.append(jnp.concatenate([src[rows, lane : lane + hd] for lane in lanes], axis=0))
            cells = jnp.concatenate(cells, axis=1).astype(F32)
            cols = slice(k * width + o * mine, k * width + (o + 1) * mine)
            qkv_f[:, cols] = cells
            total = total + jnp.sum(cells * wq[:, cols].astype(F32), axis=1, keepdims=True)
    c.start(("out", 3))
    for k, (src, dst) in enumerate(((up_v, up_f), (down_v, down_f), (out_v, out_f))):
        c.wait(("in", at + 1 + k))
        dst[...] = src[...].astype(F32)
        c.start(("out", k))
        if k < 2:
            c.wait(("x in", k))
            c.start(("x out", k))
    c.wait(("in", at + 4))
    gain_two_o[...] = row_of(jnp.sum(up_f[...] * wu[...].astype(F32), axis=1, keepdims=True) / my_gain(gain_two))
    gain_one_o[...] = row_of(total / my_gain(gain_one))
    c.wait(("x out", 0), ("x out", 1), *[("out", k) for k in range(4)])


def last_pass(blocks, new, rg, down, up, out, qs, w_qkv, w_up, gain_one, gain_two):
    share, width = out.shape
    v = lambda *s, t=BF16: pltpu.VMEM(s, t)
    f = lambda *s: jax.ShapeDtypeStruct(s, F32)
    hbm = pl.BlockSpec(memory_space=pl.ANY)
    vmem = pl.BlockSpec(memory_space=pltpu.VMEM)
    scratch = [
        v(*down.shape), v(*up.shape), v(*out.shape), v(share, 3 * width), v(*up.shape), v(width, 1, t=F32),
        v(*down.shape, t=F32), v(*up.shape, t=F32), v(*out.shape, t=F32), v(share, 3 * width, t=F32),
        v(2, new.shape[0], new.shape[2], t=F32),
    ]
    scratch += [v(*q.shape) for q in qs] + [pltpu.SemaphoreType.DMA((1, 20))]
    return pl.pallas_call(
        functools.partial(last_kernel, blocks),
        out_shape=[f(*new.shape), f(*rg.shape), f(1, share), f(1, share), f(share, 3 * width), f(*out.shape), f(*up.shape), f(*down.shape)],
        in_specs=[hbm] * 7 + [vmem] * 2 + [hbm] * len(qs),
        out_specs=[hbm, hbm, vmem, vmem] + [hbm] * 4,
        scratch_shapes=scratch,
        compiler_params=pltpu.CompilerParams(vmem_limit_bytes=VMEM_LIMIT),
    )(new, rg, down, up, out, w_qkv, w_up, gain_one, gain_two, *qs)


def per_device(residual, documents, gain_one, gain_two, w_qkv, w_out, w_up, w_down, cotangent):
    blocks = lax.axis_size("seq")
    n = lax.axis_size("batch")
    tok = residual.shape[1]
    x = jnp.transpose(residual, (2, 0, 1))
    cot = jnp.transpose(cotangent, (2, 0, 1))
    attT, hT, kT, qT, oT, lse, start, k, v, w_mine, grad_gelu, grad_two = fore_pass(
        n, tok, blocks, x, gain_one, documents, w_qkv, cot, w_down
    )
    new, grad_middle, doT, grad_up, grad_out, down_half, down_ready = mid_pass(
        n, blocks, x, cot, attT, gain_two, w_out, w_up, w_down, grad_gelu, grad_two
    )
    sum_down, sum_up, sum_out, grad_x, *sum_qkv = back_pass(
        n, tok, blocks, (doT, k, v, kT, qT, oT, lse, start, hT, w_mine, x, grad_middle),
        down_half, down_ready, grad_up, grad_out, gain_one, w_up.shape[1] // w_up.shape[0],
    )
    new, grad_x, one, two, sum_qkv, sum_out, sum_up, sum_down = last_pass(
        blocks, new, grad_x, sum_down, sum_up, sum_out, sum_qkv, w_qkv, w_up, gain_one, gain_two
    )
    new, grad_x = jnp.transpose(new, (1, 2, 0)), jnp.transpose(grad_x, (1, 2, 0))
    return (new, grad_x, one[0], two[0], sum_qkv, sum_out, sum_up, sum_down)


def solution(mesh):
    placed = (
        P("batch", "seq", None),
        P("batch", "seq"),
        P(),
        P(),
        P(),
        P(),
        P(),
        P(),
        P("batch", "seq", None),
    )
    return jax.shard_map(
        per_device,
        mesh=mesh,
        in_specs=placed,
        out_specs=(
            P("batch", "seq", None),
            P("batch", "seq", None),
            P("seq"),
            P("seq"),
            P("seq", None),
            P("seq", None),
            P("seq", None),
            P("seq", None),
        ),
        check_vma=False,
    )
```

```python
import functools
import math

import jax
import jax.numpy as jnp
from jax import lax
from jax.experimental import pallas as pl
from jax.experimental.pallas import tpu as pltpu
from jax.sharding import PartitionSpec as P

H = 12
HD = 64
EPSILON = 1e-06
NEG = -1e30
F32, BF16 = jnp.float32, jnp.bfloat16
VMEM_LIMIT = 62 * 2**20


def dot(a, b):
    return lax.dot_general(a, b, (((1,), (0,)), ((), ())), preferred_element_type=F32)


def dot_nt(a, b):
    return lax.dot_general(a, b, (((1,), (1,)), ((), ())), preferred_element_type=F32)


def dot_tn(a, b):
    return lax.dot_general(a, b, (((0,), (0,)), ((), ())), preferred_element_type=F32)


def expand(narrow):
    return jnp.concatenate([narrow, -jnp.sum(narrow, axis=0, keepdims=True)], axis=0)


def shrink(full_vec):
    return full_vec[:-1] - jnp.mean(full_vec, axis=0, keepdims=True)


def shrink_back(grad_narrow):
    padded = jnp.concatenate([grad_narrow, jnp.zeros_like(grad_narrow[:1])], axis=0)
    return padded - jnp.sum(grad_narrow, axis=0, keepdims=True) / padded.shape[0]


def root(full_vec):
    return lax.rsqrt(jnp.mean(full_vec * full_vec, axis=0, keepdims=True) + EPSILON)


def norm_back(narrow, gain, grad_h):
    full_vec = expand(narrow)
    r = root(full_vec)
    scaled = gain * grad_h
    grad_full = r * (scaled - full_vec * (r * r * jnp.mean(scaled * full_vec, axis=0, keepdims=True)))
    return grad_full[:-1] - grad_full[-1:]


def column(gain_ref):
    return jnp.broadcast_to(gain_ref[...].reshape(1, gain_ref.shape[0]), (8, gain_ref.shape[0])).T[:, 0:1]


MESH = pl.DeviceIdType.MESH


class Place:
    def __init__(self, n):
        self.s = lax.axis_index("seq")
        self.b = lax.axis_index("batch")
        self.core = lax.rem(self.s, 2)
        self.chip = self.s // 2
        self.y = lax.rem(self.b, 2)
        self.z = lax.rem(self.b // 2, 4)
        self.far = self.b // 8
        self.n = n

    def core_mate(self):
        return (self.s + 1 - 2 * self.core, self.b)

    def chip_mate(self):
        return (self.s + 2 - 4 * self.chip, self.b)

    def cross_mate(self):
        return (3 - self.s, self.b)

    def y_mate(self):
        return (self.s, self.b + 1 - 2 * self.y)

    def z_of(self, d):
        return lax.rem(self.z + d, 4)

    def z_mate(self, d):
        return (self.s, self.b + 2 * (self.z_of(d) - self.z))

    def z_pair(self, bit):
        here = lax.rem(self.z // bit, 2)
        return (self.s, self.b + 2 * bit * (1 - 2 * here))

    def far_mate(self, d):
        f = lax.rem(self.far + d, self.n // 8)
        return (self.s, self.b + 8 * (f - self.far))

    def next_row(self):
        return (self.s, lax.rem(self.b + 1, self.n))

    def prior_row(self):
        return (self.s, lax.rem(self.b + self.n - 1, self.n))

    def all_mates(self):
        mates = [self.core_mate(), self.chip_mate(), self.cross_mate(), self.y_mate()]
        mates += [self.z_mate(d) for d in (1, 2, 3)]
        mates += [self.far_mate(d) for d in range(1, self.n // 8)]
        return mates + [self.next_row(), self.prior_row()]


def greet(mates):
    barrier = pltpu.get_barrier_semaphore()
    for mate in mates:
        pl.semaphore_signal(barrier, inc=1, device_id=mate, device_id_type=MESH)
    pl.semaphore_wait(barrier, len(mates))


class Copies:
    def __init__(self, sems):
        self.sems, self.made = sems, {}

    def remote(self, name, src, dst, mate):
        k = len(self.made)

        def make():
            return pltpu.make_async_remote_copy(
                src_ref=src(),
                dst_ref=dst(),
                send_sem=self.sems.at[0, k],
                recv_sem=self.sems.at[1, k],
                device_id=mate(),
                device_id_type=MESH,
            )

        assert name not in self.made
        self.made[name] = make

    def local(self, name, src, dst):
        k = len(self.made)

        def make():
            return pltpu.make_async_copy(src(), dst(), self.sems.at[0, k])

        assert name not in self.made
        self.made[name] = make

    def start(self, *names):
        for name in names:
            self.made[name]().start()

    def wait(self, *names):
        for name in names:
            self.made[name]().wait()

    def wait_recv(self, *names):
        for name in names:
            self.made[name]().wait_recv()

    def wait_send(self, *names):
        for name in names:
            self.made[name]().wait_send()


def rows_at(at, count):
    return pl.ds(pl.multiple_of(at, 16), count)


def blockwise(rows, body):
    step = next(s for s in (48, 32, 16) if rows % s == 0)

    def one(i, carry):
        body(i * step, step)
        return carry

    lax.fori_loop(0, rows // step, one, 0)


PAIRS, QUARTERS, PAIRS_Z = range(3)


class Sum:
    def __init__(self, place, copies, name, mode, way, src, first, rows, cols, bufs, out):
        self.p, self.c, self.name, self.mode, self.way = place, copies, name, mode, way
        bits = [(place.y, place.y_mate), (lax.rem(place.z, 2), lambda: place.z_pair(1))]
        (self.one, self.one_mate), (self.two, self.two_mate) = bits[::-1] if way == PAIRS_Z else bits
        self.src, self.first, self.rows, self.cols, self.out = src, first, rows, cols, out
        bufs = list(bufs)
        self.own, self.ry, self.rz, self.res, self.rf = bufs[:5]
        self.rc = bufs[5] if mode in "xy" else None
        self.rx = bufs[-1] if mode not in ("share", "ready") else None
        self.mine = (lambda: self.own.at[self.p.chip]) if mode in "xy" else (lambda: self.own.at[0])
        self.define()

    @staticmethod
    def scratch(mode, way, rows, cols, n):
        def v(*s):
            return pltpu.VMEM(s, BF16)

        half, spot = rows // 2, rows // (8 if way == QUARTERS else 4)
        out = [v(2 if mode in "xy" else 1, rows, cols), v(2 if mode == "y" else 1, half, cols)]
        out += [v(3 if way == QUARTERS else 2, spot, cols), v(rows, cols), v(n // 8 if n > 8 else 1, spot if n > 8 else 16, cols)]
        if mode in "xy":
            out.append(v(2, rows, cols))
        if mode not in ("share", "ready"):
            out.append(v(rows if mode == "x" else half, cols))
        return out

    def id(self, what):
        return (self.name, what)

    def at_half(self, one):
        return rows_at(one * (self.rows // 2), self.rows // 2)

    def at_spot(self):
        p, half = self.p, self.rows // 2
        if self.way == QUARTERS:
            return rows_at(p.y * half + p.z * (half // 4), half // 4)
        return rows_at(self.one * half + self.two * (half // 2), half // 2)

    def define(self):
        p, c, half, far = self.p, self.c, self.rows // 2, self.p.n // 8
        if self.mode in "xy":
            first = pl.ds(self.first, self.rows)
            for order in (1, 0):
                chip = lambda order=order: lax.rem(p.chip + order, 2)
                c.remote(
                    self.id(("core", order)),
                    lambda chip=chip: self.src.at[2 * chip() + 1 - p.core, first],
                    lambda chip=chip: self.rc.at[chip()],
                    p.core_mate,
                )
                c.local(
                    self.id(("own", order)),
                    lambda chip=chip: self.src.at[2 * chip() + p.core, first],
                    lambda chip=chip: self.own.at[chip()],
                )
        other = lambda: self.own.at[1 - p.chip]
        if self.mode == "x":
            c.remote(self.id("x"), other, lambda: self.rx, p.chip_mate)
        if self.mode == "y":
            c.remote(self.id("y1"), lambda: other().at[self.at_half(1 - self.one)], lambda: self.ry.at[1], self.one_mate)
            c.remote(self.id("x"), lambda: other().at[self.at_half(self.one)], lambda: self.rx, p.chip_mate)
        if self.mode == "ready":
            c.local(self.id("own"), lambda: self.src, lambda: self.own.at[0, self.at_half(self.one)])
        if self.mode == "half":
            c.remote(self.id("x"), lambda: self.src.at[1 - p.chip], lambda: self.rx, p.chip_mate)
            c.local(self.id("own"), lambda: self.src.at[p.chip], lambda: self.own.at[0, self.at_half(self.one)])
        elif self.mode != "ready":
            c.remote(self.id("y"), lambda: self.mine().at[self.at_half(1 - self.one)], lambda: self.ry.at[0], self.one_mate)
        spot = lambda: self.res.at[self.at_spot()]
        if self.way == QUARTERS:
            for d in (2, 1, 3):
                c.remote(
                    self.id(("z", d)),
                    lambda d=d: self.mine().at[rows_at(p.y * half + p.z_of(d) * (half // 4), half // 4)],
                    lambda d=d: self.rz.at[3 - d],
                    lambda d=d: p.z_mate(d),
                )
                c.remote(self.id(("bz", d)), spot, spot, lambda d=d: p.z_mate(d))
        else:
            away = lambda: rows_at(self.one * half + (1 - self.two) * (half // 2), half // 2)
            c.remote(self.id("z1"), lambda: self.mine().at[away()], lambda: self.rz.at[0], self.two_mate)
            c.remote(self.id("z2"), lambda: self.mine().at[self.at_spot()], lambda: self.rz.at[1], lambda: p.z_pair(2))
            c.remote(self.id("bz1"), spot, spot, self.two_mate)
        for d in range(1, far):
            c.remote(self.id(("far", d)), lambda: self.rf.at[p.far], lambda: self.rf.at[p.far], lambda d=d: p.far_mate(d))
        my_half = lambda: self.res.at[self.at_half(self.one)]
        c.remote(self.id("by"), my_half, my_half, self.one_mate)
        for k, (src, dst) in enumerate(self.out):
            c.local(self.id(("out", k)), lambda src=src: self.res.at[src], lambda dst=dst: dst)

    def add(self, dst, at, rows, *others):
        def body(first, step):
            here = rows_at(at + first, step)
            total = dst[here, :].astype(F32)
            for other, offset in others:
                total = total + other[rows_at(offset + first, step), :].astype(F32)
            dst[here, :] = total.astype(BF16)

        blockwise(rows, body)

    def p0(self):
        if self.mode == "half":
            self.c.start(self.id("x"), self.id("own"))
        if self.mode == "ready":
            self.c.start(self.id("own"))
        if self.mode in "xy":
            for order in (1, 0):
                self.c.start(self.id(("core", order)), self.id(("own", order)))

    def p1(self):
        self.c.wait(self.id(("core", 1)), self.id(("own", 1)))
        other = 1 - self.p.chip
        self.add(self.own.at[other], 0, self.rows, (self.rc.at[other], 0))
        self.c.start(self.id("x" if self.mode == "x" else "y1"))

    def p1b(self):
        self.c.wait(self.id(("core", 0)), self.id(("own", 0)))
        self.add(self.mine(), 0, self.rows, (self.rc.at[self.p.chip], 0))
        if self.mode == "y":
            self.c.start(self.id("y"))

    def p2(self):
        half = self.rows // 2
        if self.mode == "y":
            self.c.wait(self.id("y1"))
            self.add(self.own.at[1 - self.p.chip], self.one * half, half, (self.ry.at[1], 0))
            self.c.start(self.id("x"))
            return
        if self.mode == "x":
            self.c.wait(self.id("x"))
            self.add(self.mine(), (1 - self.one) * half, half, (self.rx, (1 - self.one) * half))
        self.c.start(self.id("y"))

    def p3(self):
        half, more = self.rows // 2, []
        if self.mode not in ("half", "ready"):
            self.c.wait(self.id("y"))
            more.append((self.ry.at[0], 0))
        if self.mode == "x":
            more.append((self.rx, self.one * half))
        if self.mode in ("y", "half"):
            self.c.wait(self.id("x"))
            more.append((self.rx, 0))
        if self.mode in ("half", "ready"):
            self.c.wait(self.id("own"))
        self.add(self.mine(), self.one * half, half, *more)
        self.c.start(*([self.id(("z", d)) for d in (2, 1, 3)] if self.way == QUARTERS else [self.id("z1")]))

    def total(self, *others):
        p = self.p
        spot, rows = self.at_spot(), self.at_spot().size
        own, far = self.mine(), p.n // 8

        def body(first, step):
            here = rows_at(spot.start + first, step)
            there = rows_at(first, step)
            total = own[here, :].astype(F32)
            for other in others:
                total = total + other[there, :].astype(F32)
            if far > 1:
                self.rf[p.far, there, :] = total.astype(BF16)
            else:
                self.res[here, :] = total.astype(BF16)

        blockwise(rows, body)
        if far > 1:
            self.c.start(*[self.id(("far", d)) for d in range(1, far)])
            self.c.wait(*[self.id(("far", d)) for d in range(1, far)])

            def more(first, step):
                there = rows_at(first, step)
                total = self.rf[0, there, :].astype(F32)
                for k in range(1, far):
                    total = total + self.rf[k, there, :].astype(F32)
                self.res[rows_at(spot.start + first, step), :] = total.astype(BF16)

            blockwise(rows, more)

    def p4(self):
        if self.way == QUARTERS:
            self.c.wait(*[self.id(("z", d)) for d in (1, 2, 3)])
            self.total(*[self.rz.at[d] for d in range(3)])
            self.c.start(*[self.id(("bz", d)) for d in (2, 1, 3)])
            return
        self.c.wait(self.id("z1"))
        spot = self.at_spot()
        self.add(self.mine(), spot.start, spot.size, (self.rz.at[0], 0))
        self.c.start(self.id("z2"))

    def p4b(self):
        if not self.way == QUARTERS:
            self.c.wait(self.id("z2"))
            self.total(self.rz.at[1])
            self.c.start(self.id("bz1"))

    def p5(self):
        self.c.wait(*([self.id(("bz", d)) for d in (1, 2, 3)] if self.way == QUARTERS else [self.id("bz1")]))
        self.c.start(self.id("by"))

    def p6(self):
        self.c.wait(self.id("by"))
        self.c.start(*[self.id(("out", k)) for k in range(len(self.out))])

    def p7(self):
        self.c.wait(*[self.id(("out", k)) for k in range(len(self.out))])

    def phase(self, k):
        (self.p0, self.p1, self.p1b, self.p2, self.p3, self.p4, self.p4b, self.p5, self.p6)[k]()


PRIOR_KV = (("pk", 0), ("pk", 1), ("pv", 0), ("pv", 1))


def fore_kernel(n, tok, blocks, heads, *refs):
    x, gain, docs, w, cot, w_down = refs[:6]
    attT_o, hT_o, kT_o, qT_o, oT_o, lse_o, start_o, k_o, v_o, wm_o, gg_o, g2_o = refs[6:18]
    xs, ws, wm, hT, docs_all, prior_docs, start, kT, vT, qT, kk, vv, acc, m_ref, l_ref, lse, stage, cs, wd, gg, g2, sems = refs[18:]
    width = xs.shape[0] + 1
    row = blocks * tok
    mine = heads * HD
    p = Place(n)
    c = Copies(sems)
    mates = {"core": p.core_mate, "chip": p.chip_mate, "cross": p.cross_mate}
    block = lambda at: pl.ds(pl.multiple_of(at * tok, tok), tok)
    here = lambda: block(p.s)
    c.local("w", lambda: w, lambda: ws)
    c.local("cot", lambda: cot.at[:, 0, :], lambda: cs)
    c.local("wd", lambda: w_down, lambda: wd)
    c.local("gg", lambda: gg, lambda: gg_o)
    c.local("g2", lambda: g2, lambda: g2_o)
    c.local("docs", lambda: docs, lambda: docs_all.at[:, here()])
    for name, mate in mates.items():
        c.remote(("docs", name), lambda: docs, lambda: docs_all.at[:, here()], mate)
    last = pl.ds(row - tok, tok)
    c.remote("old docs", lambda: docs_all.at[:, last], lambda: prior_docs, p.next_row)
    c.remote("hc", lambda: hT.at[:, here()], lambda: hT.at[:, here()], p.core_mate)
    half = tok // 2
    for k in range(2):
        c.local(("x", k), lambda k=k: x.at[:, 0, pl.ds(k * half, half)], lambda k=k: xs.at[:, pl.ds(k * half, half)])
        piece = lambda s, k=k: hT.at[:, pl.ds(pl.multiple_of(s * tok + k * half, half), half)]
        c.remote(("hx", k), lambda piece=piece: piece(p.s), lambda piece=piece: piece(p.s), p.chip_mate)
        other = lambda piece=piece: piece(p.chip_mate()[0])
        c.remote(("ho", k), other, other, p.core_mate)
    for k in range(2):
        end, to = pl.ds(row + k * half, half), pl.ds(k * half, half)
        c.remote(("pk", k), lambda end=end: kT.at[:, end], lambda to=to: kT.at[:, to], p.next_row)
        c.remote(("pv", k), lambda end=end: vT.at[:, end], lambda to=to: vT.at[:, to], p.next_row)
    for h in range(heads):
        spot = lambda h=h: attT_o.at[pl.ds(pl.multiple_of(p.s * mine + h * HD, HD), HD)]
        for name, mate in mates.items():
            src = lambda h=h, mate=mate: stage.at[pl.ds(h * HD, HD), block(mate()[0])]
            c.remote(("att", h, name), src, spot, mate)
        c.local(("att", h, "own"), lambda h=h: stage.at[pl.ds(h * HD, HD), here()], spot)
    outs = {"hT": (hT, hT_o), "kT": (kT, kT_o), "qT": (qT, qT_o), "oT": (acc, oT_o), "lse": (lse, lse_o)}
    outs.update({"start": (start, start_o), "k": (kk, k_o), "v": (vv, v_o), "wm": (wm, wm_o)})
    for name, (src, dst) in outs.items():
        c.local(("out", name), lambda src=src: src, lambda dst=dst: dst)

    c.start(("x", 0), ("x", 1), "docs", "w")
    greet([p.core_mate(), p.chip_mate(), p.cross_mate(), p.next_row(), p.prior_row()])
    c.start(*[("docs", name) for name in mates])
    gain_col = column(gain)
    for k in range(2):
        c.wait(("x", k))
        full_vec = expand(xs[:, k * half : (k + 1) * half])
        mine_now = pl.ds(pl.multiple_of(p.s * tok + k * half, half), half)
        hT[:, mine_now] = (gain_col * full_vec * root(full_vec)).astype(BF16)
        c.start(("hx", k))
    c.start("hc", "cot", "wd")

    c.wait("w")
    for s in range(blocks):
        @pl.when(p.s == s)
        def _():
            for h in range(heads):
                for k in range(3):
                    at = k * width + s * mine + h * HD
                    to = (h * 3 + k) * HD
                    wm[:, to : to + HD] = ws[:, at : at + HD]

    c.wait("docs", *[("docs", name) for name in mates])
    c.start("old docs")
    ids = jnp.broadcast_to(docs_all[...], (8, row))
    pos = lax.broadcasted_iota(jnp.int32, (8, row), 1)
    since = jnp.where((ids != pltpu.roll(ids, 1, 1)) | (pos == 0), pos, 0)
    hop = 1
    while hop < row:
        since = jnp.maximum(since, jnp.where(pos >= hop, pltpu.roll(since, hop, 1), 0))
        hop *= 2
    start[...] = since[0:1] + tok
    m_ref[...] = jnp.full(m_ref.shape, NEG, F32)
    l_ref[...] = jnp.zeros(l_ref.shape, F32)
    acc[...] = jnp.zeros(acc.shape, F32)

    def natural(keys_at, count):
        keys = pl.ds(pl.multiple_of(keys_at, 128), count)
        for h in range(heads):
            kk[h, keys, :] = kT[h * HD : (h + 1) * HD, keys].T
            vv[h, keys, :] = vT[h * HD : (h + 1) * HD, keys].T

    def project(at, count):
        own, keys = pl.ds(pl.multiple_of(at, 128), count), pl.ds(pl.multiple_of(at + tok, 128), count)
        packed = dot_tn(wm[...], hT[:, own]).astype(BF16)
        for h in range(heads):
            to, base = slice(h * HD, (h + 1) * HD), h * 3 * HD
            qT[to, own] = packed[base : base + HD] * jnp.bfloat16(1.0 / math.sqrt(HD))
            kT[to, keys] = packed[base + HD : base + 2 * HD]
            vT[to, keys] = packed[base + 2 * HD : base + 3 * HD]
        natural(at + tok, count)

    def pair(h, q0, qw, k0, kw, causal):
        hr = pl.ds(pl.multiple_of(h * HD, HD), HD)
        qs, ks = pl.ds(pl.multiple_of(q0, 128), qw), pl.ds(pl.multiple_of(k0 + tok, 128), kw)
        s = dot(kk[h, ks, :], qT[hr, qs])
        at = lax.broadcasted_iota(jnp.int32, s.shape, 0)
        keep = at >= start[:, qs] - (k0 + tok)
        if causal:
            keep = keep & (at <= lax.broadcasted_iota(jnp.int32, s.shape, 1))
        s = jnp.where(keep, s, NEG)
        m = m_ref[h, :, qs]
        new_m = jnp.maximum(m, jnp.max(s, axis=0, keepdims=True))
        e = jnp.exp(s - new_m)
        shift = jnp.exp(m - new_m)
        m_ref[h, :, qs] = new_m
        l_ref[h, :, qs] = l_ref[h, :, qs] * shift + jnp.sum(e, axis=0, keepdims=True)
        acc[hr, qs] = acc[hr, qs] * shift + dot(vT[hr, ks], e.astype(BF16))

    def finish(h, i):
        hr, qs = pl.ds(pl.multiple_of(h * HD, HD), HD), block(i)
        out = acc[hr, qs] / l_ref[h, :, qs]
        acc[hr, qs] = out
        stage[hr, qs] = out.astype(BF16)
        lse[h, :, qs] = m_ref[h, :, qs] + jnp.log(l_ref[h, :, qs])

    def send_att(h, zero):
        for name, mate in list(mates.items()) + [("own", lambda: (p.s,))]:
            @pl.when((mate()[0] == 0) == zero)
            def _():
                c.start(("att", h, name))

    pair_rows = 2 * tok
    near, far = pair_rows * p.chip, pair_rows * (1 - p.chip)
    c.wait_recv("hc")
    lax.fori_loop(0, 2, lambda t, carry: (project(near + t * tok, tok), carry)[1], 0)

    def send_prior(k):
        c.start(("pk", k), ("pv", k))

    @pl.when(p.chip == 1)
    def _():
        send_prior(0)
        send_prior(1)

    lax.fori_loop(0, heads, lambda h, carry: (pair(h, near, pair_rows, near, pair_rows, True), carry)[1], 0)

    def forward(k):
        c.wait_recv(("hx", k))
        c.start(("ho", k))

    def far_half(k):
        project(p.chip_mate()[0] * tok + k * half, half)

        def one(t, carry):
            @pl.when(t == heads)
            def _():
                c.wait_recv(("ho", k))
                project(p.cross_mate()[0] * tok + k * half, half)

                @pl.when(p.chip == 0)
                def _():
                    send_prior(k)

            h = lax.rem(t, heads)
            at = jnp.where(t < heads, p.core, 1 - p.core) * tok + k * half

            @pl.when(p.chip == 0)
            def _():
                pair(h, pair_rows + at, half, 0, pair_rows, False)

            @pl.when(p.chip == 1)
            def _():
                pair(h, pair_rows, pair_rows, at, half, False)

            return carry

        lax.fori_loop(0, 2 * heads, one, 0)

    forward(0)
    c.wait("cot", "wd")
    g2[...] = shrink_back(cs[...]).astype(BF16)
    c.start("g2")

    def grad_gelu(t, carry):
        its = pl.ds(pl.multiple_of(t * width, width), width)
        gg[its, :] = dot(wd[its, :], g2[...]).astype(BF16)
        return carry

    lax.fori_loop(0, wd.shape[0] // width, grad_gelu, 0)
    c.start("gg")
    far_half(0)
    forward(1)
    far_half(1)

    def second(h, carry):
        pair(h, far, pair_rows, far, pair_rows, True)
        lax.fori_loop(1, blocks, lambda i, carry: (finish(h, i), carry)[1], 0)
        for k in range(heads):
            @pl.when(h == k)
            def _():
                send_att(k, False)
        return carry

    lax.fori_loop(0, heads, second, 0)
    c.wait_recv("old docs")
    from_doc = docs_all[:, 0:1]
    at = lax.broadcasted_iota(jnp.int32, (1, tok), 1)
    run = jnp.max(jnp.where(prior_docs[...] != from_doc, at + 1, 0), axis=1, keepdims=True)
    start[:, 0:tok] = jnp.where(start[:, 0:tok] == tok, run, start[:, 0:tok])
    c.wait_recv(*PRIOR_KV)
    natural(0, tok)

    def third(h, carry):
        pair(h, 0, tok, -tok, tok, False)
        finish(h, 0)
        for k in range(heads):
            @pl.when(h == k)
            def _():
                send_att(k, True)
        return carry

    lax.fori_loop(0, heads, third, 0)
    c.start(*[("out", name) for name in outs])
    c.wait_send("hc", ("hx", 0), ("hx", 1), ("ho", 0), ("ho", 1), "old docs", *PRIOR_KV)
    for h in range(heads):
        c.wait(*[("att", h, name) for name in list(mates) + ["own"]])
    c.wait("gg", "g2", *[("out", name) for name in outs])


def fore_pass(n, tok, blocks, x, gain, docs, w, cot, w_down):
    width, heads = w.shape[0], H // blocks
    row, mine = blocks * tok, heads * HD
    v = lambda *s, t=BF16: pltpu.VMEM(s, t)
    o = lambda *s, t=BF16: jax.ShapeDtypeStruct(s, t)
    hbm = pl.BlockSpec(memory_space=pl.ANY)
    scratch = [
        v(width - 1, tok, t=F32), v(width, 3 * width), v(width, 3 * mine), v(width, row),
        v(1, row, t=jnp.int32), v(1, tok, t=jnp.int32), v(1, row, t=jnp.int32),
        v(mine, row + tok), v(mine, row + tok), v(mine, row), v(heads, row + tok, HD), v(heads, row + tok, HD),
        v(mine, row, t=F32), v(heads, 1, row, t=F32), v(heads, 1, row, t=F32), v(heads, 1, row, t=F32), v(mine, row),
        v(width - 1, tok, t=F32), v(*w_down.shape), v(w_down.shape[0], tok), v(width, tok),
        pltpu.SemaphoreType.DMA((2, 31 + 4 * heads)),
    ]
    return pl.pallas_call(
        functools.partial(fore_kernel, n, tok, blocks, heads),
        out_shape=[
            o(width, tok), o(width, row), o(mine, row + tok), o(mine, row), o(mine, row, t=F32), o(heads, 1, row, t=F32),
            o(1, row, t=jnp.int32), o(heads, row + tok, HD), o(heads, row + tok, HD), o(width, 3 * mine),
            o(w_down.shape[0], tok), o(width, tok),
        ],
        in_specs=[hbm, pl.BlockSpec(memory_space=pltpu.VMEM)] + [hbm] * 4,
        out_specs=[hbm] * 12,
        scratch_shapes=scratch,
        compiler_params=pltpu.CompilerParams(collective_id=0, has_side_effects=True, vmem_limit_bytes=VMEM_LIMIT),
    )(x, gain, docs, w, cot, w_down)


def gelu_both(v, grad):
    rate = math.sqrt(2.0 / math.pi)
    square = v * v
    th = jnp.tanh(rate * v * (1.0 + 0.044715 * square))
    up = 0.5 * (1.0 + th)
    slope = up + 0.5 * v * (1.0 - th * th) * (rate * (1.0 + 3.0 * 0.044715 * square))
    return (v * up).astype(BF16), (grad * slope).astype(BF16)


def mid_kernel(n, blocks, *refs):
    x, cot, attT, gain, w_out, w_up, w_down, gg_in, g2_in = refs[:9]
    new_o, gm_o, doT_o, gu_o, go_o, half_o, ready_o = refs[9:16]
    xs, cs, at, wo, wu, wd, mid, h2, g2, g1, gg, geluT, gupT, dw, rc, ry, rx, ga, gu, go, sems = refs[16:]
    tok, width = xs.shape[1], xs.shape[0] + 1
    parts = wu.shape[1] // width
    share = width // blocks
    p = Place(n)
    c = Copies(sems)
    mates = {"cross": p.cross_mate, "chip": p.chip_mate, "core": p.core_mate}
    c.local("att", lambda: attT, lambda: at)
    c.local("wo", lambda: w_out, lambda: wo)
    c.local("x", lambda: x.at[:, 0, :], lambda: xs)
    c.local("cot", lambda: cot.at[:, 0, :], lambda: cs)
    c.local("wu", lambda: w_up, lambda: wu)
    c.local("wd", lambda: w_down, lambda: wd)
    c.local("gg", lambda: gg_in, lambda: gg)
    c.local("g2", lambda: g2_in, lambda: g2)
    c.remote(("core", 0), lambda: dw.at[0], lambda: rc.at[0], p.core_mate)
    c.remote(("core", 1), lambda: dw.at[2], lambda: rc.at[1], p.core_mate)
    part = width // 2
    fourth = part // 2
    low = lambda y: rows_at(y * fourth, fourth)
    for t in range(2):
        c.remote(("y", t), lambda t=t: dw.at[2 * t + 1, low(1 - p.y)], lambda t=t: ry.at[t], p.y_mate)
        dst = lambda t=t: half_o.at[1 - p.chip if t == 0 else p.chip]
        c.local(("half", t), lambda t=t: dw.at[2 * t + 1, low(p.y)], dst)
    high = pl.ds(part, part)
    c.remote("chip", lambda: dw.at[1, high], lambda: rx, p.chip_mate)
    later = lambda y: rows_at(part + y * fourth, fourth)
    c.remote(("y", 2), lambda: dw.at[3, later(1 - p.y)], lambda: ry.at[2], p.y_mate)
    c.local("ready", lambda: dw.at[3, later(p.y)], lambda: ready_o)
    there = lambda: doT_o.at[:, pl.ds(pl.multiple_of(p.s * tok, tok), tok)]
    for name, mate in mates.items():
        c.remote(("ga", name), lambda mate=mate: ga.at[rows_at(mate()[0] * share, share)], there, mate)
    c.local(("ga", "own"), lambda: ga.at[rows_at(p.s * share, share)], there)
    c.local("new", lambda: xs, lambda: new_o.at[:, 0, :])
    c.local("gm", lambda: cs, lambda: gm_o)
    for k in range(parts):
        c.local(("gu", k), lambda k=k: gu.at[:, pl.ds(k * share, share)], lambda k=k: gu_o.at[:, pl.ds(k * share, share)])
    c.local("go", lambda: go, lambda: go_o)

    c.start("att", "wo", "x", "wu", "gg", "g2", "cot", "wd")
    greet([p.core_mate(), p.chip_mate(), p.cross_mate(), p.y_mate()])
    c.wait("att", "wo")
    branch_one = dot_tn(wo[...], at[...])
    c.wait("x")
    mid[...] = xs[...] + shrink(branch_one)
    full_vec = expand(mid[...])
    gain_col = column(gain)
    h2[...] = (gain_col * full_vec * root(full_vec)).astype(BF16)
    c.wait("wu", "gg", "g2")

    def add(dst, at, src, rows):
        def body(first, step):
            r = rows_at(at + first, step)
            dw[dst, r, :] = (dw[dst, r, :].astype(F32) + src[rows_at(first, step), :].astype(F32)).astype(BF16)

        blockwise(rows, body)

    def chip_sum(t):
        c.wait_recv(("core", t))
        add(2 * t + 1, 0, rc.at[t], width)
        c.start(("y", t), *(["chip"] if t == 0 else []))

    def y_sum(t):
        c.wait(("y", t))
        add(2 * t + 1, p.y * fourth, ry.at[t], fourth)
        c.start(("half", t))

    def piece(t, carry):
        s = jnp.where(t == 0, p.cross_mate()[0], jnp.where(t == 1, p.chip_mate()[0], jnp.where(t == 2, p.core_mate()[0], p.s)))
        its = pl.ds(pl.multiple_of(s * width, width), width)
        gelu, grad_up = gelu_both(dot_tn(wu[:, its], h2[...]), gg[its, :].astype(F32))
        geluT[its, :] = gelu
        gupT[its, :] = grad_up
        dw[t] = dot_nt(geluT[its, :], g2[...]).astype(BF16)

        @pl.when(t == 0)
        def _():
            c.start(("core", 0))

        @pl.when(t == 2)
        def _():
            c.start(("core", 1))

        @pl.when(t == 1)
        def _():
            chip_sum(0)

        return carry

    lax.fori_loop(0, parts, piece, 0)
    chip_sum(1)
    grad_h = dot(wu[...], gupT[...])
    c.wait("cot")
    grad_middle = cs[...] + norm_back(mid[...], gain_col, grad_h)
    cs[...] = grad_middle
    g1[...] = shrink_back(grad_middle).astype(BF16)
    ga[...] = dot(wo[...], g1[...]).astype(BF16)
    c.start(*[("ga", name) for name in list(mates) + ["own"]])
    c.start("gm")
    def up_grad(k, carry):
        its = pl.ds(pl.multiple_of(k * width, width), width)
        grad = dot_nt(h2[...], gupT[its, :]).astype(BF16)
        for s in range(blocks):
            gu[s, rows_at(k * share, share), :] = grad[s * share : (s + 1) * share]
        return carry

    lax.fori_loop(0, parts // 2, up_grad, 0)
    c.wait("chip")
    add(3, part, rx, part)
    c.start(("y", 2))
    lax.fori_loop(parts // 2, parts, up_grad, 0)
    c.start(*[("gu", k) for k in range(parts)])
    out_grad = dot_nt(at[...], g1[...]).astype(BF16)
    for s in range(blocks):
        for k in range(2):
            go[s, k * share : (k + 1) * share, :] = out_grad[s * share : (s + 1) * share, k * part : (k + 1) * part]
    c.start("go")
    c.wait("wd")
    xs[...] = mid[...] + shrink(dot_tn(wd[...], geluT[...]))
    c.start("new")
    y_sum(0)
    y_sum(1)
    c.wait(("y", 2))
    add(3, part + p.y * fourth, ry.at[2], fourth)
    c.start("ready")
    c.wait_send(("core", 0), ("core", 1))
    c.wait(*[("ga", name) for name in list(mates) + ["own"]])
    c.wait("gm", "new", "go", "ready", ("half", 0), ("half", 1), *[("gu", k) for k in range(parts)])


def mid_pass(n, blocks, x, cot, attT, gain, w_out, w_up, w_down, gg, g2):
    width, tok = attT.shape
    parts, share = w_up.shape[1] // width, width // blocks
    v = lambda *s, t=BF16: pltpu.VMEM(s, t)
    o = lambda *s, t=BF16: jax.ShapeDtypeStruct(s, t)
    hbm = pl.BlockSpec(memory_space=pl.ANY)
    scratch = [
        v(width - 1, tok, t=F32), v(width - 1, tok, t=F32), v(width, tok), v(width, width), v(*w_up.shape), v(*w_down.shape),
        v(width - 1, tok, t=F32), v(width, tok), v(width, tok), v(width, tok), v(*gg.shape), v(*gg.shape), v(*gg.shape), v(4, width, width), v(2, width, width), v(3, width // 4, width), v(width // 2, width),
        v(width, tok), v(blocks, parts * share, width), v(blocks, 2 * share, width // 2),
        pltpu.SemaphoreType.DMA((2, 32)),
    ]
    return pl.pallas_call(
        functools.partial(mid_kernel, n, blocks),
        out_shape=[
            o(width - 1, 1, tok, t=F32), o(width - 1, tok, t=F32), o(share, blocks * tok), o(blocks, parts * share, width),
            o(blocks, 2 * share, width // 2), o(2, width // 4, width), o(width // 4, width),
        ],
        in_specs=[hbm] * 3 + [pl.BlockSpec(memory_space=pltpu.VMEM)] + [hbm] * 5,
        out_specs=[hbm] * 7,
        scratch_shapes=scratch,
        compiler_params=pltpu.CompilerParams(collective_id=2, has_side_effects=True, vmem_limit_bytes=VMEM_LIMIT),
    )(x, cot, attT, gain, w_out, w_up, w_down, gg, g2)


BACK_IN = ("doT", "k", "v", "kT", "qT", "oT", "lse", "start", "hT", "wm", "x", "gm")
DW = ("cross", "chip", "core", "own")
D0, D1, U0, U1, O, Q0, Q1, GRAD_H, SEND = range(9)
Q_HEADS = ((0, 1), (2,))
U_MODES = ("x", "x")
O_MODE = "y"
WAYS = (PAIRS, PAIRS, PAIRS, PAIRS, PAIRS, PAIRS_Z, PAIRS)
START, READY, PRIOR, FULL, DIAGONAL, CLOSE, END = range(7)
PLAN = {
    START: {
        (): [(D0, 0), (U1, 0), (U0, 0), (D1, 0), (O, 0)],
    },
    READY: {
        (): [(U1, 1), (D1, 4)],
    },
    PRIOR: {
        (0,): [(U1, 2)],
        (1,): [(U0, 1), (U0, 2)],
        (2,): [(D0, 4), (D1, 5), (O, 1), (O, 2)],
    },
    FULL: {
        (1, 0): [(D0, 5), (U1, 3), (O, 3)],
        (2, 1): [(D0, 6), (U0, 3), (U1, 5), (D1, 7)],
        (2, 4): [(O, 4)],
    },
    DIAGONAL: {
        (1, 0): [(D1, 6)],
        (2, 1): [(D0, 7)],
    },
    CLOSE: {
        (1,): [(U1, 4), (SEND, 0)],
        (2,): [(Q0, 3), (SEND, 1), (U0, 4), (GRAD_H, 0), (GRAD_H, 1), (GRAD_H, 2), (O, 5), (U1, 6)],
    },
    END: {
        (): [(GRAD_H, 3), (Q1, 3), (D1, 8), (GRAD_H, 4), (O, 6), (GRAD_H, 5), (Q0, 4), (U0, 5),
            (D0, 8), (Q1, 4), (U1, 7), (Q0, 5), (O, 7), (U0, 6), (Q1, 5), (GRAD_H, 6),
            (U1, 8), (O, 8), (Q0, 6), (U0, 7), (Q1, 6), (Q0, 7), (Q1, 7), (U0, 8),
            (Q0, 8), (Q1, 8)],
    },
}


def folds(cols):
    return 2 if cols % 128 else 1


def back_sums(n, width, share, part):
    way = lambda k: QUARTERS if n > 8 else WAYS[k]
    half = [(D0 + k, ("half", "ready")[k], way(D0 + k), k, 0, part, width) for k in range(2)]
    up = [(U0 + k, U_MODES[k], way(U0 + k), 0, k * part, part, width) for k in range(2)]
    sums = half + up + [(O, O_MODE, way(O), 1, 0, 2 * share, part)]
    for k, hs in enumerate(Q_HEADS):
        cols = share * len(hs)
        sums.append((Q0 + k, "share", way(Q0 + k), None, 0, width // folds(cols), cols * folds(cols)))
    return sums


def back_kernel(n, tok, blocks, heads, parts, *refs):
    refs = list(refs)
    take = lambda count: [refs.pop(0) for _ in range(count)]
    hbm = dict(zip(BACK_IN, take(len(BACK_IN))))
    down_half, down_ready, gu, go, gain_one = take(5)
    down_o, up_o, out_o, rg_o = take(4)
    qkv_o = take(len(Q_HEADS))
    vm = dict(zip(BACK_IN, take(len(BACK_IN))))
    dkT, dvT, delta, dP, prior_out, prior_in, g_stage, g_core, g_x, g_acc = take(10)
    dws = take(len(Q_HEADS))
    p, hd, row = Place(n), HD, blocks * tok
    mine, width = heads * hd, blocks * heads * hd
    share, part = width // blocks, width // 2
    per_part = part // share
    outs = {D0 + k: [(pl.ds(0, part), down_o.at[pl.ds(k * part, part)])] for k in range(2)}
    for k in range(2):
        outs[U0 + k] = [
            (pl.ds(j * share, share), up_o.at[:, pl.ds((k * per_part + j) * width, width)]) for j in range(per_part)
        ]
    outs[O] = [(pl.ds(k * share, share), out_o.at[:, pl.ds(k * part, part)]) for k in range(2)]
    for k in range(len(Q_HEADS)):
        outs[Q0 + k] = [(pl.ds(0, qkv_o[k].shape[0]), qkv_o[k])]
    plans = back_sums(n, width, share, part)
    bufs = [take(len(Sum.scratch(q[1], q[2], 16, 128, n))) for q in plans]
    c = Copies(refs.pop(0))
    for name in BACK_IN:
        src = (lambda: hbm["x"].at[:, 0, :]) if name == "x" else (lambda name=name: hbm[name])
        c.local(name, src, lambda name=name: vm[name])
    sums = {}
    for (name, mode, way, arr, first, rows, cols), buf in zip(plans, bufs):
        src = None if arr is None else ((down_half, down_ready) if name < U0 else (gu, go))[arr]
        sums[name] = Sum(p, c, name, mode, way, src, first, rows, cols, buf, outs[name])
    qkv = [sums[Q0 + k] for k in range(len(Q_HEADS))]
    for k, one in enumerate(qkv):
        count = one.rows // blocks
        block = lambda ref, s, count=count: ref.at[rows_at(s * count, count)]
        spot = lambda one=one, block=block: block(one.own.at[0], p.s)
        for what, mate in (("cross", p.cross_mate), ("chip", p.chip_mate), ("core", p.core_mate)):
            c.remote(("dw", k, what), lambda k=k, mate=mate, block=block: block(dws[k], mate()[0]), spot, mate)
        c.local(("dw", k, "own"), lambda k=k, block=block: block(dws[k], p.s), spot)
    for k in range(heads):
        c.remote(("prior", k), lambda k=k: prior_out.at[k], lambda k=k: prior_in.at[k], p.prior_row)
    for order in (1, 0):
        c.remote(("gh", order), lambda order=order: g_stage.at[order], lambda order=order: g_core.at[order], p.core_mate)
    c.remote(("gh", "x"), lambda: g_stage.at[1], lambda: g_x, p.chip_mate)
    c.local("rg", lambda: vm["gm"], lambda: rg_o.at[:, 0, :])

    def grad_h_part(owner):
        return dot(vm["wm"][...], dP[:, pl.ds(pl.multiple_of(owner * tok, tok), tok)])

    def core_grad(order):
        chip = lax.rem(p.chip + order, 2)
        g_stage[order] = grad_h_part(2 * chip + 1 - p.core).astype(BF16)
        c.start(("gh", order))

    def keep_grad(order):
        chip = lax.rem(p.chip + order, 2)
        g_acc[...] = grad_h_part(2 * chip + p.core)

    def chip_grad():
        c.wait(("gh", 1))
        g_stage[1] = (g_acc[...] + g_core[1].astype(F32)).astype(BF16)
        c.start(("gh", "x"))

    def own_grad():
        c.wait(("gh", 0))
        g_acc[...] += g_core[0].astype(F32)

    def input_grad():
        c.wait("x", "gm", ("gh", "x"))
        vm["gm"][...] += norm_back(vm["x"][...], column(gain_one), g_acc[...] + g_x[...].astype(F32))
        c.start("rg")

    def send_dw(k):
        rows = slice(Q_HEADS[k][0] * 3 * hd, (Q_HEADS[k][-1] + 1) * 3 * hd)
        grad = dot_nt(vm["hT"][...], dP[rows, :]).astype(BF16)
        fold = folds(grad.shape[1])
        count = share // fold
        for s in range(blocks):
            cells = [grad[s * share + f * count : s * share + (f + 1) * count] for f in range(fold)]
            dws[k][s * count : (s + 1) * count, :] = jnp.concatenate(cells, axis=1)
        c.start(*[("dw", k, what) for what in DW])

    special = {GRAD_H: [lambda: core_grad(1), lambda: core_grad(0), lambda: keep_grad(1), chip_grad, lambda: keep_grad(0)]}
    special[GRAD_H] += [own_grad, input_grad]
    special[SEND] = [lambda k=k: send_dw(k) for k in range(len(Q_HEADS))]

    def step(which, phase):
        if which in special:
            special[which][phase]()
            return
        if which >= Q0 and phase == 3:
            c.wait(*[("dw", which - Q0, what) for what in DW])
        sums[which].phase(phase)

    def steps_at(place, *now):
        for at, names in PLAN.get(place, {}).items():
            same = None
            for want, have in zip(at, now):
                same = (have == want) if same is None else same & (have == want)

            def run():
                for which, phase in names:
                    step(which, phase)

            run() if same is None else pl.when(same)(run)

    first = BACK_IN[:8]
    c.start(*first)
    greet(p.all_mates())
    steps_at(START)
    c.start(*BACK_IN[8:])
    c.wait(*first)
    dqT = vm["oT"]
    doT, kk, vv, kT, qT, lse, start = (vm[x] for x in ("doT", "k", "v", "kT", "qT", "lse", "start"))

    def make_delta(h, carry):
        rows = pl.ds(pl.multiple_of(h * hd, hd), hd)
        delta[h] = jnp.sum(doT[rows, :].astype(F32) * vm["oT"][rows, :], axis=0, keepdims=True)
        return carry

    lax.fori_loop(0, heads, make_delta, 0)
    dqT[...] = jnp.zeros_like(dqT)
    dkT[...] = jnp.zeros_like(dkT)
    dvT[...] = jnp.zeros_like(dvT)
    steps_at(READY)

    def pair(h, i, j, causal):
        hr = pl.ds(pl.multiple_of(h * hd, hd), hd)
        qs, ks = (pl.ds(pl.multiple_of(at * tok, tok), tok) for at in (i, j))
        q_blk, do_blk = qT[hr, qs], doT[hr, qs]
        s = dot(kk[h, ks, :], q_blk)
        e = jnp.exp(s - lse[h, :, qs])
        at = lax.broadcasted_iota(jnp.int32, s.shape, 0)
        keep = at >= start[:, qs] - j * tok
        if causal:
            keep = keep & (at <= lax.broadcasted_iota(jnp.int32, s.shape, 1))
        e = jnp.where(keep, e, 0.0)
        dp = dot(vv[h, ks, :], do_blk)
        ds = (e * (dp - delta[h, :, qs])).astype(BF16)
        dvT[hr, ks] += dot_nt(do_blk, e.astype(BF16))
        dkT[hr, ks] += dot_nt(q_blk, ds)
        dqT[hr, qs] += dot(kT[hr, ks], ds)

    def prior(h, carry):
        pair(h, 0, 0, False)
        hr = pl.ds(pl.multiple_of(h * hd, hd), hd)
        prior_out[h, 0:hd, :] = dkT[hr, 0:tok].astype(BF16)
        prior_out[h, hd : 2 * hd, :] = dvT[hr, 0:tok].astype(BF16)
        for k in range(heads):
            @pl.when(h == k)
            def _():
                c.start(("prior", k))
        steps_at(PRIOR, h)
        return carry

    lax.fori_loop(0, heads, prior, 0)

    def close(h):
        hr = pl.ds(pl.multiple_of(h * hd, hd), hd)
        last = pl.ds(row, tok)
        dkT[hr, last] += prior_in[h, 0:hd, :].astype(F32)
        dvT[hr, last] += prior_in[h, hd : 2 * hd, :].astype(F32)
        base = h * 3 * hd
        for k, (src, at) in enumerate(((dqT, 0), (dkT, tok), (dvT, tok))):
            val = src[hr, at:]
            val = val * (1.0 / math.sqrt(hd)) if k == 0 else val
            dP[pl.ds(pl.multiple_of(base + k * hd, hd), hd), :] = val.astype(BF16)

    def head(h, carry):
        def full(t, carry):
            i = jnp.where(t < 3, 3, jnp.where(t < 5, 2, 1))
            j = jnp.where(t < 3, t + 1, jnp.where(t < 5, t - 2, 1))
            pair(h, i, j, False)
            steps_at(FULL, h, t)
            return carry

        lax.fori_loop(0, 6, full, 0)

        def diagonal(i, carry):
            pair(h, i, i + 1, True)
            steps_at(DIAGONAL, h, i)
            return carry

        lax.fori_loop(0, blocks, diagonal, 0)
        for k in range(heads):
            @pl.when(h == k)
            def _():
                if k == 0:
                    c.wait("hT", "wm")
                c.wait(("prior", k))
        close(h)
        steps_at(CLOSE, h)
        return carry

    lax.fori_loop(0, heads, head, 0)
    steps_at(END)

    for one in sums.values():
        one.p7()
    c.wait("rg")


def back_pass(n, tok, blocks, ins, down_half, down_ready, gu, go, gain, parts):
    heads = ins[1].shape[0]
    row = blocks * tok
    width = ins[8].shape[0]
    mine = heads * HD
    share, part = width // blocks, width // 2
    v = lambda *s, t=BF16: pltpu.VMEM(s, t)
    o = lambda *s, t=BF16: jax.ShapeDtypeStruct(s, t)
    scratch = [v(width - 1, tok, t=F32) if name == "x" else pltpu.VMEM(a.shape, a.dtype) for name, a in zip(BACK_IN, ins)]
    scratch += [
        v(mine, row + tok, t=F32), v(mine, row + tok, t=F32), v(heads, 1, row, t=F32), v(3 * mine, row),
        v(heads, 2 * HD, tok), v(heads, 2 * HD, tok),
        v(2, width, tok), v(2, width, tok), v(width, tok), v(width, tok, t=F32),
    ]
    sums = back_sums(n, width, share, part)
    scratch += [v(*one[5:]) for one in sums[Q0:]]
    copies = len(ins) + 5 * heads + 8
    for _, mode, way, _, _, rows, cols in sums:
        scratch += Sum.scratch(mode, way, rows, cols, n)
        copies += 17 + n // 8
    scratch.append(pltpu.SemaphoreType.DMA((2, copies)))
    hbm = pl.BlockSpec(memory_space=pl.ANY)
    vmem = pl.BlockSpec(memory_space=pltpu.VMEM)
    return pl.pallas_call(
        functools.partial(back_kernel, n, tok, blocks, heads, parts),
        out_shape=[o(width, width), o(share, parts * width), o(share, width), o(width - 1, 1, tok, t=F32)]
        + [o(*one[5:]) for one in sums[Q0:]],
        in_specs=[hbm] * (len(ins) + 4) + [vmem],
        out_specs=[hbm] * (4 + len(Q_HEADS)),
        scratch_shapes=scratch,
        compiler_params=pltpu.CompilerParams(collective_id=1, has_side_effects=True, vmem_limit_bytes=VMEM_LIMIT),
    )(*ins, down_half, down_ready, gu, go, gain)


def last_kernel(blocks, *refs):
    new, rg, down, up, out, w_qkv, w_up, gain_one, gain_two = refs[:9]
    q_in = refs[9 : 9 + len(Q_HEADS)]
    refs = refs[9 + len(Q_HEADS) :]
    new_o, rg_o, gain_one_o, gain_two_o, qkv_o, out_o, up_o, down_o = refs[:8]
    down_v, up_v, out_v, wq, wu, gcol, down_f, up_f, out_f, qkv_f, x_v, sems = refs[8:19] + refs[-1:]
    q_v = refs[19:-1]
    s = lax.axis_index("seq")
    share, width = out_v.shape
    mine, hd = width // blocks, HD
    c = Copies(sems)
    my_rows = lambda ref: ref.at[rows_at(s * share, share)]
    loads = list(zip(q_in, q_v)) + [(my_rows(w_qkv), wq), (up, up_v), (down, down_v), (out, out_v), (my_rows(w_up), wu)]
    for k, (src, dst) in enumerate(loads):
        c.local(("in", k), lambda src=src: src, lambda dst=dst: dst)
    for k, (src, dst) in enumerate(((up_f, up_o), (down_f, down_o), (out_f, out_o), (qkv_f, qkv_o))):
        c.local(("out", k), lambda src=src: src, lambda dst=dst: dst)
    for k, (src, dst) in enumerate(((new, new_o), (rg, rg_o))):
        c.local(("x in", k), lambda k=k, src=src: src.at[:, 0, :], lambda k=k: x_v.at[k])
        c.local(("x out", k), lambda k=k: x_v.at[k], lambda k=k, dst=dst: dst.at[:, 0, :])
    at = len(q_in)
    c.start(*[("in", k) for k in range(at + 2)], ("x in", 0), ("x in", 1), *[("in", k) for k in range(at + 2, len(loads))])

    def row_of(col):
        return jnp.broadcast_to(col, (share, 128)).T[0:1, :]

    def my_gain(gain):
        gcol[...] = column(gain)
        return gcol[pl.ds(pl.multiple_of(s * share, share), share), :]

    c.wait(*[("in", k) for k in range(at + 1)])
    total = jnp.zeros((share, 1), F32)
    for k in range(3):
        for o in range(blocks):
            cells = []
            for src, hs in zip(q_v, Q_HEADS):
                fold, cols = folds(share * len(hs)), share * len(hs)
                rows = slice(o * share // fold, (o + 1) * share // fold)
                for h in range(len(hs)):
                    lanes = [f * cols + (h * 3 + k) * hd for f in range(fold)]
                    cells.append(jnp.concatenate([src[rows, lane : lane + hd] for lane in lanes], axis=0))
            cells = jnp.concatenate(cells, axis=1).astype(F32)
            cols = slice(k * width + o * mine, k * width + (o + 1) * mine)
            qkv_f[:, cols] = cells
            total = total + jnp.sum(cells * wq[:, cols].astype(F32), axis=1, keepdims=True)
    c.start(("out", 3))
    for k, (src, dst) in enumerate(((up_v, up_f), (down_v, down_f), (out_v, out_f))):
        c.wait(("in", at + 1 + k))
        dst[...] = src[...].astype(F32)
        c.start(("out", k))
        if k < 2:
            c.wait(("x in", k))
            c.start(("x out", k))
    c.wait(("in", at + 4))
    gain_two_o[...] = row_of(jnp.sum(up_f[...] * wu[...].astype(F32), axis=1, keepdims=True) / my_gain(gain_two))
    gain_one_o[...] = row_of(total / my_gain(gain_one))
    c.wait(("x out", 0), ("x out", 1), *[("out", k) for k in range(4)])


def last_pass(blocks, new, rg, down, up, out, qs, w_qkv, w_up, gain_one, gain_two):
    share, width = out.shape
    v = lambda *s, t=BF16: pltpu.VMEM(s, t)
    f = lambda *s: jax.ShapeDtypeStruct(s, F32)
    hbm = pl.BlockSpec(memory_space=pl.ANY)
    vmem = pl.BlockSpec(memory_space=pltpu.VMEM)
    scratch = [
        v(*down.shape), v(*up.shape), v(*out.shape), v(share, 3 * width), v(*up.shape), v(width, 1, t=F32),
        v(*down.shape, t=F32), v(*up.shape, t=F32), v(*out.shape, t=F32), v(share, 3 * width, t=F32),
        v(2, new.shape[0], new.shape[2], t=F32),
    ]
    scratch += [v(*q.shape) for q in qs] + [pltpu.SemaphoreType.DMA((1, 20))]
    return pl.pallas_call(
        functools.partial(last_kernel, blocks),
        out_shape=[f(*new.shape), f(*rg.shape), f(1, share), f(1, share), f(share, 3 * width), f(*out.shape), f(*up.shape), f(*down.shape)],
        in_specs=[hbm] * 7 + [vmem] * 2 + [hbm] * len(qs),
        out_specs=[hbm, hbm, vmem, vmem] + [hbm] * 4,
        scratch_shapes=scratch,
        compiler_params=pltpu.CompilerParams(vmem_limit_bytes=VMEM_LIMIT),
    )(new, rg, down, up, out, w_qkv, w_up, gain_one, gain_two, *qs)


def per_device(residual, documents, gain_one, gain_two, w_qkv, w_out, w_up, w_down, cotangent):
    blocks = lax.axis_size("seq")
    n = lax.axis_size("batch")
    tok = residual.shape[1]
    x = jnp.transpose(residual, (2, 0, 1))
    cot = jnp.transpose(cotangent, (2, 0, 1))
    attT, hT, kT, qT, oT, lse, start, k, v, w_mine, grad_gelu, grad_two = fore_pass(
        n, tok, blocks, x, gain_one, documents, w_qkv, cot, w_down
    )
    new, grad_middle, doT, grad_up, grad_out, down_half, down_ready = mid_pass(
        n, blocks, x, cot, attT, gain_two, w_out, w_up, w_down, grad_gelu, grad_two
    )
    sum_down, sum_up, sum_out, grad_x, *sum_qkv = back_pass(
        n, tok, blocks, (doT, k, v, kT, qT, oT, lse, start, hT, w_mine, x, grad_middle),
        down_half, down_ready, grad_up, grad_out, gain_one, w_up.shape[1] // w_up.shape[0],
    )
    new, grad_x, one, two, sum_qkv, sum_out, sum_up, sum_down = last_pass(
        blocks, new, grad_x, sum_down, sum_up, sum_out, sum_qkv, w_qkv, w_up, gain_one, gain_two
    )
    new, grad_x = jnp.transpose(new, (1, 2, 0)), jnp.transpose(grad_x, (1, 2, 0))
    return (new, grad_x, one[0], two[0], sum_qkv, sum_out, sum_up, sum_down)


def solution(mesh):
    placed = (
        P("batch", "seq", None),
        P("batch", "seq"),
        P(),
        P(),
        P(),
        P(),
        P(),
        P(),
        P("batch", "seq", None),
    )
    return jax.shard_map(
        per_device,
        mesh=mesh,
        in_specs=placed,
        out_specs=(
            P("batch", "seq", None),
            P("batch", "seq", None),
            P("seq"),
            P("seq"),
            P("seq", None),
            P("seq", None),
            P("seq", None),
            P("seq", None),
        ),
        check_vma=False,
    )
```

```python
import functools
import math

import jax
import jax.numpy as jnp
from jax import lax
from jax.experimental import pallas as pl
from jax.experimental.pallas import tpu as pltpu
from jax.sharding import PartitionSpec as P

H = 12
HD = 64
EPSILON = 1e-06
NEG = -1e30
F32, BF16 = jnp.float32, jnp.bfloat16
VMEM_LIMIT = 62 * 2**20


def dot(a, b):
    return lax.dot_general(a, b, (((1,), (0,)), ((), ())), preferred_element_type=F32)


def dot_nt(a, b):
    return lax.dot_general(a, b, (((1,), (1,)), ((), ())), preferred_element_type=F32)


def dot_tn(a, b):
    return lax.dot_general(a, b, (((0,), (0,)), ((), ())), preferred_element_type=F32)


def expand(narrow):
    return jnp.concatenate([narrow, -jnp.sum(narrow, axis=0, keepdims=True)], axis=0)


def shrink(full_vec):
    return full_vec[:-1] - jnp.mean(full_vec, axis=0, keepdims=True)


def shrink_back(grad_narrow):
    padded = jnp.concatenate([grad_narrow, jnp.zeros_like(grad_narrow[:1])], axis=0)
    return padded - jnp.sum(grad_narrow, axis=0, keepdims=True) / padded.shape[0]


def root(full_vec):
    return lax.rsqrt(jnp.mean(full_vec * full_vec, axis=0, keepdims=True) + EPSILON)


def norm_back(narrow, gain, grad_h):
    full_vec = expand(narrow)
    r = root(full_vec)
    scaled = gain * grad_h
    grad_full = r * (scaled - full_vec * (r * r * jnp.mean(scaled * full_vec, axis=0, keepdims=True)))
    return grad_full[:-1] - grad_full[-1:]


def column(gain_ref):
    return jnp.broadcast_to(gain_ref[...].reshape(1, gain_ref.shape[0]), (8, gain_ref.shape[0])).T[:, 0:1]


MESH = pl.DeviceIdType.MESH


class Place:
    def __init__(self, n):
        self.s = lax.axis_index("seq")
        self.b = lax.axis_index("batch")
        self.core = lax.rem(self.s, 2)
        self.chip = self.s // 2
        self.y = lax.rem(self.b, 2)
        self.z = lax.rem(self.b // 2, 4)
        self.far = self.b // 8
        self.n = n

    def core_mate(self):
        return (self.s + 1 - 2 * self.core, self.b)

    def chip_mate(self):
        return (self.s + 2 - 4 * self.chip, self.b)

    def cross_mate(self):
        return (3 - self.s, self.b)

    def y_mate(self):
        return (self.s, self.b + 1 - 2 * self.y)

    def z_of(self, d):
        return lax.rem(self.z + d, 4)

    def z_mate(self, d):
        return (self.s, self.b + 2 * (self.z_of(d) - self.z))

    def z_pair(self, bit):
        here = lax.rem(self.z // bit, 2)
        return (self.s, self.b + 2 * bit * (1 - 2 * here))

    def far_mate(self, d):
        f = lax.rem(self.far + d, self.n // 8)
        return (self.s, self.b + 8 * (f - self.far))

    def next_row(self):
        return (self.s, lax.rem(self.b + 1, self.n))

    def prior_row(self):
        return (self.s, lax.rem(self.b + self.n - 1, self.n))

    def all_mates(self):
        mates = [self.core_mate(), self.chip_mate(), self.cross_mate(), self.y_mate()]
        mates += [self.z_mate(d) for d in (1, 2, 3)]
        mates += [self.far_mate(d) for d in range(1, self.n // 8)]
        return mates + [self.next_row(), self.prior_row()]


def greet(mates):
    barrier = pltpu.get_barrier_semaphore()
    for mate in mates:
        pl.semaphore_signal(barrier, inc=1, device_id=mate, device_id_type=MESH)
    pl.semaphore_wait(barrier, len(mates))


class Copies:
    def __init__(self, sems):
        self.sems, self.made = sems, {}

    def remote(self, name, src, dst, mate):
        k = len(self.made)

        def make():
            return pltpu.make_async_remote_copy(
                src_ref=src(),
                dst_ref=dst(),
                send_sem=self.sems.at[0, k],
                recv_sem=self.sems.at[1, k],
                device_id=mate(),
                device_id_type=MESH,
            )

        assert name not in self.made
        self.made[name] = make

    def local(self, name, src, dst):
        k = len(self.made)

        def make():
            return pltpu.make_async_copy(src(), dst(), self.sems.at[0, k])

        assert name not in self.made
        self.made[name] = make

    def start(self, *names):
        for name in names:
            self.made[name]().start()

    def wait(self, *names):
        for name in names:
            self.made[name]().wait()

    def wait_recv(self, *names):
        for name in names:
            self.made[name]().wait_recv()

    def wait_send(self, *names):
        for name in names:
            self.made[name]().wait_send()


def rows_at(at, count):
    return pl.ds(pl.multiple_of(at, 16), count)


def blockwise(rows, body):
    step = next(s for s in (48, 32, 16) if rows % s == 0)

    def one(i, carry):
        body(i * step, step)
        return carry

    lax.fori_loop(0, rows // step, one, 0)


PAIRS, QUARTERS, PAIRS_Z = range(3)


class Sum:
    def __init__(self, place, copies, name, mode, way, src, first, rows, cols, bufs, out):
        self.p, self.c, self.name, self.mode, self.way = place, copies, name, mode, way
        bits = [(place.y, place.y_mate), (lax.rem(place.z, 2), lambda: place.z_pair(1))]
        (self.one, self.one_mate), (self.two, self.two_mate) = bits[::-1] if way == PAIRS_Z else bits
        self.src, self.first, self.rows, self.cols, self.out = src, first, rows, cols, out
        bufs = list(bufs)
        self.own, self.ry, self.rz, self.res, self.rf = bufs[:5]
        self.rc = bufs[5] if mode in "xy" else None
        self.rx = bufs[-1] if mode not in ("share", "ready") else None
        self.mine = (lambda: self.own.at[self.p.chip]) if mode in "xy" else (lambda: self.own.at[0])
        self.define()

    @staticmethod
    def scratch(mode, way, rows, cols, n):
        def v(*s):
            return pltpu.VMEM(s, BF16)

        half, spot = rows // 2, rows // (8 if way == QUARTERS else 4)
        out = [v(2 if mode in "xy" else 1, rows, cols), v(2 if mode == "y" else 1, half, cols)]
        out += [v(3 if way == QUARTERS else 2, spot, cols), v(rows, cols), v(n // 8 if n > 8 else 1, spot if n > 8 else 16, cols)]
        if mode in "xy":
            out.append(v(2, rows, cols))
        if mode not in ("share", "ready"):
            out.append(v(rows if mode == "x" else half, cols))
        return out

    def id(self, what):
        return (self.name, what)

    def at_half(self, one):
        return rows_at(one * (self.rows // 2), self.rows // 2)

    def at_spot(self):
        p, half = self.p, self.rows // 2
        if self.way == QUARTERS:
            return rows_at(p.y * half + p.z * (half // 4), half // 4)
        return rows_at(self.one * half + self.two * (half // 2), half // 2)

    def define(self):
        p, c, half, far = self.p, self.c, self.rows // 2, self.p.n // 8
        if self.mode in "xy":
            first = pl.ds(self.first, self.rows)
            for order in (1, 0):
                chip = lambda order=order: lax.rem(p.chip + order, 2)
                c.remote(
                    self.id(("core", order)),
                    lambda chip=chip: self.src.at[2 * chip() + 1 - p.core, first],
                    lambda chip=chip: self.rc.at[chip()],
                    p.core_mate,
                )
                c.local(
                    self.id(("own", order)),
                    lambda chip=chip: self.src.at[2 * chip() + p.core, first],
                    lambda chip=chip: self.own.at[chip()],
                )
        other = lambda: self.own.at[1 - p.chip]
        if self.mode == "x":
            c.remote(self.id("x"), other, lambda: self.rx, p.chip_mate)
        if self.mode == "y":
            c.remote(self.id("y1"), lambda: other().at[self.at_half(1 - self.one)], lambda: self.ry.at[1], self.one_mate)
            c.remote(self.id("x"), lambda: other().at[self.at_half(self.one)], lambda: self.rx, p.chip_mate)
        if self.mode == "ready":
            c.local(self.id("own"), lambda: self.src, lambda: self.own.at[0, self.at_half(self.one)])
        if self.mode == "half":
            c.remote(self.id("x"), lambda: self.src.at[1 - p.chip], lambda: self.rx, p.chip_mate)
            c.local(self.id("own"), lambda: self.src.at[p.chip], lambda: self.own.at[0, self.at_half(self.one)])
        elif self.mode != "ready":
            c.remote(self.id("y"), lambda: self.mine().at[self.at_half(1 - self.one)], lambda: self.ry.at[0], self.one_mate)
        spot = lambda: self.res.at[self.at_spot()]
        if self.way == QUARTERS:
            for d in (2, 1, 3):
                c.remote(
                    self.id(("z", d)),
                    lambda d=d: self.mine().at[rows_at(p.y * half + p.z_of(d) * (half // 4), half // 4)],
                    lambda d=d: self.rz.at[3 - d],
                    lambda d=d: p.z_mate(d),
                )
                c.remote(self.id(("bz", d)), spot, spot, lambda d=d: p.z_mate(d))
        else:
            away = lambda: rows_at(self.one * half + (1 - self.two) * (half // 2), half // 2)
            c.remote(self.id("z1"), lambda: self.mine().at[away()], lambda: self.rz.at[0], self.two_mate)
            c.remote(self.id("z2"), lambda: self.mine().at[self.at_spot()], lambda: self.rz.at[1], lambda: p.z_pair(2))
            c.remote(self.id("bz1"), spot, spot, self.two_mate)
        for d in range(1, far):
            c.remote(self.id(("far", d)), lambda: self.rf.at[p.far], lambda: self.rf.at[p.far], lambda d=d: p.far_mate(d))
        my_half = lambda: self.res.at[self.at_half(self.one)]
        c.remote(self.id("by"), my_half, my_half, self.one_mate)
        for k, (src, dst) in enumerate(self.out):
            c.local(self.id(("out", k)), lambda src=src: self.res.at[src], lambda dst=dst: dst)

    def add(self, dst, at, rows, *others):
        def body(first, step):
            here = rows_at(at + first, step)
            total = dst[here, :].astype(F32)
            for other, offset in others:
                total = total + other[rows_at(offset + first, step), :].astype(F32)
            dst[here, :] = total.astype(BF16)

        blockwise(rows, body)

    def p0(self):
        if self.mode == "half":
            self.c.start(self.id("x"), self.id("own"))
        if self.mode == "ready":
            self.c.start(self.id("own"))
        if self.mode in "xy":
            for order in (1, 0):
                self.c.start(self.id(("core", order)), self.id(("own", order)))

    def p1(self):
        self.c.wait(self.id(("core", 1)), self.id(("own", 1)))
        other = 1 - self.p.chip
        self.add(self.own.at[other], 0, self.rows, (self.rc.at[other], 0))
        self.c.start(self.id("x" if self.mode == "x" else "y1"))

    def p1b(self):
        self.c.wait(self.id(("core", 0)), self.id(("own", 0)))
        self.add(self.mine(), 0, self.rows, (self.rc.at[self.p.chip], 0))
        if self.mode == "y":
            self.c.start(self.id("y"))

    def p2(self):
        half = self.rows // 2
        if self.mode == "y":
            self.c.wait(self.id("y1"))
            self.add(self.own.at[1 - self.p.chip], self.one * half, half, (self.ry.at[1], 0))
            self.c.start(self.id("x"))
            return
        if self.mode == "x":
            self.c.wait(self.id("x"))
            self.add(self.mine(), (1 - self.one) * half, half, (self.rx, (1 - self.one) * half))
        self.c.start(self.id("y"))

    def p3(self):
        half, more = self.rows // 2, []
        if self.mode not in ("half", "ready"):
            self.c.wait(self.id("y"))
            more.append((self.ry.at[0], 0))
        if self.mode == "x":
            more.append((self.rx, self.one * half))
        if self.mode in ("y", "half"):
            self.c.wait(self.id("x"))
            more.append((self.rx, 0))
        if self.mode in ("half", "ready"):
            self.c.wait(self.id("own"))
        self.add(self.mine(), self.one * half, half, *more)
        self.c.start(*([self.id(("z", d)) for d in (2, 1, 3)] if self.way == QUARTERS else [self.id("z1")]))

    def total(self, *others):
        p = self.p
        spot, rows = self.at_spot(), self.at_spot().size
        own, far = self.mine(), p.n // 8

        def body(first, step):
            here = rows_at(spot.start + first, step)
            there = rows_at(first, step)
            total = own[here, :].astype(F32)
            for other in others:
                total = total + other[there, :].astype(F32)
            if far > 1:
                self.rf[p.far, there, :] = total.astype(BF16)
            else:
                self.res[here, :] = total.astype(BF16)

        blockwise(rows, body)
        if far > 1:
            self.c.start(*[self.id(("far", d)) for d in range(1, far)])
            self.c.wait(*[self.id(("far", d)) for d in range(1, far)])

            def more(first, step):
                there = rows_at(first, step)
                total = self.rf[0, there, :].astype(F32)
                for k in range(1, far):
                    total = total + self.rf[k, there, :].astype(F32)
                self.res[rows_at(spot.start + first, step), :] = total.astype(BF16)

            blockwise(rows, more)

    def p4(self):
        if self.way == QUARTERS:
            self.c.wait(*[self.id(("z", d)) for d in (1, 2, 3)])
            self.total(*[self.rz.at[d] for d in range(3)])
            self.c.start(*[self.id(("bz", d)) for d in (2, 1, 3)])
            return
        self.c.wait(self.id("z1"))
        spot = self.at_spot()
        self.add(self.mine(), spot.start, spot.size, (self.rz.at[0], 0))
        self.c.start(self.id("z2"))

    def p4b(self):
        if not self.way == QUARTERS:
            self.c.wait(self.id("z2"))
            self.total(self.rz.at[1])
            self.c.start(self.id("bz1"))

    def p5(self):
        self.c.wait(*([self.id(("bz", d)) for d in (1, 2, 3)] if self.way == QUARTERS else [self.id("bz1")]))
        self.c.start(self.id("by"))

    def p6(self):
        self.c.wait(self.id("by"))
        self.c.start(*[self.id(("out", k)) for k in range(len(self.out))])

    def p7(self):
        self.c.wait(*[self.id(("out", k)) for k in range(len(self.out))])

    def phase(self, k):
        (self.p0, self.p1, self.p1b, self.p2, self.p3, self.p4, self.p4b, self.p5, self.p6)[k]()


PRIOR_KV = (("pk", 0), ("pk", 1), ("pv", 0), ("pv", 1))


def fore_kernel(n, tok, blocks, heads, *refs):
    x, gain, docs, w, cot, w_down = refs[:6]
    attT_o, hT_o, kT_o, qT_o, oT_o, lse_o, start_o, k_o, v_o, wm_o, gg_o, g2_o = refs[6:18]
    xs, ws, wm, hT, docs_all, prior_docs, start, kT, vT, qT, kk, vv, acc, m_ref, l_ref, lse, stage, cs, wd, gg, g2, sems = refs[18:]
    width = xs.shape[0] + 1
    row = blocks * tok
    mine = heads * HD
    p = Place(n)
    c = Copies(sems)
    mates = {"core": p.core_mate, "chip": p.chip_mate, "cross": p.cross_mate}
    block = lambda at: pl.ds(pl.multiple_of(at * tok, tok), tok)
    here = lambda: block(p.s)
    c.local("w", lambda: w, lambda: ws)
    c.local("cot", lambda: cot.at[:, 0, :], lambda: cs)
    c.local("wd", lambda: w_down, lambda: wd)
    c.local("gg", lambda: gg, lambda: gg_o)
    c.local("g2", lambda: g2, lambda: g2_o)
    c.local("docs", lambda: docs, lambda: docs_all.at[:, here()])
    for name, mate in mates.items():
        c.remote(("docs", name), lambda: docs, lambda: docs_all.at[:, here()], mate)
    last = pl.ds(row - tok, tok)
    c.remote("old docs", lambda: docs_all.at[:, last], lambda: prior_docs, p.next_row)
    c.remote("hc", lambda: hT.at[:, here()], lambda: hT.at[:, here()], p.core_mate)
    half = tok // 2
    for k in range(2):
        c.local(("x", k), lambda k=k: x.at[:, 0, pl.ds(k * half, half)], lambda k=k: xs.at[:, pl.ds(k * half, half)])
        piece = lambda s, k=k: hT.at[:, pl.ds(pl.multiple_of(s * tok + k * half, half), half)]
        c.remote(("hx", k), lambda piece=piece: piece(p.s), lambda piece=piece: piece(p.s), p.chip_mate)
        other = lambda piece=piece: piece(p.chip_mate()[0])
        c.remote(("ho", k), other, other, p.core_mate)
    for k in range(2):
        end, to = pl.ds(row + k * half, half), pl.ds(k * half, half)
        c.remote(("pk", k), lambda end=end: kT.at[:, end], lambda to=to: kT.at[:, to], p.next_row)
        c.remote(("pv", k), lambda end=end: vT.at[:, end], lambda to=to: vT.at[:, to], p.next_row)
    for h in range(heads):
        spot = lambda h=h: attT_o.at[pl.ds(pl.multiple_of(p.s * mine + h * HD, HD), HD)]
        for name, mate in mates.items():
            src = lambda h=h, mate=mate: stage.at[pl.ds(h * HD, HD), block(mate()[0])]
            c.remote(("att", h, name), src, spot, mate)
        c.local(("att", h, "own"), lambda h=h: stage.at[pl.ds(h * HD, HD), here()], spot)
    outs = {"hT": (hT, hT_o), "kT": (kT, kT_o), "qT": (qT, qT_o), "oT": (acc, oT_o), "lse": (lse, lse_o)}
    outs.update({"start": (start, start_o), "k": (kk, k_o), "v": (vv, v_o), "wm": (wm, wm_o)})
    for name, (src, dst) in outs.items():
        c.local(("out", name), lambda src=src: src, lambda dst=dst: dst)

    c.start(("x", 0), ("x", 1), "docs", "w")
    greet([p.core_mate(), p.chip_mate(), p.cross_mate(), p.next_row(), p.prior_row()])
    c.start(*[("docs", name) for name in mates])
    gain_col = column(gain)
    for k in range(2):
        c.wait(("x", k))
        full_vec = expand(xs[:, k * half : (k + 1) * half])
        mine_now = pl.ds(pl.multiple_of(p.s * tok + k * half, half), half)
        hT[:, mine_now] = (gain_col * full_vec * root(full_vec)).astype(BF16)
        c.start(("hx", k))
    c.start("hc", "cot", "wd")

    c.wait("w")
    for s in range(blocks):
        @pl.when(p.s == s)
        def _():
            for h in range(heads):
                for k in range(3):
                    at = k * width + s * mine + h * HD
                    to = (h * 3 + k) * HD
                    wm[:, to : to + HD] = ws[:, at : at + HD]

    c.wait("docs", *[("docs", name) for name in mates])
    c.start("old docs")
    ids = jnp.broadcast_to(docs_all[...], (8, row))
    pos = lax.broadcasted_iota(jnp.int32, (8, row), 1)
    since = jnp.where((ids != pltpu.roll(ids, 1, 1)) | (pos == 0), pos, 0)
    hop = 1
    while hop < row:
        since = jnp.maximum(since, jnp.where(pos >= hop, pltpu.roll(since, hop, 1), 0))
        hop *= 2
    start[...] = since[0:1] + tok
    m_ref[...] = jnp.full(m_ref.shape, NEG, F32)
    l_ref[...] = jnp.zeros(l_ref.shape, F32)
    acc[...] = jnp.zeros(acc.shape, F32)

    def natural(keys_at, count):
        keys = pl.ds(pl.multiple_of(keys_at, 128), count)
        for h in range(heads):
            kk[h, keys, :] = kT[h * HD : (h + 1) * HD, keys].T
            vv[h, keys, :] = vT[h * HD : (h + 1) * HD, keys].T

    def project(at, count):
        own, keys = pl.ds(pl.multiple_of(at, 128), count), pl.ds(pl.multiple_of(at + tok, 128), count)
        packed = dot_tn(wm[...], hT[:, own]).astype(BF16)
        for h in range(heads):
            to, base = slice(h * HD, (h + 1) * HD), h * 3 * HD
            qT[to, own] = packed[base : base + HD] * jnp.bfloat16(1.0 / math.sqrt(HD))
            kT[to, keys] = packed[base + HD : base + 2 * HD]
            vT[to, keys] = packed[base + 2 * HD : base + 3 * HD]
        natural(at + tok, count)

    def pair(h, q0, qw, k0, kw, causal):
        hr = pl.ds(pl.multiple_of(h * HD, HD), HD)
        qs, ks = pl.ds(pl.multiple_of(q0, 128), qw), pl.ds(pl.multiple_of(k0 + tok, 128), kw)
        s = dot(kk[h, ks, :], qT[hr, qs])
        at = lax.broadcasted_iota(jnp.int32, s.shape, 0)
        keep = at >= start[:, qs] - (k0 + tok)
        if causal:
            keep = keep & (at <= lax.broadcasted_iota(jnp.int32, s.shape, 1))
        s = jnp.where(keep, s, NEG)
        m = m_ref[h, :, qs]
        new_m = jnp.maximum(m, jnp.max(s, axis=0, keepdims=True))
        e = jnp.exp(s - new_m)
        shift = jnp.exp(m - new_m)
        m_ref[h, :, qs] = new_m
        l_ref[h, :, qs] = l_ref[h, :, qs] * shift + jnp.sum(e, axis=0, keepdims=True)
        acc[hr, qs] = acc[hr, qs] * shift + dot(vT[hr, ks], e.astype(BF16))

    def finish(h, i):
        hr, qs = pl.ds(pl.multiple_of(h * HD, HD), HD), block(i)
        out = acc[hr, qs] / l_ref[h, :, qs]
        acc[hr, qs] = out
        stage[hr, qs] = out.astype(BF16)
        lse[h, :, qs] = m_ref[h, :, qs] + jnp.log(l_ref[h, :, qs])

    def send_att(h, zero):
        for name, mate in list(mates.items()) + [("own", lambda: (p.s,))]:
            @pl.when((mate()[0] == 0) == zero)
            def _():
                c.start(("att", h, name))

    pair_rows = 2 * tok
    near, far = pair_rows * p.chip, pair_rows * (1 - p.chip)
    c.wait_recv("hc")
    lax.fori_loop(0, 2, lambda t, carry: (project(near + t * tok, tok), carry)[1], 0)

    def send_prior(k):
        c.start(("pk", k), ("pv", k))

    @pl.when(p.chip == 1)
    def _():
        send_prior(0)
        send_prior(1)

    lax.fori_loop(0, heads, lambda h, carry: (pair(h, near, pair_rows, near, pair_rows, True), carry)[1], 0)

    def forward(k):
        c.wait_recv(("hx", k))
        c.start(("ho", k))

    def far_half(k):
        project(p.chip_mate()[0] * tok + k * half, half)

        def one(t, carry):
            @pl.when(t == heads)
            def _():
                c.wait_recv(("ho", k))
                project(p.cross_mate()[0] * tok + k * half, half)

                @pl.when(p.chip == 0)
                def _():
                    send_prior(k)

            h = lax.rem(t, heads)
            at = jnp.where(t < heads, p.core, 1 - p.core) * tok + k * half

            @pl.when(p.chip == 0)
            def _():
                pair(h, pair_rows + at, half, 0, pair_rows, False)

            @pl.when(p.chip == 1)
            def _():
                pair(h, pair_rows, pair_rows, at, half, False)

            return carry

        lax.fori_loop(0, 2 * heads, one, 0)

    forward(0)
    c.wait("cot", "wd")
    g2[...] = shrink_back(cs[...]).astype(BF16)
    c.start("g2")

    def grad_gelu(t, carry):
        its = pl.ds(pl.multiple_of(t * width, width), width)
        gg[its, :] = dot(wd[its, :], g2[...]).astype(BF16)
        return carry

    lax.fori_loop(0, wd.shape[0] // width, grad_gelu, 0)
    c.start("gg")
    far_half(0)
    forward(1)
    far_half(1)

    def second(h, carry):
        pair(h, far, pair_rows, far, pair_rows, True)
        lax.fori_loop(1, blocks, lambda i, carry: (finish(h, i), carry)[1], 0)
        for k in range(heads):
            @pl.when(h == k)
            def _():
                send_att(k, False)
        return carry

    lax.fori_loop(0, heads, second, 0)
    c.wait_recv("old docs")
    from_doc = docs_all[:, 0:1]
    at = lax.broadcasted_iota(jnp.int32, (1, tok), 1)
    run = jnp.max(jnp.where(prior_docs[...] != from_doc, at + 1, 0), axis=1, keepdims=True)
    start[:, 0:tok] = jnp.where(start[:, 0:tok] == tok, run, start[:, 0:tok])
    c.wait_recv(*PRIOR_KV)
    natural(0, tok)
    early = ("hT", "wm", "qT", "kT", "k", "v", "start")
    c.start(*[("out", name) for name in early])

    def third(h, carry):
        pair(h, 0, tok, -tok, tok, False)
        finish(h, 0)
        for k in range(heads):
            @pl.when(h == k)
            def _():
                send_att(k, True)
        return carry

    lax.fori_loop(0, heads, third, 0)
    c.start(*[("out", name) for name in outs if name not in early])
    c.wait_send("hc", ("hx", 0), ("hx", 1), ("ho", 0), ("ho", 1), "old docs", *PRIOR_KV)
    for h in range(heads):
        c.wait(*[("att", h, name) for name in list(mates) + ["own"]])
    c.wait("gg", "g2", *[("out", name) for name in outs])


def fore_pass(n, tok, blocks, x, gain, docs, w, cot, w_down):
    width, heads = w.shape[0], H // blocks
    row, mine = blocks * tok, heads * HD
    v = lambda *s, t=BF16: pltpu.VMEM(s, t)
    o = lambda *s, t=BF16: jax.ShapeDtypeStruct(s, t)
    hbm = pl.BlockSpec(memory_space=pl.ANY)
    scratch = [
        v(width - 1, tok, t=F32), v(width, 3 * width), v(width, 3 * mine), v(width, row),
        v(1, row, t=jnp.int32), v(1, tok, t=jnp.int32), v(1, row, t=jnp.int32),
        v(mine, row + tok), v(mine, row + tok), v(mine, row), v(heads, row + tok, HD), v(heads, row + tok, HD),
        v(mine, row, t=F32), v(heads, 1, row, t=F32), v(heads, 1, row, t=F32), v(heads, 1, row, t=F32), v(mine, row),
        v(width - 1, tok, t=F32), v(*w_down.shape), v(w_down.shape[0], tok), v(width, tok),
        pltpu.SemaphoreType.DMA((2, 31 + 4 * heads)),
    ]
    return pl.pallas_call(
        functools.partial(fore_kernel, n, tok, blocks, heads),
        out_shape=[
            o(width, tok), o(width, row), o(mine, row + tok), o(mine, row), o(mine, row, t=F32), o(heads, 1, row, t=F32),
            o(1, row, t=jnp.int32), o(heads, row + tok, HD), o(heads, row + tok, HD), o(width, 3 * mine),
            o(w_down.shape[0], tok), o(width, tok),
        ],
        in_specs=[hbm, pl.BlockSpec(memory_space=pltpu.VMEM)] + [hbm] * 4,
        out_specs=[hbm] * 12,
        scratch_shapes=scratch,
        compiler_params=pltpu.CompilerParams(collective_id=0, has_side_effects=True, vmem_limit_bytes=VMEM_LIMIT),
    )(x, gain, docs, w, cot, w_down)


def gelu_both(v, grad):
    rate = math.sqrt(2.0 / math.pi)
    square = v * v
    th = jnp.tanh(rate * v * (1.0 + 0.044715 * square))
    up = 0.5 * (1.0 + th)
    slope = up + 0.5 * v * (1.0 - th * th) * (rate * (1.0 + 3.0 * 0.044715 * square))
    return (v * up).astype(BF16), (grad * slope).astype(BF16)


def mid_kernel(n, blocks, *refs):
    x, cot, attT, gain, w_out, w_up, w_down, gg_in, g2_in = refs[:9]
    new_o, gm_o, doT_o, gu_o, go_o, half_o, ready_o = refs[9:16]
    xs, cs, at, wo, wu, wd, mid, h2, g2, g1, gg, geluT, gupT, dw, rc, ry, rx, ga, gu, go, sems = refs[16:]
    tok, width = xs.shape[1], xs.shape[0] + 1
    parts = wu.shape[1] // width
    share = width // blocks
    p = Place(n)
    c = Copies(sems)
    mates = {"cross": p.cross_mate, "chip": p.chip_mate, "core": p.core_mate}
    c.local("att", lambda: attT, lambda: at)
    c.local("wo", lambda: w_out, lambda: wo)
    c.local("x", lambda: x.at[:, 0, :], lambda: xs)
    c.local("cot", lambda: cot.at[:, 0, :], lambda: cs)
    c.local("wu", lambda: w_up, lambda: wu)
    c.local("wd", lambda: w_down, lambda: wd)
    c.local("gg", lambda: gg_in, lambda: gg)
    c.local("g2", lambda: g2_in, lambda: g2)
    c.remote(("core", 0), lambda: dw.at[0], lambda: rc.at[0], p.core_mate)
    c.remote(("core", 1), lambda: dw.at[2], lambda: rc.at[1], p.core_mate)
    part = width // 2
    fourth = part // 2
    low = lambda y: rows_at(y * fourth, fourth)
    for t in range(2):
        c.remote(("y", t), lambda t=t: dw.at[2 * t + 1, low(1 - p.y)], lambda t=t: ry.at[t], p.y_mate)
        dst = lambda t=t: half_o.at[1 - p.chip if t == 0 else p.chip]
        c.local(("half", t), lambda t=t: dw.at[2 * t + 1, low(p.y)], dst)
    high = pl.ds(part, part)
    c.remote("chip", lambda: dw.at[1, high], lambda: rx, p.chip_mate)
    later = lambda y: rows_at(part + y * fourth, fourth)
    c.remote(("y", 2), lambda: dw.at[3, later(1 - p.y)], lambda: ry.at[2], p.y_mate)
    c.local("ready", lambda: dw.at[3, later(p.y)], lambda: ready_o)
    there = lambda: doT_o.at[:, pl.ds(pl.multiple_of(p.s * tok, tok), tok)]
    for name, mate in mates.items():
        c.remote(("ga", name), lambda mate=mate: ga.at[rows_at(mate()[0] * share, share)], there, mate)
    c.local(("ga", "own"), lambda: ga.at[rows_at(p.s * share, share)], there)
    c.local("new", lambda: xs, lambda: new_o.at[:, 0, :])
    c.local("gm", lambda: cs, lambda: gm_o)
    for k in range(parts):
        c.local(("gu", k), lambda k=k: gu.at[:, pl.ds(k * share, share)], lambda k=k: gu_o.at[:, pl.ds(k * share, share)])
    c.local("go", lambda: go, lambda: go_o)

    c.start("att", "wo", "x", "wu", "gg", "g2", "cot", "wd")
    greet([p.core_mate(), p.chip_mate(), p.cross_mate(), p.y_mate()])
    c.wait("att", "wo")
    branch_one = dot_tn(wo[...], at[...])
    c.wait("x")
    mid[...] = xs[...] + shrink(branch_one)
    full_vec = expand(mid[...])
    gain_col = column(gain)
    h2[...] = (gain_col * full_vec * root(full_vec)).astype(BF16)
    c.wait("wu", "gg", "g2")

    def add(dst, at, src, rows):
        def body(first, step):
            r = rows_at(at + first, step)
            dw[dst, r, :] = (dw[dst, r, :].astype(F32) + src[rows_at(first, step), :].astype(F32)).astype(BF16)

        blockwise(rows, body)

    def chip_sum(t):
        c.wait_recv(("core", t))
        add(2 * t + 1, 0, rc.at[t], width)
        c.start(("y", t), *(["chip"] if t == 0 else []))

    def y_sum(t):
        c.wait(("y", t))
        add(2 * t + 1, p.y * fourth, ry.at[t], fourth)
        c.start(("half", t))

    def piece(t, carry):
        s = jnp.where(t == 0, p.cross_mate()[0], jnp.where(t == 1, p.chip_mate()[0], jnp.where(t == 2, p.core_mate()[0], p.s)))
        its = pl.ds(pl.multiple_of(s * width, width), width)
        gelu, grad_up = gelu_both(dot_tn(wu[:, its], h2[...]), gg[its, :].astype(F32))
        geluT[its, :] = gelu
        gupT[its, :] = grad_up
        dw[t] = dot_nt(geluT[its, :], g2[...]).astype(BF16)

        @pl.when(t == 0)
        def _():
            c.start(("core", 0))

        @pl.when(t == 2)
        def _():
            c.start(("core", 1))

        @pl.when(t == 1)
        def _():
            chip_sum(0)

        return carry

    lax.fori_loop(0, parts, piece, 0)
    chip_sum(1)
    grad_h = dot(wu[...], gupT[...])
    c.wait("cot")
    grad_middle = cs[...] + norm_back(mid[...], gain_col, grad_h)
    cs[...] = grad_middle
    g1[...] = shrink_back(grad_middle).astype(BF16)
    ga[...] = dot(wo[...], g1[...]).astype(BF16)
    c.start(*[("ga", name) for name in list(mates) + ["own"]])
    c.start("gm")
    def up_grad(k, carry):
        its = pl.ds(pl.multiple_of(k * width, width), width)
        grad = dot_nt(h2[...], gupT[its, :]).astype(BF16)
        for s in range(blocks):
            gu[s, rows_at(k * share, share), :] = grad[s * share : (s + 1) * share]
        return carry

    lax.fori_loop(0, parts // 2, up_grad, 0)
    c.wait("chip")
    add(3, part, rx, part)
    c.start(("y", 2))
    lax.fori_loop(parts // 2, parts, up_grad, 0)
    c.start(*[("gu", k) for k in range(parts)])
    out_grad = dot_nt(at[...], g1[...]).astype(BF16)
    for s in range(blocks):
        for k in range(2):
            go[s, k * share : (k + 1) * share, :] = out_grad[s * share : (s + 1) * share, k * part : (k + 1) * part]
    c.start("go")
    c.wait("wd")
    xs[...] = mid[...] + shrink(dot_tn(wd[...], geluT[...]))
    c.start("new")
    y_sum(0)
    y_sum(1)
    c.wait(("y", 2))
    add(3, part + p.y * fourth, ry.at[2], fourth)
    c.start("ready")
    c.wait_send(("core", 0), ("core", 1))
    c.wait(*[("ga", name) for name in list(mates) + ["own"]])
    c.wait("gm", "new", "go", "ready", ("half", 0), ("half", 1), *[("gu", k) for k in range(parts)])


def mid_pass(n, blocks, x, cot, attT, gain, w_out, w_up, w_down, gg, g2):
    width, tok = attT.shape
    parts, share = w_up.shape[1] // width, width // blocks
    v = lambda *s, t=BF16: pltpu.VMEM(s, t)
    o = lambda *s, t=BF16: jax.ShapeDtypeStruct(s, t)
    hbm = pl.BlockSpec(memory_space=pl.ANY)
    scratch = [
        v(width - 1, tok, t=F32), v(width - 1, tok, t=F32), v(width, tok), v(width, width), v(*w_up.shape), v(*w_down.shape),
        v(width - 1, tok, t=F32), v(width, tok), v(width, tok), v(width, tok), v(*gg.shape), v(*gg.shape), v(*gg.shape), v(4, width, width), v(2, width, width), v(3, width // 4, width), v(width // 2, width),
        v(width, tok), v(blocks, parts * share, width), v(blocks, 2 * share, width // 2),
        pltpu.SemaphoreType.DMA((2, 32)),
    ]
    return pl.pallas_call(
        functools.partial(mid_kernel, n, blocks),
        out_shape=[
            o(width - 1, 1, tok, t=F32), o(width - 1, tok, t=F32), o(share, blocks * tok), o(blocks, parts * share, width),
            o(blocks, 2 * share, width // 2), o(2, width // 4, width), o(width // 4, width),
        ],
        in_specs=[hbm] * 3 + [pl.BlockSpec(memory_space=pltpu.VMEM)] + [hbm] * 5,
        out_specs=[hbm] * 7,
        scratch_shapes=scratch,
        compiler_params=pltpu.CompilerParams(collective_id=2, has_side_effects=True, vmem_limit_bytes=VMEM_LIMIT),
    )(x, cot, attT, gain, w_out, w_up, w_down, gg, g2)


BACK_IN = ("doT", "k", "v", "kT", "qT", "oT", "lse", "start", "hT", "wm", "x", "gm")
DW = ("cross", "chip", "core", "own")
D0, D1, U0, U1, O, Q0, Q1, GRAD_H, SEND = range(9)
Q_HEADS = ((0, 1), (2,))
U_MODES = ("x", "x")
O_MODE = "y"
WAYS = (PAIRS, PAIRS, PAIRS, PAIRS, PAIRS, PAIRS_Z, PAIRS)
START, READY, PRIOR, FULL, DIAGONAL, CLOSE, END = range(7)
PLAN = {
    START: {
        (): [(D0, 0), (U1, 0), (U0, 0), (D1, 0), (O, 0)],
    },
    READY: {
        (): [(U1, 1), (D1, 4)],
    },
    PRIOR: {
        (0,): [(U1, 2)],
        (1,): [(U0, 1), (U0, 2)],
        (2,): [(D0, 4), (D1, 5), (O, 1), (O, 2)],
    },
    FULL: {
        (1, 0): [(D0, 5), (U1, 3), (O, 3)],
        (2, 1): [(D0, 6), (U0, 3), (U1, 5), (D1, 7)],
        (2, 4): [(O, 4)],
    },
    DIAGONAL: {
        (1, 0): [(D1, 6)],
        (2, 1): [(D0, 7)],
    },
    CLOSE: {
        (1,): [(U1, 4), (SEND, 0)],
        (2,): [(Q0, 3), (SEND, 1), (U0, 4), (GRAD_H, 0), (GRAD_H, 1), (GRAD_H, 2), (O, 5), (U1, 6)],
    },
    END: {
        (): [(GRAD_H, 3), (Q1, 3), (D1, 8), (GRAD_H, 4), (O, 6), (GRAD_H, 5), (Q0, 4), (U0, 5),
            (D0, 8), (Q1, 4), (U1, 7), (Q0, 5), (O, 7), (U0, 6), (Q1, 5), (GRAD_H, 6),
            (U1, 8), (O, 8), (Q0, 6), (U0, 7), (Q1, 6), (Q0, 7), (Q1, 7), (U0, 8),
            (Q0, 8), (Q1, 8)],
    },
}


def folds(cols):
    return 2 if cols % 128 else 1


def back_sums(n, width, share, part):
    way = lambda k: QUARTERS if n > 8 else WAYS[k]
    half = [(D0 + k, ("half", "ready")[k], way(D0 + k), k, 0, part, width) for k in range(2)]
    up = [(U0 + k, U_MODES[k], way(U0 + k), 0, k * part, part, width) for k in range(2)]
    sums = half + up + [(O, O_MODE, way(O), 1, 0, 2 * share, part)]
    for k, hs in enumerate(Q_HEADS):
        cols = share * len(hs)
        sums.append((Q0 + k, "share", way(Q0 + k), None, 0, width // folds(cols), cols * folds(cols)))
    return sums


def back_kernel(n, tok, blocks, heads, parts, *refs):
    refs = list(refs)
    take = lambda count: [refs.pop(0) for _ in range(count)]
    hbm = dict(zip(BACK_IN, take(len(BACK_IN))))
    down_half, down_ready, gu, go, gain_one = take(5)
    down_o, up_o, out_o, rg_o = take(4)
    qkv_o = take(len(Q_HEADS))
    vm = dict(zip(BACK_IN, take(len(BACK_IN))))
    dkT, dvT, delta, dP, prior_out, prior_in, g_stage, g_core, g_x, g_acc = take(10)
    dws = take(len(Q_HEADS))
    p, hd, row = Place(n), HD, blocks * tok
    mine, width = heads * hd, blocks * heads * hd
    share, part = width // blocks, width // 2
    per_part = part // share
    outs = {D0 + k: [(pl.ds(0, part), down_o.at[pl.ds(k * part, part)])] for k in range(2)}
    for k in range(2):
        outs[U0 + k] = [
            (pl.ds(j * share, share), up_o.at[:, pl.ds((k * per_part + j) * width, width)]) for j in range(per_part)
        ]
    outs[O] = [(pl.ds(k * share, share), out_o.at[:, pl.ds(k * part, part)]) for k in range(2)]
    for k in range(len(Q_HEADS)):
        outs[Q0 + k] = [(pl.ds(0, qkv_o[k].shape[0]), qkv_o[k])]
    plans = back_sums(n, width, share, part)
    bufs = [take(len(Sum.scratch(q[1], q[2], 16, 128, n))) for q in plans]
    c = Copies(refs.pop(0))
    for name in BACK_IN:
        src = (lambda: hbm["x"].at[:, 0, :]) if name == "x" else (lambda name=name: hbm[name])
        c.local(name, src, lambda name=name: vm[name])
    sums = {}
    for (name, mode, way, arr, first, rows, cols), buf in zip(plans, bufs):
        src = None if arr is None else ((down_half, down_ready) if name < U0 else (gu, go))[arr]
        sums[name] = Sum(p, c, name, mode, way, src, first, rows, cols, buf, outs[name])
    qkv = [sums[Q0 + k] for k in range(len(Q_HEADS))]
    for k, one in enumerate(qkv):
        count = one.rows // blocks
        block = lambda ref, s, count=count: ref.at[rows_at(s * count, count)]
        spot = lambda one=one, block=block: block(one.own.at[0], p.s)
        for what, mate in (("cross", p.cross_mate), ("chip", p.chip_mate), ("core", p.core_mate)):
            c.remote(("dw", k, what), lambda k=k, mate=mate, block=block: block(dws[k], mate()[0]), spot, mate)
        c.local(("dw", k, "own"), lambda k=k, block=block: block(dws[k], p.s), spot)
    for k in range(heads):
        c.remote(("prior", k), lambda k=k: prior_out.at[k], lambda k=k: prior_in.at[k], p.prior_row)
    for order in (1, 0):
        c.remote(("gh", order), lambda order=order: g_stage.at[order], lambda order=order: g_core.at[order], p.core_mate)
    c.remote(("gh", "x"), lambda: g_stage.at[1], lambda: g_x, p.chip_mate)
    c.local("rg", lambda: vm["gm"], lambda: rg_o.at[:, 0, :])

    def grad_h_part(owner):
        return dot(vm["wm"][...], dP[:, pl.ds(pl.multiple_of(owner * tok, tok), tok)])

    def core_grad(order):
        chip = lax.rem(p.chip + order, 2)
        g_stage[order] = grad_h_part(2 * chip + 1 - p.core).astype(BF16)
        c.start(("gh", order))

    def keep_grad(order):
        chip = lax.rem(p.chip + order, 2)
        g_acc[...] = grad_h_part(2 * chip + p.core)

    def chip_grad():
        c.wait(("gh", 1))
        g_stage[1] = (g_acc[...] + g_core[1].astype(F32)).astype(BF16)
        c.start(("gh", "x"))

    def own_grad():
        c.wait(("gh", 0))
        g_acc[...] += g_core[0].astype(F32)

    def input_grad():
        c.wait("x", "gm", ("gh", "x"))
        vm["gm"][...] += norm_back(vm["x"][...], column(gain_one), g_acc[...] + g_x[...].astype(F32))
        c.start("rg")

    def send_dw(k):
        rows = slice(Q_HEADS[k][0] * 3 * hd, (Q_HEADS[k][-1] + 1) * 3 * hd)
        grad = dot_nt(vm["hT"][...], dP[rows, :]).astype(BF16)
        fold = folds(grad.shape[1])
        count = share // fold
        for s in range(blocks):
            cells = [grad[s * share + f * count : s * share + (f + 1) * count] for f in range(fold)]
            dws[k][s * count : (s + 1) * count, :] = jnp.concatenate(cells, axis=1)
        c.start(*[("dw", k, what) for what in DW])

    special = {GRAD_H: [lambda: core_grad(1), lambda: core_grad(0), lambda: keep_grad(1), chip_grad, lambda: keep_grad(0)]}
    special[GRAD_H] += [own_grad, input_grad]
    special[SEND] = [lambda k=k: send_dw(k) for k in range(len(Q_HEADS))]

    def step(which, phase):
        if which in special:
            special[which][phase]()
            return
        if which >= Q0 and phase == 3:
            c.wait(*[("dw", which - Q0, what) for what in DW])
        sums[which].phase(phase)

    def steps_at(place, *now):
        for at, names in PLAN.get(place, {}).items():
            same = None
            for want, have in zip(at, now):
                same = (have == want) if same is None else same & (have == want)

            def run():
                for which, phase in names:
                    step(which, phase)

            run() if same is None else pl.when(same)(run)

    first = BACK_IN[:8]
    c.start(*first)
    greet(p.all_mates())
    steps_at(START)
    c.start(*BACK_IN[8:])
    c.wait(*first)
    dqT = vm["oT"]
    doT, kk, vv, kT, qT, lse, start = (vm[x] for x in ("doT", "k", "v", "kT", "qT", "lse", "start"))

    def make_delta(h, carry):
        rows = pl.ds(pl.multiple_of(h * hd, hd), hd)
        delta[h] = jnp.sum(doT[rows, :].astype(F32) * vm["oT"][rows, :], axis=0, keepdims=True)
        return carry

    lax.fori_loop(0, heads, make_delta, 0)
    dqT[...] = jnp.zeros_like(dqT)
    dkT[...] = jnp.zeros_like(dkT)
    dvT[...] = jnp.zeros_like(dvT)
    steps_at(READY)

    def pair(h, i, j, causal):
        hr = pl.ds(pl.multiple_of(h * hd, hd), hd)
        qs, ks = (pl.ds(pl.multiple_of(at * tok, tok), tok) for at in (i, j))
        q_blk, do_blk = qT[hr, qs], doT[hr, qs]
        s = dot(kk[h, ks, :], q_blk)
        e = jnp.exp(s - lse[h, :, qs])
        at = lax.broadcasted_iota(jnp.int32, s.shape, 0)
        keep = at >= start[:, qs] - j * tok
        if causal:
            keep = keep & (at <= lax.broadcasted_iota(jnp.int32, s.shape, 1))
        e = jnp.where(keep, e, 0.0)
        dp = dot(vv[h, ks, :], do_blk)
        ds = (e * (dp - delta[h, :, qs])).astype(BF16)
        dvT[hr, ks] += dot_nt(do_blk, e.astype(BF16))
        dkT[hr, ks] += dot_nt(q_blk, ds)
        dqT[hr, qs] += dot(kT[hr, ks], ds)

    def prior(h, carry):
        pair(h, 0, 0, False)
        hr = pl.ds(pl.multiple_of(h * hd, hd), hd)
        prior_out[h, 0:hd, :] = dkT[hr, 0:tok].astype(BF16)
        prior_out[h, hd : 2 * hd, :] = dvT[hr, 0:tok].astype(BF16)
        for k in range(heads):
            @pl.when(h == k)
            def _():
                c.start(("prior", k))
        steps_at(PRIOR, h)
        return carry

    lax.fori_loop(0, heads, prior, 0)

    def close(h):
        hr = pl.ds(pl.multiple_of(h * hd, hd), hd)
        last = pl.ds(row, tok)
        dkT[hr, last] += prior_in[h, 0:hd, :].astype(F32)
        dvT[hr, last] += prior_in[h, hd : 2 * hd, :].astype(F32)
        base = h * 3 * hd
        for k, (src, at) in enumerate(((dqT, 0), (dkT, tok), (dvT, tok))):
            val = src[hr, at:]
            val = val * (1.0 / math.sqrt(hd)) if k == 0 else val
            dP[pl.ds(pl.multiple_of(base + k * hd, hd), hd), :] = val.astype(BF16)

    def head(h, carry):
        def full(t, carry):
            i = jnp.where(t < 3, 3, jnp.where(t < 5, 2, 1))
            j = jnp.where(t < 3, t + 1, jnp.where(t < 5, t - 2, 1))
            pair(h, i, j, False)
            steps_at(FULL, h, t)
            return carry

        lax.fori_loop(0, 6, full, 0)

        def diagonal(i, carry):
            pair(h, i, i + 1, True)
            steps_at(DIAGONAL, h, i)
            return carry

        lax.fori_loop(0, blocks, diagonal, 0)
        for k in range(heads):
            @pl.when(h == k)
            def _():
                if k == 0:
                    c.wait("hT", "wm")
                c.wait(("prior", k))
        close(h)
        steps_at(CLOSE, h)
        return carry

    lax.fori_loop(0, heads, head, 0)
    steps_at(END)

    for one in sums.values():
        one.p7()
    c.wait("rg")


def back_pass(n, tok, blocks, ins, down_half, down_ready, gu, go, gain, parts):
    heads = ins[1].shape[0]
    row = blocks * tok
    width = ins[8].shape[0]
    mine = heads * HD
    share, part = width // blocks, width // 2
    v = lambda *s, t=BF16: pltpu.VMEM(s, t)
    o = lambda *s, t=BF16: jax.ShapeDtypeStruct(s, t)
    scratch = [v(width - 1, tok, t=F32) if name == "x" else pltpu.VMEM(a.shape, a.dtype) for name, a in zip(BACK_IN, ins)]
    scratch += [
        v(mine, row + tok, t=F32), v(mine, row + tok, t=F32), v(heads, 1, row, t=F32), v(3 * mine, row),
        v(heads, 2 * HD, tok), v(heads, 2 * HD, tok),
        v(2, width, tok), v(2, width, tok), v(width, tok), v(width, tok, t=F32),
    ]
    sums = back_sums(n, width, share, part)
    scratch += [v(*one[5:]) for one in sums[Q0:]]
    copies = len(ins) + 5 * heads + 8
    for _, mode, way, _, _, rows, cols in sums:
        scratch += Sum.scratch(mode, way, rows, cols, n)
        copies += 17 + n // 8
    scratch.append(pltpu.SemaphoreType.DMA((2, copies)))
    hbm = pl.BlockSpec(memory_space=pl.ANY)
    vmem = pl.BlockSpec(memory_space=pltpu.VMEM)
    return pl.pallas_call(
        functools.partial(back_kernel, n, tok, blocks, heads, parts),
        out_shape=[o(width, width), o(share, parts * width), o(share, width), o(width - 1, 1, tok, t=F32)]
        + [o(*one[5:]) for one in sums[Q0:]],
        in_specs=[hbm] * (len(ins) + 4) + [vmem],
        out_specs=[hbm] * (4 + len(Q_HEADS)),
        scratch_shapes=scratch,
        compiler_params=pltpu.CompilerParams(collective_id=1, has_side_effects=True, vmem_limit_bytes=VMEM_LIMIT),
    )(*ins, down_half, down_ready, gu, go, gain)


def last_kernel(blocks, *refs):
    new, rg, down, up, out, w_qkv, w_up, gain_one, gain_two = refs[:9]
    q_in = refs[9 : 9 + len(Q_HEADS)]
    refs = refs[9 + len(Q_HEADS) :]
    new_o, rg_o, gain_one_o, gain_two_o, qkv_o, out_o, up_o, down_o = refs[:8]
    down_v, up_v, out_v, wq, wu, gcol, down_f, up_f, out_f, qkv_f, x_v, sems = refs[8:19] + refs[-1:]
    q_v = refs[19:-1]
    s = lax.axis_index("seq")
    share, width = out_v.shape
    mine, hd = width // blocks, HD
    c = Copies(sems)
    my_rows = lambda ref: ref.at[rows_at(s * share, share)]
    loads = list(zip(q_in, q_v)) + [(my_rows(w_qkv), wq), (up, up_v), (down, down_v), (out, out_v), (my_rows(w_up), wu)]
    for k, (src, dst) in enumerate(loads):
        c.local(("in", k), lambda src=src: src, lambda dst=dst: dst)
    for k, (src, dst) in enumerate(((up_f, up_o), (down_f, down_o), (out_f, out_o), (qkv_f, qkv_o))):
        c.local(("out", k), lambda src=src: src, lambda dst=dst: dst)
    for k, (src, dst) in enumerate(((new, new_o), (rg, rg_o))):
        c.local(("x in", k), lambda k=k, src=src: src.at[:, 0, :], lambda k=k: x_v.at[k])
        c.local(("x out", k), lambda k=k: x_v.at[k], lambda k=k, dst=dst: dst.at[:, 0, :])
    at = len(q_in)
    c.start(*[("in", k) for k in range(at + 2)], ("x in", 0), ("x in", 1), *[("in", k) for k in range(at + 2, len(loads))])

    def row_of(col):
        return jnp.broadcast_to(col, (share, 128)).T[0:1, :]

    def my_gain(gain):
        gcol[...] = column(gain)
        return gcol[pl.ds(pl.multiple_of(s * share, share), share), :]

    c.wait(*[("in", k) for k in range(at + 1)])
    total = jnp.zeros((share, 1), F32)
    for k in range(3):
        for o in range(blocks):
            cells = []
            for src, hs in zip(q_v, Q_HEADS):
                fold, cols = folds(share * len(hs)), share * len(hs)
                rows = slice(o * share // fold, (o + 1) * share // fold)
                for h in range(len(hs)):
                    lanes = [f * cols + (h * 3 + k) * hd for f in range(fold)]
                    cells.append(jnp.concatenate([src[rows, lane : lane + hd] for lane in lanes], axis=0))
            cells = jnp.concatenate(cells, axis=1).astype(F32)
            cols = slice(k * width + o * mine, k * width + (o + 1) * mine)
            qkv_f[:, cols] = cells
            total = total + jnp.sum(cells * wq[:, cols].astype(F32), axis=1, keepdims=True)
    c.start(("out", 3))
    for k, (src, dst) in enumerate(((up_v, up_f), (down_v, down_f), (out_v, out_f))):
        c.wait(("in", at + 1 + k))
        dst[...] = src[...].astype(F32)
        c.start(("out", k))
        if k < 2:
            c.wait(("x in", k))
            c.start(("x out", k))
    c.wait(("in", at + 4))
    gain_two_o[...] = row_of(jnp.sum(up_f[...] * wu[...].astype(F32), axis=1, keepdims=True) / my_gain(gain_two))
    gain_one_o[...] = row_of(total / my_gain(gain_one))
    c.wait(("x out", 0), ("x out", 1), *[("out", k) for k in range(4)])


def last_pass(blocks, new, rg, down, up, out, qs, w_qkv, w_up, gain_one, gain_two):
    share, width = out.shape
    v = lambda *s, t=BF16: pltpu.VMEM(s, t)
    f = lambda *s: jax.ShapeDtypeStruct(s, F32)
    hbm = pl.BlockSpec(memory_space=pl.ANY)
    vmem = pl.BlockSpec(memory_space=pltpu.VMEM)
    scratch = [
        v(*down.shape), v(*up.shape), v(*out.shape), v(share, 3 * width), v(*up.shape), v(width, 1, t=F32),
        v(*down.shape, t=F32), v(*up.shape, t=F32), v(*out.shape, t=F32), v(share, 3 * width, t=F32),
        v(2, new.shape[0], new.shape[2], t=F32),
    ]
    scratch += [v(*q.shape) for q in qs] + [pltpu.SemaphoreType.DMA((1, 20))]
    return pl.pallas_call(
        functools.partial(last_kernel, blocks),
        out_shape=[f(*new.shape), f(*rg.shape), f(1, share), f(1, share), f(share, 3 * width), f(*out.shape), f(*up.shape), f(*down.shape)],
        in_specs=[hbm] * 7 + [vmem] * 2 + [hbm] * len(qs),
        out_specs=[hbm, hbm, vmem, vmem] + [hbm] * 4,
        scratch_shapes=scratch,
        compiler_params=pltpu.CompilerParams(vmem_limit_bytes=VMEM_LIMIT),
    )(new, rg, down, up, out, w_qkv, w_up, gain_one, gain_two, *qs)


def per_device(residual, documents, gain_one, gain_two, w_qkv, w_out, w_up, w_down, cotangent):
    blocks = lax.axis_size("seq")
    n = lax.axis_size("batch")
    tok = residual.shape[1]
    x = jnp.transpose(residual, (2, 0, 1))
    cot = jnp.transpose(cotangent, (2, 0, 1))
    attT, hT, kT, qT, oT, lse, start, k, v, w_mine, grad_gelu, grad_two = fore_pass(
        n, tok, blocks, x, gain_one, documents, w_qkv, cot, w_down
    )
    new, grad_middle, doT, grad_up, grad_out, down_half, down_ready = mid_pass(
        n, blocks, x, cot, attT, gain_two, w_out, w_up, w_down, grad_gelu, grad_two
    )
    sum_down, sum_up, sum_out, grad_x, *sum_qkv = back_pass(
        n, tok, blocks, (doT, k, v, kT, qT, oT, lse, start, hT, w_mine, x, grad_middle),
        down_half, down_ready, grad_up, grad_out, gain_one, w_up.shape[1] // w_up.shape[0],
    )
    new, grad_x, one, two, sum_qkv, sum_out, sum_up, sum_down = last_pass(
        blocks, new, grad_x, sum_down, sum_up, sum_out, sum_qkv, w_qkv, w_up, gain_one, gain_two
    )
    new, grad_x = jnp.transpose(new, (1, 2, 0)), jnp.transpose(grad_x, (1, 2, 0))
    return (new, grad_x, one[0], two[0], sum_qkv, sum_out, sum_up, sum_down)


def solution(mesh):
    placed = (
        P("batch", "seq", None),
        P("batch", "seq"),
        P(),
        P(),
        P(),
        P(),
        P(),
        P(),
        P("batch", "seq", None),
    )
    return jax.shard_map(
        per_device,
        mesh=mesh,
        in_specs=placed,
        out_specs=(
            P("batch", "seq", None),
            P("batch", "seq", None),
            P("seq"),
            P("seq"),
            P("seq", None),
            P("seq", None),
            P("seq", None),
            P("seq", None),
        ),
        check_vma=False,
    )
```
